32 devices in a mesh: dp: 16 (over z, x, core), fsdp: 2 (over y).
Axes of the slice: x: 2, y: 2, z: 4, core: 2. Of those that a mesh axis runs over, the one named last changes fastest.
Arguments:
- tokens: bfloat16 [4096, 1024], P('dp'), may hold values from -8 to 8
- teacher: bfloat16 [32, 6144], P('dp'), may hold values from -8 to 8
- norm_gain: float32 [1024], replicated, may hold values from 0.25 to 1.75
- w_in: bfloat16 [1024, 4096], P(None, 'fsdp'), may hold values from -0.1875 to 0.1875
- b_in: float32 [4096], P('fsdp'), may hold values from -3 to 3
- w_out: bfloat16 [1024, 4096], P(None, 'fsdp'), may hold values from -0.09375 to 0.09375
- b_out: float32 [1024], replicated, may hold values from -3 to 3
- final_gain: float32 [1024], replicated, may hold values from 0.25 to 1.75
Outputs:
- loss_value: float32 [], replicated
- grad_in: bfloat16 [1024, 4096], P('dp', 'fsdp')
- grad_out: bfloat16 [1024, 4096], P('dp', 'fsdp')
The draws below stay inside these ranges and needn't reach their ends.
All inputs are finite; a program needn't handle non-finite values.
Results may differ from the reference program's by a relative error of at most 0.008.
Values may be sent and summed in bfloat16 or wider, within the bound.
No kernel may reach another device: no remote copies, remote signals or barrier semaphores. Data moves between devices by JAX's collectives and lax.ppermute only.
A program may use at most 64 MiB of HBM per device.

```python
import jax
import jax.numpy as jnp
from jax import lax

D = 1024
DT = 6144
H = 4096
P_SIZE = 128
BLOCK = 2
IMAGES = 32
TOKENS = 4096
N_DP = 16


def draw_tokens(key, part):
    image_key, noise_key = jax.random.split(jax.random.fold_in(key, 11))
    image_part = jax.random.normal(image_key, (IMAGES, 1, D), jnp.float32)
    noise_part = jax.random.normal(noise_key, (IMAGES, P_SIZE, D), jnp.float32)
    values = jnp.clip(image_part + noise_part, -8.0, 8.0)
    return values.reshape(TOKENS, D).astype(jnp.bfloat16)


def draw_teacher(key, part):
    common_key, noise_key = jax.random.split(jax.random.fold_in(key, 23))
    common = jax.random.normal(common_key, (1, DT), jnp.float32)
    position = (jnp.arange(IMAGES, dtype=jnp.float32) + 0.5) / IMAGES
    noise = jax.random.normal(noise_key, (IMAGES, DT), jnp.float32)
    strength = 0.9 * position
    values = jnp.clip(noise + strength[:, None] * common, -8.0, 8.0)
    return values.astype(jnp.bfloat16)


def block_scale(rng, shape, shards, smallest, high):
    factor_of = 1.0
    for dim, parts in shards:
        heights = jax.random.uniform(jax.random.fold_in(jax.random.fold_in(rng, 6), dim), (parts,), jnp.float32, smallest / len(shards), high / len(shards))
        factor_of = factor_of * jnp.repeat(jnp.exp(heights), shape[dim] // parts).reshape((-1,) + (1,) * (len(shape) - 1 - dim))
    return factor_of


def gaussian(key, extent, deviation, reach, cuts=(), kind=jnp.bfloat16):
    entries = deviation * jax.random.normal(key, extent, jnp.float32)
    if cuts:
        entries = entries * block_scale(key, extent, cuts, -0.22, 0.18)
    return jnp.clip(entries, -reach, reach).astype(kind)


def setup_inputs(seed: int = 0) -> dict:
    seeds = jax.random.split(jax.random.key(seed), 9)
    tokens = draw_tokens(jax.random.fold_in(seeds[8], 71), 0)
    teacher = draw_teacher(jax.random.fold_in(seeds[8], 71), 0)
    norm_gain = jnp.clip(1.0 + 0.15 * jax.random.normal(seeds[2], (D,), jnp.float32), 0.25, 1.75)
    w_in = gaussian(seeds[3], (D, H), D ** -0.5, 0.1875, ((1, 2),))
    b_in = gaussian(seeds[4], (H,), 0.5, 3.0, ((0, 2),), jnp.float32)
    w_out = gaussian(seeds[5], (D, H), H ** -0.5, 0.09375, ((1, 2),))
    b_out = gaussian(seeds[6], (D,), 0.5, 3.0, (), jnp.float32)
    final_gain = jnp.clip(1.0 + 0.15 * jax.random.normal(seeds[7], (D,), jnp.float32), 0.25, 1.75)
    return dict(tokens=tokens, teacher=teacher, norm_gain=norm_gain, w_in=w_in, b_in=b_in, w_out=w_out, b_out=b_out, final_gain=final_gain)


loss_scale = 4096.0

def gelu_tanh(values):
    inner = 0.7978845608 * (values + 0.044715 * values * values * values)
    return 0.5 * values * (1.0 + jnp.tanh(inner))

def gelu_slope(values):
    inner = 0.7978845608 * (values + 0.044715 * values * values * values)
    tangent = jnp.tanh(inner)
    return 0.5 * (1.0 + tangent) + 0.5 * values * (1.0 - tangent * tangent) * 0.7978845608 * (1.0 + 3.0 * 0.044715 * values * values)

def layer_norm(values, gain_vec):
    centered = values - lax.optimization_barrier(jnp.mean(values, axis=-1, keepdims=True))
    inv_std = lax.rsqrt(lax.optimization_barrier(jnp.mean(centered * centered, axis=-1, keepdims=True)) + 1e-05)
    normed = centered * inv_std
    return (normed * gain_vec, normed, inv_std)

def reference(tokens, teacher, norm_gain, w_in, b_in, w_out, b_out, final_gain):
    tok_blocks = tokens.reshape(N_DP, BLOCK * P_SIZE, D)

    def forward_block(tok_block):
        token_values = tok_block.astype(jnp.float32)
        normed_tokens = layer_norm(token_values, norm_gain)[0].astype(jnp.bfloat16)
        pre_act = jnp.dot(normed_tokens, w_in, preferred_element_type=jnp.float32) + b_in
        pooled = gelu_tanh(pre_act).reshape(BLOCK, P_SIZE, H).mean(axis=1).astype(jnp.bfloat16)
        token_mean = token_values.reshape(BLOCK, P_SIZE, D).mean(axis=1)
        return (pooled, token_mean)
    pooled, token_mean = lax.map(forward_block, tok_blocks)
    pooled = pooled.reshape(IMAGES, H)
    token_mean = token_mean.reshape(IMAGES, D)
    branch = lax.dot_general(pooled, w_out, (((1,), (1,)), ((), ())), preferred_element_type=jnp.float32)
    embedding = token_mean + branch + b_out
    scaled_unit, normed_embed, inv_std = layer_norm(embedding, final_gain)
    unit_norm = jnp.sqrt(lax.optimization_barrier(jnp.sum(scaled_unit * scaled_unit, axis=-1, keepdims=True)) + 1e-06)
    unit_dir = scaled_unit / unit_norm
    student = unit_dir.astype(jnp.bfloat16)
    teacher_f = teacher.astype(jnp.float32)
    target = (teacher_f / jnp.sqrt(lax.optimization_barrier(jnp.sum(teacher_f * teacher_f, axis=-1, keepdims=True)) + 1e-06)).astype(jnp.bfloat16)
    resid = jnp.dot(student, student.T, preferred_element_type=jnp.float32) - jnp.dot(target, target.T, preferred_element_type=jnp.float32)
    loss_value = jnp.sum(resid * resid) / IMAGES
    dstudent = loss_scale * 4.0 / IMAGES * jnp.dot(resid.astype(jnp.bfloat16), student, preferred_element_type=jnp.float32)
    dunit = (dstudent - unit_dir * lax.optimization_barrier(jnp.sum(unit_dir * dstudent, axis=-1, keepdims=True))) / unit_norm
    gain_grad = dunit * final_gain
    dembed = inv_std * (gain_grad - lax.optimization_barrier(jnp.mean(gain_grad, axis=-1, keepdims=True)) - normed_embed * lax.optimization_barrier(jnp.mean(gain_grad * normed_embed, axis=-1, keepdims=True)))
    dembed_b = dembed.astype(jnp.bfloat16)
    grad_out = lax.dot_general(dembed_b, pooled, (((0,), (0,)), ((), ())), preferred_element_type=jnp.float32).astype(jnp.bfloat16)
    dpooled = jnp.dot(dembed_b, w_out, preferred_element_type=jnp.float32)

    def grad_block(running, pieces):
        tok_block, dpool_block = pieces
        token_values = tok_block.astype(jnp.float32)
        normed_tokens = layer_norm(token_values, norm_gain)[0].astype(jnp.bfloat16)
        pre_act = jnp.dot(normed_tokens, w_in, preferred_element_type=jnp.float32) + b_in
        slope = gelu_slope(pre_act.reshape(BLOCK, P_SIZE, H))
        dhidden = (dpool_block[:, None, :] / P_SIZE * slope).reshape(BLOCK * P_SIZE, H).astype(jnp.bfloat16)
        term = lax.dot_general(normed_tokens, dhidden, (((0,), (0,)), ((), ())), preferred_element_type=jnp.float32)
        return (running + term, None)
    grad_in, _ = lax.scan(grad_block, jnp.zeros((D, H), jnp.float32), (tok_blocks, dpooled.reshape(N_DP, BLOCK, H)))
    return (loss_value, grad_in.astype(jnp.bfloat16), grad_out)
```

```python
import jax
import jax.numpy as jnp
from jax import lax
from jax.sharding import PartitionSpec as P

loss_scale = 4096.0


def gelu_tanh(values):
    inner = 0.7978845608 * (values + 0.044715 * values * values * values)
    return 0.5 * values * (1.0 + jnp.tanh(inner))


def gelu_slope(values):
    inner = 0.7978845608 * (values + 0.044715 * values * values * values)
    tangent = jnp.tanh(inner)
    return 0.5 * (1.0 + tangent) + 0.5 * values * (1.0 - tangent * tangent) * 0.7978845608 * (
        1.0 + 3.0 * 0.044715 * values * values
    )


def layer_norm(values, gain_vec):
    centered = values - jnp.mean(values, axis=-1, keepdims=True)
    inv_std = lax.rsqrt(jnp.mean(centered * centered, axis=-1, keepdims=True) + 1e-05)
    normed = centered * inv_std
    return (normed * gain_vec, normed, inv_std)


def contract_last(left_side, right_side):
    return lax.dot_general(
        left_side, right_side, (((1,), (1,)), ((), ())), preferred_element_type=jnp.float32
    )


def contract_first(left_side, right_side):
    return lax.dot_general(
        left_side, right_side, (((0,), (0,)), ((), ())), preferred_element_type=jnp.float32
    )


def partner_pairs(count, mask):
    return [(i, i ^ mask) for i in range(count)]


def levels_of(count):
    if count <= 16:
        return [(1, count)]
    inner = 1
    while inner * inner < count:
        inner *= 2
    return [(1, inner), (inner, count // inner)]


def gather_blocks(value, axis):
    count = lax.axis_size(axis)
    for stride, size in levels_of(count):
        parts = [value]
        for step in range(1, size):
            parts.append(lax.ppermute(value, axis, partner_pairs(count, step * stride)))
        value = jnp.concatenate(parts, axis=0)
    return value


def sum_over(value, axis):
    count = lax.axis_size(axis)
    parts = [value]
    for step in range(1, count):
        parts.append(lax.ppermute(value, axis, partner_pairs(count, step)))
    if count <= 2:
        return sum(parts[1:], parts[0])
    stacked = jnp.stack(parts)
    order = jnp.arange(count) ^ lax.axis_index(axis)
    return jnp.sum(jnp.take(stacked, order, axis=0), axis=0)


def body(tokens, teacher, norm_gain, w_in, b_in, w_out, b_out, final_gain):
    dp_size = lax.axis_size("dp")
    fsdp_size = lax.axis_size("fsdp")
    dp_index = lax.axis_index("dp")
    fsdp_index = lax.axis_index("fsdp")
    block_rows = teacher.shape[0]
    model_width = tokens.shape[1]
    per_image = tokens.shape[0] // block_rows
    image_count = block_rows * dp_size
    out_rows = model_width // dp_size

    place = lax.broadcasted_iota(jnp.int32, (image_count, image_count), 0)
    source = lax.broadcasted_iota(jnp.int32, (image_count, image_count), 1)
    reorder = (
        ((place // block_rows) ^ dp_index) * block_rows + place % block_rows == source
    ).astype(jnp.bfloat16)

    def in_order(rows):
        return jnp.dot(reorder, rows, preferred_element_type=jnp.float32).astype(jnp.bfloat16)

    teacher_width = teacher.shape[1] // fsdp_size
    own_teacher = lax.dynamic_slice_in_dim(teacher, fsdp_index * teacher_width, teacher_width, 1)
    all_teacher = in_order(gather_blocks(own_teacher, "dp"))
    target_raw = sum_over(contract_last(all_teacher, all_teacher), "fsdp")
    eye = place == source
    square_col = jnp.sum(jnp.where(eye, target_raw, 0.0), axis=1, keepdims=True)
    square_row = jnp.sum(jnp.where(eye, target_raw, 0.0), axis=0, keepdims=True)
    target_gram = target_raw * lax.rsqrt(square_col + 1e-06) * lax.rsqrt(square_row + 1e-06)

    token_values = tokens.astype(jnp.float32)
    normed_tokens = layer_norm(token_values, norm_gain)[0].astype(jnp.bfloat16)
    pre_act = jnp.dot(normed_tokens, w_in, preferred_element_type=jnp.float32) + b_in
    hidden = pre_act.shape[1]
    pooled = (
        gelu_tanh(pre_act).reshape(block_rows, per_image, hidden).mean(axis=1).astype(jnp.bfloat16)
    )
    token_mean = token_values.reshape(block_rows, per_image, model_width).mean(axis=1)
    own_embedding = token_mean + sum_over(contract_last(pooled, w_out), "fsdp") + b_out

    gathered = in_order(
        gather_blocks(
            jnp.concatenate([own_embedding.astype(jnp.bfloat16), pooled], axis=1), "dp"
        )
    )
    embedding = gathered[:, :model_width].astype(jnp.float32)
    all_pooled = gathered[:, model_width:]
    scaled_unit, normed_embed, inv_std = layer_norm(embedding, final_gain)
    unit_norm = jnp.sqrt(jnp.sum(scaled_unit * scaled_unit, axis=-1, keepdims=True) + 1e-06)
    unit_dir = scaled_unit / unit_norm
    student = unit_dir.astype(jnp.bfloat16)
    resid = contract_last(student, student) - target_gram
    loss_value = jnp.sum(resid * resid) / image_count
    dstudent = (
        loss_scale
        * 4.0
        / image_count
        * jnp.dot(resid.astype(jnp.bfloat16), student, preferred_element_type=jnp.float32)
    )
    dunit = (dstudent - unit_dir * jnp.sum(unit_dir * dstudent, axis=-1, keepdims=True)) / unit_norm
    gain_grad = dunit * final_gain
    dembed = inv_std * (
        gain_grad
        - jnp.mean(gain_grad, axis=-1, keepdims=True)
        - normed_embed * jnp.mean(gain_grad * normed_embed, axis=-1, keepdims=True)
    )
    dembed_b = dembed.astype(jnp.bfloat16)

    own_dembed = lax.dynamic_slice_in_dim(dembed_b, dp_index * block_rows, block_rows, 0)
    dpooled = jnp.dot(own_dembed, w_out, preferred_element_type=jnp.float32)
    slope = gelu_slope(pre_act.reshape(block_rows, per_image, hidden))
    dhidden = (
        (dpooled[:, None, :] / per_image * slope)
        .reshape(block_rows * per_image, hidden)
        .astype(jnp.bfloat16)
    )
    in_term = contract_first(normed_tokens, dhidden).astype(jnp.bfloat16)
    grad_in = lax.psum_scatter(in_term, "dp", scatter_dimension=0, tiled=True)
    out_columns = lax.dynamic_slice_in_dim(dembed_b, dp_index * out_rows, out_rows, 1)
    grad_out = contract_first(out_columns, all_pooled).astype(jnp.bfloat16)
    return (loss_value, grad_in, grad_out)


def solution(mesh):
    return jax.shard_map(
        body,
        mesh=mesh,
        in_specs=(
            P("dp", None),
            P("dp", None),
            P(),
            P(None, "fsdp"),
            P("fsdp"),
            P(None, "fsdp"),
            P(),
            P(),
        ),
        out_specs=(P(), P("dp", "fsdp"), P("dp", "fsdp")),
        check_vma=False,
    )
```

```python
import jax
import jax.numpy as jnp
from jax import lax
from jax.sharding import PartitionSpec as P

loss_scale = 4096.0


def gelu_tanh(values):
    inner = 0.7978845608 * (values + 0.044715 * values * values * values)
    return 0.5 * values * (1.0 + jnp.tanh(inner))


def gelu_slope(values):
    inner = 0.7978845608 * (values + 0.044715 * values * values * values)
    tangent = jnp.tanh(inner)
    return 0.5 * (1.0 + tangent) + 0.5 * values * (1.0 - tangent * tangent) * 0.7978845608 * (
        1.0 + 3.0 * 0.044715 * values * values
    )


def layer_norm(values, gain_vec):
    centered = values - jnp.mean(values, axis=-1, keepdims=True)
    inv_std = lax.rsqrt(jnp.mean(centered * centered, axis=-1, keepdims=True) + 1e-05)
    normed = centered * inv_std
    return (normed * gain_vec, normed, inv_std)


def contract_last(left_side, right_side):
    return lax.dot_general(
        left_side, right_side, (((1,), (1,)), ((), ())), preferred_element_type=jnp.float32
    )


def contract_first(left_side, right_side):
    return lax.dot_general(
        left_side, right_side, (((0,), (0,)), ((), ())), preferred_element_type=jnp.float32
    )


def exchange(blocks, axes):
    return lax.all_to_all(blocks, axes, split_axis=0, concat_axis=0, tiled=True)


def gather_blocks(value, axes):
    count = lax.axis_size(axes)
    return exchange(jnp.broadcast_to(value[None], (count,) + value.shape), axes)


def body(tokens, teacher, norm_gain, w_in, b_in, w_out, b_out, final_gain):
    dp_size = lax.axis_size("dp")
    fsdp_size = lax.axis_size("fsdp")
    dp_index = lax.axis_index("dp")
    fsdp_index = lax.axis_index("fsdp")
    block_rows = teacher.shape[0]
    model_width = tokens.shape[1]
    per_image = tokens.shape[0] // block_rows
    image_count = block_rows * dp_size
    out_rows = model_width // dp_size

    everyone = ("dp", "fsdp")
    slice_width = teacher.shape[1] // (dp_size * fsdp_size)
    teacher_slices = teacher.reshape(block_rows, dp_size, fsdp_size, slice_width)
    own_slices = lax.dynamic_index_in_dim(teacher_slices, fsdp_index, 2, keepdims=False)
    teacher_columns = exchange(own_slices.transpose(1, 0, 2), "dp").reshape(
        image_count, slice_width
    )
    target_part = contract_last(teacher_columns, teacher_columns)

    token_values = tokens.astype(jnp.float32)
    normed_tokens = layer_norm(token_values, norm_gain)[0].astype(jnp.bfloat16)
    pre_act = jnp.dot(normed_tokens, w_in, preferred_element_type=jnp.float32) + b_in
    hidden = pre_act.shape[1]
    pooled = (
        gelu_tanh(pre_act).reshape(block_rows, per_image, hidden).mean(axis=1).astype(jnp.bfloat16)
    )
    token_mean = token_values.reshape(block_rows, per_image, model_width).mean(axis=1)
    branch = contract_last(pooled, w_out)
    shared = jnp.where(fsdp_index == 0, token_mean + b_out, 0.0)
    embed_part = (branch + shared).astype(jnp.bfloat16).reshape(-1)
    if image_count * image_count <= embed_part.size:
        upper = target_part.astype(jnp.bfloat16)
        lower = (target_part - upper.astype(jnp.float32)).astype(jnp.bfloat16)
        payload = jnp.concatenate([embed_part, upper.reshape(-1), lower.reshape(-1)])
        arrived = gather_blocks(payload, everyone)
        embed_parts = arrived[:, : embed_part.size]
        gram_parts = arrived[:, embed_part.size :].astype(jnp.float32)
        target_raw = jnp.sum(
            gram_parts.reshape(-1, image_count, image_count), axis=0
        )
    else:
        embed_parts = gather_blocks(embed_part, everyone)
        target_raw = lax.psum(target_part, everyone)
    embedding = jnp.sum(
        embed_parts.reshape(dp_size, fsdp_size, block_rows, model_width).astype(jnp.float32),
        axis=1,
    ).reshape(image_count, model_width)
    all_pooled = gather_blocks(pooled, "dp").reshape(image_count, hidden)
    eye = jnp.eye(image_count, dtype=bool)
    square_col = jnp.sum(jnp.where(eye, target_raw, 0.0), axis=1, keepdims=True)
    square_row = jnp.sum(jnp.where(eye, target_raw, 0.0), axis=0, keepdims=True)
    target_gram = target_raw * lax.rsqrt(square_col + 1e-06) * lax.rsqrt(square_row + 1e-06)
    scaled_unit, normed_embed, inv_std = layer_norm(embedding, final_gain)
    unit_norm = jnp.sqrt(jnp.sum(scaled_unit * scaled_unit, axis=-1, keepdims=True) + 1e-06)
    unit_dir = scaled_unit / unit_norm
    student = unit_dir.astype(jnp.bfloat16)
    resid = contract_last(student, student) - target_gram
    loss_value = jnp.sum(resid * resid) / image_count
    dstudent = (
        loss_scale
        * 4.0
        / image_count
        * jnp.dot(resid.astype(jnp.bfloat16), student, preferred_element_type=jnp.float32)
    )
    dunit = (dstudent - unit_dir * jnp.sum(unit_dir * dstudent, axis=-1, keepdims=True)) / unit_norm
    gain_grad = dunit * final_gain
    dembed = inv_std * (
        gain_grad
        - jnp.mean(gain_grad, axis=-1, keepdims=True)
        - normed_embed * jnp.mean(gain_grad * normed_embed, axis=-1, keepdims=True)
    )
    dembed_b = dembed.astype(jnp.bfloat16)

    own_dembed = lax.dynamic_slice_in_dim(dembed_b, dp_index * block_rows, block_rows, 0)
    dpooled = jnp.dot(own_dembed, w_out, preferred_element_type=jnp.float32)
    slope = gelu_slope(pre_act.reshape(block_rows, per_image, hidden))
    dhidden = (
        (dpooled[:, None, :] / per_image * slope)
        .reshape(block_rows * per_image, hidden)
        .astype(jnp.bfloat16)
    )
    in_term = contract_first(normed_tokens, dhidden).astype(jnp.bfloat16)
    in_parts = exchange(in_term.reshape(dp_size, out_rows, hidden), "dp")
    grad_in = jnp.sum(in_parts.astype(jnp.float32), axis=0).astype(jnp.bfloat16)
    out_columns = lax.dynamic_slice_in_dim(dembed_b, dp_index * out_rows, out_rows, 1)
    grad_out = contract_first(out_columns, all_pooled).astype(jnp.bfloat16)
    return (loss_value, grad_in, grad_out)


def solution(mesh):
    return jax.shard_map(
        body,
        mesh=mesh,
        in_specs=(
            P("dp", None),
            P("dp", None),
            P(),
            P(None, "fsdp"),
            P("fsdp"),
            P(None, "fsdp"),
            P(),
            P(),
        ),
        out_specs=(P(), P("dp", "fsdp"), P("dp", "fsdp")),
        check_vma=False,
    )
```

```python
import jax
import jax.numpy as jnp
from jax import lax
from jax.sharding import PartitionSpec as P

loss_scale = 4096.0


def gelu_tanh(values):
    inner = 0.7978845608 * (values + 0.044715 * values * values * values)
    return 0.5 * values * (1.0 + jnp.tanh(inner))


def gelu_slope(values):
    inner = 0.7978845608 * (values + 0.044715 * values * values * values)
    tangent = jnp.tanh(inner)
    return 0.5 * (1.0 + tangent) + 0.5 * values * (1.0 - tangent * tangent) * 0.7978845608 * (
        1.0 + 3.0 * 0.044715 * values * values
    )


def layer_norm(values, gain_vec):
    centered = values - jnp.mean(values, axis=-1, keepdims=True)
    inv_std = lax.rsqrt(jnp.mean(centered * centered, axis=-1, keepdims=True) + 1e-05)
    normed = centered * inv_std
    return (normed * gain_vec, normed, inv_std)


def contract_last(left_side, right_side):
    return lax.dot_general(
        left_side, right_side, (((1,), (1,)), ((), ())), preferred_element_type=jnp.float32
    )


def contract_first(left_side, right_side):
    return lax.dot_general(
        left_side, right_side, (((0,), (0,)), ((), ())), preferred_element_type=jnp.float32
    )


def exchange(blocks, axes):
    return lax.all_to_all(blocks, axes, split_axis=0, concat_axis=0, tiled=True)


def gather_blocks(value, axes):
    count = lax.axis_size(axes)
    return exchange(jnp.broadcast_to(value[None], (count,) + value.shape), axes)


def mates_of(dp_size, hidden):
    mates = 4
    while dp_size % mates or hidden % (128 * mates):
        mates //= 2
    return mates


def mate_blocks(value, mates):
    blocks = [value]
    step = mates // 2
    while step:
        pairs = [(i, i ^ step) for i in range(lax.axis_size("dp"))]
        blocks = blocks + [lax.ppermute(block, "dp", pairs) for block in blocks]
        step //= 2
    order = [0]
    step = mates // 2
    while step:
        order = order + [k ^ step for k in order]
        step //= 2
    return [blocks[order.index(k)] for k in range(mates)]


def body(tokens, teacher, norm_gain, w_in, b_in, w_out, b_out, final_gain):
    dp_size = lax.axis_size("dp")
    fsdp_size = lax.axis_size("fsdp")
    dp_index = lax.axis_index("dp")
    fsdp_index = lax.axis_index("fsdp")
    block_rows = teacher.shape[0]
    model_width = tokens.shape[1]
    per_image = tokens.shape[0] // block_rows
    image_count = block_rows * dp_size
    out_rows = model_width // dp_size

    everyone = ("dp", "fsdp")
    mates = mates_of(dp_size, w_in.shape[1])
    share = w_in.shape[1] // mates
    first_unit = (dp_index % mates) * share
    token_values = tokens.astype(jnp.float32)
    normed_tokens = layer_norm(token_values, norm_gain)[0].astype(jnp.bfloat16)
    mate_tokens = jnp.concatenate(mate_blocks(normed_tokens, mates), axis=0)
    all_teacher = gather_blocks(teacher, "dp").reshape(image_count, teacher.shape[1])
    pre_act = jnp.dot(normed_tokens, w_in, preferred_element_type=jnp.float32) + b_in
    hidden = pre_act.shape[1]
    pooled = (
        gelu_tanh(pre_act).reshape(block_rows, per_image, hidden).mean(axis=1).astype(jnp.bfloat16)
    )
    token_mean = token_values.reshape(block_rows, per_image, model_width).mean(axis=1)
    branch = contract_last(pooled, w_out)
    shared = jnp.where(fsdp_index == 0, token_mean + b_out, 0.0)
    embed_part = (branch + shared).astype(jnp.bfloat16).reshape(-1)
    embed_parts = gather_blocks(embed_part, everyone)
    target_raw = contract_last(all_teacher, all_teacher)
    embedding = jnp.sum(
        embed_parts.reshape(dp_size, fsdp_size, block_rows, model_width).astype(jnp.float32),
        axis=1,
    ).reshape(image_count, model_width)
    w_share = lax.dynamic_slice_in_dim(w_in, first_unit, share, 1)
    b_share = lax.dynamic_slice_in_dim(b_in, first_unit, share, 0)
    mate_slope = gelu_slope(
        jnp.dot(mate_tokens, w_share, preferred_element_type=jnp.float32) + b_share
    )
    eye = jnp.eye(image_count, dtype=bool)
    square_col = jnp.sum(jnp.where(eye, target_raw, 0.0), axis=1, keepdims=True)
    square_row = jnp.sum(jnp.where(eye, target_raw, 0.0), axis=0, keepdims=True)
    target_gram = target_raw * lax.rsqrt(square_col + 1e-06) * lax.rsqrt(square_row + 1e-06)
    scaled_unit, normed_embed, inv_std = layer_norm(embedding, final_gain)
    unit_norm = jnp.sqrt(jnp.sum(scaled_unit * scaled_unit, axis=-1, keepdims=True) + 1e-06)
    unit_dir = scaled_unit / unit_norm
    student = unit_dir.astype(jnp.bfloat16)
    resid = contract_last(student, student) - target_gram
    loss_value = jnp.sum(resid * resid) / image_count
    dstudent = (
        loss_scale
        * 4.0
        / image_count
        * jnp.dot(resid.astype(jnp.bfloat16), student, preferred_element_type=jnp.float32)
    )
    dunit = (dstudent - unit_dir * jnp.sum(unit_dir * dstudent, axis=-1, keepdims=True)) / unit_norm
    gain_grad = dunit * final_gain
    dembed = inv_std * (
        gain_grad
        - jnp.mean(gain_grad, axis=-1, keepdims=True)
        - normed_embed * jnp.mean(gain_grad * normed_embed, axis=-1, keepdims=True)
    )
    dembed_b = dembed.astype(jnp.bfloat16)

    mate_dembed = jnp.concatenate(
        [
            lax.dynamic_slice_in_dim(dembed_b, (dp_index ^ k) * block_rows, block_rows, 0)
            for k in range(mates)
        ]
    )
    out_share = lax.dynamic_slice_in_dim(w_out, first_unit, share, 1)
    dpooled = jnp.dot(mate_dembed, out_share, preferred_element_type=jnp.float32)
    dhidden = (
        (dpooled[:, None, :] / per_image * mate_slope.reshape(-1, per_image, share))
        .reshape(-1, share)
        .astype(jnp.bfloat16)
    )
    in_term = contract_first(mate_tokens, dhidden).astype(jnp.bfloat16)
    pooled_rows = pooled.reshape(1, -1, share)
    arrived = exchange(
        jnp.concatenate(
            [
                in_term.reshape(dp_size, out_rows, share),
                jnp.broadcast_to(pooled_rows, (dp_size,) + pooled_rows.shape[1:]),
            ],
            axis=1,
        ),
        "dp",
    )
    in_parts = arrived[:, :out_rows].reshape(-1, mates, out_rows, share)
    grad_in = (
        jnp.sum(in_parts.astype(jnp.float32), axis=0)
        .astype(jnp.bfloat16)
        .transpose(1, 0, 2)
        .reshape(out_rows, hidden)
    )
    all_pooled = arrived[:, out_rows:].reshape(image_count, hidden)
    out_columns = lax.dynamic_slice_in_dim(dembed_b, dp_index * out_rows, out_rows, 1)
    grad_out = contract_first(out_columns, all_pooled).astype(jnp.bfloat16)
    return (loss_value, grad_in, grad_out)


def solution(mesh):
    return jax.shard_map(
        body,
        mesh=mesh,
        in_specs=(
            P("dp", None),
            P("dp", None),
            P(),
            P(None, "fsdp"),
            P("fsdp"),
            P(None, "fsdp"),
            P(),
            P(),
        ),
        out_specs=(P(), P("dp", "fsdp"), P("dp", "fsdp")),
        check_vma=False,
    )
```

```python
import jax
import jax.numpy as jnp
from jax import lax
from jax.experimental import pallas as pl
from jax.experimental.pallas import tpu as pltpu
from jax.sharding import PartitionSpec as P

loss_scale = 4096.0
lanes = 128
f32 = jnp.float32
bf16 = jnp.bfloat16


def gelu_tanh(values):
    inner = 0.7978845608 * (values + 0.044715 * values * values * values)
    return 0.5 * values * (1.0 + jnp.tanh(inner))


def gelu_slope(values):
    square = values * values
    tangent = jnp.tanh(0.7978845608 * (values + 0.044715 * values * square))
    return 0.5 * (1.0 + tangent) + 0.5 * values * (1.0 - tangent * tangent) * 0.7978845608 * (
        1.0 + 3.0 * 0.044715 * square
    )


def contract_last(left_side, right_side):
    return lax.dot_general(
        left_side, right_side, (((1,), (1,)), ((), ())), preferred_element_type=f32
    )


def fold_rows(values, width):
    count = values.shape[1] // width
    return jnp.concatenate(
        [
            values[i : i + 1, k * width : (k + 1) * width]
            for i in range(values.shape[0])
            for k in range(count)
        ],
        axis=0,
    )


def vmem_params(*semantics):
    return pltpu.CompilerParams(vmem_limit_bytes=56 * 2**20)


def norm_tokens(tokens, norm_gain, teacher, copies, fold):
    rows, width = tokens.shape
    images = teacher.shape[0]
    per_image = rows // images

    def kernel(tokens_ref, gain_ref, teacher_ref, normed_ref, mean_ref, out_ref):
        values = tokens_ref[...].astype(f32)
        centered = values - jnp.mean(values, axis=-1, keepdims=True)
        inv_std = lax.rsqrt(jnp.mean(centered * centered, axis=-1, keepdims=True) + 1e-05)
        normed_ref[...] = (centered * inv_std * gain_ref[...]).astype(bf16)
        mean_ref[0] = jnp.mean(values, axis=0, keepdims=True)

        @pl.when(pl.program_id(0) == 0)
        def _():
            folded = fold_rows(teacher_ref[...].astype(f32), fold).astype(bf16)
            out_ref[...] = jnp.broadcast_to(folded[None], out_ref.shape)

    payload = (copies, images * teacher.shape[1] // fold, fold)
    return pl.pallas_call(
        kernel,
        grid=(images,),
        in_specs=[
            pl.BlockSpec((per_image, width), lambda i: (i, 0)),
            pl.BlockSpec((1, width), lambda i: (0, 0)),
            pl.BlockSpec(teacher.shape, lambda i: (0, 0)),
        ],
        out_specs=[
            pl.BlockSpec((per_image, width), lambda i: (i, 0)),
            pl.BlockSpec((1, 1, width), lambda i: (i, 0, 0)),
            pl.BlockSpec(payload, lambda i: (0, 0, 0)),
        ],
        out_shape=[
            jax.ShapeDtypeStruct((rows, width), bf16),
            jax.ShapeDtypeStruct((images, 1, width), f32),
            jax.ShapeDtypeStruct(payload, bf16),
        ],
        compiler_params=vmem_params(),
        cost_estimate=pl.CostEstimate(
            flops=10 * rows * width, bytes_accessed=4 * rows * width, transcendentals=0
        ),
        name="norm_tokens",
    )(tokens, norm_gain[None], teacher)


def forward(first, normed, token_mean, w_in, b_in, w_out, b_out, copies):
    rows, width = normed.shape
    hidden = w_in.shape[1]
    images = token_mean.shape[0]
    per_image = rows // images
    tile = min(512, hidden)
    steps = hidden // tile
    folds = width // lanes

    def kernel(
        first_ref, normed_ref, mean_ref, in_ref, bias_ref, out_w_ref, out_b_ref,
        pooled_ref, payload_ref, total_ref,
    ):
        step = pl.program_id(0)
        pre_act = jnp.dot(normed_ref[...], in_ref[...], preferred_element_type=f32) + bias_ref[...]
        pooled = jnp.mean(gelu_tanh(pre_act).reshape(images, per_image, tile), axis=1).astype(bf16)
        pooled_ref[...] = pooled
        part = contract_last(pooled, out_w_ref[...])

        @pl.when(step == 0)
        def _():
            total_ref[...] = jnp.where(
                first_ref[0] == 0, mean_ref[:, 0, :] + out_b_ref[...], 0.0
            ) + part

        @pl.when(step > 0)
        def _():
            total_ref[...] += part

        @pl.when(step == steps - 1)
        def _():
            folded = fold_rows(total_ref[...], lanes).astype(bf16)
            payload_ref[...] = jnp.broadcast_to(folded[None], payload_ref.shape)

    payload = (copies, images * folds, lanes)
    return pl.pallas_call(
        kernel,
        grid_spec=pltpu.PrefetchScalarGridSpec(
            num_scalar_prefetch=1,
            grid=(steps,),
            in_specs=[
                pl.BlockSpec((rows, width), lambda j, s: (0, 0)),
                pl.BlockSpec((images, 1, width), lambda j, s: (0, 0, 0)),
                pl.BlockSpec((width, tile), lambda j, s: (0, j)),
                pl.BlockSpec((1, tile), lambda j, s: (0, j)),
                pl.BlockSpec((width, tile), lambda j, s: (0, j)),
                pl.BlockSpec((1, width), lambda j, s: (0, 0)),
            ],
            out_specs=[
                pl.BlockSpec((images, tile), lambda j, s: (0, j)),
                pl.BlockSpec(payload, lambda j, s: (0, 0, 0)),
            ],
            scratch_shapes=[pltpu.VMEM((images, width), f32)],
        ),
        out_shape=[
            jax.ShapeDtypeStruct((images, hidden), bf16),
            jax.ShapeDtypeStruct(payload, bf16),
        ],
        compiler_params=vmem_params(),
        cost_estimate=pl.CostEstimate(
            flops=2 * rows * width * hidden,
            bytes_accessed=4 * width * hidden,
            transcendentals=rows * hidden,
        ),
        name="forward",
    )(first, normed, token_mean, w_in, b_in[None], w_out, b_out[None])


def mate_slopes(share_index, blocks, w_in, b_in, share):
    rows, width = blocks[0].shape
    count = len(blocks)

    def kernel(index_ref, *refs):
        token_refs, (in_ref, bias_ref, slope_ref, turned_ref) = refs[:count], refs[count:]
        for k in range(count):
            block = token_refs[k][...]
            pre_act = jnp.dot(block, in_ref[...], preferred_element_type=f32) + bias_ref[...]
            slope_ref[k * rows : (k + 1) * rows] = gelu_slope(pre_act).astype(bf16)
            turned_ref[:, k * rows : (k + 1) * rows] = block.T

    return pl.pallas_call(
        kernel,
        grid_spec=pltpu.PrefetchScalarGridSpec(
            num_scalar_prefetch=1,
            grid=(1,),
            in_specs=[pl.BlockSpec((rows, width), lambda j, s: (0, 0))] * count
            + [
                pl.BlockSpec((width, share), lambda j, s: (0, s[0])),
                pl.BlockSpec((1, share), lambda j, s: (0, s[0])),
            ],
            out_specs=[
                pl.BlockSpec((count * rows, share), lambda j, s: (0, 0)),
                pl.BlockSpec((width, count * rows), lambda j, s: (0, 0)),
            ],
        ),
        out_shape=[
            jax.ShapeDtypeStruct((count * rows, share), bf16),
            jax.ShapeDtypeStruct((width, count * rows), bf16),
        ],
        compiler_params=vmem_params(),
        cost_estimate=pl.CostEstimate(
            flops=2 * rows * count * width * share,
            bytes_accessed=4 * rows * count * width,
            transcendentals=rows * count * share,
        ),
        name="mate_slopes",
    )(share_index, *blocks, w_in, b_in[None])


def target_gram(arrived, images):
    senders, folded, fold = arrived.shape
    folds = senders * folded // images

    def kernel(arrived_ref, gram_ref, wide_ref):
        wide_ref[...] = arrived_ref[...].astype(f32).reshape(images, folds, fold)
        gram = jnp.zeros((images, images), f32)
        for k in range(folds):
            piece = wide_ref[:, k, :].astype(bf16)
            gram += contract_last(piece, piece)
        row = lax.broadcasted_iota(jnp.int32, gram.shape, 0)
        column = lax.broadcasted_iota(jnp.int32, gram.shape, 1)
        diagonal = jnp.where(row == column, gram, 0.0)
        down = lax.rsqrt(jnp.sum(diagonal, axis=1, keepdims=True) + 1e-06)
        across = lax.rsqrt(jnp.sum(diagonal, axis=0, keepdims=True) + 1e-06)
        gram_ref[...] = gram * down * across

    return pl.pallas_call(
        kernel,
        out_shape=jax.ShapeDtypeStruct((images, images), f32),
        scratch_shapes=[pltpu.VMEM((images, folds, fold), f32)],
        compiler_params=vmem_params(),
        cost_estimate=pl.CostEstimate(
            flops=2 * images * images * folds * fold,
            bytes_accessed=2 * images * folds * fold,
            transcendentals=0,
        ),
        name="target_gram",
    )(arrived)


def backward(
    index, arrived, gram, final_gain, pooled, w_out, slope, turned, mates, dp_size, per_image
):
    senders, folded, _ = arrived.shape
    width = w_out.shape[0]
    images = gram.shape[0]
    own_images, hidden = pooled.shape
    fsdp_size = senders // dp_size
    folds = width // lanes
    share = hidden // mates
    mate_rows = turned.shape[1]
    out_rows = width // dp_size
    piece = min(share, 256)
    pieces = share // piece
    extra = own_images * hidden // piece
    group = max(1, 256 // out_rows)
    steps = dp_size // group
    in_rows = out_rows * pieces

    def kernel(
        index_ref, arrived_ref, gram_ref, gain_ref, pooled_ref, out_w_ref, slope_ref, turned_ref,
        loss_ref, dembed_ref, payload_ref, wide_ref, hidden_ref, extra_ref,
    ):
        @pl.when(pl.program_id(0) == 0)
        def _():
            parts = arrived_ref[...].astype(f32).reshape(dp_size, fsdp_size, folded, lanes)
            wide_ref[...] = jnp.sum(parts, axis=1).reshape(images, folds, lanes)
            embedding = jnp.concatenate([wide_ref[:, k, :] for k in range(folds)], axis=1)
            gain = gain_ref[...]
            centered = embedding - jnp.mean(embedding, axis=-1, keepdims=True)
            inv_std = lax.rsqrt(jnp.mean(centered * centered, axis=-1, keepdims=True) + 1e-05)
            normed = centered * inv_std
            scaled = normed * gain
            square = jnp.sum(scaled * scaled, axis=-1, keepdims=True) + 1e-06
            inv_norm = lax.rsqrt(square)
            unit = scaled * inv_norm
            student = unit.astype(bf16)
            resid = contract_last(student, student) - gram_ref[...]
            loss_ref[0, 0] = jnp.sum(resid * resid) / images
            dstudent = (loss_scale * 4.0 / images) * jnp.dot(
                resid.astype(bf16), student, preferred_element_type=f32
            )
            dunit = (
                dstudent - unit * jnp.sum(unit * dstudent, axis=-1, keepdims=True)
            ) * inv_norm
            gain_grad = dunit * gain
            dembed = inv_std * (
                gain_grad
                - jnp.mean(gain_grad, axis=-1, keepdims=True)
                - normed * jnp.mean(gain_grad * normed, axis=-1, keepdims=True)
            )
            dembed_b = dembed.astype(bf16)
            dembed_ref[...] = dembed_b
            shape = (mates * own_images, images)
            row = lax.broadcasted_iota(jnp.int32, shape, 0)
            column = lax.broadcasted_iota(jnp.int32, shape, 1)
            owner = (row // own_images) ^ index_ref[0]
            pick = (owner * own_images + row % own_images == column).astype(f32).astype(bf16)
            mate_dembed = jnp.dot(pick, dembed_b, preferred_element_type=f32).astype(bf16)
            dpooled = jnp.dot(mate_dembed, out_w_ref[...], preferred_element_type=f32) / per_image
            for k in range(mates * own_images):
                rows = slice(k * per_image, (k + 1) * per_image)
                hidden_ref[rows] = (dpooled[k : k + 1] * slope_ref[rows].astype(f32)).astype(bf16)
            extra_ref[...] = fold_rows(pooled_ref[...].astype(f32), piece).astype(bf16)

        term = jnp.dot(turned_ref[...], hidden_ref[...], preferred_element_type=f32).astype(bf16)
        for d in range(group):
            for k in range(pieces):
                payload_ref[d, k * out_rows : (k + 1) * out_rows] = term[
                    d * out_rows : (d + 1) * out_rows, k * piece : (k + 1) * piece
                ]
            payload_ref[d, in_rows:] = extra_ref[...]

    return pl.pallas_call(
        kernel,
        grid_spec=pltpu.PrefetchScalarGridSpec(
            num_scalar_prefetch=1,
            grid=(steps,),
            in_specs=[
                pl.BlockSpec(arrived.shape, lambda j, s: (0, 0, 0)),
                pl.BlockSpec(gram.shape, lambda j, s: (0, 0)),
                pl.BlockSpec((1, width), lambda j, s: (0, 0)),
                pl.BlockSpec(pooled.shape, lambda j, s: (0, 0)),
                pl.BlockSpec((width, share), lambda j, s: (0, s[0] % mates)),
                pl.BlockSpec(slope.shape, lambda j, s: (0, 0)),
                pl.BlockSpec((group * out_rows, mate_rows), lambda j, s: (j, 0)),
            ],
            out_specs=[
                pl.BlockSpec(memory_space=pltpu.SMEM),
                pl.BlockSpec((images, width), lambda j, s: (0, 0)),
                pl.BlockSpec((group, in_rows + extra, piece), lambda j, s: (j, 0, 0)),
            ],
            scratch_shapes=[
                pltpu.VMEM((images, folds, lanes), f32),
                pltpu.VMEM((mate_rows, share), bf16),
                pltpu.VMEM((extra, piece), bf16),
            ],
        ),
        out_shape=[
            jax.ShapeDtypeStruct((1, 1), f32),
            jax.ShapeDtypeStruct((images, width), bf16),
            jax.ShapeDtypeStruct((dp_size, in_rows + extra, piece), bf16),
        ],
        compiler_params=vmem_params(),
        cost_estimate=pl.CostEstimate(
            flops=2 * mate_rows * width * share,
            bytes_accessed=2 * mate_rows * (width + share),
            transcendentals=0,
        ),
        name="backward",
    )(index, arrived, gram, final_gain[None], pooled, w_out, slope, turned)


def finish(index, arrived, dembed, mates, hidden):
    dp_size, rows, piece = arrived.shape
    images, width = dembed.shape
    out_rows = width // dp_size
    pieces = hidden // mates // piece
    in_rows = out_rows * pieces
    folds = hidden // piece

    def kernel(index_ref, arrived_ref, dembed_ref, in_ref, out_ref, wide_ref):
        for q in range(mates):
            total = jnp.sum(
                jnp.stack([arrived_ref[s, :in_rows].astype(f32) for s in range(q, dp_size, mates)]),
                axis=0,
            ).astype(bf16)
            for k in range(pieces):
                start = (q * pieces + k) * piece
                in_ref[:, start : start + piece] = total[k * out_rows : (k + 1) * out_rows]
        row = lax.broadcasted_iota(jnp.int32, (out_rows, width), 0)
        column = lax.broadcasted_iota(jnp.int32, (out_rows, width), 1)
        pick = (row + index_ref[0] * out_rows == column).astype(f32).astype(bf16)
        columns = contract_last(pick, dembed_ref[...]).astype(bf16)
        wide_ref[...] = arrived_ref[:, in_rows:].astype(f32).reshape(images, folds, piece)
        for k in range(folds):
            out_ref[:, k * piece : (k + 1) * piece] = jnp.dot(
                columns, wide_ref[:, k, :].astype(bf16), preferred_element_type=f32
            ).astype(bf16)

    return pl.pallas_call(
        kernel,
        in_specs=[
            pl.BlockSpec(memory_space=pltpu.SMEM),
            pl.BlockSpec(memory_space=pltpu.VMEM),
            pl.BlockSpec(memory_space=pltpu.VMEM),
        ],
        out_shape=[jax.ShapeDtypeStruct((out_rows, hidden), bf16)] * 2,
        scratch_shapes=[pltpu.VMEM((images, folds, piece), f32)],
        compiler_params=vmem_params(),
        cost_estimate=pl.CostEstimate(
            flops=2 * images * out_rows * hidden,
            bytes_accessed=2 * dp_size * rows * piece,
            transcendentals=0,
        ),
        name="finish",
    )(index, arrived, dembed)


def exchange(blocks, axes):
    return lax.all_to_all(blocks, axes, split_axis=0, concat_axis=0, tiled=True)


def mates_of(dp_size, hidden):
    mates = 4
    while dp_size % mates or hidden % (lanes * mates):
        mates //= 2
    return mates


def mate_blocks(value, mates):
    blocks = {0: value}
    step = mates // 2
    while step:
        pairs = [(i, i ^ step) for i in range(lax.axis_size("dp"))]
        for k in list(blocks):
            blocks[k ^ step] = lax.ppermute(blocks[k], "dp", pairs)
        step //= 2
    return [blocks[k] for k in range(mates)]


def body(tokens, teacher, norm_gain, w_in, b_in, w_out, b_out, final_gain):
    dp_size = lax.axis_size("dp")
    fsdp_size = lax.axis_size("fsdp")
    images = teacher.shape[0] * dp_size
    per_image = tokens.shape[0] // teacher.shape[0]
    hidden = w_in.shape[1]
    mates = mates_of(dp_size, hidden)
    index = lax.axis_index("dp").astype(jnp.int32)[None]
    first = lax.axis_index("fsdp").astype(jnp.int32)[None]

    normed, token_mean, teacher_rows = norm_tokens(
        tokens, norm_gain, teacher, dp_size, teacher.shape[1] // 8
    )
    blocks = mate_blocks(normed, mates)
    all_teacher = exchange(teacher_rows, "dp")
    pooled, embed_rows = forward(
        first, normed, token_mean, w_in, b_in, w_out, b_out, dp_size * fsdp_size
    )
    all_embed = exchange(embed_rows, ("dp", "fsdp"))
    gram = target_gram(all_teacher, images)
    slope, turned = mate_slopes(index % mates, blocks, w_in, b_in, hidden // mates)
    loss, dembed, parts = backward(
        index, all_embed, gram, final_gain, pooled, w_out, slope, turned, mates, dp_size, per_image
    )
    grad_in, grad_out = finish(index, exchange(parts, "dp"), dembed, mates, hidden)
    return (loss[0, 0], grad_in, grad_out)


def solution(mesh):
    return jax.shard_map(
        body,
        mesh=mesh,
        in_specs=(
            P("dp", None),
            P("dp", None),
            P(),
            P(None, "fsdp"),
            P("fsdp"),
            P(None, "fsdp"),
            P(),
            P(),
        ),
        out_specs=(P(), P("dp", "fsdp"), P("dp", "fsdp")),
        check_vma=False,
    )
```

```python
import jax
import jax.numpy as jnp
from jax import lax
from jax.experimental import pallas as pl
from jax.experimental.pallas import tpu as pltpu
from jax.sharding import PartitionSpec as P

loss_scale = 4096.0
lanes = 128
f32 = jnp.float32
bf16 = jnp.bfloat16


def gelu_tanh(values):
    inner = 0.7978845608 * (values + 0.044715 * values * values * values)
    return 0.5 * values * (1.0 + jnp.tanh(inner))


def gelu_slope(values):
    square = values * values
    tangent = jnp.tanh(0.7978845608 * (values + 0.044715 * values * square))
    return 0.5 * (1.0 + tangent) + 0.5 * values * (1.0 - tangent * tangent) * 0.7978845608 * (
        1.0 + 3.0 * 0.044715 * square
    )


def contract_last(left_side, right_side):
    return lax.dot_general(
        left_side, right_side, (((1,), (1,)), ((), ())), preferred_element_type=f32
    )


def fold_rows(values, width):
    count = values.shape[1] // width
    return jnp.concatenate(
        [
            values[i : i + 1, k * width : (k + 1) * width]
            for i in range(values.shape[0])
            for k in range(count)
        ],
        axis=0,
    )


def vmem_params(elements):
    return pltpu.CompilerParams(vmem_limit_bytes=min(56 * 2**20, 8 * elements + 8 * 2**20))


def norm_tokens(tokens, norm_gain, teacher, copies, fold):
    rows, width = tokens.shape
    images = teacher.shape[0]
    per_image = rows // images

    def kernel(tokens_ref, gain_ref, teacher_ref, normed_ref, mean_ref, out_ref):
        values = tokens_ref[...].astype(f32)
        centered = values - jnp.mean(values, axis=-1, keepdims=True)
        inv_std = lax.rsqrt(jnp.mean(centered * centered, axis=-1, keepdims=True) + 1e-05)
        normed_ref[...] = (centered * inv_std * gain_ref[...]).astype(bf16)
        mean_ref[0] = jnp.mean(values, axis=0, keepdims=True)

        @pl.when(pl.program_id(0) == 0)
        def _():
            folded = fold_rows(teacher_ref[...].astype(f32), fold).astype(bf16)
            out_ref[...] = jnp.broadcast_to(folded[None], out_ref.shape)

    payload = (copies, images * teacher.shape[1] // fold, fold)
    return pl.pallas_call(
        kernel,
        grid=(images,),
        in_specs=[
            pl.BlockSpec((per_image, width), lambda i: (i, 0)),
            pl.BlockSpec((1, width), lambda i: (0, 0)),
            pl.BlockSpec(teacher.shape, lambda i: (0, 0)),
        ],
        out_specs=[
            pl.BlockSpec((per_image, width), lambda i: (i, 0)),
            pl.BlockSpec((1, 1, width), lambda i: (i, 0, 0)),
            pl.BlockSpec(payload, lambda i: (0, 0, 0)),
        ],
        out_shape=[
            jax.ShapeDtypeStruct((rows, width), bf16),
            jax.ShapeDtypeStruct((images, 1, width), f32),
            jax.ShapeDtypeStruct(payload, bf16),
        ],
        compiler_params=vmem_params(rows * width // images + teacher.size * copies),
        cost_estimate=pl.CostEstimate(
            flops=10 * rows * width, bytes_accessed=4 * rows * width, transcendentals=0
        ),
        name="norm_tokens",
    )(tokens, norm_gain[None], teacher)


def forward(first, normed, token_mean, w_in, b_in, w_out, b_out, copies):
    rows, width = normed.shape
    hidden = w_in.shape[1]
    images = token_mean.shape[0]
    per_image = rows // images
    tile = min(512, hidden)
    steps = hidden // tile
    folds = width // lanes

    def kernel(
        first_ref, normed_ref, mean_ref, in_ref, bias_ref, out_b_ref, out_w_ref,
        pooled_ref, payload_ref, weight_ref, sem,
    ):
        step = pl.program_id(0)
        load = pltpu.make_async_copy(out_w_ref, weight_ref, sem)

        @pl.when(step == 0)
        def _():
            load.start()

        pre_act = jnp.dot(normed_ref[...], in_ref[...], preferred_element_type=f32) + bias_ref[...]
        pooled = jnp.mean(gelu_tanh(pre_act).reshape(images, per_image, tile), axis=1).astype(bf16)
        for j in range(steps):

            @pl.when(step == j)
            def _():
                pooled_ref[:, j * tile : (j + 1) * tile] = pooled

        @pl.when(step == steps - 1)
        def _():
            load.wait()
            total = contract_last(pooled_ref[...], weight_ref[...])
            total += jnp.where(first_ref[0] == 0, mean_ref[:, 0, :] + out_b_ref[...], 0.0)
            folded = fold_rows(total, lanes).astype(bf16)
            payload_ref[...] = jnp.broadcast_to(folded[None], payload_ref.shape)

    payload = (copies, images * folds, lanes)
    return pl.pallas_call(
        kernel,
        grid_spec=pltpu.PrefetchScalarGridSpec(
            num_scalar_prefetch=1,
            grid=(steps,),
            in_specs=[
                pl.BlockSpec((rows, width), lambda j, s: (0, 0)),
                pl.BlockSpec((images, 1, width), lambda j, s: (0, 0, 0)),
                pl.BlockSpec((width, tile), lambda j, s: (0, j)),
                pl.BlockSpec((1, tile), lambda j, s: (0, j)),
                pl.BlockSpec((1, width), lambda j, s: (0, 0)),
                pl.BlockSpec(memory_space=pl.ANY),
            ],
            out_specs=[
                pl.BlockSpec((images, hidden), lambda j, s: (0, 0)),
                pl.BlockSpec(payload, lambda j, s: (0, 0, 0)),
            ],
            scratch_shapes=[pltpu.VMEM((width, hidden), bf16), pltpu.SemaphoreType.DMA],
        ),
        out_shape=[
            jax.ShapeDtypeStruct((images, hidden), bf16),
            jax.ShapeDtypeStruct(payload, bf16),
        ],
        compiler_params=vmem_params(rows * width + width * hidden + copies * images * width),
        cost_estimate=pl.CostEstimate(
            flops=2 * rows * width * hidden,
            bytes_accessed=4 * width * hidden,
            transcendentals=rows * hidden,
        ),
        name="forward",
    )(first, normed, token_mean, w_in, b_in[None], b_out[None], w_out)


def mate_slopes(share_index, blocks, w_in, b_in, share):
    rows, width = blocks[0].shape
    count = len(blocks)
    tile = min(256, share)
    steps = share // tile
    turn = count * rows // steps

    def kernel(index_ref, *refs):
        token_refs = refs[:count]
        in_ref, bias_ref, slope_ref, turned_ref, held_ref, sems = refs[count:]

        @pl.when(pl.program_id(0) == 0)
        def _():
            loads = [
                pltpu.make_async_copy(
                    token_refs[k], held_ref.at[pl.ds(k * rows, rows)], sems.at[k]
                )
                for k in range(count)
            ]
            for load in loads:
                load.start()
            for load in loads:
                load.wait()

        pre_act = jnp.dot(held_ref[...], in_ref[...], preferred_element_type=f32) + bias_ref[...]
        slope_ref[...] = gelu_slope(pre_act).astype(bf16)
        start = pl.multiple_of(pl.program_id(0) * turn, turn)
        turned_ref[...] = held_ref[pl.ds(start, turn)].T

    return pl.pallas_call(
        kernel,
        grid_spec=pltpu.PrefetchScalarGridSpec(
            num_scalar_prefetch=1,
            grid=(steps,),
            in_specs=[pl.BlockSpec(memory_space=pl.ANY)] * count
            + [
                pl.BlockSpec((width, tile), lambda j, s: (0, s[0] * steps + j)),
                pl.BlockSpec((1, tile), lambda j, s: (0, s[0] * steps + j)),
            ],
            out_specs=[
                pl.BlockSpec((count * rows, tile), lambda j, s: (0, j)),
                pl.BlockSpec((width, turn), lambda j, s: (0, j)),
            ],
            scratch_shapes=[
                pltpu.VMEM((count * rows, width), bf16),
                pltpu.SemaphoreType.DMA((count,)),
            ],
        ),
        out_shape=[
            jax.ShapeDtypeStruct((count * rows, share), bf16),
            jax.ShapeDtypeStruct((width, count * rows), bf16),
        ],
        compiler_params=vmem_params(count * rows * (2 * width + share)),
        cost_estimate=pl.CostEstimate(
            flops=2 * rows * count * width * share,
            bytes_accessed=4 * rows * count * width,
            transcendentals=rows * count * share,
        ),
        name="mate_slopes",
    )(share_index, *blocks, w_in, b_in[None])


def target_gram(arrived, images):
    senders, folded, fold = arrived.shape
    folds = senders * folded // images

    def kernel(arrived_ref, gram_ref, wide_ref):
        wide_ref[...] = arrived_ref[...].astype(f32).reshape(images, folds, fold)
        rows = jnp.concatenate([wide_ref[:, k, :].astype(bf16) for k in range(folds)], axis=1)
        gram = contract_last(rows, rows)
        row = lax.broadcasted_iota(jnp.int32, gram.shape, 0)
        column = lax.broadcasted_iota(jnp.int32, gram.shape, 1)
        diagonal = jnp.where(row == column, gram, 0.0)
        down = lax.rsqrt(jnp.sum(diagonal, axis=1, keepdims=True) + 1e-06)
        across = lax.rsqrt(jnp.sum(diagonal, axis=0, keepdims=True) + 1e-06)
        gram_ref[...] = gram * down * across

    return pl.pallas_call(
        kernel,
        out_shape=jax.ShapeDtypeStruct((images, images), f32),
        scratch_shapes=[pltpu.VMEM((images, folds, fold), f32)],
        compiler_params=vmem_params(images * folds * fold),
        cost_estimate=pl.CostEstimate(
            flops=2 * images * images * folds * fold,
            bytes_accessed=2 * images * folds * fold,
            transcendentals=0,
        ),
        name="target_gram",
    )(arrived)


def backward(
    index, arrived, gram, final_gain, pooled, w_out, slope, turned, mates, dp_size, per_image
):
    senders, folded, _ = arrived.shape
    width = w_out.shape[0]
    images = gram.shape[0]
    own_images, hidden = pooled.shape
    fsdp_size = senders // dp_size
    folds = width // lanes
    share = hidden // mates
    mate_rows = turned.shape[1]
    out_rows = width // dp_size
    piece = min(share, 256)
    pieces = share // piece
    extra = own_images * hidden // piece
    group = max(1, 512 // out_rows)
    steps = dp_size // group
    in_rows = out_rows * pieces

    def kernel(
        index_ref, arrived_ref, gram_ref, gain_ref, pooled_ref, out_w_any, slope_any, turned_any,
        loss_ref, dembed_ref, payload_ref,
        wide_ref, hidden_ref, extra_ref, out_w_ref, slope_ref, turned_ref, sems,
    ):
        step = pl.program_id(0)

        @pl.when(step == 0)
        def _():
            first_unit = pl.multiple_of(lax.rem(index_ref[0], mates) * share, share)
            loads = [
                pltpu.make_async_copy(
                    out_w_any.at[:, pl.ds(first_unit, share)], out_w_ref, sems.at[0]
                ),
                pltpu.make_async_copy(slope_any, slope_ref, sems.at[1]),
                pltpu.make_async_copy(turned_any, turned_ref, sems.at[2]),
            ]
            for load in loads:
                load.start()
            parts = arrived_ref[...].astype(f32).reshape(dp_size, fsdp_size, folded, lanes)
            wide_ref[...] = jnp.sum(parts, axis=1).reshape(images, folds, lanes)
            embedding = jnp.concatenate([wide_ref[:, k, :] for k in range(folds)], axis=1)
            gain = gain_ref[...]
            centered = embedding - jnp.mean(embedding, axis=-1, keepdims=True)
            inv_std = lax.rsqrt(jnp.mean(centered * centered, axis=-1, keepdims=True) + 1e-05)
            normed = centered * inv_std
            scaled = normed * gain
            square = jnp.sum(scaled * scaled, axis=-1, keepdims=True) + 1e-06
            inv_norm = lax.rsqrt(square)
            unit = scaled * inv_norm
            student = unit.astype(bf16)
            resid = contract_last(student, student) - gram_ref[...]
            loss_ref[0, 0] = jnp.sum(resid * resid) / images
            dstudent = (loss_scale * 4.0 / images) * jnp.dot(
                resid.astype(bf16), student, preferred_element_type=f32
            )
            dunit = (
                dstudent - unit * jnp.sum(unit * dstudent, axis=-1, keepdims=True)
            ) * inv_norm
            gain_grad = dunit * gain
            dembed = inv_std * (
                gain_grad
                - jnp.mean(gain_grad, axis=-1, keepdims=True)
                - normed * jnp.mean(gain_grad * normed, axis=-1, keepdims=True)
            )
            dembed_b = dembed.astype(bf16)
            dembed_ref[...] = dembed_b
            shape = (mates * own_images, images)
            row = lax.broadcasted_iota(jnp.int32, shape, 0)
            column = lax.broadcasted_iota(jnp.int32, shape, 1)
            owner = (row // own_images) ^ index_ref[0]
            pick = (owner * own_images + row % own_images == column).astype(f32).astype(bf16)
            mate_dembed = jnp.dot(pick, dembed_b, preferred_element_type=f32).astype(bf16)
            loads[0].wait()
            dpooled = jnp.dot(mate_dembed, out_w_ref[...], preferred_element_type=f32) / per_image
            loads[1].wait()
            for k in range(mates * own_images):
                rows = slice(k * per_image, (k + 1) * per_image)
                hidden_ref[rows] = (dpooled[k : k + 1] * slope_ref[rows].astype(f32)).astype(bf16)
            extra_ref[...] = fold_rows(pooled_ref[...].astype(f32), piece).astype(bf16)
            loads[2].wait()

        taken = group * out_rows
        rows = turned_ref[pl.ds(pl.multiple_of(step * taken, taken), taken)]
        term = jnp.dot(rows, hidden_ref[...], preferred_element_type=f32).astype(bf16)
        for d in range(group):
            for k in range(pieces):
                payload_ref[d, k * out_rows : (k + 1) * out_rows] = term[
                    d * out_rows : (d + 1) * out_rows, k * piece : (k + 1) * piece
                ]
            payload_ref[d, in_rows:] = extra_ref[...]

    return pl.pallas_call(
        kernel,
        grid_spec=pltpu.PrefetchScalarGridSpec(
            num_scalar_prefetch=1,
            grid=(steps,),
            in_specs=[
                pl.BlockSpec(arrived.shape, lambda j, s: (0, 0, 0)),
                pl.BlockSpec(gram.shape, lambda j, s: (0, 0)),
                pl.BlockSpec((1, width), lambda j, s: (0, 0)),
                pl.BlockSpec(pooled.shape, lambda j, s: (0, 0)),
                pl.BlockSpec(memory_space=pl.ANY),
                pl.BlockSpec(memory_space=pl.ANY),
                pl.BlockSpec(memory_space=pl.ANY),
            ],
            out_specs=[
                pl.BlockSpec(memory_space=pltpu.SMEM),
                pl.BlockSpec((images, width), lambda j, s: (0, 0)),
                pl.BlockSpec((group, in_rows + extra, piece), lambda j, s: (j, 0, 0)),
            ],
            scratch_shapes=[
                pltpu.VMEM((images, folds, lanes), f32),
                pltpu.VMEM((mate_rows, share), bf16),
                pltpu.VMEM((extra, piece), bf16),
                pltpu.VMEM((width, share), bf16),
                pltpu.VMEM(slope.shape, bf16),
                pltpu.VMEM(turned.shape, bf16),
                pltpu.SemaphoreType.DMA((3,)),
            ],
        ),
        out_shape=[
            jax.ShapeDtypeStruct((1, 1), f32),
            jax.ShapeDtypeStruct((images, width), bf16),
            jax.ShapeDtypeStruct((dp_size, in_rows + extra, piece), bf16),
        ],
        compiler_params=vmem_params(2 * mate_rows * (width + share) + arrived.size),
        cost_estimate=pl.CostEstimate(
            flops=2 * mate_rows * width * share,
            bytes_accessed=2 * mate_rows * (width + share),
            transcendentals=0,
        ),
        name="backward",
    )(index, arrived, gram, final_gain[None], pooled, w_out, slope, turned)


def own_columns(index, dembed, out_rows):
    images, width = dembed.shape

    def kernel(index_ref, dembed_ref, columns_ref):
        row = lax.broadcasted_iota(jnp.int32, (out_rows, width), 0)
        column = lax.broadcasted_iota(jnp.int32, (out_rows, width), 1)
        pick = (row + index_ref[0] * out_rows == column).astype(f32).astype(bf16)
        columns_ref[...] = contract_last(pick, dembed_ref[...]).astype(bf16)

    return pl.pallas_call(
        kernel,
        in_specs=[
            pl.BlockSpec(memory_space=pltpu.SMEM),
            pl.BlockSpec(memory_space=pltpu.VMEM),
        ],
        out_shape=jax.ShapeDtypeStruct((out_rows, images), bf16),
        cost_estimate=pl.CostEstimate(
            flops=2 * images * out_rows * width,
            bytes_accessed=2 * images * width,
            transcendentals=0,
        ),
        name="own_columns",
    )(index, dembed)


def finish(arrived, columns, mates, hidden):
    dp_size, _, piece = arrived.shape
    out_rows, images = columns.shape
    pieces = hidden // mates // piece
    in_rows = out_rows * pieces
    folds = hidden // piece

    def kernel(arrived_ref, columns_ref, in_ref, out_ref, wide_ref):
        wide_ref[...] = arrived_ref[:, in_rows:].astype(f32).reshape(images, folds, piece)
        rows = jnp.concatenate([wide_ref[:, k, :].astype(bf16) for k in range(folds)], axis=1)
        out_ref[...] = jnp.dot(columns_ref[...], rows, preferred_element_type=f32).astype(bf16)
        for q in range(mates):
            for k in range(pieces):
                taken = slice(k * out_rows, (k + 1) * out_rows)
                total = arrived_ref[q, taken].astype(f32)
                for s in range(q + mates, dp_size, mates):
                    total += arrived_ref[s, taken].astype(f32)
                start = (q * pieces + k) * piece
                in_ref[:, start : start + piece] = total.astype(bf16)

    return pl.pallas_call(
        kernel,
        out_shape=[jax.ShapeDtypeStruct((out_rows, hidden), bf16)] * 2,
        scratch_shapes=[pltpu.VMEM((images, folds, piece), f32)],
        compiler_params=vmem_params(arrived.size),
        cost_estimate=pl.CostEstimate(
            flops=2 * images * out_rows * hidden,
            bytes_accessed=2 * arrived.size,
            transcendentals=0,
        ),
        name="finish",
    )(arrived, columns)


def exchange(blocks, axes):
    return lax.all_to_all(blocks, axes, split_axis=0, concat_axis=0, tiled=True)


def mates_of(dp_size, hidden):
    mates = 4
    while dp_size % mates or hidden % (lanes * mates):
        mates //= 2
    return mates


def swap(value, step):
    return lax.ppermute(value, "dp", [(i, i ^ step) for i in range(lax.axis_size("dp"))])


def after(value, other):
    return lax.optimization_barrier((value, other))[0]


def body(tokens, teacher, norm_gain, w_in, b_in, w_out, b_out, final_gain):
    dp_size = lax.axis_size("dp")
    fsdp_size = lax.axis_size("fsdp")
    images = teacher.shape[0] * dp_size
    per_image = tokens.shape[0] // teacher.shape[0]
    hidden = w_in.shape[1]
    mates = mates_of(dp_size, hidden)
    index = lax.axis_index("dp").astype(jnp.int32)[None]
    first = lax.axis_index("fsdp").astype(jnp.int32)[None]

    normed, token_mean, teacher_rows = norm_tokens(
        tokens, norm_gain, teacher, dp_size, teacher.shape[1] // 8
    )
    blocks = {0: normed}
    step = mates // 2
    if step:
        blocks[step] = swap(normed, step)
    if step > 1:
        blocks[1] = swap(normed, 1)
    all_teacher = exchange(teacher_rows, "dp")
    pooled, embed_rows = forward(
        first, normed, token_mean, w_in, b_in, w_out, b_out, dp_size * fsdp_size
    )
    if step > 1:
        blocks[step + 1] = swap(after(blocks[step], pooled), 1)
    blocks = [blocks[k] for k in range(mates)]
    all_embed = exchange(embed_rows, ("dp", "fsdp"))
    gram = target_gram(all_teacher, images)
    slope, turned = mate_slopes(index % mates, blocks, w_in, b_in, hidden // mates)
    loss, dembed, parts = backward(
        index, all_embed, gram, final_gain, pooled, w_out, slope, turned, mates, dp_size, per_image
    )
    arrived = exchange(parts, "dp")
    columns = own_columns(index, dembed, dembed.shape[1] // dp_size)
    grad_in, grad_out = finish(arrived, columns, mates, hidden)
    return (loss[0, 0], grad_in, grad_out)


def solution(mesh):
    return jax.shard_map(
        body,
        mesh=mesh,
        in_specs=(
            P("dp", None),
            P("dp", None),
            P(),
            P(None, "fsdp"),
            P("fsdp"),
            P(None, "fsdp"),
            P(),
            P(),
        ),
        out_specs=(P(), P("dp", "fsdp"), P("dp", "fsdp")),
        check_vma=False,
    )
```

```python
import jax
import jax.numpy as jnp
from jax import lax
from jax.experimental import pallas as pl
from jax.experimental.pallas import tpu as pltpu
from jax.sharding import PartitionSpec as P

loss_scale = 4096.0
lanes = 128
f32 = jnp.float32
bf16 = jnp.bfloat16


def gelu_tanh(values):
    inner = 0.7978845608 * (values + 0.044715 * values * values * values)
    return 0.5 * values * (1.0 + jnp.tanh(inner))


def gelu_slope(values):
    square = values * values
    tangent = jnp.tanh(0.7978845608 * (values + 0.044715 * values * square))
    return 0.5 * (1.0 + tangent) + 0.5 * values * (1.0 - tangent * tangent) * 0.7978845608 * (
        1.0 + 3.0 * 0.044715 * square
    )


def contract_last(left_side, right_side):
    return lax.dot_general(
        left_side, right_side, (((1,), (1,)), ((), ())), preferred_element_type=f32
    )


def fold_rows(values, width):
    count = values.shape[1] // width
    return jnp.concatenate(
        [
            values[i : i + 1, k * width : (k + 1) * width]
            for i in range(values.shape[0])
            for k in range(count)
        ],
        axis=0,
    )


def vmem_params(elements):
    return pltpu.CompilerParams(vmem_limit_bytes=min(56 * 2**20, 8 * elements + 8 * 2**20))


in_hbm = pl.BlockSpec(memory_space=pltpu.HBM)
in_any = pl.BlockSpec(memory_space=pl.ANY)


def hbm(value):
    return pltpu.with_memory_space_constraint(value, pltpu.HBM)


def norm_tokens(tokens, norm_gain, teacher, copies, fold):
    rows, width = tokens.shape
    images = teacher.shape[0]
    per_image = rows // images

    def kernel(tokens_ref, gain_ref, teacher_ref, normed_ref, mean_ref, out_ref):
        values = tokens_ref[...].astype(f32)
        centered = values - jnp.mean(values, axis=-1, keepdims=True)
        inv_std = lax.rsqrt(jnp.mean(centered * centered, axis=-1, keepdims=True) + 1e-05)
        normed_ref[...] = (centered * inv_std * gain_ref[...]).astype(bf16)
        mean_ref[0] = jnp.mean(values, axis=0, keepdims=True)

        @pl.when(pl.program_id(0) == 0)
        def _():
            folded = fold_rows(teacher_ref[...].astype(f32), fold).astype(bf16)
            out_ref[...] = jnp.broadcast_to(folded[None], out_ref.shape)

    payload = (copies, images * teacher.shape[1] // fold, fold)
    return pl.pallas_call(
        kernel,
        grid=(images,),
        in_specs=[
            pl.BlockSpec((per_image, width), lambda i: (i, 0)),
            pl.BlockSpec((1, width), lambda i: (0, 0)),
            pl.BlockSpec(teacher.shape, lambda i: (0, 0)),
        ],
        out_specs=[
            pl.BlockSpec((per_image, width), lambda i: (i, 0)),
            pl.BlockSpec((1, 1, width), lambda i: (i, 0, 0)),
            pl.BlockSpec(payload, lambda i: (0, 0, 0)),
        ],
        out_shape=[
            jax.ShapeDtypeStruct((rows, width), bf16),
            jax.ShapeDtypeStruct((images, 1, width), f32),
            pltpu.HBM(payload, bf16),
        ],
        compiler_params=vmem_params(6 * rows * width),
        cost_estimate=pl.CostEstimate(
            flops=10 * rows * width, bytes_accessed=4 * rows * width, transcendentals=0
        ),
        name="norm_tokens",
    )(hbm(tokens), hbm(norm_gain[None]), hbm(teacher))


def forward(first, normed, token_mean, w_in, b_in, w_out, b_out, copies):
    rows, width = normed.shape
    hidden = w_in.shape[1]
    images = token_mean.shape[0]
    per_image = rows // images
    tile = min(512, hidden)
    steps = hidden // tile
    folds = width // lanes

    def kernel(
        first_ref, normed_ref, mean_ref, bias_ref, out_b_ref, in_any_ref, out_any_ref,
        pooled_ref, payload_ref, in_ref, out_w_ref, sems,
    ):
        step = pl.program_id(0)
        loads = [
            pltpu.make_async_copy(
                in_any_ref.at[:, pl.ds(j * tile, tile)], in_ref.at[j], sems.at[j]
            )
            for j in range(steps)
        ]
        loads.append(pltpu.make_async_copy(out_any_ref, out_w_ref, sems.at[steps]))

        @pl.when(step == 0)
        def _():
            for load in loads:
                load.start()

        for j in range(steps):

            @pl.when(step == j)
            def _():
                loads[j].wait()

        pre_act = (
            jnp.dot(normed_ref[...], in_ref[step], preferred_element_type=f32) + bias_ref[...]
        )
        pooled = jnp.mean(gelu_tanh(pre_act).reshape(images, per_image, tile), axis=1).astype(bf16)
        for j in range(steps):

            @pl.when(step == j)
            def _():
                pooled_ref[:, j * tile : (j + 1) * tile] = pooled

        @pl.when(step == steps - 1)
        def _():
            loads[steps].wait()
            total = contract_last(pooled_ref[...], out_w_ref[...])
            total += jnp.where(first_ref[0] == 0, mean_ref[:, 0, :] + out_b_ref[...], 0.0)
            folded = fold_rows(total, lanes).astype(bf16)
            payload_ref[...] = jnp.broadcast_to(folded[None], payload_ref.shape)

    payload = (copies, images * folds, lanes)
    return pl.pallas_call(
        kernel,
        grid_spec=pltpu.PrefetchScalarGridSpec(
            num_scalar_prefetch=1,
            grid=(steps,),
            in_specs=[
                pl.BlockSpec((rows, width), lambda j, s: (0, 0)),
                pl.BlockSpec((images, 1, width), lambda j, s: (0, 0, 0)),
                pl.BlockSpec((1, tile), lambda j, s: (0, j)),
                pl.BlockSpec((1, width), lambda j, s: (0, 0)),
                in_hbm,
                in_hbm,
            ],
            out_specs=[
                pl.BlockSpec((images, hidden), lambda j, s: (0, 0)),
                pl.BlockSpec(payload, lambda j, s: (0, 0, 0)),
            ],
            scratch_shapes=[
                pltpu.VMEM((steps, width, tile), bf16),
                pltpu.VMEM((width, hidden), bf16),
                pltpu.SemaphoreType.DMA((steps + 1,)),
            ],
        ),
        out_shape=[
            jax.ShapeDtypeStruct((images, hidden), bf16),
            pltpu.HBM(payload, bf16),
        ],
        compiler_params=vmem_params(width * hidden + copies * images * width),
        cost_estimate=pl.CostEstimate(
            flops=2 * rows * width * hidden,
            bytes_accessed=4 * width * hidden,
            transcendentals=rows * hidden,
        ),
        name="forward",
    )(first, normed, token_mean, hbm(b_in[None]), hbm(b_out[None]), hbm(w_in), hbm(w_out))


def mate_slopes(share_index, blocks, w_in, b_in, share):
    rows, width = blocks[0].shape
    count = len(blocks)
    tile = min(256, share)
    steps = share // tile
    turn = count * rows // steps

    def kernel(index_ref, *refs):
        token_refs = refs[:count]
        bias_ref, in_any_ref, slope_ref, turned_ref, held_ref, in_ref, sems = refs[count:]
        step = pl.program_id(0)
        first_unit = index_ref[0] * share
        weights = [
            pltpu.make_async_copy(
                in_any_ref.at[:, pl.ds(pl.multiple_of(first_unit + j * tile, tile), tile)],
                in_ref.at[j],
                sems.at[count + j],
            )
            for j in range(steps)
        ]

        @pl.when(step == 0)
        def _():
            loads = [
                pltpu.make_async_copy(
                    token_refs[k], held_ref.at[pl.ds(k * rows, rows)], sems.at[k]
                )
                for k in range(count)
            ]
            for load in loads + weights:
                load.start()
            for load in loads:
                load.wait()

        for j in range(steps):

            @pl.when(step == j)
            def _():
                weights[j].wait()

        pre_act = jnp.dot(held_ref[...], in_ref[step], preferred_element_type=f32) + bias_ref[...]
        slope_ref[...] = gelu_slope(pre_act).astype(bf16)
        start = pl.multiple_of(step * turn, turn)
        turned_ref[...] = held_ref[pl.ds(start, turn)].T

    return pl.pallas_call(
        kernel,
        grid_spec=pltpu.PrefetchScalarGridSpec(
            num_scalar_prefetch=1,
            grid=(steps,),
            in_specs=[in_any] * count
            + [pl.BlockSpec((1, tile), lambda j, s: (0, s[0] * steps + j)), in_hbm],
            out_specs=[
                pl.BlockSpec((count * rows, tile), lambda j, s: (0, j)),
                pl.BlockSpec((width, turn), lambda j, s: (0, j)),
            ],
            scratch_shapes=[
                pltpu.VMEM((count * rows, width), bf16),
                pltpu.VMEM((steps, width, tile), bf16),
                pltpu.SemaphoreType.DMA((count + steps,)),
            ],
        ),
        out_shape=[
            jax.ShapeDtypeStruct((count * rows, share), bf16),
            jax.ShapeDtypeStruct((width, count * rows), bf16),
        ],
        compiler_params=vmem_params(count * rows * (width + share)),
        cost_estimate=pl.CostEstimate(
            flops=2 * rows * count * width * share,
            bytes_accessed=4 * rows * count * width,
            transcendentals=rows * count * share,
        ),
        name="mate_slopes",
    )(share_index, *blocks, hbm(b_in[None]), hbm(w_in))


def target_gram(arrived, images):
    senders, folded, fold = arrived.shape
    folds = senders * folded // images

    def kernel(arrived_ref, gram_ref, wide_ref):
        wide_ref[...] = arrived_ref[...].astype(f32).reshape(images, folds, fold)
        rows = jnp.concatenate([wide_ref[:, k, :].astype(bf16) for k in range(folds)], axis=1)
        gram = contract_last(rows, rows)
        row = lax.broadcasted_iota(jnp.int32, gram.shape, 0)
        column = lax.broadcasted_iota(jnp.int32, gram.shape, 1)
        diagonal = jnp.where(row == column, gram, 0.0)
        down = lax.rsqrt(jnp.sum(diagonal, axis=1, keepdims=True) + 1e-06)
        across = lax.rsqrt(jnp.sum(diagonal, axis=0, keepdims=True) + 1e-06)
        gram_ref[...] = gram * down * across

    return pl.pallas_call(
        kernel,
        out_shape=jax.ShapeDtypeStruct((images, images), f32),
        scratch_shapes=[pltpu.VMEM((images, folds, fold), f32)],
        compiler_params=vmem_params(images * folds * fold),
        cost_estimate=pl.CostEstimate(
            flops=2 * images * images * folds * fold,
            bytes_accessed=2 * images * folds * fold,
            transcendentals=0,
        ),
        name="target_gram",
    )(arrived)


def backward(
    index, arrived, gram, final_gain, pooled, w_out, slope, turned, mates, dp_size, per_image
):
    senders, folded, _ = arrived.shape
    width = w_out.shape[0]
    images = gram.shape[0]
    own_images, hidden = pooled.shape
    fsdp_size = senders // dp_size
    folds = width // lanes
    share = hidden // mates
    mate_rows = turned.shape[1]
    out_rows = width // dp_size
    piece = min(share, 256)
    pieces = share // piece
    extra = own_images * hidden // piece
    group = max(1, 512 // out_rows)
    steps = dp_size // group
    in_rows = out_rows * pieces

    def kernel(
        index_ref, arrived_any, gram_ref, gain_ref, pooled_ref, out_w_any, slope_any, turned_any,
        loss_ref, dembed_ref, payload_any,
        wide_ref, hidden_ref, extra_ref, out_w_ref, slope_ref, turned_ref, arrived_ref, payload_ref, sems,
    ):
        step = pl.program_id(0)

        @pl.when(step == 0)
        def _():
            first_unit = pl.multiple_of(lax.rem(index_ref[0], mates) * share, share)
            loads = [
                pltpu.make_async_copy(
                    out_w_any.at[:, pl.ds(first_unit, share)], out_w_ref, sems.at[0]
                ),
                pltpu.make_async_copy(slope_any, slope_ref, sems.at[1]),
                pltpu.make_async_copy(turned_any, turned_ref, sems.at[2]),
                pltpu.make_async_copy(arrived_any, arrived_ref, sems.at[3]),
            ]
            for load in loads[::-1]:
                load.start()
            loads[3].wait()
            parts = arrived_ref[...].astype(f32).reshape(dp_size, fsdp_size, folded, lanes)
            wide_ref[...] = jnp.sum(parts, axis=1).reshape(images, folds, lanes)
            embedding = jnp.concatenate([wide_ref[:, k, :] for k in range(folds)], axis=1)
            gain = gain_ref[...]
            centered = embedding - jnp.mean(embedding, axis=-1, keepdims=True)
            inv_std = lax.rsqrt(jnp.mean(centered * centered, axis=-1, keepdims=True) + 1e-05)
            normed = centered * inv_std
            scaled = normed * gain
            square = jnp.sum(scaled * scaled, axis=-1, keepdims=True) + 1e-06
            inv_norm = lax.rsqrt(square)
            unit = scaled * inv_norm
            student = unit.astype(bf16)
            resid = contract_last(student, student) - gram_ref[...]
            loss_ref[0, 0] = jnp.sum(resid * resid) / images
            dstudent = (loss_scale * 4.0 / images) * jnp.dot(
                resid.astype(bf16), student, preferred_element_type=f32
            )
            dunit = (
                dstudent - unit * jnp.sum(unit * dstudent, axis=-1, keepdims=True)
            ) * inv_norm
            gain_grad = dunit * gain
            dembed = inv_std * (
                gain_grad
                - jnp.mean(gain_grad, axis=-1, keepdims=True)
                - normed * jnp.mean(gain_grad * normed, axis=-1, keepdims=True)
            )
            dembed_b = dembed.astype(bf16)
            dembed_ref[...] = dembed_b
            shape = (mates * own_images, images)
            row = lax.broadcasted_iota(jnp.int32, shape, 0)
            column = lax.broadcasted_iota(jnp.int32, shape, 1)
            owner = (row // own_images) ^ index_ref[0]
            pick = (owner * own_images + row % own_images == column).astype(f32).astype(bf16)
            mate_dembed = jnp.dot(pick, dembed_b, preferred_element_type=f32).astype(bf16)
            loads[0].wait()
            dpooled = jnp.dot(mate_dembed, out_w_ref[...], preferred_element_type=f32) / per_image
            loads[1].wait()
            for k in range(mates * own_images):
                rows = slice(k * per_image, (k + 1) * per_image)
                hidden_ref[rows] = (dpooled[k : k + 1] * slope_ref[rows].astype(f32)).astype(bf16)
            extra_ref[...] = fold_rows(pooled_ref[...].astype(f32), piece).astype(bf16)
            loads[2].wait()

        taken = group * out_rows
        rows = turned_ref[pl.ds(pl.multiple_of(step * taken, taken), taken)]
        term = jnp.dot(rows, hidden_ref[...], preferred_element_type=f32).astype(bf16)
        for d in range(group):
            for k in range(pieces):
                payload_ref[step, d, k * out_rows : (k + 1) * out_rows] = term[
                    d * out_rows : (d + 1) * out_rows, k * piece : (k + 1) * piece
                ]
            payload_ref[step, d, in_rows:] = extra_ref[...]
        stores = [
            pltpu.make_async_copy(
                payload_ref.at[j], payload_any.at[pl.ds(j * group, group)], sems.at[4 + j]
            )
            for j in range(steps)
        ]
        for j in range(steps):

            @pl.when(step == j)
            def _():
                stores[j].start()

        @pl.when(step == steps - 1)
        def _():
            for store in stores:
                store.wait()

    return pl.pallas_call(
        kernel,
        grid_spec=pltpu.PrefetchScalarGridSpec(
            num_scalar_prefetch=1,
            grid=(steps,),
            in_specs=[
                in_any,
                pl.BlockSpec(gram.shape, lambda j, s: (0, 0)),
                pl.BlockSpec((1, width), lambda j, s: (0, 0)),
                pl.BlockSpec(pooled.shape, lambda j, s: (0, 0)),
                in_hbm,
                in_any,
                in_any,
            ],
            out_specs=[
                pl.BlockSpec(memory_space=pltpu.SMEM),
                pl.BlockSpec((images, width), lambda j, s: (0, 0)),
                in_hbm,
            ],
            scratch_shapes=[
                pltpu.VMEM((images, folds, lanes), f32),
                pltpu.VMEM((mate_rows, share), bf16),
                pltpu.VMEM((extra, piece), bf16),
                pltpu.VMEM((width, share), bf16),
                pltpu.VMEM(slope.shape, bf16),
                pltpu.VMEM(turned.shape, bf16),
                pltpu.VMEM(arrived.shape, bf16),
                pltpu.VMEM((steps, group, in_rows + extra, piece), bf16),
                pltpu.SemaphoreType.DMA((4 + steps,)),
            ],
        ),
        out_shape=[
            jax.ShapeDtypeStruct((1, 1), f32),
            jax.ShapeDtypeStruct((images, width), bf16),
            pltpu.HBM((dp_size, in_rows + extra, piece), bf16),
        ],
        compiler_params=vmem_params(mate_rows * (width + share) // 2 + arrived.size),
        cost_estimate=pl.CostEstimate(
            flops=2 * mate_rows * width * share,
            bytes_accessed=2 * mate_rows * (width + share),
            transcendentals=0,
        ),
        name="backward",
    )(index, arrived, gram, hbm(final_gain[None]), pooled, hbm(w_out), slope, turned)


def own_columns(index, dembed, out_rows):
    images, width = dembed.shape

    def kernel(index_ref, dembed_ref, columns_ref):
        row = lax.broadcasted_iota(jnp.int32, (out_rows, width), 0)
        column = lax.broadcasted_iota(jnp.int32, (out_rows, width), 1)
        pick = (row + index_ref[0] * out_rows == column).astype(f32).astype(bf16)
        columns_ref[...] = contract_last(pick, dembed_ref[...]).astype(bf16)

    return pl.pallas_call(
        kernel,
        in_specs=[
            pl.BlockSpec(memory_space=pltpu.SMEM),
            pl.BlockSpec(memory_space=pltpu.VMEM),
        ],
        out_shape=jax.ShapeDtypeStruct((out_rows, images), bf16),
        compiler_params=vmem_params(images * width),
        cost_estimate=pl.CostEstimate(
            flops=2 * images * out_rows * width,
            bytes_accessed=2 * images * width,
            transcendentals=0,
        ),
        name="own_columns",
    )(index, dembed)


def finish(arrived, columns, mates, hidden):
    dp_size, _, piece = arrived.shape
    out_rows, images = columns.shape
    pieces = hidden // mates // piece
    in_rows = out_rows * pieces
    folds = hidden // piece

    def kernel(arrived_ref, columns_ref, in_ref, out_ref, wide_ref):
        wide_ref[...] = arrived_ref[:, in_rows:].astype(f32).reshape(images, folds, piece)
        rows = jnp.concatenate([wide_ref[:, k, :].astype(bf16) for k in range(folds)], axis=1)
        out_ref[...] = jnp.dot(columns_ref[...], rows, preferred_element_type=f32).astype(bf16)
        for q in range(mates):
            for k in range(pieces):
                taken = slice(k * out_rows, (k + 1) * out_rows)
                total = arrived_ref[q, taken].astype(f32)
                for s in range(q + mates, dp_size, mates):
                    total += arrived_ref[s, taken].astype(f32)
                start = (q * pieces + k) * piece
                in_ref[:, start : start + piece] = total.astype(bf16)

    return pl.pallas_call(
        kernel,
        out_shape=[jax.ShapeDtypeStruct((out_rows, hidden), bf16)] * 2,
        scratch_shapes=[pltpu.VMEM((images, folds, piece), f32)],
        compiler_params=vmem_params(arrived.size),
        cost_estimate=pl.CostEstimate(
            flops=2 * images * out_rows * hidden,
            bytes_accessed=2 * arrived.size,
            transcendentals=0,
        ),
        name="finish",
    )(arrived, columns)


def exchange(blocks, axes):
    return lax.all_to_all(blocks, axes, split_axis=0, concat_axis=0, tiled=True)


def mates_of(dp_size, hidden):
    mates = 4
    while dp_size % mates or hidden % (lanes * mates):
        mates //= 2
    return mates


def swap(value, step):
    return lax.ppermute(value, "dp", [(i, i ^ step) for i in range(lax.axis_size("dp"))])


def after(value, other):
    return lax.optimization_barrier((value, other))[0]


def body(tokens, teacher, norm_gain, w_in, b_in, w_out, b_out, final_gain):
    dp_size = lax.axis_size("dp")
    fsdp_size = lax.axis_size("fsdp")
    images = teacher.shape[0] * dp_size
    per_image = tokens.shape[0] // teacher.shape[0]
    hidden = w_in.shape[1]
    mates = mates_of(dp_size, hidden)
    index = lax.axis_index("dp").astype(jnp.int32)[None]
    first = lax.axis_index("fsdp").astype(jnp.int32)[None]

    normed, token_mean, teacher_rows = norm_tokens(
        tokens, norm_gain, teacher, dp_size, teacher.shape[1] // 8
    )
    blocks = {0: normed}
    step = mates // 2
    if step:
        blocks[step] = swap(normed, step)
    if step > 1:
        blocks[1] = swap(normed, 1)
    all_teacher = exchange(teacher_rows, "dp")
    pooled, embed_rows = forward(
        first, normed, token_mean, w_in, b_in, w_out, b_out, dp_size * fsdp_size
    )
    if step > 1:
        blocks[step + 1] = swap(after(blocks[step], pooled), 1)
    blocks = [blocks[k] for k in range(mates)]
    all_embed = exchange(embed_rows, ("dp", "fsdp"))
    gram = target_gram(all_teacher, images)
    slope, turned = mate_slopes(index % mates, blocks, w_in, b_in, hidden // mates)
    loss, dembed, parts = backward(
        index, all_embed, gram, final_gain, pooled, w_out, slope, turned, mates, dp_size, per_image
    )
    arrived = exchange(parts, "dp")
    columns = own_columns(index, dembed, dembed.shape[1] // dp_size)
    grad_in, grad_out = finish(arrived, columns, mates, hidden)
    return (loss[0, 0], grad_in, grad_out)


def solution(mesh):
    return jax.shard_map(
        body,
        mesh=mesh,
        in_specs=(
            P("dp", None),
            P("dp", None),
            P(),
            P(None, "fsdp"),
            P("fsdp"),
            P(None, "fsdp"),
            P(),
            P(),
        ),
        out_specs=(P(), P("dp", "fsdp"), P("dp", "fsdp")),
        check_vma=False,
    )
```

```python
import jax
import jax.numpy as jnp
from jax import lax
from jax.experimental import pallas as pl
from jax.experimental.pallas import tpu as pltpu
from jax.sharding import PartitionSpec as P

loss_scale = 4096.0
lanes = 128
f32 = jnp.float32
bf16 = jnp.bfloat16


def gelu_tanh(values):
    inner = 0.7978845608 * (values + 0.044715 * values * values * values)
    return 0.5 * values * (1.0 + jnp.tanh(inner))


def gelu_slope(values):
    square = values * values
    tangent = jnp.tanh(0.7978845608 * (values + 0.044715 * values * square))
    return 0.5 * (1.0 + tangent) + 0.5 * values * (1.0 - tangent * tangent) * 0.7978845608 * (
        1.0 + 3.0 * 0.044715 * square
    )


def contract_last(left_side, right_side):
    return lax.dot_general(
        left_side, right_side, (((1,), (1,)), ((), ())), preferred_element_type=f32
    )


def fold_rows(values, width):
    count = values.shape[1] // width
    return jnp.concatenate(
        [
            values[i : i + 1, k * width : (k + 1) * width]
            for i in range(values.shape[0])
            for k in range(count)
        ],
        axis=0,
    )


def vmem_params(elements):
    return pltpu.CompilerParams(vmem_limit_bytes=min(56 * 2**20, 8 * elements + 8 * 2**20))


in_hbm = pl.BlockSpec(memory_space=pltpu.HBM)
in_any = pl.BlockSpec(memory_space=pl.ANY)


def hbm(value):
    return pltpu.with_memory_space_constraint(value, pltpu.HBM)


def near(value, keep):
    return pltpu.with_memory_space_constraint(value, pltpu.VMEM) if keep else value


def near_shape(shape, dtype, keep):
    return pltpu.VMEM(shape, dtype) if keep else jax.ShapeDtypeStruct(shape, dtype)


def norm_tokens(first, tokens, norm_gain, teacher, w_in, copies, splits):
    rows, width = tokens.shape
    images = teacher.shape[0]
    per_image = rows // images
    features = teacher.shape[1] // splits
    fold = features // 8
    keep = rows <= 512

    def kernel(
        first_ref, tokens_ref, gain_ref, teacher_ref, in_any, normed_ref, mean_ref, out_ref, in_ref, sem
    ):
        load = pltpu.make_async_copy(in_any, in_ref, sem)

        @pl.when(pl.program_id(0) == 0)
        def _():
            load.start()
            start = 0
            if splits > 1:
                start = pl.multiple_of(first_ref[0] * features, features)
            taken = teacher_ref[:, pl.ds(start, features)]
            folded = fold_rows(taken.astype(f32), fold).astype(bf16)
            out_ref[...] = jnp.broadcast_to(folded[None], out_ref.shape)

        values = tokens_ref[...].astype(f32)
        centered = values - jnp.mean(values, axis=-1, keepdims=True)
        inv_std = lax.rsqrt(jnp.mean(centered * centered, axis=-1, keepdims=True) + 1e-05)
        normed_ref[...] = (centered * inv_std * gain_ref[...]).astype(bf16)
        mean_ref[0] = jnp.mean(values, axis=0, keepdims=True)

        @pl.when(pl.program_id(0) == images - 1)
        def _():
            load.wait()

    payload = (copies, images * 8, fold)
    return pl.pallas_call(
        kernel,
        grid_spec=pltpu.PrefetchScalarGridSpec(
            num_scalar_prefetch=1,
            grid=(images,),
            in_specs=[
                pl.BlockSpec((per_image, width), lambda i, s: (i, 0)),
                pl.BlockSpec((1, width), lambda i, s: (0, 0)),
                pl.BlockSpec(teacher.shape, lambda i, s: (0, 0)),
                in_hbm,
            ],
            out_specs=[
                pl.BlockSpec((per_image, width), lambda i, s: (i, 0)),
                pl.BlockSpec((1, 1, width), lambda i, s: (i, 0, 0)),
                pl.BlockSpec(payload, lambda i, s: (0, 0, 0)),
                in_any,
            ],
            scratch_shapes=[pltpu.SemaphoreType.DMA],
        ),
        out_shape=[
            near_shape((rows, width), bf16, keep),
            jax.ShapeDtypeStruct((images, 1, width), f32),
            pltpu.HBM(payload, bf16),
            near_shape(w_in.shape, bf16, keep),
        ],
        compiler_params=vmem_params(3 * per_image * width + copies * images * features),
        cost_estimate=pl.CostEstimate(
            flops=10 * rows * width, bytes_accessed=4 * rows * width, transcendentals=0
        ),
        name="norm_tokens",
    )(first, hbm(tokens), hbm(norm_gain[None]), hbm(teacher), hbm(w_in))


def forward(first, normed, token_mean, w_in, b_in, w_out, b_out, copies):
    rows, width = normed.shape
    hidden = w_in.shape[1]
    images = token_mean.shape[0]
    per_image = rows // images
    tile = min(512, hidden)
    steps = hidden // tile
    folds = width // lanes
    keep = rows <= 512

    def kernel(
        first_ref, normed_ref, mean_ref, bias_ref, out_b_ref, in_any_ref, out_any_ref,
        pooled_ref, payload_ref, in_ref, out_w_ref, sems,
    ):
        step = pl.program_id(0)
        loads = [
            pltpu.make_async_copy(
                in_any_ref.at[:, pl.ds(j * tile, tile)], in_ref.at[j], sems.at[j]
            )
            for j in range(steps)
        ]
        loads.append(pltpu.make_async_copy(out_any_ref, out_w_ref, sems.at[steps]))

        @pl.when(step == 0)
        def _():
            for load in loads:
                load.start()

        for j in range(steps):

            @pl.when(step == j)
            def _():
                loads[j].wait()

        pre_act = (
            jnp.dot(normed_ref[...], in_ref[step], preferred_element_type=f32) + bias_ref[...]
        )
        pooled = jnp.mean(gelu_tanh(pre_act).reshape(images, per_image, tile), axis=1).astype(bf16)
        for j in range(steps):

            @pl.when(step == j)
            def _():
                pooled_ref[:, j * tile : (j + 1) * tile] = pooled

        @pl.when(step == steps - 1)
        def _():
            loads[steps].wait()
            total = contract_last(pooled_ref[...], out_w_ref[...])
            total += jnp.where(first_ref[0] == 0, mean_ref[:, 0, :] + out_b_ref[...], 0.0)
            folded = fold_rows(total, lanes).astype(bf16)
            payload_ref[...] = jnp.broadcast_to(folded[None], payload_ref.shape)

    payload = (copies, images * folds, lanes)
    return pl.pallas_call(
        kernel,
        grid_spec=pltpu.PrefetchScalarGridSpec(
            num_scalar_prefetch=1,
            grid=(steps,),
            in_specs=[
                pl.BlockSpec((rows, width), lambda j, s: (0, 0)),
                pl.BlockSpec((images, 1, width), lambda j, s: (0, 0, 0)),
                pl.BlockSpec((1, tile), lambda j, s: (0, j)),
                pl.BlockSpec((1, width), lambda j, s: (0, 0)),
                in_any,
                in_hbm,
            ],
            out_specs=[
                pl.BlockSpec((images, hidden), lambda j, s: (0, 0)),
                pl.BlockSpec(payload, lambda j, s: (0, 0, 0)),
            ],
            scratch_shapes=[
                pltpu.VMEM((steps, width, tile), bf16),
                pltpu.VMEM((width, hidden), bf16),
                pltpu.SemaphoreType.DMA((steps + 1,)),
            ],
        ),
        out_shape=[
            jax.ShapeDtypeStruct((images, hidden), bf16),
            pltpu.HBM(payload, bf16),
        ],
        compiler_params=vmem_params(width * hidden + copies * images * width),
        cost_estimate=pl.CostEstimate(
            flops=2 * rows * width * hidden,
            bytes_accessed=4 * width * hidden,
            transcendentals=rows * hidden,
        ),
        name="forward",
    )(first, near(normed, keep), token_mean, hbm(b_in[None]), hbm(b_out[None]), near(w_in, keep), hbm(w_out))


def mate_slopes(share_index, blocks, w_in, b_in, share):
    rows, width = blocks[0].shape
    count = len(blocks)
    tile = min(256, share)
    steps = share // tile
    turn = count * rows // steps
    keep = rows <= 512

    def kernel(index_ref, *refs):
        token_refs = refs[:count]
        bias_ref, in_any_ref, slope_ref, turned_ref, held_ref, in_ref, sems = refs[count:]
        step = pl.program_id(0)
        first_unit = index_ref[0] * share
        weights = [
            pltpu.make_async_copy(
                in_any_ref.at[:, pl.ds(pl.multiple_of(first_unit + j * tile, tile), tile)],
                in_ref.at[j],
                sems.at[count + j],
            )
            for j in range(steps)
        ]

        @pl.when(step == 0)
        def _():
            loads = [
                pltpu.make_async_copy(
                    token_refs[k], held_ref.at[pl.ds(k * rows, rows)], sems.at[k]
                )
                for k in range(count)
            ]
            for load in loads + weights:
                load.start()
            for load in loads:
                load.wait()

        for j in range(steps):

            @pl.when(step == j)
            def _():
                weights[j].wait()

        pre_act = jnp.dot(held_ref[...], in_ref[step], preferred_element_type=f32) + bias_ref[...]
        slope_ref[...] = gelu_slope(pre_act).astype(bf16)
        start = pl.multiple_of(step * turn, turn)
        turned_ref[...] = held_ref[pl.ds(start, turn)].T

    return pl.pallas_call(
        kernel,
        grid_spec=pltpu.PrefetchScalarGridSpec(
            num_scalar_prefetch=1,
            grid=(steps,),
            in_specs=[in_any] * count
            + [pl.BlockSpec((1, tile), lambda j, s: (0, s[0] * steps + j)), in_any],
            out_specs=[
                pl.BlockSpec((count * rows, tile), lambda j, s: (0, j)),
                pl.BlockSpec((width, turn), lambda j, s: (0, j)),
            ],
            scratch_shapes=[
                pltpu.VMEM((count * rows, width), bf16),
                pltpu.VMEM((steps, width, tile), bf16),
                pltpu.SemaphoreType.DMA((count + steps,)),
            ],
        ),
        out_shape=[
            near_shape((count * rows, share), bf16, keep),
            near_shape((width, count * rows), bf16, keep),
        ],
        compiler_params=vmem_params(count * rows * (width + share)),
        cost_estimate=pl.CostEstimate(
            flops=2 * rows * count * width * share,
            bytes_accessed=4 * rows * count * width,
            transcendentals=rows * count * share,
        ),
        name="mate_slopes",
    )(share_index, *[near(block, keep) for block in blocks], hbm(b_in[None]), near(w_in, keep))


def target_gram(arrived, images):
    senders, folded, fold = arrived.shape
    folds = senders * folded // images
    keep = images <= 64

    def kernel(arrived_ref, gram_ref, wide_ref):
        wide_ref[...] = arrived_ref[...].astype(f32).reshape(images, folds, fold)
        rows = jnp.concatenate([wide_ref[:, k, :].astype(bf16) for k in range(folds)], axis=1)
        gram_ref[...] = contract_last(rows, rows)

    return pl.pallas_call(
        kernel,
        out_shape=jax.ShapeDtypeStruct((images, images), f32),
        scratch_shapes=[pltpu.VMEM((images, folds, fold), f32)],
        compiler_params=vmem_params(images * folds * fold),
        cost_estimate=pl.CostEstimate(
            flops=2 * images * images * folds * fold,
            bytes_accessed=2 * images * folds * fold,
            transcendentals=0,
        ),
        name="target_gram",
    )(near(arrived, keep))


def unit_gram(parts):
    images = parts[0].shape[0]

    def kernel(*refs):
        gram_ref = refs[-1]
        gram = sum((ref[...] for ref in refs[1:-1]), refs[0][...])
        row = lax.broadcasted_iota(jnp.int32, gram.shape, 0)
        column = lax.broadcasted_iota(jnp.int32, gram.shape, 1)
        diagonal = jnp.where(row == column, gram, 0.0)
        down = lax.rsqrt(jnp.sum(diagonal, axis=1, keepdims=True) + 1e-06)
        across = lax.rsqrt(jnp.sum(diagonal, axis=0, keepdims=True) + 1e-06)
        gram_ref[...] = gram * down * across

    return pl.pallas_call(
        kernel,
        out_shape=jax.ShapeDtypeStruct((images, images), f32),
        compiler_params=vmem_params(4 * images * images),
        cost_estimate=pl.CostEstimate(
            flops=8 * images * images, bytes_accessed=8 * images * images, transcendentals=0
        ),
        name="unit_gram",
    )(*parts)


def backward(
    index, arrived, gram, final_gain, pooled, w_out, slopes, turns, mates, dp_size, per_image
):
    senders, folded, _ = arrived.shape
    width = w_out.shape[0]
    images = gram.shape[0]
    own_images, hidden = pooled.shape
    fsdp_size = senders // dp_size
    folds = width // lanes
    share = hidden // mates
    mate_rows = sum(turned.shape[1] for turned in turns)
    parts = len(turns)
    out_rows = width // dp_size
    piece = min(share, 256)
    pieces = share // piece
    extra = own_images * hidden // piece
    group = max(1, 512 // out_rows)
    steps = dp_size // group
    in_rows = out_rows * pieces
    keep = images <= 64

    def kernel(index_ref, arrived_any, gram_ref, gain_ref, pooled_ref, out_w_any, *refs):
        slope_any, turned_any, refs = refs[:parts], refs[parts : 2 * parts], refs[2 * parts :]
        loss_ref, dembed_ref, payload_any, wide_ref, hidden_ref, extra_ref = refs[:6]
        out_w_ref, slope_ref, turned_ref, arrived_ref, payload_ref, sems = refs[6:]
        step = pl.program_id(0)

        @pl.when(step == 0)
        def _():
            first_unit = pl.multiple_of(lax.rem(index_ref[0], mates) * share, share)
            loads = [
                pltpu.make_async_copy(
                    out_w_any.at[:, pl.ds(first_unit, share)], out_w_ref, sems.at[0]
                ),
                pltpu.make_async_copy(arrived_any, arrived_ref, sems.at[1]),
            ]
            start = 0
            for k in range(parts):
                taken = pl.ds(start, turned_any[k].shape[1])
                loads += [
                    pltpu.make_async_copy(slope_any[k], slope_ref.at[taken], sems.at[2 + 2 * k]),
                    pltpu.make_async_copy(
                        turned_any[k], turned_ref.at[:, taken], sems.at[3 + 2 * k]
                    ),
                ]
                start += turned_any[k].shape[1]
            loads[1].start()
            for load in loads[:1] + loads[2:]:
                load.start()
            loads[1].wait()
            embeds = arrived_ref[...].astype(f32).reshape(dp_size, fsdp_size, folded, lanes)
            wide_ref[...] = jnp.sum(embeds, axis=1).reshape(images, folds, lanes)
            embedding = jnp.concatenate([wide_ref[:, k, :] for k in range(folds)], axis=1)
            gain = gain_ref[...]
            centered = embedding - jnp.mean(embedding, axis=-1, keepdims=True)
            inv_std = lax.rsqrt(jnp.mean(centered * centered, axis=-1, keepdims=True) + 1e-05)
            normed = centered * inv_std
            scaled = normed * gain
            square = jnp.sum(scaled * scaled, axis=-1, keepdims=True) + 1e-06
            inv_norm = lax.rsqrt(square)
            unit = scaled * inv_norm
            student = unit.astype(bf16)
            resid = contract_last(student, student) - gram_ref[...]
            loss_ref[0, 0] = jnp.sum(resid * resid) / images
            dstudent = (loss_scale * 4.0 / images) * jnp.dot(
                resid.astype(bf16), student, preferred_element_type=f32
            )
            dunit = (
                dstudent - unit * jnp.sum(unit * dstudent, axis=-1, keepdims=True)
            ) * inv_norm
            gain_grad = dunit * gain
            dembed = inv_std * (
                gain_grad
                - jnp.mean(gain_grad, axis=-1, keepdims=True)
                - normed * jnp.mean(gain_grad * normed, axis=-1, keepdims=True)
            )
            dembed_b = dembed.astype(bf16)
            dembed_ref[...] = dembed_b
            shape = (mates * own_images, images)
            row = lax.broadcasted_iota(jnp.int32, shape, 0)
            column = lax.broadcasted_iota(jnp.int32, shape, 1)
            owner = (row // own_images) ^ index_ref[0]
            pick = (owner * own_images + row % own_images == column).astype(f32).astype(bf16)
            mate_dembed = jnp.dot(pick, dembed_b, preferred_element_type=f32).astype(bf16)
            loads[0].wait()
            dpooled = jnp.dot(mate_dembed, out_w_ref[...], preferred_element_type=f32) / per_image
            for load in loads[2::2]:
                load.wait()
            for k in range(mates * own_images):
                rows = slice(k * per_image, (k + 1) * per_image)
                hidden_ref[rows] = (dpooled[k : k + 1] * slope_ref[rows].astype(f32)).astype(bf16)
            extra_ref[...] = fold_rows(pooled_ref[...].astype(f32), piece).astype(bf16)
            for load in loads[3::2]:
                load.wait()

        taken = group * out_rows
        rows = turned_ref[pl.ds(pl.multiple_of(step * taken, taken), taken)]
        term = jnp.dot(rows, hidden_ref[...], preferred_element_type=f32).astype(bf16)
        for d in range(group):
            for k in range(pieces):
                payload_ref[step, d, k * out_rows : (k + 1) * out_rows] = term[
                    d * out_rows : (d + 1) * out_rows, k * piece : (k + 1) * piece
                ]
            payload_ref[step, d, in_rows:] = extra_ref[...]
        stores = [
            pltpu.make_async_copy(
                payload_ref.at[j], payload_any.at[pl.ds(j * group, group)], sems.at[2 + 2 * parts + j]
            )
            for j in range(steps)
        ]
        for j in range(steps):

            @pl.when(step == j)
            def _():
                stores[j].start()

        @pl.when(step == steps - 1)
        def _():
            for store in stores:
                store.wait()

    return pl.pallas_call(
        kernel,
        grid_spec=pltpu.PrefetchScalarGridSpec(
            num_scalar_prefetch=1,
            grid=(steps,),
            in_specs=[
                in_any,
                pl.BlockSpec(gram.shape, lambda j, s: (0, 0)),
                pl.BlockSpec((1, width), lambda j, s: (0, 0)),
                pl.BlockSpec(pooled.shape, lambda j, s: (0, 0)),
                in_any,
            ]
            + [in_any] * (2 * parts),
            out_specs=[
                pl.BlockSpec(memory_space=pltpu.SMEM),
                pl.BlockSpec((images, width), lambda j, s: (0, 0)),
                in_hbm,
            ],
            scratch_shapes=[
                pltpu.VMEM((images, folds, lanes), f32),
                pltpu.VMEM((mate_rows, share), bf16),
                pltpu.VMEM((extra, piece), bf16),
                pltpu.VMEM((width, share), bf16),
                pltpu.VMEM((mate_rows, share), bf16),
                pltpu.VMEM((width, mate_rows), bf16),
                pltpu.VMEM(arrived.shape, bf16),
                pltpu.VMEM((steps, group, in_rows + extra, piece), bf16),
                pltpu.SemaphoreType.DMA((2 + 2 * parts + steps,)),
            ],
        ),
        out_shape=[
            jax.ShapeDtypeStruct((1, 1), f32),
            jax.ShapeDtypeStruct((images, width), bf16),
            pltpu.HBM((dp_size, in_rows + extra, piece), bf16),
        ],
        compiler_params=vmem_params(mate_rows * (width + share) // 2 + arrived.size),
        cost_estimate=pl.CostEstimate(
            flops=2 * mate_rows * width * share,
            bytes_accessed=2 * mate_rows * (width + share),
            transcendentals=0,
        ),
        name="backward",
    )(
        index, near(arrived, keep), gram, hbm(final_gain[None]), pooled, hbm(w_out),
        *[near(slope, keep) for slope in slopes], *[near(turned, keep) for turned in turns],
    )


def own_columns(index, dembed, out_rows):
    images, width = dembed.shape
    keep = images <= 64

    def kernel(index_ref, dembed_ref, columns_ref):
        row = lax.broadcasted_iota(jnp.int32, (out_rows, width), 0)
        column = lax.broadcasted_iota(jnp.int32, (out_rows, width), 1)
        pick = (row + index_ref[0] * out_rows == column).astype(f32).astype(bf16)
        columns_ref[...] = contract_last(pick, dembed_ref[...]).astype(bf16)

    return pl.pallas_call(
        kernel,
        in_specs=[
            pl.BlockSpec(memory_space=pltpu.SMEM),
            pl.BlockSpec(memory_space=pltpu.VMEM),
        ],
        out_shape=near_shape((out_rows, images), bf16, keep),
        compiler_params=vmem_params(images * width),
        cost_estimate=pl.CostEstimate(
            flops=2 * images * out_rows * width,
            bytes_accessed=2 * images * width,
            transcendentals=0,
        ),
        name="own_columns",
    )(index, dembed)


def finish(arrived, columns, mates, hidden):
    dp_size, _, piece = arrived.shape
    out_rows, images = columns.shape
    pieces = hidden // mates // piece
    in_rows = out_rows * pieces
    folds = hidden // piece
    keep = images <= 64

    def kernel(arrived_ref, columns_ref, in_ref, out_ref, wide_ref):
        wide_ref[...] = arrived_ref[:, in_rows:].astype(f32).reshape(images, folds, piece)
        rows = jnp.concatenate([wide_ref[:, k, :].astype(bf16) for k in range(folds)], axis=1)
        out_ref[...] = jnp.dot(columns_ref[...], rows, preferred_element_type=f32).astype(bf16)
        for q in range(mates):
            for k in range(pieces):
                taken = slice(k * out_rows, (k + 1) * out_rows)
                total = arrived_ref[q, taken].astype(f32)
                for s in range(q + mates, dp_size, mates):
                    total += arrived_ref[s, taken].astype(f32)
                start = (q * pieces + k) * piece
                in_ref[:, start : start + piece] = total.astype(bf16)

    return pl.pallas_call(
        kernel,
        out_shape=[jax.ShapeDtypeStruct((out_rows, hidden), bf16)] * 2,
        scratch_shapes=[pltpu.VMEM((images, folds, piece), f32)],
        compiler_params=vmem_params(arrived.size),
        cost_estimate=pl.CostEstimate(
            flops=2 * images * out_rows * hidden,
            bytes_accessed=2 * arrived.size,
            transcendentals=0,
        ),
        name="finish",
    )(near(arrived, keep), near(columns, keep))


def exchange(blocks, axes):
    return lax.all_to_all(blocks, axes, split_axis=0, concat_axis=0, tiled=True)


def mates_of(dp_size, hidden):
    mates = 4
    while dp_size % mates or hidden % (lanes * mates):
        mates //= 2
    return mates


def swap(value, axis, step):
    return lax.ppermute(value, axis, [(i, i ^ step) for i in range(lax.axis_size(axis))])


def after(value, other):
    return lax.optimization_barrier((value, other))[0]


def body(tokens, teacher, norm_gain, w_in, b_in, w_out, b_out, final_gain):
    dp_size = lax.axis_size("dp")
    fsdp_size = lax.axis_size("fsdp")
    images = teacher.shape[0] * dp_size
    per_image = tokens.shape[0] // teacher.shape[0]
    hidden = w_in.shape[1]
    mates = mates_of(dp_size, hidden)
    index = lax.axis_index("dp").astype(jnp.int32)[None]
    first = lax.axis_index("fsdp").astype(jnp.int32)[None]

    splits = fsdp_size if teacher.shape[1] % (fsdp_size * 8 * lanes) == 0 else 1

    normed, token_mean, teacher_rows, w_in_near = norm_tokens(
        first, tokens, norm_gain, teacher, w_in, dp_size, splits
    )
    blocks = {0: normed}
    step = mates // 2
    if step:
        blocks[step] = swap(normed, "dp", step)
    if step > 1:
        blocks[1] = swap(normed, "dp", 1)
    all_teacher = exchange(teacher_rows, "dp")
    pooled, embed_rows = forward(
        first, normed, token_mean, w_in_near, b_in, w_out, b_out, dp_size * fsdp_size
    )
    all_embed = exchange(embed_rows, ("dp", "fsdp"))
    gram = target_gram(after(all_teacher, pooled), images)
    if step > 1:
        blocks[step + 1] = swap(after(blocks[step], gram), "dp", 1)
    if splits == 1:
        grams = [gram]
    elif splits == 2:
        grams = [gram, swap(gram, "fsdp", 1)]
    else:
        grams = [lax.psum(gram, "fsdp")]
    slopes, turns = zip(
        *[
            mate_slopes(
                index % mates,
                [blocks[k] for k in range(start, min(start + 2, mates))],
                w_in_near,
                b_in,
                hidden // mates,
            )
            for start in range(0, mates, 2)
        ]
    )
    loss, dembed, parts = backward(
        index, all_embed, unit_gram(grams), final_gain, pooled, w_out, slopes, turns,
        mates, dp_size, per_image,
    )
    arrived = exchange(parts, "dp")
    columns = own_columns(index, dembed, dembed.shape[1] // dp_size)
    grad_in, grad_out = finish(arrived, columns, mates, hidden)
    return (loss[0, 0], grad_in, grad_out)


def solution(mesh):
    return jax.shard_map(
        body,
        mesh=mesh,
        in_specs=(
            P("dp", None),
            P("dp", None),
            P(),
            P(None, "fsdp"),
            P("fsdp"),
            P(None, "fsdp"),
            P(),
            P(),
        ),
        out_specs=(P(), P("dp", "fsdp"), P("dp", "fsdp")),
        check_vma=False,
    )
```

```python
import jax
import jax.numpy as jnp
from jax import lax
from jax.experimental import pallas as pl
from jax.experimental.pallas import tpu as pltpu
from jax.sharding import PartitionSpec as P

loss_scale = 4096.0
lanes = 128
f32 = jnp.float32
bf16 = jnp.bfloat16


def gelu_tanh(values):
    inner = 0.7978845608 * (values + 0.044715 * values * values * values)
    return 0.5 * values * (1.0 + jnp.tanh(inner))


def gelu_slope(values):
    square = values * values
    tangent = jnp.tanh(0.7978845608 * (values + 0.044715 * values * square))
    return 0.5 * (1.0 + tangent) + 0.5 * values * (1.0 - tangent * tangent) * 0.7978845608 * (
        1.0 + 3.0 * 0.044715 * square
    )


def contract_last(left_side, right_side):
    return lax.dot_general(
        left_side, right_side, (((1,), (1,)), ((), ())), preferred_element_type=f32
    )


def fold_rows(values, width):
    count = values.shape[1] // width
    return jnp.concatenate(
        [
            values[i : i + 1, k * width : (k + 1) * width]
            for i in range(values.shape[0])
            for k in range(count)
        ],
        axis=0,
    )


def vmem_params(elements):
    return pltpu.CompilerParams(vmem_limit_bytes=min(56 * 2**20, 8 * elements + 8 * 2**20))


in_hbm = pl.BlockSpec(memory_space=pltpu.HBM)
in_any = pl.BlockSpec(memory_space=pl.ANY)


def hbm(value):
    return pltpu.with_memory_space_constraint(value, pltpu.HBM)


def near(value, keep):
    return pltpu.with_memory_space_constraint(value, pltpu.VMEM) if keep else value


def near_shape(shape, dtype, keep):
    return pltpu.VMEM(shape, dtype) if keep else jax.ShapeDtypeStruct(shape, dtype)


def normalize(values, gain):
    centered = values - jnp.mean(values, axis=-1, keepdims=True)
    inv_std = lax.rsqrt(jnp.mean(centered * centered, axis=-1, keepdims=True) + 1e-05)
    return (centered * inv_std * gain).astype(bf16)


def teacher_payload(first, teacher, copies, splits):
    images = teacher.shape[0]
    features = teacher.shape[1] // splits
    fold = features // 8

    def kernel(first_ref, teacher_ref, out_ref):
        start = 0
        if splits > 1:
            start = pl.multiple_of(first_ref[0] * features, features)
        folded = fold_rows(teacher_ref[:, pl.ds(start, features)].astype(f32), fold).astype(bf16)
        out_ref[...] = jnp.broadcast_to(folded[None], out_ref.shape)

    return pl.pallas_call(
        kernel,
        in_specs=[
            pl.BlockSpec(memory_space=pltpu.SMEM),
            pl.BlockSpec(memory_space=pltpu.VMEM),
        ],
        out_shape=pltpu.HBM((copies, images * 8, fold), bf16),
        compiler_params=vmem_params(copies * images * features),
        cost_estimate=pl.CostEstimate(
            flops=copies * images * features,
            bytes_accessed=2 * copies * images * features,
            transcendentals=0,
        ),
        name="teacher_payload",
    )(first, hbm(teacher))


def forward(first, tokens, norm_gain, w_in, b_in, w_out, b_out, copies, images):
    rows, width = tokens.shape
    hidden = w_in.shape[1]
    per_image = rows // images
    tile = min(512, hidden)
    steps = hidden // tile
    folds = width // lanes

    def kernel(
        first_ref, gain_ref, bias_ref, out_b_ref, tokens_any, in_any_ref, out_any_ref,
        pooled_ref, payload_ref, tokens_ref, in_ref, out_w_ref, sems,
    ):
        loads = [
            pltpu.make_async_copy(
                in_any_ref.at[:, pl.ds(j * tile, tile)], in_ref.at[j], sems.at[j]
            )
            for j in range(steps)
        ]
        loads.append(pltpu.make_async_copy(out_any_ref, out_w_ref, sems.at[steps]))
        loads.append(pltpu.make_async_copy(tokens_any, tokens_ref, sems.at[steps + 1]))
        loads[-1].start()
        for load in loads[:-1]:
            load.start()
        loads[-1].wait()
        values = tokens_ref[...].astype(f32)
        normed = normalize(values, gain_ref[...])
        token_mean = jnp.mean(values.reshape(images, per_image, width), axis=1)
        for j in range(steps):
            taken = slice(j * tile, (j + 1) * tile)
            loads[j].wait()
            pre_act = jnp.dot(normed, in_ref[j], preferred_element_type=f32) + bias_ref[:, taken]
            pooled_ref[:, taken] = jnp.mean(
                gelu_tanh(pre_act).reshape(images, per_image, tile), axis=1
            ).astype(bf16)
        loads[steps].wait()
        total = contract_last(pooled_ref[...], out_w_ref[...])
        total += jnp.where(first_ref[0] == 0, token_mean + out_b_ref[...], 0.0)
        folded = fold_rows(total, lanes).astype(bf16)
        payload_ref[...] = jnp.broadcast_to(folded[None], payload_ref.shape)

    whole = pl.BlockSpec(memory_space=pltpu.VMEM)
    payload = (copies, images * folds, lanes)
    return pl.pallas_call(
        kernel,
        in_specs=[pl.BlockSpec(memory_space=pltpu.SMEM)] + [whole] * 3 + [in_hbm] * 3,
        out_specs=[whole, whole],
        out_shape=[
            jax.ShapeDtypeStruct((images, hidden), bf16),
            pltpu.HBM(payload, bf16),
        ],
        scratch_shapes=[
            pltpu.VMEM((rows, width), bf16),
            pltpu.VMEM((steps, width, tile), bf16),
            pltpu.VMEM((width, hidden), bf16),
            pltpu.SemaphoreType.DMA((steps + 2,)),
        ],
        compiler_params=vmem_params(
            rows * width + width * hidden + copies * images * width
        ),
        cost_estimate=pl.CostEstimate(
            flops=2 * rows * width * hidden,
            bytes_accessed=4 * width * hidden,
            transcendentals=rows * hidden,
        ),
        name="forward",
    )(
        first, hbm(norm_gain[None]), hbm(b_in[None]), hbm(b_out[None]),
        hbm(tokens), hbm(w_in), hbm(w_out),
    )


def mate_slopes(share_index, blocks, norm_gain, w_in, b_in, share):
    rows, width = blocks[0].shape
    count = len(blocks)
    tile = min(256, share)
    steps = share // tile
    turn = count * rows // steps
    keep = rows <= 512

    def kernel(index_ref, *refs):
        token_refs = refs[:count]
        gain_ref, bias_ref, in_any_ref, slope_ref, turned_ref = refs[count : count + 5]
        held_ref, normed_ref, in_ref, sems = refs[count + 5 :]
        step = pl.program_id(0)
        first_unit = index_ref[0] * share
        weights = [
            pltpu.make_async_copy(
                in_any_ref.at[:, pl.ds(pl.multiple_of(first_unit + j * tile, tile), tile)],
                in_ref.at[j],
                sems.at[count + j],
            )
            for j in range(steps)
        ]

        @pl.when(step == 0)
        def _():
            loads = [
                pltpu.make_async_copy(token_refs[k], held_ref.at[k], sems.at[k])
                for k in range(count)
            ]
            for load in loads + weights:
                load.start()
            for k in range(count):
                loads[k].wait()
                start = pl.multiple_of((index_ref[0] ^ k) * rows, rows)
                normed_ref[pl.ds(start, rows)] = normalize(
                    held_ref[k].astype(f32), gain_ref[...]
                )

        for j in range(steps):

            @pl.when(step == j)
            def _():
                weights[j].wait()

        pre_act = (
            jnp.dot(normed_ref[...], in_ref[step], preferred_element_type=f32) + bias_ref[...]
        )
        slope_ref[...] = gelu_slope(pre_act).astype(bf16)
        start = pl.multiple_of(step * turn, turn)
        turned_ref[...] = normed_ref[pl.ds(start, turn)].T

    return pl.pallas_call(
        kernel,
        grid_spec=pltpu.PrefetchScalarGridSpec(
            num_scalar_prefetch=1,
            grid=(steps,),
            in_specs=[in_any] * count
            + [
                pl.BlockSpec((1, width), lambda j, s: (0, 0)),
                pl.BlockSpec((1, tile), lambda j, s: (0, s[0] * steps + j)),
                in_hbm,
            ],
            out_specs=[
                pl.BlockSpec((count * rows, tile), lambda j, s: (0, j)),
                pl.BlockSpec((width, turn), lambda j, s: (0, j)),
            ],
            scratch_shapes=[
                pltpu.VMEM((count, rows, width), bf16),
                pltpu.VMEM((count * rows, width), bf16),
                pltpu.VMEM((steps, width, tile), bf16),
                pltpu.SemaphoreType.DMA((count + steps,)),
            ],
        ),
        out_shape=[
            near_shape((count * rows, share), bf16, keep),
            near_shape((width, count * rows), bf16, keep),
        ],
        compiler_params=vmem_params(count * rows * (width + share)),
        cost_estimate=pl.CostEstimate(
            flops=2 * rows * count * width * share,
            bytes_accessed=4 * rows * count * width,
            transcendentals=rows * count * share,
        ),
        name="mate_slopes",
    )(
        share_index,
        *[near(block, keep) if k % 2 else hbm(block) for k, block in enumerate(blocks)],
        hbm(norm_gain[None]),
        hbm(b_in[None]),
        hbm(w_in),
    )


def target_gram(arrived, images):
    senders, folded, fold = arrived.shape
    folds = senders * folded // images
    keep = images <= 64

    def kernel(arrived_ref, gram_ref, wide_ref):
        wide_ref[...] = arrived_ref[...].astype(f32).reshape(images, folds, fold)
        rows = jnp.concatenate([wide_ref[:, k, :].astype(bf16) for k in range(folds)], axis=1)
        gram_ref[...] = contract_last(rows, rows)

    return pl.pallas_call(
        kernel,
        out_shape=jax.ShapeDtypeStruct((images, images), f32),
        scratch_shapes=[pltpu.VMEM((images, folds, fold), f32)],
        compiler_params=vmem_params(images * folds * fold),
        cost_estimate=pl.CostEstimate(
            flops=2 * images * images * folds * fold,
            bytes_accessed=2 * images * folds * fold,
            transcendentals=0,
        ),
        name="target_gram",
    )(near(arrived, keep))


def unit_gram(parts):
    images = parts[0].shape[0]

    def kernel(*refs):
        gram_ref = refs[-1]
        gram = sum((ref[...] for ref in refs[1:-1]), refs[0][...])
        row = lax.broadcasted_iota(jnp.int32, gram.shape, 0)
        column = lax.broadcasted_iota(jnp.int32, gram.shape, 1)
        diagonal = jnp.where(row == column, gram, 0.0)
        down = lax.rsqrt(jnp.sum(diagonal, axis=1, keepdims=True) + 1e-06)
        across = lax.rsqrt(jnp.sum(diagonal, axis=0, keepdims=True) + 1e-06)
        gram_ref[...] = gram * down * across

    return pl.pallas_call(
        kernel,
        out_shape=jax.ShapeDtypeStruct((images, images), f32),
        compiler_params=vmem_params(4 * images * images),
        cost_estimate=pl.CostEstimate(
            flops=8 * images * images, bytes_accessed=8 * images * images, transcendentals=0
        ),
        name="unit_gram",
    )(*parts)


def backward(
    index, arrived, gram, final_gain, pooled, w_out, slopes, turns, mates, dp_size, per_image
):
    senders, folded, _ = arrived.shape
    width = w_out.shape[0]
    images = gram.shape[0]
    own_images, hidden = pooled.shape
    fsdp_size = senders // dp_size
    folds = width // lanes
    share = hidden // mates
    mate_rows = sum(turned.shape[1] for turned in turns)
    parts = len(turns)
    out_rows = width // dp_size
    piece = min(share, 256)
    pieces = share // piece
    extra = own_images * hidden // piece
    group = max(1, 512 // out_rows)
    steps = dp_size // group
    in_rows = out_rows * pieces
    keep = images <= 64

    def kernel(index_ref, arrived_any, gram_ref, gain_ref, pooled_ref, out_w_any, *refs):
        slope_any, turned_any, refs = refs[:parts], refs[parts : 2 * parts], refs[2 * parts :]
        loss_ref, dembed_ref, payload_any, wide_ref, hidden_ref, extra_ref = refs[:6]
        out_w_ref, slope_ref, turned_ref, arrived_ref, payload_ref, sems = refs[6:]
        step = pl.program_id(0)

        @pl.when(step == 0)
        def _():
            first_unit = pl.multiple_of(lax.rem(index_ref[0], mates) * share, share)
            loads = [
                pltpu.make_async_copy(
                    out_w_any.at[:, pl.ds(first_unit, share)], out_w_ref, sems.at[0]
                ),
                pltpu.make_async_copy(arrived_any, arrived_ref, sems.at[1]),
            ]
            start = 0
            for k in range(parts):
                taken = pl.ds(start, turned_any[k].shape[1])
                loads += [
                    pltpu.make_async_copy(slope_any[k], slope_ref.at[taken], sems.at[2 + 2 * k]),
                    pltpu.make_async_copy(
                        turned_any[k], turned_ref.at[:, taken], sems.at[3 + 2 * k]
                    ),
                ]
                start += turned_any[k].shape[1]
            loads[1].start()
            for load in loads[:1] + loads[2:]:
                load.start()
            loads[1].wait()
            embeds = arrived_ref[...].astype(f32).reshape(dp_size, fsdp_size, folded, lanes)
            wide_ref[...] = jnp.sum(embeds, axis=1).reshape(images, folds, lanes)
            embedding = jnp.concatenate([wide_ref[:, k, :] for k in range(folds)], axis=1)
            gain = gain_ref[...]
            centered = embedding - jnp.mean(embedding, axis=-1, keepdims=True)
            inv_std = lax.rsqrt(jnp.mean(centered * centered, axis=-1, keepdims=True) + 1e-05)
            normed = centered * inv_std
            scaled = normed * gain
            square = jnp.sum(scaled * scaled, axis=-1, keepdims=True) + 1e-06
            inv_norm = lax.rsqrt(square)
            unit = scaled * inv_norm
            student = unit.astype(bf16)
            resid = contract_last(student, student) - gram_ref[...]
            loss_ref[0, 0] = jnp.sum(resid * resid) / images
            dstudent = (loss_scale * 4.0 / images) * jnp.dot(
                resid.astype(bf16), student, preferred_element_type=f32
            )
            dunit = (
                dstudent - unit * jnp.sum(unit * dstudent, axis=-1, keepdims=True)
            ) * inv_norm
            gain_grad = dunit * gain
            dembed = inv_std * (
                gain_grad
                - jnp.mean(gain_grad, axis=-1, keepdims=True)
                - normed * jnp.mean(gain_grad * normed, axis=-1, keepdims=True)
            )
            dembed_b = dembed.astype(bf16)
            dembed_ref[...] = dembed_b
            rows = mates * own_images
            start = pl.multiple_of(index_ref[0] // mates * rows, rows)
            mate_dembed = dembed_ref[pl.ds(start, rows)]
            loads[0].wait()
            dpooled = jnp.dot(mate_dembed, out_w_ref[...], preferred_element_type=f32) / per_image
            for load in loads[2::2]:
                load.wait()
            for k in range(mates * own_images):
                rows = slice(k * per_image, (k + 1) * per_image)
                hidden_ref[rows] = (dpooled[k : k + 1] * slope_ref[rows].astype(f32)).astype(bf16)
            extra_ref[...] = fold_rows(pooled_ref[...].astype(f32), piece).astype(bf16)
            for load in loads[3::2]:
                load.wait()

        taken = group * out_rows
        rows = turned_ref[pl.ds(pl.multiple_of(step * taken, taken), taken)]
        term = jnp.dot(rows, hidden_ref[...], preferred_element_type=f32).astype(bf16)
        for d in range(group):
            for k in range(pieces):
                payload_ref[step, d, k * out_rows : (k + 1) * out_rows] = term[
                    d * out_rows : (d + 1) * out_rows, k * piece : (k + 1) * piece
                ]
            payload_ref[step, d, in_rows:] = extra_ref[...]
        stores = [
            pltpu.make_async_copy(
                payload_ref.at[j], payload_any.at[pl.ds(j * group, group)], sems.at[2 + 2 * parts + j]
            )
            for j in range(steps)
        ]
        for j in range(steps):

            @pl.when(step == j)
            def _():
                stores[j].start()

        @pl.when(step == steps - 1)
        def _():
            for store in stores:
                store.wait()

    return pl.pallas_call(
        kernel,
        grid_spec=pltpu.PrefetchScalarGridSpec(
            num_scalar_prefetch=1,
            grid=(steps,),
            in_specs=[
                in_any,
                pl.BlockSpec(gram.shape, lambda j, s: (0, 0)),
                pl.BlockSpec((1, width), lambda j, s: (0, 0)),
                pl.BlockSpec(pooled.shape, lambda j, s: (0, 0)),
                in_any,
            ]
            + [in_any] * (2 * parts),
            out_specs=[
                pl.BlockSpec(memory_space=pltpu.SMEM),
                pl.BlockSpec((images, width), lambda j, s: (0, 0)),
                in_hbm,
            ],
            scratch_shapes=[
                pltpu.VMEM((images, folds, lanes), f32),
                pltpu.VMEM((mate_rows, share), bf16),
                pltpu.VMEM((extra, piece), bf16),
                pltpu.VMEM((width, share), bf16),
                pltpu.VMEM((mate_rows, share), bf16),
                pltpu.VMEM((width, mate_rows), bf16),
                pltpu.VMEM(arrived.shape, bf16),
                pltpu.VMEM((steps, group, in_rows + extra, piece), bf16),
                pltpu.SemaphoreType.DMA((2 + 2 * parts + steps,)),
            ],
        ),
        out_shape=[
            jax.ShapeDtypeStruct((1, 1), f32),
            jax.ShapeDtypeStruct((images, width), bf16),
            pltpu.HBM((dp_size, in_rows + extra, piece), bf16),
        ],
        compiler_params=vmem_params(mate_rows * (width + share) // 2 + arrived.size),
        cost_estimate=pl.CostEstimate(
            flops=2 * mate_rows * width * share,
            bytes_accessed=2 * mate_rows * (width + share),
            transcendentals=0,
        ),
        name="backward",
    )(
        index, near(arrived, keep), gram, hbm(final_gain[None]), pooled, hbm(w_out),
        *[near(slope, keep) for slope in slopes], *[near(turned, keep) for turned in turns],
    )


def own_columns(index, dembed, out_rows):
    images, width = dembed.shape
    keep = images <= 64

    def kernel(index_ref, dembed_ref, columns_ref):
        row = lax.broadcasted_iota(jnp.int32, (out_rows, width), 0)
        column = lax.broadcasted_iota(jnp.int32, (out_rows, width), 1)
        pick = (row + index_ref[0] * out_rows == column).astype(f32).astype(bf16)
        columns_ref[...] = contract_last(pick, dembed_ref[...]).astype(bf16)

    return pl.pallas_call(
        kernel,
        in_specs=[
            pl.BlockSpec(memory_space=pltpu.SMEM),
            pl.BlockSpec(memory_space=pltpu.VMEM),
        ],
        out_shape=near_shape((out_rows, images), bf16, keep),
        compiler_params=vmem_params(images * width),
        cost_estimate=pl.CostEstimate(
            flops=2 * images * out_rows * width,
            bytes_accessed=2 * images * width,
            transcendentals=0,
        ),
        name="own_columns",
    )(index, dembed)


def finish(arrived, columns, mates, hidden):
    dp_size, _, piece = arrived.shape
    out_rows, images = columns.shape
    pieces = hidden // mates // piece
    in_rows = out_rows * pieces
    folds = hidden // piece
    keep = images <= 64

    def kernel(arrived_ref, columns_ref, in_ref, out_ref, wide_ref):
        wide_ref[...] = arrived_ref[:, in_rows:].astype(f32).reshape(images, folds, piece)
        rows = jnp.concatenate([wide_ref[:, k, :].astype(bf16) for k in range(folds)], axis=1)
        out_ref[...] = jnp.dot(columns_ref[...], rows, preferred_element_type=f32).astype(bf16)
        for q in range(mates):
            for k in range(pieces):
                taken = slice(k * out_rows, (k + 1) * out_rows)
                total = arrived_ref[q, taken].astype(f32)
                for s in range(q + mates, dp_size, mates):
                    total += arrived_ref[s, taken].astype(f32)
                start = (q * pieces + k) * piece
                in_ref[:, start : start + piece] = total.astype(bf16)

    return pl.pallas_call(
        kernel,
        out_shape=[jax.ShapeDtypeStruct((out_rows, hidden), bf16)] * 2,
        scratch_shapes=[pltpu.VMEM((images, folds, piece), f32)],
        compiler_params=vmem_params(arrived.size),
        cost_estimate=pl.CostEstimate(
            flops=2 * images * out_rows * hidden,
            bytes_accessed=2 * arrived.size,
            transcendentals=0,
        ),
        name="finish",
    )(near(arrived, keep), near(columns, keep))


def exchange(blocks, axes):
    return lax.all_to_all(blocks, axes, split_axis=0, concat_axis=0, tiled=True)


def mates_of(dp_size, hidden):
    mates = 4
    while dp_size % mates or hidden % (lanes * mates):
        mates //= 2
    return mates


def swap(value, axis, step):
    return lax.ppermute(value, axis, [(i, i ^ step) for i in range(lax.axis_size(axis))])


def after(value, other):
    return lax.optimization_barrier((value, other))[0]


def body(tokens, teacher, norm_gain, w_in, b_in, w_out, b_out, final_gain):
    dp_size = lax.axis_size("dp")
    fsdp_size = lax.axis_size("fsdp")
    images = teacher.shape[0] * dp_size
    per_image = tokens.shape[0] // teacher.shape[0]
    hidden = w_in.shape[1]
    mates = mates_of(dp_size, hidden)
    index = lax.axis_index("dp").astype(jnp.int32)[None]
    first = lax.axis_index("fsdp").astype(jnp.int32)[None]

    splits = fsdp_size if teacher.shape[1] % (fsdp_size * 8 * lanes) == 0 else 1

    blocks = {0: tokens}
    step = mates // 2
    if step:
        blocks[step] = swap(tokens, "dp", step)
    if step > 1:
        blocks[1] = swap(tokens, "dp", 1)
    all_teacher = exchange(teacher_payload(first, teacher, dp_size, splits), "dp")
    pooled, embed_rows = forward(
        first, tokens, norm_gain, w_in, b_in, w_out, b_out, dp_size * fsdp_size, teacher.shape[0]
    )
    if step > 1:
        blocks[step + 1] = swap(after(blocks[step], pooled), "dp", 1)
    all_embed = exchange(embed_rows, ("dp", "fsdp"))
    gram = target_gram(after(all_teacher, pooled), images)
    slope, turned = mate_slopes(
        index % mates, [blocks[k] for k in range(mates)], norm_gain, w_in, b_in, hidden // mates
    )
    if splits == 1:
        grams = [gram]
    elif splits == 2:
        grams = [gram, after(swap(gram, "fsdp", 1), slope)]
    else:
        grams = [lax.psum(gram, "fsdp")]
    loss, dembed, parts = backward(
        index, all_embed, unit_gram(grams), final_gain, pooled, w_out, [slope], [turned],
        mates, dp_size, per_image,
    )
    arrived = exchange(parts, "dp")
    columns = own_columns(index, dembed, dembed.shape[1] // dp_size)
    grad_in, grad_out = finish(arrived, columns, mates, hidden)
    return (loss[0, 0], grad_in, grad_out)


def solution(mesh):
    return jax.shard_map(
        body,
        mesh=mesh,
        in_specs=(
            P("dp", None),
            P("dp", None),
            P(),
            P(None, "fsdp"),
            P("fsdp"),
            P(None, "fsdp"),
            P(),
            P(),
        ),
        out_specs=(P(), P("dp", "fsdp"), P("dp", "fsdp")),
        check_vma=False,
    )
```

```python
import jax
import jax.numpy as jnp
from jax import lax
from jax.experimental import pallas as pl
from jax.experimental.pallas import tpu as pltpu
from jax.sharding import PartitionSpec as P

loss_scale = 4096.0
lanes = 128
f32 = jnp.float32
bf16 = jnp.bfloat16


def gelu_tanh(values):
    inner = 0.7978845608 * (values + 0.044715 * values * values * values)
    return 0.5 * values * (1.0 + jnp.tanh(inner))


def gelu_slope(values):
    square = values * values
    tangent = jnp.tanh(0.7978845608 * (values + 0.044715 * values * square))
    return 0.5 * (1.0 + tangent) + 0.5 * values * (1.0 - tangent * tangent) * 0.7978845608 * (
        1.0 + 3.0 * 0.044715 * square
    )


def contract_last(left_side, right_side):
    return lax.dot_general(
        left_side, right_side, (((1,), (1,)), ((), ())), preferred_element_type=f32
    )


def fold_rows(values, width):
    count = values.shape[1] // width
    return jnp.concatenate(
        [
            values[i : i + 1, k * width : (k + 1) * width]
            for i in range(values.shape[0])
            for k in range(count)
        ],
        axis=0,
    )


def vmem_params(elements):
    return pltpu.CompilerParams(vmem_limit_bytes=min(56 * 2**20, 8 * elements + 8 * 2**20))


in_hbm = pl.BlockSpec(memory_space=pltpu.HBM)
in_any = pl.BlockSpec(memory_space=pl.ANY)


def hbm(value):
    return pltpu.with_memory_space_constraint(value, pltpu.HBM)


def near(value, keep):
    return pltpu.with_memory_space_constraint(value, pltpu.VMEM) if keep else value


def near_shape(shape, dtype, keep):
    return pltpu.VMEM(shape, dtype) if keep else jax.ShapeDtypeStruct(shape, dtype)


def normalize(values, gain):
    centered = values - jnp.mean(values, axis=-1, keepdims=True)
    inv_std = lax.rsqrt(jnp.mean(centered * centered, axis=-1, keepdims=True) + 1e-05)
    return (centered * inv_std * gain).astype(bf16)


def teacher_payload(first, teacher, copies, splits):
    images = teacher.shape[0]
    features = teacher.shape[1] // splits
    fold = features // 8

    def kernel(first_ref, teacher_ref, out_ref):
        start = 0
        if splits > 1:
            start = pl.multiple_of(first_ref[0] * features, features)
        folded = fold_rows(teacher_ref[:, pl.ds(start, features)].astype(f32), fold).astype(bf16)
        out_ref[...] = jnp.broadcast_to(folded[None], out_ref.shape)

    return pl.pallas_call(
        kernel,
        in_specs=[
            pl.BlockSpec(memory_space=pltpu.SMEM),
            pl.BlockSpec(memory_space=pltpu.VMEM),
        ],
        out_shape=pltpu.HBM((copies, images * 8, fold), bf16),
        compiler_params=vmem_params(copies * images * features),
        cost_estimate=pl.CostEstimate(
            flops=copies * images * features,
            bytes_accessed=2 * copies * images * features,
            transcendentals=0,
        ),
        name="teacher_payload",
    )(first, hbm(teacher))


def forward(first, tokens, norm_gain, w_in, b_in, w_out, b_out, copies, images):
    rows, width = tokens.shape
    hidden = w_in.shape[1]
    per_image = rows // images
    tile = min(512, hidden)
    steps = hidden // tile
    folds = width // lanes

    def kernel(
        first_ref, gain_ref, bias_ref, out_b_ref, tokens_any, in_any_ref, out_any_ref,
        pooled_ref, payload_ref, tokens_ref, in_ref, out_w_ref, sems,
    ):
        loads = [
            pltpu.make_async_copy(
                in_any_ref.at[:, pl.ds(j * tile, tile)], in_ref.at[j], sems.at[j]
            )
            for j in range(steps)
        ]
        loads.append(pltpu.make_async_copy(out_any_ref, out_w_ref, sems.at[steps]))
        loads.append(pltpu.make_async_copy(tokens_any, tokens_ref, sems.at[steps + 1]))
        loads[-1].start()
        for load in loads[:-1]:
            load.start()
        loads[-1].wait()
        values = tokens_ref[...].astype(f32)
        normed = normalize(values, gain_ref[...])
        token_mean = jnp.mean(values.reshape(images, per_image, width), axis=1)
        for j in range(steps):
            taken = slice(j * tile, (j + 1) * tile)
            loads[j].wait()
            pre_act = jnp.dot(normed, in_ref[j], preferred_element_type=f32) + bias_ref[:, taken]
            pooled_ref[:, taken] = jnp.mean(
                gelu_tanh(pre_act).reshape(images, per_image, tile), axis=1
            ).astype(bf16)
        loads[steps].wait()
        total = contract_last(pooled_ref[...], out_w_ref[...])
        total += jnp.where(first_ref[0] == 0, token_mean + out_b_ref[...], 0.0)
        folded = fold_rows(total, lanes).astype(bf16)
        payload_ref[...] = jnp.broadcast_to(folded[None], payload_ref.shape)

    whole = pl.BlockSpec(memory_space=pltpu.VMEM)
    payload = (copies, images * folds, lanes)
    return pl.pallas_call(
        kernel,
        in_specs=[pl.BlockSpec(memory_space=pltpu.SMEM)] + [whole] * 3 + [in_hbm] * 3,
        out_specs=[whole, whole],
        out_shape=[
            jax.ShapeDtypeStruct((images, hidden), bf16),
            pltpu.HBM(payload, bf16),
        ],
        scratch_shapes=[
            pltpu.VMEM((rows, width), bf16),
            pltpu.VMEM((steps, width, tile), bf16),
            pltpu.VMEM((width, hidden), bf16),
            pltpu.SemaphoreType.DMA((steps + 2,)),
        ],
        compiler_params=vmem_params(
            rows * width + width * hidden + copies * images * width
        ),
        cost_estimate=pl.CostEstimate(
            flops=2 * rows * width * hidden,
            bytes_accessed=4 * width * hidden,
            transcendentals=rows * hidden,
        ),
        name="forward",
    )(
        first, hbm(norm_gain[None]), hbm(b_in[None]), hbm(b_out[None]),
        hbm(tokens), hbm(w_in), hbm(w_out),
    )


def mate_slopes(share_index, blocks, norm_gain, w_in, b_in, share):
    rows, width = blocks[0].shape
    count = len(blocks)
    tile = min(256, share)
    steps = share // tile
    turn = count * rows // steps
    keep = rows <= 512

    def kernel(index_ref, *refs):
        token_refs = refs[:count]
        gain_ref, bias_ref, in_any_ref, slope_ref, turned_ref = refs[count : count + 5]
        held_ref, normed_ref, in_ref, sems = refs[count + 5 :]
        step = pl.program_id(0)
        first_unit = index_ref[0] * share
        weights = [
            pltpu.make_async_copy(
                in_any_ref.at[:, pl.ds(pl.multiple_of(first_unit + j * tile, tile), tile)],
                in_ref.at[j],
                sems.at[count + j],
            )
            for j in range(steps)
        ]

        @pl.when(step == 0)
        def _():
            loads = [
                pltpu.make_async_copy(token_refs[k], held_ref.at[k], sems.at[k])
                for k in range(count)
            ]
            for load in loads + weights:
                load.start()
            for k in range(count):
                loads[k].wait()
                start = pl.multiple_of((index_ref[0] ^ k) * rows, rows)
                normed_ref[pl.ds(start, rows)] = normalize(
                    held_ref[k].astype(f32), gain_ref[...]
                )

        for j in range(steps):

            @pl.when(step == j)
            def _():
                weights[j].wait()

        pre_act = (
            jnp.dot(normed_ref[...], in_ref[step], preferred_element_type=f32) + bias_ref[...]
        )
        slope_ref[...] = gelu_slope(pre_act).astype(bf16)
        start = pl.multiple_of(step * turn, turn)
        turned_ref[...] = normed_ref[pl.ds(start, turn)].T

    return pl.pallas_call(
        kernel,
        grid_spec=pltpu.PrefetchScalarGridSpec(
            num_scalar_prefetch=1,
            grid=(steps,),
            in_specs=[in_any] * count
            + [
                pl.BlockSpec((1, width), lambda j, s: (0, 0)),
                pl.BlockSpec((1, tile), lambda j, s: (0, s[0] * steps + j)),
                in_hbm,
            ],
            out_specs=[
                pl.BlockSpec((count * rows, tile), lambda j, s: (0, j)),
                pl.BlockSpec((width, turn), lambda j, s: (0, j)),
            ],
            scratch_shapes=[
                pltpu.VMEM((count, rows, width), bf16),
                pltpu.VMEM((count * rows, width), bf16),
                pltpu.VMEM((steps, width, tile), bf16),
                pltpu.SemaphoreType.DMA((count + steps,)),
            ],
        ),
        out_shape=[
            near_shape((count * rows, share), bf16, keep),
            near_shape((width, count * rows), bf16, keep),
        ],
        compiler_params=vmem_params(count * rows * (width + share)),
        cost_estimate=pl.CostEstimate(
            flops=2 * rows * count * width * share,
            bytes_accessed=4 * rows * count * width,
            transcendentals=rows * count * share,
        ),
        name="mate_slopes",
    )(
        share_index,
        *[hbm(block) for block in blocks],
        hbm(norm_gain[None]),
        hbm(b_in[None]),
        hbm(w_in),
    )


def target_gram(arrived, images):
    senders, folded, fold = arrived.shape
    folds = senders * folded // images
    keep = images <= 64

    def kernel(arrived_ref, gram_ref, wide_ref):
        wide_ref[...] = arrived_ref[...].astype(f32).reshape(images, folds, fold)
        rows = jnp.concatenate([wide_ref[:, k, :].astype(bf16) for k in range(folds)], axis=1)
        gram_ref[...] = contract_last(rows, rows)

    return pl.pallas_call(
        kernel,
        out_shape=jax.ShapeDtypeStruct((images, images), f32),
        scratch_shapes=[pltpu.VMEM((images, folds, fold), f32)],
        compiler_params=vmem_params(images * folds * fold),
        cost_estimate=pl.CostEstimate(
            flops=2 * images * images * folds * fold,
            bytes_accessed=2 * images * folds * fold,
            transcendentals=0,
        ),
        name="target_gram",
    )(near(arrived, keep))


def unit_gram(parts):
    images = parts[0].shape[0]

    def kernel(*refs):
        gram_ref = refs[-1]
        gram = sum((ref[...] for ref in refs[1:-1]), refs[0][...])
        row = lax.broadcasted_iota(jnp.int32, gram.shape, 0)
        column = lax.broadcasted_iota(jnp.int32, gram.shape, 1)
        diagonal = jnp.where(row == column, gram, 0.0)
        down = lax.rsqrt(jnp.sum(diagonal, axis=1, keepdims=True) + 1e-06)
        across = lax.rsqrt(jnp.sum(diagonal, axis=0, keepdims=True) + 1e-06)
        gram_ref[...] = gram * down * across

    return pl.pallas_call(
        kernel,
        out_shape=jax.ShapeDtypeStruct((images, images), f32),
        compiler_params=vmem_params(4 * images * images),
        cost_estimate=pl.CostEstimate(
            flops=8 * images * images, bytes_accessed=8 * images * images, transcendentals=0
        ),
        name="unit_gram",
    )(*parts)


def backward(
    index, arrived, gram, final_gain, pooled, w_out, slopes, turns, mates, dp_size, per_image
):
    senders, folded, _ = arrived.shape
    width = w_out.shape[0]
    images = gram.shape[0]
    own_images, hidden = pooled.shape
    fsdp_size = senders // dp_size
    folds = width // lanes
    share = hidden // mates
    mate_rows = sum(turned.shape[1] for turned in turns)
    parts = len(turns)
    out_rows = width // dp_size
    piece = min(share, 256)
    pieces = share // piece
    extra = own_images * hidden // piece
    group = max(1, 512 // out_rows)
    steps = dp_size // group
    in_rows = out_rows * pieces
    keep = images <= 64

    def kernel(index_ref, arrived_any, gram_ref, gain_ref, pooled_ref, out_w_any, *refs):
        slope_any, turned_any, refs = refs[:parts], refs[parts : 2 * parts], refs[2 * parts :]
        loss_ref, dembed_ref, payload_any, wide_ref, hidden_ref, extra_ref = refs[:6]
        out_w_ref, slope_ref, turned_ref, arrived_ref, payload_ref, sems = refs[6:]
        step = pl.program_id(0)

        @pl.when(step == 0)
        def _():
            first_unit = pl.multiple_of(lax.rem(index_ref[0], mates) * share, share)
            loads = [
                pltpu.make_async_copy(
                    out_w_any.at[:, pl.ds(first_unit, share)], out_w_ref, sems.at[0]
                ),
                pltpu.make_async_copy(arrived_any, arrived_ref, sems.at[1]),
            ]
            start = 0
            for k in range(parts):
                taken = pl.ds(start, turned_any[k].shape[1])
                loads += [
                    pltpu.make_async_copy(slope_any[k], slope_ref.at[taken], sems.at[2 + 2 * k]),
                    pltpu.make_async_copy(
                        turned_any[k], turned_ref.at[:, taken], sems.at[3 + 2 * k]
                    ),
                ]
                start += turned_any[k].shape[1]
            loads[1].start()
            for load in loads[:1] + loads[2:]:
                load.start()
            loads[1].wait()
            embeds = arrived_ref[...].astype(f32).reshape(dp_size, fsdp_size, folded, lanes)
            wide_ref[...] = jnp.sum(embeds, axis=1).reshape(images, folds, lanes)
            embedding = jnp.concatenate([wide_ref[:, k, :] for k in range(folds)], axis=1)
            gain = gain_ref[...]
            centered = embedding - jnp.mean(embedding, axis=-1, keepdims=True)
            inv_std = lax.rsqrt(jnp.mean(centered * centered, axis=-1, keepdims=True) + 1e-05)
            normed = centered * inv_std
            scaled = normed * gain
            square = jnp.sum(scaled * scaled, axis=-1, keepdims=True) + 1e-06
            inv_norm = lax.rsqrt(square)
            unit = scaled * inv_norm
            student = unit.astype(bf16)
            resid = contract_last(student, student) - gram_ref[...]
            loss_ref[0, 0] = jnp.sum(resid * resid) / images
            dstudent = (loss_scale * 4.0 / images) * jnp.dot(
                resid.astype(bf16), student, preferred_element_type=f32
            )
            dunit = (
                dstudent - unit * jnp.sum(unit * dstudent, axis=-1, keepdims=True)
            ) * inv_norm
            gain_grad = dunit * gain
            dembed = inv_std * (
                gain_grad
                - jnp.mean(gain_grad, axis=-1, keepdims=True)
                - normed * jnp.mean(gain_grad * normed, axis=-1, keepdims=True)
            )
            dembed_b = dembed.astype(bf16)
            dembed_ref[...] = dembed_b
            rows = mates * own_images
            start = pl.multiple_of(index_ref[0] // mates * rows, rows)
            mate_dembed = dembed_ref[pl.ds(start, rows)]
            loads[0].wait()
            dpooled = jnp.dot(mate_dembed, out_w_ref[...], preferred_element_type=f32) / per_image
            for load in loads[2::2]:
                load.wait()
            for k in range(mates * own_images):
                rows = slice(k * per_image, (k + 1) * per_image)
                hidden_ref[rows] = (dpooled[k : k + 1] * slope_ref[rows].astype(f32)).astype(bf16)
            extra_ref[...] = fold_rows(pooled_ref[...].astype(f32), piece).astype(bf16)
            for load in loads[3::2]:
                load.wait()

        taken = group * out_rows
        rows = turned_ref[pl.ds(pl.multiple_of(step * taken, taken), taken)]
        term = jnp.dot(rows, hidden_ref[...], preferred_element_type=f32).astype(bf16)
        for d in range(group):
            for k in range(pieces):
                payload_ref[step, d, k * out_rows : (k + 1) * out_rows] = term[
                    d * out_rows : (d + 1) * out_rows, k * piece : (k + 1) * piece
                ]
            payload_ref[step, d, in_rows:] = extra_ref[...]
        stores = [
            pltpu.make_async_copy(
                payload_ref.at[j], payload_any.at[pl.ds(j * group, group)], sems.at[2 + 2 * parts + j]
            )
            for j in range(steps)
        ]
        for j in range(steps):

            @pl.when(step == j)
            def _():
                stores[j].start()

        @pl.when(step == steps - 1)
        def _():
            for store in stores:
                store.wait()

    return pl.pallas_call(
        kernel,
        grid_spec=pltpu.PrefetchScalarGridSpec(
            num_scalar_prefetch=1,
            grid=(steps,),
            in_specs=[
                in_any,
                pl.BlockSpec(gram.shape, lambda j, s: (0, 0)),
                pl.BlockSpec((1, width), lambda j, s: (0, 0)),
                pl.BlockSpec(pooled.shape, lambda j, s: (0, 0)),
                in_any,
            ]
            + [in_any] * (2 * parts),
            out_specs=[
                pl.BlockSpec(memory_space=pltpu.SMEM),
                pl.BlockSpec((images, width), lambda j, s: (0, 0)),
                in_hbm,
            ],
            scratch_shapes=[
                pltpu.VMEM((images, folds, lanes), f32),
                pltpu.VMEM((mate_rows, share), bf16),
                pltpu.VMEM((extra, piece), bf16),
                pltpu.VMEM((width, share), bf16),
                pltpu.VMEM((mate_rows, share), bf16),
                pltpu.VMEM((width, mate_rows), bf16),
                pltpu.VMEM(arrived.shape, bf16),
                pltpu.VMEM((steps, group, in_rows + extra, piece), bf16),
                pltpu.SemaphoreType.DMA((2 + 2 * parts + steps,)),
            ],
        ),
        out_shape=[
            jax.ShapeDtypeStruct((1, 1), f32),
            jax.ShapeDtypeStruct((images, width), bf16),
            pltpu.HBM((dp_size, in_rows + extra, piece), bf16),
        ],
        compiler_params=vmem_params(mate_rows * (width + share) // 2 + arrived.size),
        cost_estimate=pl.CostEstimate(
            flops=2 * mate_rows * width * share,
            bytes_accessed=2 * mate_rows * (width + share),
            transcendentals=0,
        ),
        name="backward",
    )(
        index, near(arrived, keep), gram, hbm(final_gain[None]), pooled, hbm(w_out),
        *[near(slope, keep) for slope in slopes], *[near(turned, keep) for turned in turns],
    )


def own_columns(index, dembed, out_rows):
    images, width = dembed.shape
    keep = images <= 64

    def kernel(index_ref, dembed_ref, columns_ref):
        row = lax.broadcasted_iota(jnp.int32, (out_rows, width), 0)
        column = lax.broadcasted_iota(jnp.int32, (out_rows, width), 1)
        pick = (row + index_ref[0] * out_rows == column).astype(f32).astype(bf16)
        columns_ref[...] = contract_last(pick, dembed_ref[...]).astype(bf16)

    return pl.pallas_call(
        kernel,
        in_specs=[
            pl.BlockSpec(memory_space=pltpu.SMEM),
            pl.BlockSpec(memory_space=pltpu.VMEM),
        ],
        out_shape=near_shape((out_rows, images), bf16, keep),
        compiler_params=vmem_params(images * width),
        cost_estimate=pl.CostEstimate(
            flops=2 * images * out_rows * width,
            bytes_accessed=2 * images * width,
            transcendentals=0,
        ),
        name="own_columns",
    )(index, dembed)


def finish(arrived, columns, mates, hidden):
    dp_size, _, piece = arrived.shape
    out_rows, images = columns.shape
    pieces = hidden // mates // piece
    in_rows = out_rows * pieces
    folds = hidden // piece
    keep = images <= 64

    def kernel(arrived_ref, columns_ref, in_ref, out_ref, wide_ref):
        wide_ref[...] = arrived_ref[:, in_rows:].astype(f32).reshape(images, folds, piece)
        rows = jnp.concatenate([wide_ref[:, k, :].astype(bf16) for k in range(folds)], axis=1)
        out_ref[...] = jnp.dot(columns_ref[...], rows, preferred_element_type=f32).astype(bf16)
        for q in range(mates):
            for k in range(pieces):
                taken = slice(k * out_rows, (k + 1) * out_rows)
                total = arrived_ref[q, taken].astype(f32)
                for s in range(q + mates, dp_size, mates):
                    total += arrived_ref[s, taken].astype(f32)
                start = (q * pieces + k) * piece
                in_ref[:, start : start + piece] = total.astype(bf16)

    return pl.pallas_call(
        kernel,
        out_shape=[jax.ShapeDtypeStruct((out_rows, hidden), bf16)] * 2,
        scratch_shapes=[pltpu.VMEM((images, folds, piece), f32)],
        compiler_params=vmem_params(arrived.size),
        cost_estimate=pl.CostEstimate(
            flops=2 * images * out_rows * hidden,
            bytes_accessed=2 * arrived.size,
            transcendentals=0,
        ),
        name="finish",
    )(near(arrived, keep), near(columns, keep))


def exchange(blocks, axes):
    return lax.all_to_all(blocks, axes, split_axis=0, concat_axis=0, tiled=True)


def mates_of(dp_size, hidden):
    mates = 4
    while dp_size % mates or hidden % (lanes * mates):
        mates //= 2
    return mates


def swap(value, axis, step):
    return lax.ppermute(value, axis, [(i, i ^ step) for i in range(lax.axis_size(axis))])


def after(value, other):
    return lax.optimization_barrier((value, other))[0]


def body(tokens, teacher, norm_gain, w_in, b_in, w_out, b_out, final_gain):
    dp_size = lax.axis_size("dp")
    fsdp_size = lax.axis_size("fsdp")
    images = teacher.shape[0] * dp_size
    per_image = tokens.shape[0] // teacher.shape[0]
    hidden = w_in.shape[1]
    mates = mates_of(dp_size, hidden)
    index = lax.axis_index("dp").astype(jnp.int32)[None]
    first = lax.axis_index("fsdp").astype(jnp.int32)[None]

    splits = fsdp_size if teacher.shape[1] % (fsdp_size * 8 * lanes) == 0 else 1

    blocks = {0: tokens}
    step = mates // 2
    if step:
        blocks[step] = swap(tokens, "dp", step)
    if step > 1:
        blocks[1] = swap(tokens, "dp", 1)
    all_teacher = exchange(teacher_payload(first, teacher, dp_size, splits), "dp")
    pooled, embed_rows = forward(
        first, tokens, norm_gain, w_in, b_in, w_out, b_out, dp_size * fsdp_size, teacher.shape[0]
    )
    all_embed = exchange(embed_rows, ("dp", "fsdp"))
    gram = target_gram(after(all_teacher, [pooled] + [blocks[k] for k in (1,) if k in blocks]), images)
    if step > 1:
        blocks[step + 1] = swap(after(blocks[step], gram), "dp", 1)
    slope, turned = mate_slopes(
        index % mates, [blocks[k] for k in range(mates)], norm_gain, w_in, b_in, hidden // mates
    )
    if splits == 1:
        grams = [gram]
    elif splits == 2:
        grams = [gram, after(swap(gram, "fsdp", 1), slope)]
    else:
        grams = [lax.psum(gram, "fsdp")]
    loss, dembed, parts = backward(
        index, all_embed, unit_gram(grams), final_gain, pooled, w_out, [slope], [turned],
        mates, dp_size, per_image,
    )
    arrived = exchange(parts, "dp")
    columns = own_columns(index, dembed, dembed.shape[1] // dp_size)
    grad_in, grad_out = finish(arrived, columns, mates, hidden)
    return (loss[0, 0], grad_in, grad_out)


def solution(mesh):
    return jax.shard_map(
        body,
        mesh=mesh,
        in_specs=(
            P("dp", None),
            P("dp", None),
            P(),
            P(None, "fsdp"),
            P("fsdp"),
            P(None, "fsdp"),
            P(),
            P(),
        ),
        out_specs=(P(), P("dp", "fsdp"), P("dp", "fsdp")),
        check_vma=False,
    )
```

```python
import jax
import jax.numpy as jnp
from jax import lax
from jax.experimental import pallas as pl
from jax.experimental.pallas import tpu as pltpu
from jax.sharding import PartitionSpec as P

loss_scale = 4096.0
lanes = 128
f32 = jnp.float32
bf16 = jnp.bfloat16


def gelu_tanh(values):
    inner = 0.7978845608 * (values + 0.044715 * values * values * values)
    return 0.5 * values * (1.0 + jnp.tanh(inner))


def gelu_slope(values):
    square = values * values
    tangent = jnp.tanh(0.7978845608 * (values + 0.044715 * values * square))
    return 0.5 * (1.0 + tangent) + 0.5 * values * (1.0 - tangent * tangent) * 0.7978845608 * (
        1.0 + 3.0 * 0.044715 * square
    )


def contract_last(left_side, right_side):
    return lax.dot_general(
        left_side, right_side, (((1,), (1,)), ((), ())), preferred_element_type=f32
    )


def fold_rows(values, width):
    count = values.shape[1] // width
    return jnp.concatenate(
        [
            values[i : i + 1, k * width : (k + 1) * width]
            for i in range(values.shape[0])
            for k in range(count)
        ],
        axis=0,
    )


def vmem_params(elements):
    return pltpu.CompilerParams(vmem_limit_bytes=min(56 * 2**20, 8 * elements + 8 * 2**20))


in_hbm = pl.BlockSpec(memory_space=pltpu.HBM)
in_any = pl.BlockSpec(memory_space=pl.ANY)


def hbm(value):
    return pltpu.with_memory_space_constraint(value, pltpu.HBM)


def near(value, keep):
    return pltpu.with_memory_space_constraint(value, pltpu.VMEM) if keep else value


def near_shape(shape, dtype, keep):
    return pltpu.VMEM(shape, dtype) if keep else jax.ShapeDtypeStruct(shape, dtype)


def normalize(values, gain):
    centered = values - jnp.mean(values, axis=-1, keepdims=True)
    inv_std = lax.rsqrt(jnp.mean(centered * centered, axis=-1, keepdims=True) + 1e-05)
    return (centered * inv_std * gain).astype(bf16)


def teacher_payload(first, teacher, copies, splits):
    images = teacher.shape[0]
    features = teacher.shape[1] // splits
    fold = features // 8

    def kernel(first_ref, teacher_ref, out_ref):
        start = 0
        if splits > 1:
            start = pl.multiple_of(first_ref[0] * features, features)
        folded = fold_rows(teacher_ref[:, pl.ds(start, features)].astype(f32), fold).astype(bf16)
        out_ref[...] = jnp.broadcast_to(folded[None], out_ref.shape)

    return pl.pallas_call(
        kernel,
        in_specs=[
            pl.BlockSpec(memory_space=pltpu.SMEM),
            pl.BlockSpec(memory_space=pltpu.VMEM),
        ],
        out_shape=pltpu.HBM((copies, images * 8, fold), bf16),
        compiler_params=vmem_params(copies * images * features),
        cost_estimate=pl.CostEstimate(
            flops=copies * images * features,
            bytes_accessed=2 * copies * images * features,
            transcendentals=0,
        ),
        name="teacher_payload",
    )(first, hbm(teacher))


def forward(first, tokens, norm_gain, w_in, b_in, w_out, b_out, copies, images):
    rows, width = tokens.shape
    hidden = w_in.shape[1]
    per_image = rows // images
    tile = min(512, hidden)
    steps = hidden // tile
    folds = width // lanes

    def kernel(
        first_ref, gain_ref, bias_ref, out_b_ref, tokens_any, in_any_ref, out_any_ref,
        pooled_ref, payload_ref, tokens_ref, in_ref, out_w_ref, sems,
    ):
        loads = [
            pltpu.make_async_copy(
                in_any_ref.at[:, pl.ds(j * tile, tile)], in_ref.at[j], sems.at[j]
            )
            for j in range(steps)
        ]
        loads.append(pltpu.make_async_copy(out_any_ref, out_w_ref, sems.at[steps]))
        loads.append(pltpu.make_async_copy(tokens_any, tokens_ref, sems.at[steps + 1]))
        loads[-1].start()
        for load in loads[:-1]:
            load.start()
        loads[-1].wait()
        values = tokens_ref[...].astype(f32)
        normed = normalize(values, gain_ref[...])
        token_mean = jnp.mean(values.reshape(images, per_image, width), axis=1)
        for j in range(steps):
            taken = slice(j * tile, (j + 1) * tile)
            loads[j].wait()
            pre_act = jnp.dot(normed, in_ref[j], preferred_element_type=f32) + bias_ref[:, taken]
            pooled_ref[:, taken] = jnp.mean(
                gelu_tanh(pre_act).reshape(images, per_image, tile), axis=1
            ).astype(bf16)
        loads[steps].wait()
        total = contract_last(pooled_ref[...], out_w_ref[...])
        total += jnp.where(first_ref[0] == 0, token_mean + out_b_ref[...], 0.0)
        folded = fold_rows(total, lanes).astype(bf16)
        payload_ref[...] = jnp.broadcast_to(folded[None], payload_ref.shape)

    whole = pl.BlockSpec(memory_space=pltpu.VMEM)
    payload = (copies, images * folds, lanes)
    return pl.pallas_call(
        kernel,
        in_specs=[pl.BlockSpec(memory_space=pltpu.SMEM)] + [whole] * 3 + [in_hbm] * 3,
        out_specs=[whole, whole],
        out_shape=[
            jax.ShapeDtypeStruct((images, hidden), bf16),
            pltpu.HBM(payload, bf16),
        ],
        scratch_shapes=[
            pltpu.VMEM((rows, width), bf16),
            pltpu.VMEM((steps, width, tile), bf16),
            pltpu.VMEM((width, hidden), bf16),
            pltpu.SemaphoreType.DMA((steps + 2,)),
        ],
        compiler_params=vmem_params(
            rows * width + width * hidden + copies * images * width
        ),
        cost_estimate=pl.CostEstimate(
            flops=2 * rows * width * hidden,
            bytes_accessed=4 * width * hidden,
            transcendentals=rows * hidden,
        ),
        name="forward",
    )(
        first, hbm(norm_gain[None]), hbm(b_in[None]), hbm(b_out[None]),
        hbm(tokens), hbm(w_in), hbm(w_out),
    )


def mate_slopes(share_index, blocks, norm_gain, w_in, b_in, share):
    rows, width = blocks[0].shape
    count = len(blocks)
    keep = rows <= 512

    def kernel(index_ref, *refs):
        token_refs = refs[:count]
        gain_ref, bias_ref, in_any_ref, slope_ref, turned_ref = refs[count : count + 5]
        held_ref, in_ref, sems = refs[count + 5 :]
        first_unit = pl.multiple_of(index_ref[0] * share, share)
        weight = pltpu.make_async_copy(
            in_any_ref.at[:, pl.ds(first_unit, share)], in_ref, sems.at[count]
        )
        loads = [
            pltpu.make_async_copy(token_refs[k], held_ref.at[k], sems.at[k]) for k in range(count)
        ]
        loads[0].start()
        weight.start()
        for load in loads[1:]:
            load.start()
        for k in range(count):
            taken = slice(k * rows, (k + 1) * rows)
            loads[k].wait()
            normed = normalize(held_ref[k].astype(f32), gain_ref[...])
            if k == 0:
                weight.wait()
            pre_act = jnp.dot(normed, in_ref[...], preferred_element_type=f32) + bias_ref[...]
            slope_ref[taken] = gelu_slope(pre_act).astype(bf16)
            turned_ref[:, taken] = normed.T

    return pl.pallas_call(
        kernel,
        grid_spec=pltpu.PrefetchScalarGridSpec(
            num_scalar_prefetch=1,
            grid=(1,),
            in_specs=[in_any] * count
            + [
                pl.BlockSpec((1, width), lambda j, s: (0, 0)),
                pl.BlockSpec((1, share), lambda j, s: (0, s[0])),
                in_hbm,
            ],
            out_specs=[
                pl.BlockSpec((count * rows, share), lambda j, s: (0, 0)),
                pl.BlockSpec((width, count * rows), lambda j, s: (0, 0)),
            ],
            scratch_shapes=[
                pltpu.VMEM((count, rows, width), bf16),
                pltpu.VMEM((width, share), bf16),
                pltpu.SemaphoreType.DMA((count + 1,)),
            ],
        ),
        out_shape=[
            near_shape((count * rows, share), bf16, keep),
            near_shape((width, count * rows), bf16, keep),
        ],
        compiler_params=vmem_params(count * rows * (width + share)),
        cost_estimate=pl.CostEstimate(
            flops=2 * rows * count * width * share,
            bytes_accessed=4 * rows * count * width,
            transcendentals=rows * count * share,
        ),
        name="mate_slopes",
    )(
        share_index,
        *[hbm(block) for block in blocks],
        hbm(norm_gain[None]),
        hbm(b_in[None]),
        hbm(w_in),
    )


def target_gram(arrived, images):
    senders, folded, fold = arrived.shape
    folds = senders * folded // images
    keep = images <= 64

    def kernel(arrived_ref, gram_ref, wide_ref):
        wide_ref[...] = arrived_ref[...].astype(f32).reshape(images, folds, fold)
        rows = jnp.concatenate([wide_ref[:, k, :].astype(bf16) for k in range(folds)], axis=1)
        gram_ref[...] = contract_last(rows, rows)

    return pl.pallas_call(
        kernel,
        out_shape=jax.ShapeDtypeStruct((images, images), f32),
        scratch_shapes=[pltpu.VMEM((images, folds, fold), f32)],
        compiler_params=vmem_params(images * folds * fold),
        cost_estimate=pl.CostEstimate(
            flops=2 * images * images * folds * fold,
            bytes_accessed=2 * images * folds * fold,
            transcendentals=0,
        ),
        name="target_gram",
    )(near(arrived, keep))


def unit_gram(parts):
    images = parts[0].shape[0]

    def kernel(*refs):
        gram_ref = refs[-1]
        gram = sum((ref[...] for ref in refs[1:-1]), refs[0][...])
        row = lax.broadcasted_iota(jnp.int32, gram.shape, 0)
        column = lax.broadcasted_iota(jnp.int32, gram.shape, 1)
        diagonal = jnp.where(row == column, gram, 0.0)
        down = lax.rsqrt(jnp.sum(diagonal, axis=1, keepdims=True) + 1e-06)
        across = lax.rsqrt(jnp.sum(diagonal, axis=0, keepdims=True) + 1e-06)
        gram_ref[...] = gram * down * across

    return pl.pallas_call(
        kernel,
        out_shape=jax.ShapeDtypeStruct((images, images), f32),
        compiler_params=vmem_params(4 * images * images),
        cost_estimate=pl.CostEstimate(
            flops=8 * images * images, bytes_accessed=8 * images * images, transcendentals=0
        ),
        name="unit_gram",
    )(*parts)


def backward(
    index, arrived, gram, final_gain, pooled, w_out, slopes, turns, mates, dp_size, per_image
):
    senders, folded, _ = arrived.shape
    width = w_out.shape[0]
    images = gram.shape[0]
    own_images, hidden = pooled.shape
    fsdp_size = senders // dp_size
    folds = width // lanes
    share = hidden // mates
    mate_rows = sum(turned.shape[1] for turned in turns)
    parts = len(turns)
    out_rows = width // dp_size
    piece = min(share, 256)
    pieces = share // piece
    extra = own_images * hidden // piece
    group = max(1, 512 // out_rows)
    steps = dp_size // group
    in_rows = out_rows * pieces
    keep = images <= 64

    def kernel(index_ref, arrived_any, gram_ref, gain_ref, pooled_ref, out_w_any, *refs):
        slope_any, turned_any, refs = refs[:parts], refs[parts : 2 * parts], refs[2 * parts :]
        loss_ref, dembed_ref, payload_any, wide_ref, hidden_ref, extra_ref = refs[:6]
        out_w_ref, slope_ref, turned_ref, arrived_ref, payload_ref, sems = refs[6:]
        step = pl.program_id(0)

        @pl.when(step == 0)
        def _():
            first_unit = pl.multiple_of(lax.rem(index_ref[0], mates) * share, share)
            loads = [
                pltpu.make_async_copy(
                    out_w_any.at[:, pl.ds(first_unit, share)], out_w_ref, sems.at[0]
                ),
                pltpu.make_async_copy(arrived_any, arrived_ref, sems.at[1]),
            ]
            block = mate_rows // mates
            own = lax.rem(index_ref[0], mates)
            k = 0
            for slope_part, turned_part in zip(slope_any, turned_any):
                for j in range(slope_part.shape[0] // block):
                    taken = pl.ds(j * block, block)
                    place = pl.ds(pl.multiple_of((own ^ k) * block, block), block)
                    loads += [
                        pltpu.make_async_copy(
                            slope_part.at[taken], slope_ref.at[place], sems.at[2 + 2 * k]
                        ),
                        pltpu.make_async_copy(
                            turned_part.at[:, taken], turned_ref.at[:, place], sems.at[3 + 2 * k]
                        ),
                    ]
                    k += 1
            loads[1].start()
            for load in loads[:1] + loads[2:]:
                load.start()
            loads[1].wait()
            embeds = arrived_ref[...].astype(f32).reshape(dp_size, fsdp_size, folded, lanes)
            wide_ref[...] = jnp.sum(embeds, axis=1).reshape(images, folds, lanes)
            embedding = jnp.concatenate([wide_ref[:, k, :] for k in range(folds)], axis=1)
            gain = gain_ref[...]
            centered = embedding - jnp.mean(embedding, axis=-1, keepdims=True)
            inv_std = lax.rsqrt(jnp.mean(centered * centered, axis=-1, keepdims=True) + 1e-05)
            normed = centered * inv_std
            scaled = normed * gain
            square = jnp.sum(scaled * scaled, axis=-1, keepdims=True) + 1e-06
            inv_norm = lax.rsqrt(square)
            unit = scaled * inv_norm
            student = unit.astype(bf16)
            resid = contract_last(student, student) - gram_ref[...]
            loss_ref[0, 0] = jnp.sum(resid * resid) / images
            dstudent = (loss_scale * 4.0 / images) * jnp.dot(
                resid.astype(bf16), student, preferred_element_type=f32
            )
            dunit = (
                dstudent - unit * jnp.sum(unit * dstudent, axis=-1, keepdims=True)
            ) * inv_norm
            gain_grad = dunit * gain
            dembed = inv_std * (
                gain_grad
                - jnp.mean(gain_grad, axis=-1, keepdims=True)
                - normed * jnp.mean(gain_grad * normed, axis=-1, keepdims=True)
            )
            dembed_b = dembed.astype(bf16)
            dembed_ref[...] = dembed_b
            rows = mates * own_images
            start = pl.multiple_of(index_ref[0] // mates * rows, rows)
            mate_dembed = dembed_ref[pl.ds(start, rows)]
            loads[0].wait()
            dpooled = jnp.dot(mate_dembed, out_w_ref[...], preferred_element_type=f32) / per_image
            for load in loads[2::2]:
                load.wait()
            for k in range(mates * own_images):
                rows = slice(k * per_image, (k + 1) * per_image)
                hidden_ref[rows] = (dpooled[k : k + 1] * slope_ref[rows].astype(f32)).astype(bf16)
            extra_ref[...] = fold_rows(pooled_ref[...].astype(f32), piece).astype(bf16)
            for load in loads[3::2]:
                load.wait()

        taken = group * out_rows
        rows = turned_ref[pl.ds(pl.multiple_of(step * taken, taken), taken)]
        term = jnp.dot(rows, hidden_ref[...], preferred_element_type=f32).astype(bf16)
        for d in range(group):
            for k in range(pieces):
                payload_ref[step, d, k * out_rows : (k + 1) * out_rows] = term[
                    d * out_rows : (d + 1) * out_rows, k * piece : (k + 1) * piece
                ]
            payload_ref[step, d, in_rows:] = extra_ref[...]
        stores = [
            pltpu.make_async_copy(
                payload_ref.at[j], payload_any.at[pl.ds(j * group, group)], sems.at[2 + 2 * mates + j]
            )
            for j in range(steps)
        ]
        for j in range(steps):

            @pl.when(step == j)
            def _():
                stores[j].start()

        @pl.when(step == steps - 1)
        def _():
            for store in stores:
                store.wait()

    return pl.pallas_call(
        kernel,
        grid_spec=pltpu.PrefetchScalarGridSpec(
            num_scalar_prefetch=1,
            grid=(steps,),
            in_specs=[
                in_any,
                pl.BlockSpec(gram.shape, lambda j, s: (0, 0)),
                pl.BlockSpec((1, width), lambda j, s: (0, 0)),
                pl.BlockSpec(pooled.shape, lambda j, s: (0, 0)),
                in_any,
            ]
            + [in_any] * (2 * parts),
            out_specs=[
                pl.BlockSpec(memory_space=pltpu.SMEM),
                pl.BlockSpec((images, width), lambda j, s: (0, 0)),
                in_hbm,
            ],
            scratch_shapes=[
                pltpu.VMEM((images, folds, lanes), f32),
                pltpu.VMEM((mate_rows, share), bf16),
                pltpu.VMEM((extra, piece), bf16),
                pltpu.VMEM((width, share), bf16),
                pltpu.VMEM((mate_rows, share), bf16),
                pltpu.VMEM((width, mate_rows), bf16),
                pltpu.VMEM(arrived.shape, bf16),
                pltpu.VMEM((steps, group, in_rows + extra, piece), bf16),
                pltpu.SemaphoreType.DMA((2 + 2 * mates + steps,)),
            ],
        ),
        out_shape=[
            jax.ShapeDtypeStruct((1, 1), f32),
            jax.ShapeDtypeStruct((images, width), bf16),
            pltpu.HBM((dp_size, in_rows + extra, piece), bf16),
        ],
        compiler_params=vmem_params(mate_rows * (width + share) // 2 + arrived.size),
        cost_estimate=pl.CostEstimate(
            flops=2 * mate_rows * width * share,
            bytes_accessed=2 * mate_rows * (width + share),
            transcendentals=0,
        ),
        name="backward",
    )(
        index, near(arrived, keep), gram, hbm(final_gain[None]), pooled, hbm(w_out),
        *[near(slope, keep) for slope in slopes], *[near(turned, keep) for turned in turns],
    )


def own_columns(index, dembed, out_rows):
    images, width = dembed.shape
    keep = images <= 64

    def kernel(index_ref, dembed_ref, columns_ref):
        row = lax.broadcasted_iota(jnp.int32, (out_rows, width), 0)
        column = lax.broadcasted_iota(jnp.int32, (out_rows, width), 1)
        pick = (row + index_ref[0] * out_rows == column).astype(f32).astype(bf16)
        columns_ref[...] = contract_last(pick, dembed_ref[...]).astype(bf16)

    return pl.pallas_call(
        kernel,
        in_specs=[
            pl.BlockSpec(memory_space=pltpu.SMEM),
            pl.BlockSpec(memory_space=pltpu.VMEM),
        ],
        out_shape=near_shape((out_rows, images), bf16, keep),
        compiler_params=vmem_params(images * width),
        cost_estimate=pl.CostEstimate(
            flops=2 * images * out_rows * width,
            bytes_accessed=2 * images * width,
            transcendentals=0,
        ),
        name="own_columns",
    )(index, dembed)


def finish(arrived, columns, mates, hidden):
    dp_size, _, piece = arrived.shape
    out_rows, images = columns.shape
    pieces = hidden // mates // piece
    in_rows = out_rows * pieces
    folds = hidden // piece
    keep = images <= 64

    def kernel(arrived_ref, columns_ref, in_ref, out_ref, wide_ref):
        wide_ref[...] = arrived_ref[:, in_rows:].astype(f32).reshape(images, folds, piece)
        rows = jnp.concatenate([wide_ref[:, k, :].astype(bf16) for k in range(folds)], axis=1)
        out_ref[...] = jnp.dot(columns_ref[...], rows, preferred_element_type=f32).astype(bf16)
        for q in range(mates):
            for k in range(pieces):
                taken = slice(k * out_rows, (k + 1) * out_rows)
                total = arrived_ref[q, taken].astype(f32)
                for s in range(q + mates, dp_size, mates):
                    total += arrived_ref[s, taken].astype(f32)
                start = (q * pieces + k) * piece
                in_ref[:, start : start + piece] = total.astype(bf16)

    return pl.pallas_call(
        kernel,
        out_shape=[jax.ShapeDtypeStruct((out_rows, hidden), bf16)] * 2,
        scratch_shapes=[pltpu.VMEM((images, folds, piece), f32)],
        compiler_params=vmem_params(arrived.size),
        cost_estimate=pl.CostEstimate(
            flops=2 * images * out_rows * hidden,
            bytes_accessed=2 * arrived.size,
            transcendentals=0,
        ),
        name="finish",
    )(near(arrived, keep), near(columns, keep))


def exchange(blocks, axes):
    return lax.all_to_all(blocks, axes, split_axis=0, concat_axis=0, tiled=True)


def mates_of(dp_size, hidden):
    mates = 8 if hidden % (8 * 256) == 0 else 4
    while dp_size % mates or hidden % (lanes * mates):
        mates //= 2
    return mates


def swap(value, axis, step):
    return lax.ppermute(value, axis, [(i, i ^ step) for i in range(lax.axis_size(axis))])


def after(value, other):
    return lax.optimization_barrier((value, other))[0]


def body(tokens, teacher, norm_gain, w_in, b_in, w_out, b_out, final_gain):
    dp_size = lax.axis_size("dp")
    fsdp_size = lax.axis_size("fsdp")
    images = teacher.shape[0] * dp_size
    per_image = tokens.shape[0] // teacher.shape[0]
    hidden = w_in.shape[1]
    mates = mates_of(dp_size, hidden)
    index = lax.axis_index("dp").astype(jnp.int32)[None]
    first = lax.axis_index("fsdp").astype(jnp.int32)[None]

    splits = fsdp_size if teacher.shape[1] % (fsdp_size * 8 * lanes) == 0 else 1

    blocks = {0: tokens}
    for bit in (2, 4, 1):
        if bit < mates:
            blocks[bit] = swap(tokens, "dp", bit)
    all_teacher = exchange(teacher_payload(first, teacher, dp_size, splits), "dp")
    pooled, embed_rows = forward(
        first, tokens, norm_gain, w_in, b_in, w_out, b_out, dp_size * fsdp_size, teacher.shape[0]
    )
    all_embed = exchange(embed_rows, ("dp", "fsdp"))
    gram = target_gram(after(all_teacher, [pooled] + [blocks[k] for k in (1,) if k in blocks]), images)
    for k, source, bit in ((6, 4, 2), (3, 2, 1), (5, 4, 1)):
        if k < mates:
            blocks[k] = swap(after(blocks[source], gram), "dp", bit)
    near_mates = [blocks[k] for k in range(min(mates, 6))]
    slope, turned = mate_slopes(index % mates, near_mates, norm_gain, w_in, b_in, hidden // mates)
    slopes, turns = [slope], [turned]
    if mates > 6:
        blocks[7] = swap(after(blocks[6], [slope, all_embed]), "dp", 1)
        far_mates = [blocks[6], blocks[7]]
        slope, turned = mate_slopes(
            index % mates, far_mates, norm_gain, w_in, b_in, hidden // mates
        )
        slopes, turns = slopes + [slope], turns + [turned]
    if splits == 1:
        grams = [gram]
    elif splits == 2:
        grams = [gram, after(swap(gram, "fsdp", 1), slopes[0])]
    else:
        grams = [lax.psum(gram, "fsdp")]
    loss, dembed, parts = backward(
        index, all_embed, unit_gram(grams), final_gain, pooled, w_out, slopes, turns,
        mates, dp_size, per_image,
    )
    arrived = exchange(parts, "dp")
    columns = own_columns(index, dembed, dembed.shape[1] // dp_size)
    grad_in, grad_out = finish(arrived, columns, mates, hidden)
    return (loss[0, 0], grad_in, grad_out)


def solution(mesh):
    return jax.shard_map(
        body,
        mesh=mesh,
        in_specs=(
            P("dp", None),
            P("dp", None),
            P(),
            P(None, "fsdp"),
            P("fsdp"),
            P(None, "fsdp"),
            P(),
            P(),
        ),
        out_specs=(P(), P("dp", "fsdp"), P("dp", "fsdp")),
        check_vma=False,
    )
```

```python
import jax
import jax.numpy as jnp
from jax import lax
from jax.experimental import pallas as pl
from jax.experimental.pallas import tpu as pltpu
from jax.sharding import PartitionSpec as P

loss_scale = 4096.0
lanes = 128
f32 = jnp.float32
bf16 = jnp.bfloat16


def gelu_tanh(values):
    inner = 0.7978845608 * (values + 0.044715 * values * values * values)
    return 0.5 * values * (1.0 + jnp.tanh(inner))


def gelu_slope(values):
    square = values * values
    tangent = jnp.tanh(0.7978845608 * (values + 0.044715 * values * square))
    return 0.5 * (1.0 + tangent) + 0.5 * values * (1.0 - tangent * tangent) * 0.7978845608 * (
        1.0 + 3.0 * 0.044715 * square
    )


def contract_last(left_side, right_side):
    return lax.dot_general(
        left_side, right_side, (((1,), (1,)), ((), ())), preferred_element_type=f32
    )


def fold_rows(values, width):
    count = values.shape[1] // width
    return jnp.concatenate(
        [
            values[i : i + 1, k * width : (k + 1) * width]
            for i in range(values.shape[0])
            for k in range(count)
        ],
        axis=0,
    )


def vmem_params(elements):
    return pltpu.CompilerParams(vmem_limit_bytes=min(56 * 2**20, 8 * elements + 8 * 2**20))


in_hbm = pl.BlockSpec(memory_space=pltpu.HBM)
in_any = pl.BlockSpec(memory_space=pl.ANY)


def hbm(value):
    return pltpu.with_memory_space_constraint(value, pltpu.HBM)


def near(value, keep):
    return pltpu.with_memory_space_constraint(value, pltpu.VMEM) if keep else value


def near_shape(shape, dtype, keep):
    return pltpu.VMEM(shape, dtype) if keep else jax.ShapeDtypeStruct(shape, dtype)


def normalize(values, gain):
    centered = values - jnp.mean(values, axis=-1, keepdims=True)
    inv_std = lax.rsqrt(jnp.mean(centered * centered, axis=-1, keepdims=True) + 1e-05)
    return (centered * inv_std * gain).astype(bf16)


def teacher_payload(first, teacher, copies, splits):
    images = teacher.shape[0]
    features = teacher.shape[1] // splits
    fold = features // 8

    def kernel(first_ref, teacher_ref, out_ref):
        start = 0
        if splits > 1:
            start = pl.multiple_of(first_ref[0] * features, features)
        folded = fold_rows(teacher_ref[:, pl.ds(start, features)].astype(f32), fold).astype(bf16)
        out_ref[...] = jnp.broadcast_to(folded[None], out_ref.shape)

    return pl.pallas_call(
        kernel,
        in_specs=[
            pl.BlockSpec(memory_space=pltpu.SMEM),
            pl.BlockSpec(memory_space=pltpu.VMEM),
        ],
        out_shape=pltpu.HBM((copies, images * 8, fold), bf16),
        compiler_params=vmem_params(copies * images * features),
        cost_estimate=pl.CostEstimate(
            flops=copies * images * features,
            bytes_accessed=2 * copies * images * features,
            transcendentals=0,
        ),
        name="teacher_payload",
    )(first, hbm(teacher))


def forward(first, tokens, norm_gain, w_in, b_in, w_out, b_out, copies, images):
    rows, width = tokens.shape
    hidden = w_in.shape[1]
    per_image = rows // images
    tile = min(512, hidden)
    steps = hidden // tile
    folds = width // lanes

    def kernel(
        first_ref, gain_ref, bias_ref, out_b_ref, tokens_any, in_any_ref, out_any_ref,
        pooled_ref, payload_ref, tokens_ref, in_ref, out_w_ref, sems,
    ):
        loads = [
            pltpu.make_async_copy(
                in_any_ref.at[:, pl.ds(j * tile, tile)], in_ref.at[j], sems.at[j]
            )
            for j in range(steps)
        ]
        loads.append(pltpu.make_async_copy(out_any_ref, out_w_ref, sems.at[steps]))
        loads.append(pltpu.make_async_copy(tokens_any, tokens_ref, sems.at[steps + 1]))
        loads[-1].start()
        for load in loads[:-1]:
            load.start()
        loads[-1].wait()
        values = tokens_ref[...].astype(f32)
        normed = normalize(values, gain_ref[...])
        token_mean = jnp.mean(values.reshape(images, per_image, width), axis=1)
        for j in range(steps):
            taken = slice(j * tile, (j + 1) * tile)
            loads[j].wait()
            pre_act = jnp.dot(normed, in_ref[j], preferred_element_type=f32) + bias_ref[:, taken]
            pooled_ref[:, taken] = jnp.mean(
                gelu_tanh(pre_act).reshape(images, per_image, tile), axis=1
            ).astype(bf16)
        loads[steps].wait()
        total = contract_last(pooled_ref[...], out_w_ref[...])
        total += jnp.where(first_ref[0] == 0, token_mean + out_b_ref[...], 0.0)
        folded = fold_rows(total, lanes).astype(bf16)
        payload_ref[...] = jnp.broadcast_to(folded[None], payload_ref.shape)

    whole = pl.BlockSpec(memory_space=pltpu.VMEM)
    payload = (copies, images * folds, lanes)
    return pl.pallas_call(
        kernel,
        in_specs=[pl.BlockSpec(memory_space=pltpu.SMEM)] + [whole] * 3 + [in_hbm] * 3,
        out_specs=[whole, whole],
        out_shape=[
            jax.ShapeDtypeStruct((images, hidden), bf16),
            pltpu.HBM(payload, bf16),
        ],
        scratch_shapes=[
            pltpu.VMEM((rows, width), bf16),
            pltpu.VMEM((steps, width, tile), bf16),
            pltpu.VMEM((width, hidden), bf16),
            pltpu.SemaphoreType.DMA((steps + 2,)),
        ],
        compiler_params=vmem_params(
            rows * width + width * hidden + copies * images * width
        ),
        cost_estimate=pl.CostEstimate(
            flops=2 * rows * width * hidden,
            bytes_accessed=4 * width * hidden,
            transcendentals=rows * hidden,
        ),
        name="forward",
    )(
        first, hbm(norm_gain[None]), hbm(b_in[None]), hbm(b_out[None]),
        hbm(tokens), hbm(w_in), hbm(w_out),
    )


def mate_slopes(share_index, blocks, norm_gain, w_in, b_in, share):
    rows, width = blocks[0].shape
    count = len(blocks)
    keep = rows <= 512

    def kernel(index_ref, *refs):
        token_refs = refs[:count]
        gain_ref, bias_ref, in_any_ref, slope_ref, turned_ref = refs[count : count + 5]
        held_ref, in_ref, sems = refs[count + 5 :]
        first_unit = pl.multiple_of(index_ref[0] * share, share)
        weight = pltpu.make_async_copy(
            in_any_ref.at[:, pl.ds(first_unit, share)], in_ref, sems.at[count]
        )
        loads = [
            pltpu.make_async_copy(token_refs[k], held_ref.at[k], sems.at[k]) for k in range(count)
        ]
        loads[0].start()
        weight.start()
        for load in loads[1:]:
            load.start()
        for k in range(count):
            taken = slice(k * rows, (k + 1) * rows)
            loads[k].wait()
            normed = normalize(held_ref[k].astype(f32), gain_ref[...])
            if k == 0:
                weight.wait()
            pre_act = jnp.dot(normed, in_ref[...], preferred_element_type=f32) + bias_ref[...]
            slope_ref[taken] = gelu_slope(pre_act).astype(bf16)
            turned_ref[:, taken] = normed.T

    return pl.pallas_call(
        kernel,
        grid_spec=pltpu.PrefetchScalarGridSpec(
            num_scalar_prefetch=1,
            grid=(1,),
            in_specs=[in_any] * count
            + [
                pl.BlockSpec((1, width), lambda j, s: (0, 0)),
                pl.BlockSpec((1, share), lambda j, s: (0, s[0])),
                in_hbm,
            ],
            out_specs=[
                pl.BlockSpec((count * rows, share), lambda j, s: (0, 0)),
                pl.BlockSpec((width, count * rows), lambda j, s: (0, 0)),
            ],
            scratch_shapes=[
                pltpu.VMEM((count, rows, width), bf16),
                pltpu.VMEM((width, share), bf16),
                pltpu.SemaphoreType.DMA((count + 1,)),
            ],
        ),
        out_shape=[
            near_shape((count * rows, share), bf16, keep),
            near_shape((width, count * rows), bf16, keep),
        ],
        compiler_params=vmem_params(count * rows * (width + share)),
        cost_estimate=pl.CostEstimate(
            flops=2 * rows * count * width * share,
            bytes_accessed=4 * rows * count * width,
            transcendentals=rows * count * share,
        ),
        name="mate_slopes",
    )(
        share_index,
        *[hbm(block) for block in blocks],
        hbm(norm_gain[None]),
        hbm(b_in[None]),
        hbm(w_in),
    )


def target_gram(arrived, images):
    senders, folded, fold = arrived.shape
    folds = senders * folded // images
    keep = images <= 64

    def kernel(arrived_ref, gram_ref, wide_ref):
        wide_ref[...] = arrived_ref[...].astype(f32).reshape(images, folds, fold)
        rows = jnp.concatenate([wide_ref[:, k, :].astype(bf16) for k in range(folds)], axis=1)
        gram_ref[...] = contract_last(rows, rows)

    return pl.pallas_call(
        kernel,
        out_shape=jax.ShapeDtypeStruct((images, images), f32),
        scratch_shapes=[pltpu.VMEM((images, folds, fold), f32)],
        compiler_params=vmem_params(images * folds * fold),
        cost_estimate=pl.CostEstimate(
            flops=2 * images * images * folds * fold,
            bytes_accessed=2 * images * folds * fold,
            transcendentals=0,
        ),
        name="target_gram",
    )(near(arrived, keep))


def unit_gram(parts):
    images = parts[0].shape[0]

    def kernel(*refs):
        gram_ref = refs[-1]
        gram = sum((ref[...] for ref in refs[1:-1]), refs[0][...])
        row = lax.broadcasted_iota(jnp.int32, gram.shape, 0)
        column = lax.broadcasted_iota(jnp.int32, gram.shape, 1)
        diagonal = jnp.where(row == column, gram, 0.0)
        down = lax.rsqrt(jnp.sum(diagonal, axis=1, keepdims=True) + 1e-06)
        across = lax.rsqrt(jnp.sum(diagonal, axis=0, keepdims=True) + 1e-06)
        gram_ref[...] = gram * down * across

    return pl.pallas_call(
        kernel,
        out_shape=jax.ShapeDtypeStruct((images, images), f32),
        compiler_params=vmem_params(4 * images * images),
        cost_estimate=pl.CostEstimate(
            flops=8 * images * images, bytes_accessed=8 * images * images, transcendentals=0
        ),
        name="unit_gram",
    )(*parts)


def backward(
    index, arrived, gram, final_gain, pooled, w_out, slopes, turns, mates, dp_size, per_image
):
    senders, folded, _ = arrived.shape
    width = w_out.shape[0]
    images = gram.shape[0]
    own_images, hidden = pooled.shape
    fsdp_size = senders // dp_size
    folds = width // lanes
    share = hidden // mates
    parts = len(turns)
    part_rows = [turned.shape[1] for turned in turns]
    mate_rows = sum(part_rows)
    out_rows = width // dp_size
    piece = min(share, 256)
    pieces = share // piece
    extra = own_images * hidden // piece
    group = max(1, 512 // out_rows)
    steps = dp_size // group
    in_rows = out_rows * pieces
    keep = images <= 64

    def kernel(index_ref, arrived_ref, gram_ref, gain_ref, pooled_ref, out_w_any, *refs):
        slope_refs, turned_refs, refs = refs[:parts], refs[parts : 2 * parts], refs[2 * parts :]
        loss_ref, dembed_ref, payload_any, wide_ref, hidden_ref = refs[:5]
        out_w_ref, payload_ref, sems = refs[5:]
        first_unit = pl.multiple_of(lax.rem(index_ref[0], mates) * share, share)
        load = pltpu.make_async_copy(
            out_w_any.at[:, pl.ds(first_unit, share)], out_w_ref, sems.at[steps]
        )
        load.start()
        embeds = arrived_ref[...].astype(f32).reshape(dp_size, fsdp_size, folded, lanes)
        wide_ref[...] = jnp.sum(embeds, axis=1).reshape(images, folds, lanes)
        embedding = jnp.concatenate([wide_ref[:, k, :] for k in range(folds)], axis=1)
        gain = gain_ref[...]
        centered = embedding - jnp.mean(embedding, axis=-1, keepdims=True)
        inv_std = lax.rsqrt(jnp.mean(centered * centered, axis=-1, keepdims=True) + 1e-05)
        normed = centered * inv_std
        scaled = normed * gain
        square = jnp.sum(scaled * scaled, axis=-1, keepdims=True) + 1e-06
        inv_norm = lax.rsqrt(square)
        unit = scaled * inv_norm
        student = unit.astype(bf16)
        resid = contract_last(student, student) - gram_ref[...]
        loss_ref[0, 0] = jnp.sum(resid * resid) / images
        dstudent = (loss_scale * 4.0 / images) * jnp.dot(
            resid.astype(bf16), student, preferred_element_type=f32
        )
        dunit = (dstudent - unit * jnp.sum(unit * dstudent, axis=-1, keepdims=True)) * inv_norm
        gain_grad = dunit * gain
        dembed = inv_std * (
            gain_grad
            - jnp.mean(gain_grad, axis=-1, keepdims=True)
            - normed * jnp.mean(gain_grad * normed, axis=-1, keepdims=True)
        )
        dembed_b = dembed.astype(bf16)
        dembed_ref[...] = dembed_b
        shape = (mates * own_images, images)
        row = lax.broadcasted_iota(jnp.int32, shape, 0)
        column = lax.broadcasted_iota(jnp.int32, shape, 1)
        owner = (row // own_images) ^ index_ref[0]
        pick = (owner * own_images + row % own_images == column).astype(f32).astype(bf16)
        mate_dembed = jnp.dot(pick, dembed_b, preferred_element_type=f32).astype(bf16)
        load.wait()
        dpooled = jnp.dot(mate_dembed, out_w_ref[...], preferred_element_type=f32) / per_image
        k = 0
        for part in range(parts):
            for j in range(part_rows[part] // per_image):
                rows = slice(k * per_image, (k + 1) * per_image)
                taken = slice(j * per_image, (j + 1) * per_image)
                hidden_ref[rows] = (
                    dpooled[k : k + 1] * slope_refs[part][taken].astype(f32)
                ).astype(bf16)
                k += 1
        folded_pooled = fold_rows(pooled_ref[...].astype(f32), piece).astype(bf16)
        stores = []
        for step in range(steps):
            taken = slice(step * group * out_rows, (step + 1) * group * out_rows)
            term, start = 0.0, 0
            for part in range(parts):
                rows = slice(start, start + part_rows[part])
                start += part_rows[part]
                term += jnp.dot(
                    turned_refs[part][taken], hidden_ref[rows], preferred_element_type=f32
                )
            term = term.astype(bf16)
            for d in range(group):
                for k in range(pieces):
                    payload_ref[step, d, k * out_rows : (k + 1) * out_rows] = term[
                        d * out_rows : (d + 1) * out_rows, k * piece : (k + 1) * piece
                    ]
                payload_ref[step, d, in_rows:] = folded_pooled
            stores.append(
                pltpu.make_async_copy(
                    payload_ref.at[step],
                    payload_any.at[pl.ds(step * group, group)],
                    sems.at[step],
                )
            )
            stores[-1].start()
        for store in stores:
            store.wait()

    whole = pl.BlockSpec(memory_space=pltpu.VMEM)
    smem = pl.BlockSpec(memory_space=pltpu.SMEM)
    return pl.pallas_call(
        kernel,
        in_specs=[smem, whole, whole, whole, whole, in_hbm] + [whole] * (2 * parts),
        out_specs=[smem, whole, in_hbm],
        out_shape=[
            jax.ShapeDtypeStruct((1, 1), f32),
            jax.ShapeDtypeStruct((images, width), bf16),
            pltpu.HBM((dp_size, in_rows + extra, piece), bf16),
        ],
        scratch_shapes=[
            pltpu.VMEM((images, folds, lanes), f32),
            pltpu.VMEM((mate_rows, share), bf16),
            pltpu.VMEM((width, share), bf16),
            pltpu.VMEM((steps, group, in_rows + extra, piece), bf16),
            pltpu.SemaphoreType.DMA((steps + 1,)),
        ],
        compiler_params=vmem_params(mate_rows * (width + share) // 2 + arrived.size),
        cost_estimate=pl.CostEstimate(
            flops=2 * mate_rows * width * share,
            bytes_accessed=2 * mate_rows * (width + share),
            transcendentals=0,
        ),
        name="backward",
    )(
        index, near(arrived, keep), gram, hbm(final_gain[None]), pooled, hbm(w_out),
        *[near(slope, keep) for slope in slopes], *[near(turned, keep) for turned in turns],
    )


def own_columns(index, dembed, out_rows):
    images, width = dembed.shape
    keep = images <= 64

    def kernel(index_ref, dembed_ref, columns_ref):
        row = lax.broadcasted_iota(jnp.int32, (out_rows, width), 0)
        column = lax.broadcasted_iota(jnp.int32, (out_rows, width), 1)
        pick = (row + index_ref[0] * out_rows == column).astype(f32).astype(bf16)
        columns_ref[...] = contract_last(pick, dembed_ref[...]).astype(bf16)

    return pl.pallas_call(
        kernel,
        in_specs=[
            pl.BlockSpec(memory_space=pltpu.SMEM),
            pl.BlockSpec(memory_space=pltpu.VMEM),
        ],
        out_shape=near_shape((out_rows, images), bf16, keep),
        compiler_params=vmem_params(images * width),
        cost_estimate=pl.CostEstimate(
            flops=2 * images * out_rows * width,
            bytes_accessed=2 * images * width,
            transcendentals=0,
        ),
        name="own_columns",
    )(index, dembed)


def finish(arrived, columns, mates, hidden):
    dp_size, _, piece = arrived.shape
    out_rows, images = columns.shape
    pieces = hidden // mates // piece
    in_rows = out_rows * pieces
    folds = hidden // piece
    keep = images <= 64

    def kernel(arrived_ref, columns_ref, in_ref, out_ref, wide_ref):
        wide_ref[...] = arrived_ref[:, in_rows:].astype(f32).reshape(images, folds, piece)
        rows = jnp.concatenate([wide_ref[:, k, :].astype(bf16) for k in range(folds)], axis=1)
        out_ref[...] = jnp.dot(columns_ref[...], rows, preferred_element_type=f32).astype(bf16)
        for q in range(mates):
            for k in range(pieces):
                taken = slice(k * out_rows, (k + 1) * out_rows)
                total = arrived_ref[q, taken].astype(f32)
                for s in range(q + mates, dp_size, mates):
                    total += arrived_ref[s, taken].astype(f32)
                start = (q * pieces + k) * piece
                in_ref[:, start : start + piece] = total.astype(bf16)

    return pl.pallas_call(
        kernel,
        out_shape=[jax.ShapeDtypeStruct((out_rows, hidden), bf16)] * 2,
        scratch_shapes=[pltpu.VMEM((images, folds, piece), f32)],
        compiler_params=vmem_params(arrived.size),
        cost_estimate=pl.CostEstimate(
            flops=2 * images * out_rows * hidden,
            bytes_accessed=2 * arrived.size,
            transcendentals=0,
        ),
        name="finish",
    )(near(arrived, keep), near(columns, keep))


def exchange(blocks, axes):
    return lax.all_to_all(blocks, axes, split_axis=0, concat_axis=0, tiled=True)


def mates_of(dp_size, hidden):
    mates = 4
    while dp_size % mates or hidden % (lanes * mates):
        mates //= 2
    return mates


def swap(value, axis, step):
    return lax.ppermute(value, axis, [(i, i ^ step) for i in range(lax.axis_size(axis))])


def after(value, other):
    return lax.optimization_barrier((value, other))[0]


def body(tokens, teacher, norm_gain, w_in, b_in, w_out, b_out, final_gain):
    dp_size = lax.axis_size("dp")
    fsdp_size = lax.axis_size("fsdp")
    images = teacher.shape[0] * dp_size
    per_image = tokens.shape[0] // teacher.shape[0]
    hidden = w_in.shape[1]
    mates = mates_of(dp_size, hidden)
    index = lax.axis_index("dp").astype(jnp.int32)[None]
    first = lax.axis_index("fsdp").astype(jnp.int32)[None]

    splits = fsdp_size if teacher.shape[1] % (fsdp_size * 8 * lanes) == 0 else 1

    blocks = {0: tokens}
    for bit in (2, 4, 1):
        if bit < mates:
            blocks[bit] = swap(tokens, "dp", bit)
    all_teacher = exchange(teacher_payload(first, teacher, dp_size, splits), "dp")
    pooled, embed_rows = forward(
        first, tokens, norm_gain, w_in, b_in, w_out, b_out, dp_size * fsdp_size, teacher.shape[0]
    )
    all_embed = exchange(embed_rows, ("dp", "fsdp"))
    gram = target_gram(after(all_teacher, [pooled] + [blocks[k] for k in (1,) if k in blocks]), images)
    for k, source, bit in ((6, 4, 2), (3, 2, 1), (5, 4, 1)):
        if k < mates:
            blocks[k] = swap(after(blocks[source], gram), "dp", bit)
    near_mates = [blocks[k] for k in range(min(mates, 6))]
    slope, turned = mate_slopes(index % mates, near_mates, norm_gain, w_in, b_in, hidden // mates)
    slopes, turns = [slope], [turned]
    if mates > 6:
        blocks[7] = swap(after(blocks[6], [slope, all_embed]), "dp", 1)
        far_mates = [blocks[6], blocks[7]]
        slope, turned = mate_slopes(
            index % mates, far_mates, norm_gain, w_in, b_in, hidden // mates
        )
        slopes, turns = slopes + [slope], turns + [turned]
    if splits == 1:
        grams = [gram]
    elif splits == 2:
        grams = [gram, after(swap(gram, "fsdp", 1), slopes[-1])]
    else:
        grams = [lax.psum(gram, "fsdp")]
    loss, dembed, parts = backward(
        index, all_embed, unit_gram(grams), final_gain, pooled, w_out, slopes, turns,
        mates, dp_size, per_image,
    )
    arrived = exchange(parts, "dp")
    columns = own_columns(index, dembed, dembed.shape[1] // dp_size)
    grad_in, grad_out = finish(arrived, columns, mates, hidden)
    return (loss[0, 0], grad_in, grad_out)


def solution(mesh):
    return jax.shard_map(
        body,
        mesh=mesh,
        in_specs=(
            P("dp", None),
            P("dp", None),
            P(),
            P(None, "fsdp"),
            P("fsdp"),
            P(None, "fsdp"),
            P(),
            P(),
        ),
        out_specs=(P(), P("dp", "fsdp"), P("dp", "fsdp")),
        check_vma=False,
    )
```

```python
import jax
import jax.numpy as jnp
from jax import lax
from jax.experimental import pallas as pl
from jax.experimental.pallas import tpu as pltpu
from jax.sharding import PartitionSpec as P

loss_scale = 4096.0
lanes = 128
f32 = jnp.float32
bf16 = jnp.bfloat16


def gelu_tanh(values):
    inner = 0.7978845608 * (values + 0.044715 * values * values * values)
    return 0.5 * values * (1.0 + jnp.tanh(inner))


def gelu_slope(values):
    square = values * values
    tangent = jnp.tanh(0.7978845608 * (values + 0.044715 * values * square))
    return 0.5 * (1.0 + tangent) + 0.5 * values * (1.0 - tangent * tangent) * 0.7978845608 * (
        1.0 + 3.0 * 0.044715 * square
    )


def contract_last(left_side, right_side):
    return lax.dot_general(
        left_side, right_side, (((1,), (1,)), ((), ())), preferred_element_type=f32
    )


def fold_rows(values, width):
    count = values.shape[1] // width
    return jnp.concatenate(
        [
            values[i : i + 1, k * width : (k + 1) * width]
            for i in range(values.shape[0])
            for k in range(count)
        ],
        axis=0,
    )


def vmem_params(elements):
    return pltpu.CompilerParams(vmem_limit_bytes=min(56 * 2**20, 8 * elements + 8 * 2**20))


in_hbm = pl.BlockSpec(memory_space=pltpu.HBM)
in_any = pl.BlockSpec(memory_space=pl.ANY)


def hbm(value):
    return pltpu.with_memory_space_constraint(value, pltpu.HBM)


def near(value, keep):
    return pltpu.with_memory_space_constraint(value, pltpu.VMEM) if keep else value


def near_shape(shape, dtype, keep):
    return pltpu.VMEM(shape, dtype) if keep else jax.ShapeDtypeStruct(shape, dtype)


def normalize(values, gain):
    centered = values - jnp.mean(values, axis=-1, keepdims=True)
    inv_std = lax.rsqrt(jnp.mean(centered * centered, axis=-1, keepdims=True) + 1e-05)
    return (centered * inv_std * gain).astype(bf16)


def teacher_payload(first, teacher, copies, splits):
    images = teacher.shape[0]
    features = teacher.shape[1] // splits
    fold = features // 8

    def kernel(first_ref, teacher_ref, out_ref):
        start = 0
        if splits > 1:
            start = pl.multiple_of(first_ref[0] * features, features)
        folded = fold_rows(teacher_ref[:, pl.ds(start, features)].astype(f32), fold).astype(bf16)
        out_ref[...] = jnp.broadcast_to(folded[None], out_ref.shape)

    return pl.pallas_call(
        kernel,
        in_specs=[
            pl.BlockSpec(memory_space=pltpu.SMEM),
            pl.BlockSpec(memory_space=pltpu.VMEM),
        ],
        out_shape=pltpu.HBM((copies, images * 8, fold), bf16),
        compiler_params=vmem_params(copies * images * features),
        cost_estimate=pl.CostEstimate(
            flops=copies * images * features,
            bytes_accessed=2 * copies * images * features,
            transcendentals=0,
        ),
        name="teacher_payload",
    )(first, hbm(teacher))


def forward(first, tokens, norm_gain, w_in, b_in, w_out, b_out, copies, images):
    rows, width = tokens.shape
    hidden = w_in.shape[1]
    per_image = rows // images
    tile = min(512, hidden)
    steps = hidden // tile
    folds = width // lanes

    def kernel(
        first_ref, gain_ref, bias_ref, out_b_ref, tokens_any, in_any_ref, out_any_ref,
        pooled_ref, payload_ref, tokens_ref, in_ref, out_w_ref, sems,
    ):
        loads = [
            pltpu.make_async_copy(
                in_any_ref.at[:, pl.ds(j * tile, tile)], in_ref.at[j], sems.at[j]
            )
            for j in range(steps)
        ]
        loads.append(pltpu.make_async_copy(out_any_ref, out_w_ref, sems.at[steps]))
        loads.append(pltpu.make_async_copy(tokens_any, tokens_ref, sems.at[steps + 1]))
        loads[-1].start()
        for load in loads[:-1]:
            load.start()
        loads[-1].wait()
        values = tokens_ref[...].astype(f32)
        normed = normalize(values, gain_ref[...])
        token_mean = jnp.mean(values.reshape(images, per_image, width), axis=1)
        for j in range(steps):
            taken = slice(j * tile, (j + 1) * tile)
            loads[j].wait()
            pre_act = jnp.dot(normed, in_ref[j], preferred_element_type=f32) + bias_ref[:, taken]
            pooled_ref[:, taken] = jnp.mean(
                gelu_tanh(pre_act).reshape(images, per_image, tile), axis=1
            ).astype(bf16)
        loads[steps].wait()
        total = contract_last(pooled_ref[...], out_w_ref[...])
        total += jnp.where(first_ref[0] == 0, token_mean + out_b_ref[...], 0.0)
        folded = fold_rows(total, lanes).astype(bf16)
        payload_ref[...] = jnp.broadcast_to(folded[None], payload_ref.shape)

    whole = pl.BlockSpec(memory_space=pltpu.VMEM)
    payload = (copies, images * folds, lanes)
    return pl.pallas_call(
        kernel,
        in_specs=[pl.BlockSpec(memory_space=pltpu.SMEM)] + [whole] * 3 + [in_hbm] * 3,
        out_specs=[whole, whole],
        out_shape=[
            jax.ShapeDtypeStruct((images, hidden), bf16),
            pltpu.HBM(payload, bf16),
        ],
        scratch_shapes=[
            pltpu.VMEM((rows, width), bf16),
            pltpu.VMEM((steps, width, tile), bf16),
            pltpu.VMEM((width, hidden), bf16),
            pltpu.SemaphoreType.DMA((steps + 2,)),
        ],
        compiler_params=vmem_params(
            rows * width + width * hidden + copies * images * width
        ),
        cost_estimate=pl.CostEstimate(
            flops=2 * rows * width * hidden,
            bytes_accessed=4 * width * hidden,
            transcendentals=rows * hidden,
        ),
        name="forward",
    )(
        first, hbm(norm_gain[None]), hbm(b_in[None]), hbm(b_out[None]),
        hbm(tokens), hbm(w_in), hbm(w_out),
    )


def mate_slopes(share_index, blocks, norm_gain, w_in, b_in, share):
    rows, width = blocks[0].shape
    count = len(blocks)
    keep = rows <= 512

    def kernel(index_ref, *refs):
        token_refs = refs[:count]
        gain_ref, bias_ref, in_any_ref, slope_ref, turned_ref = refs[count : count + 5]
        held_ref, in_ref, sems = refs[count + 5 :]
        first_unit = pl.multiple_of(index_ref[0] * share, share)
        weight = pltpu.make_async_copy(
            in_any_ref.at[:, pl.ds(first_unit, share)], in_ref, sems.at[count]
        )
        loads = [
            pltpu.make_async_copy(token_refs[k], held_ref.at[k], sems.at[k]) for k in range(count)
        ]
        loads[0].start()
        weight.start()
        for load in loads[1:]:
            load.start()
        for k in range(count):
            taken = slice(k * rows, (k + 1) * rows)
            loads[k].wait()
            normed = normalize(held_ref[k].astype(f32), gain_ref[...])
            if k == 0:
                weight.wait()
            pre_act = jnp.dot(normed, in_ref[...], preferred_element_type=f32) + bias_ref[...]
            slope_ref[taken] = gelu_slope(pre_act).astype(bf16)
            turned_ref[:, taken] = normed.T

    return pl.pallas_call(
        kernel,
        grid_spec=pltpu.PrefetchScalarGridSpec(
            num_scalar_prefetch=1,
            grid=(1,),
            in_specs=[in_any] * count
            + [
                pl.BlockSpec((1, width), lambda j, s: (0, 0)),
                pl.BlockSpec((1, share), lambda j, s: (0, s[0])),
                in_hbm,
            ],
            out_specs=[
                pl.BlockSpec((count * rows, share), lambda j, s: (0, 0)),
                pl.BlockSpec((width, count * rows), lambda j, s: (0, 0)),
            ],
            scratch_shapes=[
                pltpu.VMEM((count, rows, width), bf16),
                pltpu.VMEM((width, share), bf16),
                pltpu.SemaphoreType.DMA((count + 1,)),
            ],
        ),
        out_shape=[
            near_shape((count * rows, share), bf16, keep),
            near_shape((width, count * rows), bf16, keep),
        ],
        compiler_params=vmem_params(count * rows * (width + share)),
        cost_estimate=pl.CostEstimate(
            flops=2 * rows * count * width * share,
            bytes_accessed=4 * rows * count * width,
            transcendentals=rows * count * share,
        ),
        name="mate_slopes",
    )(
        share_index,
        *[hbm(block) for block in blocks],
        hbm(norm_gain[None]),
        hbm(b_in[None]),
        hbm(w_in),
    )


def target_gram(arrived, images):
    senders, folded, fold = arrived.shape
    folds = senders * folded // images
    keep = images <= 64

    def kernel(arrived_ref, gram_ref, wide_ref):
        wide_ref[...] = arrived_ref[...].astype(f32).reshape(images, folds, fold)
        rows = jnp.concatenate([wide_ref[:, k, :].astype(bf16) for k in range(folds)], axis=1)
        gram_ref[...] = contract_last(rows, rows)

    return pl.pallas_call(
        kernel,
        out_shape=jax.ShapeDtypeStruct((images, images), f32),
        scratch_shapes=[pltpu.VMEM((images, folds, fold), f32)],
        compiler_params=vmem_params(images * folds * fold),
        cost_estimate=pl.CostEstimate(
            flops=2 * images * images * folds * fold,
            bytes_accessed=2 * images * folds * fold,
            transcendentals=0,
        ),
        name="target_gram",
    )(near(arrived, keep))


def unit_gram(parts):
    images = parts[0].shape[0]

    def kernel(*refs):
        gram_ref = refs[-1]
        gram = sum((ref[...] for ref in refs[1:-1]), refs[0][...])
        row = lax.broadcasted_iota(jnp.int32, gram.shape, 0)
        column = lax.broadcasted_iota(jnp.int32, gram.shape, 1)
        diagonal = jnp.where(row == column, gram, 0.0)
        down = lax.rsqrt(jnp.sum(diagonal, axis=1, keepdims=True) + 1e-06)
        across = lax.rsqrt(jnp.sum(diagonal, axis=0, keepdims=True) + 1e-06)
        gram_ref[...] = gram * down * across

    return pl.pallas_call(
        kernel,
        out_shape=jax.ShapeDtypeStruct((images, images), f32),
        compiler_params=vmem_params(4 * images * images),
        cost_estimate=pl.CostEstimate(
            flops=8 * images * images, bytes_accessed=8 * images * images, transcendentals=0
        ),
        name="unit_gram",
    )(*parts)


def backward(
    index, arrived, gram, final_gain, pooled, w_out, slopes, turns, mates, dp_size, per_image
):
    senders, folded, _ = arrived.shape
    width = w_out.shape[0]
    images = gram.shape[0]
    own_images, hidden = pooled.shape
    fsdp_size = senders // dp_size
    folds = width // lanes
    share = hidden // mates
    parts = len(turns)
    part_rows = [turned.shape[1] for turned in turns]
    mate_rows = sum(part_rows)
    out_rows = width // dp_size
    piece = min(share, 256)
    pieces = share // piece
    extra = own_images * hidden // piece
    groups = dp_size // mates
    group_rows = mates * out_rows
    part_shape = (pieces * group_rows + extra, piece)
    keep = images <= 64

    def kernel(index_ref, arrived_ref, gram_ref, gain_ref, pooled_ref, out_w_any, *refs):
        slope_refs, turned_refs, refs = refs[:parts], refs[parts : 2 * parts], refs[2 * parts :]
        loss_ref, dembed_ref, refs = refs[0], refs[1], refs[2:]
        part_refs, refs = refs[:groups], refs[groups:]
        wide_ref, hidden_ref, out_w_ref, payload_ref, sems = refs
        first_unit = pl.multiple_of(lax.rem(index_ref[0], mates) * share, share)
        load = pltpu.make_async_copy(
            out_w_any.at[:, pl.ds(first_unit, share)], out_w_ref, sems.at[0]
        )
        load.start()
        embeds = arrived_ref[...].astype(f32).reshape(dp_size, fsdp_size, folded, lanes)
        wide_ref[...] = jnp.sum(embeds, axis=1).reshape(images, folds, lanes)
        embedding = jnp.concatenate([wide_ref[:, k, :] for k in range(folds)], axis=1)
        gain = gain_ref[...]
        centered = embedding - jnp.mean(embedding, axis=-1, keepdims=True)
        inv_std = lax.rsqrt(jnp.mean(centered * centered, axis=-1, keepdims=True) + 1e-05)
        normed = centered * inv_std
        scaled = normed * gain
        square = jnp.sum(scaled * scaled, axis=-1, keepdims=True) + 1e-06
        inv_norm = lax.rsqrt(square)
        unit = scaled * inv_norm
        student = unit.astype(bf16)
        resid = contract_last(student, student) - gram_ref[...]
        loss_ref[0, 0] = jnp.sum(resid * resid) / images
        dstudent = (loss_scale * 4.0 / images) * jnp.dot(
            resid.astype(bf16), student, preferred_element_type=f32
        )
        dunit = (dstudent - unit * jnp.sum(unit * dstudent, axis=-1, keepdims=True)) * inv_norm
        gain_grad = dunit * gain
        dembed = inv_std * (
            gain_grad
            - jnp.mean(gain_grad, axis=-1, keepdims=True)
            - normed * jnp.mean(gain_grad * normed, axis=-1, keepdims=True)
        )
        dembed_b = dembed.astype(bf16)
        dembed_ref[...] = dembed_b
        shape = (mates * own_images, images)
        row = lax.broadcasted_iota(jnp.int32, shape, 0)
        column = lax.broadcasted_iota(jnp.int32, shape, 1)
        owner = (row // own_images) ^ index_ref[0]
        pick = (owner * own_images + row % own_images == column).astype(f32).astype(bf16)
        mate_dembed = jnp.dot(pick, dembed_b, preferred_element_type=f32).astype(bf16)
        load.wait()
        dpooled = jnp.dot(mate_dembed, out_w_ref[...], preferred_element_type=f32) / per_image
        k = 0
        for part in range(parts):
            for j in range(part_rows[part] // per_image):
                rows = slice(k * per_image, (k + 1) * per_image)
                taken = slice(j * per_image, (j + 1) * per_image)
                hidden_ref[rows] = (
                    dpooled[k : k + 1] * slope_refs[part][taken].astype(f32)
                ).astype(bf16)
                k += 1
        folded_pooled = fold_rows(pooled_ref[...].astype(f32), piece).astype(bf16)
        stores = []
        for k in list(range(1, groups))[::-1] + [0]:
            first_row = pl.multiple_of(
                ((index_ref[0] // mates) ^ k) * group_rows, group_rows
            )
            term, start = 0.0, 0
            for part in range(parts):
                rows = slice(start, start + part_rows[part])
                start += part_rows[part]
                term += jnp.dot(
                    turned_refs[part][pl.ds(first_row, group_rows)],
                    hidden_ref[rows],
                    preferred_element_type=f32,
                )
            term = term.astype(bf16)
            for j in range(pieces):
                payload_ref[k, j * group_rows : (j + 1) * group_rows] = term[
                    :, j * piece : (j + 1) * piece
                ]
            payload_ref[k, pieces * group_rows :] = folded_pooled
            stores.append(pltpu.make_async_copy(payload_ref.at[k], part_refs[k], sems.at[k]))
            stores[-1].start()
        for store in stores:
            store.wait()

    whole = pl.BlockSpec(memory_space=pltpu.VMEM)
    smem = pl.BlockSpec(memory_space=pltpu.SMEM)
    return pl.pallas_call(
        kernel,
        in_specs=[smem, whole, whole, whole, whole, in_hbm] + [whole] * (2 * parts),
        out_specs=[smem, whole, in_any] + [in_hbm] * (groups - 1),
        out_shape=[
            jax.ShapeDtypeStruct((1, 1), f32),
            jax.ShapeDtypeStruct((images, width), bf16),
            near_shape(part_shape, bf16, keep),
        ]
        + [pltpu.HBM(part_shape, bf16)] * (groups - 1),
        scratch_shapes=[
            pltpu.VMEM((images, folds, lanes), f32),
            pltpu.VMEM((mate_rows, share), bf16),
            pltpu.VMEM((width, share), bf16),
            pltpu.VMEM((groups,) + part_shape, bf16),
            pltpu.SemaphoreType.DMA((groups,)),
        ],
        compiler_params=vmem_params(mate_rows * (width + share) // 2 + arrived.size),
        cost_estimate=pl.CostEstimate(
            flops=2 * mate_rows * width * share,
            bytes_accessed=2 * mate_rows * (width + share),
            transcendentals=0,
        ),
        name="backward",
    )(
        index, near(arrived, keep), gram, hbm(final_gain[None]), pooled, hbm(w_out),
        *[near(slope, keep) for slope in slopes], *[near(turned, keep) for turned in turns],
    )


def own_columns(index, dembed, out_rows):
    images, width = dembed.shape
    keep = images <= 64

    def kernel(index_ref, dembed_ref, columns_ref):
        row = lax.broadcasted_iota(jnp.int32, (out_rows, width), 0)
        column = lax.broadcasted_iota(jnp.int32, (out_rows, width), 1)
        pick = (row + index_ref[0] * out_rows == column).astype(f32).astype(bf16)
        columns_ref[...] = contract_last(pick, dembed_ref[...]).astype(bf16)

    return pl.pallas_call(
        kernel,
        in_specs=[
            pl.BlockSpec(memory_space=pltpu.SMEM),
            pl.BlockSpec(memory_space=pltpu.VMEM),
        ],
        out_shape=near_shape((out_rows, images), bf16, keep),
        compiler_params=vmem_params(images * width),
        cost_estimate=pl.CostEstimate(
            flops=2 * images * out_rows * width,
            bytes_accessed=2 * images * width,
            transcendentals=0,
        ),
        name="own_columns",
    )(index, dembed)


def sum_groups(index, parts, mates, out_rows, extra):
    groups = len(parts)
    rows, piece = parts[0].shape
    group_rows = mates * out_rows
    pieces = (rows - extra) // group_rows
    block = (pieces * out_rows + groups * extra, piece)

    def kernel(index_ref, *refs):
        part_refs, block_refs, total_ref = refs[:groups], refs[groups:-1], refs[-1]
        total = part_refs[0][: rows - extra].astype(f32)
        for part_ref in part_refs[1:]:
            total += part_ref[: rows - extra].astype(f32)
        total_ref[...] = total.astype(bf16)
        for j in range(mates):
            mate = lax.rem(index_ref[0], mates) ^ j
            for k in range(pieces):
                start = pl.multiple_of(k * group_rows + mate * out_rows, out_rows)
                block_refs[j][k * out_rows : (k + 1) * out_rows] = total_ref[
                    pl.ds(start, out_rows)
                ]
            for k in range(groups):
                start = pieces * out_rows + k * extra
                block_refs[j][start : start + extra] = part_refs[k][rows - extra :]

    return pl.pallas_call(
        kernel,
        in_specs=[pl.BlockSpec(memory_space=pltpu.SMEM)]
        + [pl.BlockSpec(memory_space=pltpu.VMEM)] * groups,
        out_shape=[jax.ShapeDtypeStruct(block, bf16)] * mates,
        scratch_shapes=[pltpu.VMEM((rows - extra, piece), bf16)],
        compiler_params=vmem_params(groups * rows * piece),
        cost_estimate=pl.CostEstimate(
            flops=groups * rows * piece, bytes_accessed=4 * groups * rows * piece, transcendentals=0
        ),
        name="sum_groups",
    )(index, *parts)


def finish(index, blocks, columns, hidden, own_images):
    mates = len(blocks)
    rows, piece = blocks[0].shape
    out_rows, images = columns.shape
    pieces = hidden // mates // piece
    in_rows = out_rows * pieces
    folds = hidden // piece
    extra = own_images * folds
    groups = (rows - in_rows) // extra

    def kernel(index_ref, *refs):
        block_refs, (columns_ref, in_ref, out_ref, wide_ref) = refs[:mates], refs[mates:]
        for j in range(mates):
            mate = lax.rem(index_ref[0], mates) ^ j
            for k in range(pieces):
                start = pl.multiple_of((mate * pieces + k) * piece, piece)
                in_ref[:, pl.ds(start, piece)] = block_refs[j][k * out_rows : (k + 1) * out_rows]
            for k in range(groups):
                sender = ((index_ref[0] // mates) ^ k) * mates + mate
                start = in_rows + k * extra
                taken = block_refs[j][start : start + extra].astype(f32)
                wide_ref[pl.ds(sender * own_images, own_images)] = taken.reshape(
                    own_images, folds, piece
                )
        pooled = jnp.concatenate([wide_ref[:, k, :].astype(bf16) for k in range(folds)], axis=1)
        out_ref[...] = jnp.dot(columns_ref[...], pooled, preferred_element_type=f32).astype(bf16)

    return pl.pallas_call(
        kernel,
        in_specs=[pl.BlockSpec(memory_space=pltpu.SMEM)]
        + [pl.BlockSpec(memory_space=pltpu.VMEM)] * (mates + 1),
        out_shape=[jax.ShapeDtypeStruct((out_rows, hidden), bf16)] * 2,
        scratch_shapes=[pltpu.VMEM((images, folds, piece), f32)],
        compiler_params=vmem_params(2 * images * folds * piece + out_rows * hidden),
        cost_estimate=pl.CostEstimate(
            flops=2 * images * out_rows * hidden,
            bytes_accessed=2 * mates * rows * piece,
            transcendentals=0,
        ),
        name="finish",
    )(index, *blocks, columns)


def exchange(blocks, axes):
    return lax.all_to_all(blocks, axes, split_axis=0, concat_axis=0, tiled=True)


def mates_of(dp_size, hidden):
    mates = 4
    while dp_size % mates or hidden % (lanes * mates):
        mates //= 2
    return mates


def swap(value, axis, step):
    return lax.ppermute(value, axis, [(i, i ^ step) for i in range(lax.axis_size(axis))])


def after(value, other):
    return lax.optimization_barrier((value, other))[0]


def body(tokens, teacher, norm_gain, w_in, b_in, w_out, b_out, final_gain):
    dp_size = lax.axis_size("dp")
    fsdp_size = lax.axis_size("fsdp")
    images = teacher.shape[0] * dp_size
    per_image = tokens.shape[0] // teacher.shape[0]
    hidden = w_in.shape[1]
    mates = mates_of(dp_size, hidden)
    index = lax.axis_index("dp").astype(jnp.int32)[None]
    first = lax.axis_index("fsdp").astype(jnp.int32)[None]

    splits = fsdp_size if teacher.shape[1] % (fsdp_size * 8 * lanes) == 0 else 1

    blocks = {0: tokens}
    for bit in (2, 4, 1):
        if bit < mates:
            blocks[bit] = swap(tokens, "dp", bit)
    all_teacher = exchange(teacher_payload(first, teacher, dp_size, splits), "dp")
    pooled, embed_rows = forward(
        first, tokens, norm_gain, w_in, b_in, w_out, b_out, dp_size * fsdp_size, teacher.shape[0]
    )
    all_embed = exchange(embed_rows, ("dp", "fsdp"))
    gram = target_gram(after(all_teacher, [pooled] + [blocks[k] for k in (1,) if k in blocks]), images)
    for k, source, bit in ((6, 4, 2), (3, 2, 1), (5, 4, 1)):
        if k < mates:
            blocks[k] = swap(after(blocks[source], gram), "dp", bit)
    near_mates = [blocks[k] for k in range(min(mates, 6))]
    slope, turned = mate_slopes(index % mates, near_mates, norm_gain, w_in, b_in, hidden // mates)
    slopes, turns = [slope], [turned]
    if mates > 6:
        blocks[7] = swap(after(blocks[6], [slope, all_embed]), "dp", 1)
        far_mates = [blocks[6], blocks[7]]
        slope, turned = mate_slopes(
            index % mates, far_mates, norm_gain, w_in, b_in, hidden // mates
        )
        slopes, turns = slopes + [slope], turns + [turned]
    if splits == 1:
        grams = [gram]
    elif splits == 2:
        grams = [gram, after(swap(gram, "fsdp", 1), slopes[-1])]
    else:
        grams = [lax.psum(gram, "fsdp")]
    loss, dembed, *parts = backward(
        index, all_embed, unit_gram(grams), final_gain, pooled, w_out, slopes, turns,
        mates, dp_size, per_image,
    )
    out_rows = dembed.shape[1] // dp_size
    parts = [parts[0]] + [swap(part, "dp", (k + 1) * mates) for k, part in enumerate(parts[1:])]
    columns = own_columns(index, dembed, out_rows)
    extra = teacher.shape[0] * hidden // parts[0].shape[1]
    shares = sum_groups(index, parts, mates, out_rows, extra)
    shares = [shares[0]] + [swap(part, "dp", j + 1) for j, part in enumerate(shares[1:])]
    grad_in, grad_out = finish(index, shares, columns, hidden, teacher.shape[0])
    return (loss[0, 0], grad_in, grad_out)


def solution(mesh):
    return jax.shard_map(
        body,
        mesh=mesh,
        in_specs=(
            P("dp", None),
            P("dp", None),
            P(),
            P(None, "fsdp"),
            P("fsdp"),
            P(None, "fsdp"),
            P(),
            P(),
        ),
        out_specs=(P(), P("dp", "fsdp"), P("dp", "fsdp")),
        check_vma=False,
    )
```

```python
import jax
import jax.numpy as jnp
from jax import lax
from jax.experimental import pallas as pl
from jax.experimental.pallas import tpu as pltpu
from jax.sharding import PartitionSpec as P

loss_scale = 4096.0
lanes = 128
f32 = jnp.float32
bf16 = jnp.bfloat16


def gelu_tanh(values):
    inner = 0.7978845608 * (values + 0.044715 * values * values * values)
    return 0.5 * values * (1.0 + jnp.tanh(inner))


def gelu_slope(values):
    square = values * values
    tangent = jnp.tanh(0.7978845608 * (values + 0.044715 * values * square))
    return 0.5 * (1.0 + tangent) + 0.5 * values * (1.0 - tangent * tangent) * 0.7978845608 * (
        1.0 + 3.0 * 0.044715 * square
    )


def contract_last(left_side, right_side):
    return lax.dot_general(
        left_side, right_side, (((1,), (1,)), ((), ())), preferred_element_type=f32
    )


def fold_rows(values, width):
    count = values.shape[1] // width
    return jnp.concatenate(
        [
            values[i : i + 1, k * width : (k + 1) * width]
            for i in range(values.shape[0])
            for k in range(count)
        ],
        axis=0,
    )


def vmem_params(elements):
    return pltpu.CompilerParams(vmem_limit_bytes=min(56 * 2**20, 8 * elements + 8 * 2**20))


in_hbm = pl.BlockSpec(memory_space=pltpu.HBM)
in_any = pl.BlockSpec(memory_space=pl.ANY)


def hbm(value):
    return pltpu.with_memory_space_constraint(value, pltpu.HBM)


def near(value, keep):
    return pltpu.with_memory_space_constraint(value, pltpu.VMEM) if keep else value


def near_shape(shape, dtype, keep):
    return pltpu.VMEM(shape, dtype) if keep else jax.ShapeDtypeStruct(shape, dtype)


def normalize(values, gain):
    centered = values - jnp.mean(values, axis=-1, keepdims=True)
    inv_std = lax.rsqrt(jnp.mean(centered * centered, axis=-1, keepdims=True) + 1e-05)
    return (centered * inv_std * gain).astype(bf16)


def teacher_payload(first, teacher, copies, splits):
    images = teacher.shape[0]
    features = teacher.shape[1] // splits
    fold = features // 8

    def kernel(first_ref, teacher_ref, out_ref):
        start = 0
        if splits > 1:
            start = pl.multiple_of(first_ref[0] * features, features)
        folded = fold_rows(teacher_ref[:, pl.ds(start, features)].astype(f32), fold).astype(bf16)
        out_ref[...] = jnp.broadcast_to(folded[None], out_ref.shape)

    return pl.pallas_call(
        kernel,
        in_specs=[
            pl.BlockSpec(memory_space=pltpu.SMEM),
            pl.BlockSpec(memory_space=pltpu.VMEM),
        ],
        out_shape=pltpu.HBM((copies, images * 8, fold), bf16),
        compiler_params=vmem_params(copies * images * features),
        cost_estimate=pl.CostEstimate(
            flops=copies * images * features,
            bytes_accessed=2 * copies * images * features,
            transcendentals=0,
        ),
        name="teacher_payload",
    )(first, hbm(teacher))


def forward(first, tokens, norm_gain, w_in, b_in, w_out, b_out, copies, images):
    rows, width = tokens.shape
    hidden = w_in.shape[1]
    per_image = rows // images
    tile = min(512, hidden)
    steps = hidden // tile
    folds = width // lanes

    def kernel(
        first_ref, gain_ref, bias_ref, out_b_ref, tokens_any, in_any_ref, out_any_ref,
        pooled_ref, payload_ref, tokens_ref, in_ref, out_w_ref, sems,
    ):
        loads = [
            pltpu.make_async_copy(
                in_any_ref.at[:, pl.ds(j * tile, tile)], in_ref.at[j], sems.at[j]
            )
            for j in range(steps)
        ]
        loads.append(pltpu.make_async_copy(out_any_ref, out_w_ref, sems.at[steps]))
        loads.append(pltpu.make_async_copy(tokens_any, tokens_ref, sems.at[steps + 1]))
        loads[-1].start()
        for load in loads[:-1]:
            load.start()
        loads[-1].wait()
        values = tokens_ref[...].astype(f32)
        normed = normalize(values, gain_ref[...])
        token_mean = jnp.mean(values.reshape(images, per_image, width), axis=1)
        for j in range(steps):
            taken = slice(j * tile, (j + 1) * tile)
            loads[j].wait()
            pre_act = jnp.dot(normed, in_ref[j], preferred_element_type=f32) + bias_ref[:, taken]
            pooled_ref[:, taken] = jnp.mean(
                gelu_tanh(pre_act).reshape(images, per_image, tile), axis=1
            ).astype(bf16)
        loads[steps].wait()
        total = contract_last(pooled_ref[...], out_w_ref[...])
        total += jnp.where(first_ref[0] == 0, token_mean + out_b_ref[...], 0.0)
        folded = fold_rows(total, lanes).astype(bf16)
        payload_ref[...] = jnp.broadcast_to(folded[None], payload_ref.shape)

    whole = pl.BlockSpec(memory_space=pltpu.VMEM)
    payload = (copies, images * folds, lanes)
    return pl.pallas_call(
        kernel,
        in_specs=[pl.BlockSpec(memory_space=pltpu.SMEM)] + [whole] * 3 + [in_hbm] * 3,
        out_specs=[whole, whole],
        out_shape=[
            jax.ShapeDtypeStruct((images, hidden), bf16),
            pltpu.HBM(payload, bf16),
        ],
        scratch_shapes=[
            pltpu.VMEM((rows, width), bf16),
            pltpu.VMEM((steps, width, tile), bf16),
            pltpu.VMEM((width, hidden), bf16),
            pltpu.SemaphoreType.DMA((steps + 2,)),
        ],
        compiler_params=vmem_params(
            rows * width + width * hidden + copies * images * width
        ),
        cost_estimate=pl.CostEstimate(
            flops=2 * rows * width * hidden,
            bytes_accessed=4 * width * hidden,
            transcendentals=rows * hidden,
        ),
        name="forward",
    )(
        first, hbm(norm_gain[None]), hbm(b_in[None]), hbm(b_out[None]),
        hbm(tokens), hbm(w_in), hbm(w_out),
    )


def mate_slopes(share_index, blocks, norm_gain, w_in, b_in, share):
    rows, width = blocks[0].shape
    count = len(blocks)
    keep = rows <= 512

    def kernel(index_ref, *refs):
        token_refs = refs[:count]
        gain_ref, bias_ref, in_any_ref, slope_ref, turned_ref = refs[count : count + 5]
        held_ref, in_ref, sems = refs[count + 5 :]
        first_unit = pl.multiple_of(index_ref[0] * share, share)
        weight = pltpu.make_async_copy(
            in_any_ref.at[:, pl.ds(first_unit, share)], in_ref, sems.at[count]
        )
        loads = [
            pltpu.make_async_copy(token_refs[k], held_ref.at[k], sems.at[k]) for k in range(count)
        ]
        loads[0].start()
        weight.start()
        for load in loads[1:]:
            load.start()
        for k in range(count):
            taken = slice(k * rows, (k + 1) * rows)
            loads[k].wait()
            normed = normalize(held_ref[k].astype(f32), gain_ref[...])
            if k == 0:
                weight.wait()
            pre_act = jnp.dot(normed, in_ref[...], preferred_element_type=f32) + bias_ref[...]
            slope_ref[taken] = gelu_slope(pre_act).astype(bf16)
            turned_ref[:, taken] = normed.T

    return pl.pallas_call(
        kernel,
        grid_spec=pltpu.PrefetchScalarGridSpec(
            num_scalar_prefetch=1,
            grid=(1,),
            in_specs=[in_any] * count
            + [
                pl.BlockSpec((1, width), lambda j, s: (0, 0)),
                pl.BlockSpec((1, share), lambda j, s: (0, s[0])),
                in_hbm,
            ],
            out_specs=[
                pl.BlockSpec((count * rows, share), lambda j, s: (0, 0)),
                pl.BlockSpec((width, count * rows), lambda j, s: (0, 0)),
            ],
            scratch_shapes=[
                pltpu.VMEM((count, rows, width), bf16),
                pltpu.VMEM((width, share), bf16),
                pltpu.SemaphoreType.DMA((count + 1,)),
            ],
        ),
        out_shape=[
            near_shape((count * rows, share), bf16, keep),
            near_shape((width, count * rows), bf16, keep),
        ],
        compiler_params=vmem_params(count * rows * (width + share)),
        cost_estimate=pl.CostEstimate(
            flops=2 * rows * count * width * share,
            bytes_accessed=4 * rows * count * width,
            transcendentals=rows * count * share,
        ),
        name="mate_slopes",
    )(
        share_index,
        *[hbm(block) for block in blocks],
        hbm(norm_gain[None]),
        hbm(b_in[None]),
        hbm(w_in),
    )


def target_gram(arrived, images):
    senders, folded, fold = arrived.shape
    folds = senders * folded // images
    keep = images <= 64

    def kernel(arrived_ref, gram_ref, wide_ref):
        wide_ref[...] = arrived_ref[...].astype(f32).reshape(images, folds, fold)
        rows = jnp.concatenate([wide_ref[:, k, :].astype(bf16) for k in range(folds)], axis=1)
        gram_ref[...] = contract_last(rows, rows)

    return pl.pallas_call(
        kernel,
        out_shape=jax.ShapeDtypeStruct((images, images), f32),
        scratch_shapes=[pltpu.VMEM((images, folds, fold), f32)],
        compiler_params=vmem_params(images * folds * fold),
        cost_estimate=pl.CostEstimate(
            flops=2 * images * images * folds * fold,
            bytes_accessed=2 * images * folds * fold,
            transcendentals=0,
        ),
        name="target_gram",
    )(near(arrived, keep))


def unit_gram(parts):
    images = parts[0].shape[0]

    def kernel(*refs):
        gram_ref = refs[-1]
        gram = sum((ref[...] for ref in refs[1:-1]), refs[0][...])
        row = lax.broadcasted_iota(jnp.int32, gram.shape, 0)
        column = lax.broadcasted_iota(jnp.int32, gram.shape, 1)
        diagonal = jnp.where(row == column, gram, 0.0)
        down = lax.rsqrt(jnp.sum(diagonal, axis=1, keepdims=True) + 1e-06)
        across = lax.rsqrt(jnp.sum(diagonal, axis=0, keepdims=True) + 1e-06)
        gram_ref[...] = gram * down * across

    return pl.pallas_call(
        kernel,
        out_shape=jax.ShapeDtypeStruct((images, images), f32),
        compiler_params=vmem_params(4 * images * images),
        cost_estimate=pl.CostEstimate(
            flops=8 * images * images, bytes_accessed=8 * images * images, transcendentals=0
        ),
        name="unit_gram",
    )(*parts)


def backward(
    index, arrived, gram, final_gain, pooled, w_out, slopes, turns, sends, mates, dp_size, per_image
):
    senders, folded, _ = arrived.shape
    width = w_out.shape[0]
    images = gram.shape[0]
    own_images, hidden = pooled.shape
    fsdp_size = senders // dp_size
    folds = width // lanes
    share = hidden // mates
    parts = len(turns)
    part_rows = [turned.shape[1] for turned in turns]
    mate_rows = sum(part_rows)
    out_rows = width // dp_size
    piece = min(share, 256)
    pieces = share // piece
    extra = own_images * hidden // piece
    groups = dp_size // mates
    group_rows = mates * out_rows
    shapes = [
        (len(send) * group_rows + (extra if i < groups else 0), piece)
        for i, send in enumerate(sends)
    ]
    keep = images <= 64

    def kernel(index_ref, arrived_ref, gram_ref, gain_ref, pooled_ref, out_w_any, *refs):
        slope_refs, turned_refs, refs = refs[:parts], refs[parts : 2 * parts], refs[2 * parts :]
        loss_ref, dembed_ref, refs = refs[0], refs[1], refs[2:]
        part_refs, refs = refs[: len(sends)], refs[len(sends) :]
        wide_ref, hidden_ref, out_w_ref, sems = refs[:4]
        payload_refs = refs[4:]
        first_unit = pl.multiple_of(lax.rem(index_ref[0], mates) * share, share)
        load = pltpu.make_async_copy(
            out_w_any.at[:, pl.ds(first_unit, share)], out_w_ref, sems.at[0]
        )
        load.start()
        embeds = arrived_ref[...].astype(f32).reshape(dp_size, fsdp_size, folded, lanes)
        wide_ref[...] = jnp.sum(embeds, axis=1).reshape(images, folds, lanes)
        embedding = jnp.concatenate([wide_ref[:, k, :] for k in range(folds)], axis=1)
        gain = gain_ref[...]
        centered = embedding - jnp.mean(embedding, axis=-1, keepdims=True)
        inv_std = lax.rsqrt(jnp.mean(centered * centered, axis=-1, keepdims=True) + 1e-05)
        normed = centered * inv_std
        scaled = normed * gain
        square = jnp.sum(scaled * scaled, axis=-1, keepdims=True) + 1e-06
        inv_norm = lax.rsqrt(square)
        unit = scaled * inv_norm
        student = unit.astype(bf16)
        resid = contract_last(student, student) - gram_ref[...]
        loss_ref[0, 0] = jnp.sum(resid * resid) / images
        dstudent = (loss_scale * 4.0 / images) * jnp.dot(
            resid.astype(bf16), student, preferred_element_type=f32
        )
        dunit = (dstudent - unit * jnp.sum(unit * dstudent, axis=-1, keepdims=True)) * inv_norm
        gain_grad = dunit * gain
        dembed = inv_std * (
            gain_grad
            - jnp.mean(gain_grad, axis=-1, keepdims=True)
            - normed * jnp.mean(gain_grad * normed, axis=-1, keepdims=True)
        )
        dembed_b = dembed.astype(bf16)
        dembed_ref[...] = dembed_b
        shape = (mates * own_images, images)
        row = lax.broadcasted_iota(jnp.int32, shape, 0)
        column = lax.broadcasted_iota(jnp.int32, shape, 1)
        owner = (row // own_images) ^ index_ref[0]
        pick = (owner * own_images + row % own_images == column).astype(f32).astype(bf16)
        mate_dembed = jnp.dot(pick, dembed_b, preferred_element_type=f32).astype(bf16)
        load.wait()
        dpooled = jnp.dot(mate_dembed, out_w_ref[...], preferred_element_type=f32) / per_image
        k = 0
        for part in range(parts):
            for j in range(part_rows[part] // per_image):
                rows = slice(k * per_image, (k + 1) * per_image)
                taken = slice(j * per_image, (j + 1) * per_image)
                hidden_ref[rows] = (
                    dpooled[k : k + 1] * slope_refs[part][taken].astype(f32)
                ).astype(bf16)
                k += 1
        folded_pooled = fold_rows(pooled_ref[...].astype(f32), piece).astype(bf16)
        stores = []
        for k in list(range(1, groups))[::-1] + [0]:
            first_row = pl.multiple_of(
                ((index_ref[0] // mates) ^ k) * group_rows, group_rows
            )
            term, start = 0.0, 0
            for part in range(parts):
                rows = slice(start, start + part_rows[part])
                start += part_rows[part]
                term += jnp.dot(
                    turned_refs[part][pl.ds(first_row, group_rows)],
                    hidden_ref[rows],
                    preferred_element_type=f32,
                )
            term = term.astype(bf16)
            for i, send in enumerate(sends):
                for at, (group, j) in enumerate(send):
                    if group == k:
                        payload_refs[i][at * group_rows : (at + 1) * group_rows] = term[
                            :, j * piece : (j + 1) * piece
                        ]
        for i, send in enumerate(sends):
            if i < groups:
                payload_refs[i][len(send) * group_rows :] = folded_pooled
            stores.append(pltpu.make_async_copy(payload_refs[i], part_refs[i], sems.at[i]))
            stores[-1].start()
        for store in stores:
            store.wait()

    whole = pl.BlockSpec(memory_space=pltpu.VMEM)
    smem = pl.BlockSpec(memory_space=pltpu.SMEM)
    return pl.pallas_call(
        kernel,
        in_specs=[smem, whole, whole, whole, whole, in_hbm] + [whole] * (2 * parts),
        out_specs=[smem, whole] + [in_any] * len(sends),
        out_shape=[
            jax.ShapeDtypeStruct((1, 1), f32),
            jax.ShapeDtypeStruct((images, width), bf16),
        ]
        + [
            near_shape(shape, bf16, keep) if i in (0, groups) else pltpu.HBM(shape, bf16)
            for i, shape in enumerate(shapes)
        ],
        scratch_shapes=[
            pltpu.VMEM((images, folds, lanes), f32),
            pltpu.VMEM((mate_rows, share), bf16),
            pltpu.VMEM((width, share), bf16),
            pltpu.SemaphoreType.DMA((len(sends),)),
        ]
        + [pltpu.VMEM(shape, bf16) for shape in shapes],
        compiler_params=vmem_params(mate_rows * (width + share) // 2 + arrived.size),
        cost_estimate=pl.CostEstimate(
            flops=2 * mate_rows * width * share,
            bytes_accessed=2 * mate_rows * (width + share),
            transcendentals=0,
        ),
        name="backward",
    )(
        index, near(arrived, keep), gram, hbm(final_gain[None]), pooled, hbm(w_out),
        *[near(slope, keep) for slope in slopes], *[near(turned, keep) for turned in turns],
    )


def own_columns(index, dembed, out_rows):
    images, width = dembed.shape
    keep = images <= 64

    def kernel(index_ref, dembed_ref, columns_ref):
        row = lax.broadcasted_iota(jnp.int32, (out_rows, width), 0)
        column = lax.broadcasted_iota(jnp.int32, (out_rows, width), 1)
        pick = (row + index_ref[0] * out_rows == column).astype(f32).astype(bf16)
        columns_ref[...] = contract_last(pick, dembed_ref[...]).astype(bf16)

    return pl.pallas_call(
        kernel,
        in_specs=[
            pl.BlockSpec(memory_space=pltpu.SMEM),
            pl.BlockSpec(memory_space=pltpu.VMEM),
        ],
        out_shape=near_shape((out_rows, images), bf16, keep),
        compiler_params=vmem_params(images * width),
        cost_estimate=pl.CostEstimate(
            flops=2 * images * out_rows * width,
            bytes_accessed=2 * images * width,
            transcendentals=0,
        ),
        name="own_columns",
    )(index, dembed)


def add_pair(kept, arrived, start):
    rows, _ = kept.shape

    def kernel(kept_ref, arrived_ref, sum_ref):
        sum_ref[...] = (
            kept_ref[...].astype(f32) + arrived_ref[start : start + rows].astype(f32)
        ).astype(bf16)

    return pl.pallas_call(
        kernel,
        out_shape=jax.ShapeDtypeStruct(kept.shape, bf16),
        compiler_params=vmem_params(kept.size + arrived.size),
        cost_estimate=pl.CostEstimate(
            flops=kept.size, bytes_accessed=6 * kept.size, transcendentals=0
        ),
        name="add_pair",
    )(kept, arrived)


def sum_groups(index, parts, sources, pooled_at, mates, out_rows, extra):
    piece = parts[0].shape[1]
    group_rows = mates * out_rows
    pieces = len(sources)
    block = (pieces * out_rows + len(pooled_at) * extra, piece)

    def kernel(index_ref, *refs):
        part_refs, refs = refs[: len(parts)], refs[len(parts) :]
        block_refs, total_ref = refs[:-1], refs[-1]
        for j in range(pieces):
            total = 0.0
            for at, start in sources[j]:
                total += part_refs[at][start : start + group_rows].astype(f32)
            total_ref[j * group_rows : (j + 1) * group_rows] = total.astype(bf16)
        for j in range(mates):
            mate = lax.rem(index_ref[0], mates) ^ j
            for k in range(pieces):
                start = pl.multiple_of(k * group_rows + mate * out_rows, out_rows)
                block_refs[j][k * out_rows : (k + 1) * out_rows] = total_ref[
                    pl.ds(start, out_rows)
                ]
            for k, (at, first) in enumerate(pooled_at):
                start = pieces * out_rows + k * extra
                block_refs[j][start : start + extra] = part_refs[at][first : first + extra]

    return pl.pallas_call(
        kernel,
        in_specs=[pl.BlockSpec(memory_space=pltpu.SMEM)]
        + [pl.BlockSpec(memory_space=pltpu.VMEM)] * len(parts),
        out_shape=[jax.ShapeDtypeStruct(block, bf16)] * mates,
        scratch_shapes=[pltpu.VMEM((pieces * group_rows, piece), bf16)],
        compiler_params=vmem_params(sum(part.size for part in parts)),
        cost_estimate=pl.CostEstimate(
            flops=sum(part.size for part in parts),
            bytes_accessed=4 * sum(part.size for part in parts),
            transcendentals=0,
        ),
        name="sum_groups",
    )(index, *parts)


def finish(index, blocks, columns, hidden, own_images):
    mates = len(blocks)
    rows, piece = blocks[0].shape
    out_rows, images = columns.shape
    pieces = hidden // mates // piece
    in_rows = out_rows * pieces
    folds = hidden // piece
    extra = own_images * folds
    groups = (rows - in_rows) // extra

    def kernel(index_ref, *refs):
        block_refs, (columns_ref, in_ref, out_ref, wide_ref) = refs[:mates], refs[mates:]
        for j in range(mates):
            mate = lax.rem(index_ref[0], mates) ^ j
            for k in range(pieces):
                start = pl.multiple_of((mate * pieces + k) * piece, piece)
                in_ref[:, pl.ds(start, piece)] = block_refs[j][k * out_rows : (k + 1) * out_rows]
            for k in range(groups):
                sender = ((index_ref[0] // mates) ^ k) * mates + mate
                start = in_rows + k * extra
                taken = block_refs[j][start : start + extra].astype(f32)
                wide_ref[pl.ds(sender * own_images, own_images)] = taken.reshape(
                    own_images, folds, piece
                )
        pooled = jnp.concatenate([wide_ref[:, k, :].astype(bf16) for k in range(folds)], axis=1)
        out_ref[...] = jnp.dot(columns_ref[...], pooled, preferred_element_type=f32).astype(bf16)

    return pl.pallas_call(
        kernel,
        in_specs=[pl.BlockSpec(memory_space=pltpu.SMEM)]
        + [pl.BlockSpec(memory_space=pltpu.VMEM)] * (mates + 1),
        out_shape=[jax.ShapeDtypeStruct((out_rows, hidden), bf16)] * 2,
        scratch_shapes=[pltpu.VMEM((images, folds, piece), f32)],
        compiler_params=vmem_params(2 * images * folds * piece + out_rows * hidden),
        cost_estimate=pl.CostEstimate(
            flops=2 * images * out_rows * hidden,
            bytes_accessed=2 * mates * rows * piece,
            transcendentals=0,
        ),
        name="finish",
    )(index, *blocks, columns)


def exchange(blocks, axes):
    return lax.all_to_all(blocks, axes, split_axis=0, concat_axis=0, tiled=True)


def mates_of(dp_size, hidden):
    mates = 4
    while dp_size % mates or hidden % (lanes * mates):
        mates //= 2
    return mates


def swap(value, axis, step):
    return lax.ppermute(value, axis, [(i, i ^ step) for i in range(lax.axis_size(axis))])


def after(value, other):
    return lax.optimization_barrier((value, other))[0]


def body(tokens, teacher, norm_gain, w_in, b_in, w_out, b_out, final_gain):
    dp_size = lax.axis_size("dp")
    fsdp_size = lax.axis_size("fsdp")
    images = teacher.shape[0] * dp_size
    per_image = tokens.shape[0] // teacher.shape[0]
    hidden = w_in.shape[1]
    mates = mates_of(dp_size, hidden)
    index = lax.axis_index("dp").astype(jnp.int32)[None]
    first = lax.axis_index("fsdp").astype(jnp.int32)[None]

    splits = fsdp_size if teacher.shape[1] % (fsdp_size * 8 * lanes) == 0 else 1

    blocks = {0: tokens}
    for bit in (2, 4, 1):
        if bit < mates:
            blocks[bit] = swap(tokens, "dp", bit)
    all_teacher = exchange(teacher_payload(first, teacher, dp_size, splits), "dp")
    pooled, embed_rows = forward(
        first, tokens, norm_gain, w_in, b_in, w_out, b_out, dp_size * fsdp_size, teacher.shape[0]
    )
    all_embed = exchange(embed_rows, ("dp", "fsdp"))
    gram = target_gram(after(all_teacher, [pooled] + [blocks[k] for k in (1,) if k in blocks]), images)
    for k, source, bit in ((6, 4, 2), (3, 2, 1), (5, 4, 1)):
        if k < mates:
            blocks[k] = swap(after(blocks[source], gram), "dp", bit)
    near_mates = [blocks[k] for k in range(min(mates, 6))]
    slope, turned = mate_slopes(index % mates, near_mates, norm_gain, w_in, b_in, hidden // mates)
    slopes, turns = [slope], [turned]
    if mates > 6:
        blocks[7] = swap(after(blocks[6], [slope, all_embed]), "dp", 1)
        far_mates = [blocks[6], blocks[7]]
        slope, turned = mate_slopes(
            index % mates, far_mates, norm_gain, w_in, b_in, hidden // mates
        )
        slopes, turns = slopes + [slope], turns + [turned]
    if splits == 1:
        grams = [gram]
    elif splits == 2:
        grams = [gram, after(swap(gram, "fsdp", 1), slopes[-1])]
    else:
        grams = [lax.psum(gram, "fsdp")]
    groups = dp_size // mates
    share = hidden // mates
    pieces = share // min(share, 256)
    out_rows = w_out.shape[0] // dp_size
    group_rows = mates * out_rows
    half = pieces // 2
    paired = groups == 4 and half > 0
    if paired:
        sends = [
            [(0, j) for j in range(pieces)],
            [(1, j) for j in range(pieces)] + [(3, j) for j in range(half)],
            [(2, j) for j in range(half, pieces)],
            [(3, j) for j in range(half, pieces)],
            [(2, j) for j in range(half)],
        ]
    else:
        sends = [[(k, j) for j in range(pieces)] for k in range(groups)]
    pooled_at = [(k, len(sends[k]) * group_rows) for k in range(groups)]
    loss, dembed, *parts = backward(
        index, all_embed, unit_gram(grams), final_gain, pooled, w_out, slopes, turns, sends,
        mates, dp_size, per_image,
    )
    swapped = [parts[0]] + [swap(parts[k], "dp", k * mates) for k in range(1, groups)]
    sources = [[(0, j * group_rows), (1, j * group_rows)] for j in range(pieces)]
    if paired:
        pair = add_pair(parts[groups], swapped[1], pieces * group_rows)
        swapped.append(swap(pair, "dp", 2 * mates))
        for j in range(pieces):
            arrays, first = ((4,), 0) if j < half else ((2, 3), half)
            sources[j] += [(k, (j - first) * group_rows) for k in arrays]
    else:
        sources = [[(k, j * group_rows) for k in range(groups)] for j in range(pieces)]
    columns = own_columns(index, dembed, out_rows)
    extra = teacher.shape[0] * hidden // parts[0].shape[1]
    shares = sum_groups(index, swapped, sources, pooled_at, mates, out_rows, extra)
    shares = [shares[0]] + [swap(part, "dp", j + 1) for j, part in enumerate(shares[1:])]
    grad_in, grad_out = finish(index, shares, columns, hidden, teacher.shape[0])
    return (loss[0, 0], grad_in, grad_out)


def solution(mesh):
    return jax.shard_map(
        body,
        mesh=mesh,
        in_specs=(
            P("dp", None),
            P("dp", None),
            P(),
            P(None, "fsdp"),
            P("fsdp"),
            P(None, "fsdp"),
            P(),
            P(),
        ),
        out_specs=(P(), P("dp", "fsdp"), P("dp", "fsdp")),
        check_vma=False,
    )
```

```python
import jax
import jax.numpy as jnp
from jax import lax
from jax.experimental import pallas as pl
from jax.experimental.pallas import tpu as pltpu
from jax.sharding import PartitionSpec as P

loss_scale = 4096.0
lanes = 128
f32 = jnp.float32
bf16 = jnp.bfloat16


def gelu_tanh(values):
    inner = 0.7978845608 * (values + 0.044715 * values * values * values)
    return 0.5 * values * (1.0 + jnp.tanh(inner))


def gelu_slope(values):
    square = values * values
    tangent = jnp.tanh(0.7978845608 * (values + 0.044715 * values * square))
    return 0.5 * (1.0 + tangent) + 0.5 * values * (1.0 - tangent * tangent) * 0.7978845608 * (
        1.0 + 3.0 * 0.044715 * square
    )


def contract_last(left_side, right_side):
    return lax.dot_general(
        left_side, right_side, (((1,), (1,)), ((), ())), preferred_element_type=f32
    )


def fold_rows(values, width):
    count = values.shape[1] // width
    return jnp.concatenate(
        [
            values[i : i + 1, k * width : (k + 1) * width]
            for i in range(values.shape[0])
            for k in range(count)
        ],
        axis=0,
    )


def vmem_params(elements):
    return pltpu.CompilerParams(vmem_limit_bytes=min(56 * 2**20, 8 * elements + 8 * 2**20))


in_hbm = pl.BlockSpec(memory_space=pltpu.HBM)
in_any = pl.BlockSpec(memory_space=pl.ANY)


def hbm(value):
    return pltpu.with_memory_space_constraint(value, pltpu.HBM)


def near(value, keep):
    return pltpu.with_memory_space_constraint(value, pltpu.VMEM) if keep else value


def near_shape(shape, dtype, keep):
    return pltpu.VMEM(shape, dtype) if keep else jax.ShapeDtypeStruct(shape, dtype)


def normalize(values, gain):
    centered = values - jnp.mean(values, axis=-1, keepdims=True)
    inv_std = lax.rsqrt(jnp.mean(centered * centered, axis=-1, keepdims=True) + 1e-05)
    return (centered * inv_std * gain).astype(bf16)


def teacher_payload(first, teacher, copies, splits):
    images = teacher.shape[0]
    features = teacher.shape[1] // splits
    fold = features // 8

    def kernel(first_ref, teacher_ref, out_ref):
        start = 0
        if splits > 1:
            start = pl.multiple_of(first_ref[0] * features, features)
        folded = fold_rows(teacher_ref[:, pl.ds(start, features)].astype(f32), fold).astype(bf16)
        out_ref[...] = jnp.broadcast_to(folded[None], out_ref.shape)

    return pl.pallas_call(
        kernel,
        in_specs=[
            pl.BlockSpec(memory_space=pltpu.SMEM),
            pl.BlockSpec(memory_space=pltpu.VMEM),
        ],
        out_shape=pltpu.HBM((copies, images * 8, fold), bf16),
        compiler_params=vmem_params(copies * images * features),
        cost_estimate=pl.CostEstimate(
            flops=copies * images * features,
            bytes_accessed=2 * copies * images * features,
            transcendentals=0,
        ),
        name="teacher_payload",
    )(first, hbm(teacher))


def forward(first, tokens, norm_gain, w_in, b_in, w_out, b_out, copies, images):
    rows, width = tokens.shape
    hidden = w_in.shape[1]
    per_image = rows // images
    tile = min(512, hidden)
    steps = hidden // tile
    folds = width // lanes

    def kernel(
        first_ref, gain_ref, bias_ref, out_b_ref, tokens_any, in_any_ref, out_any_ref,
        pooled_ref, payload_ref, tokens_ref, in_ref, out_w_ref, sems,
    ):
        loads = [
            pltpu.make_async_copy(
                in_any_ref.at[:, pl.ds(j * tile, tile)], in_ref.at[j], sems.at[j]
            )
            for j in range(steps)
        ]
        out_loads = [
            pltpu.make_async_copy(
                out_any_ref.at[:, pl.ds(j * tile, tile)], out_w_ref.at[j], sems.at[steps + j]
            )
            for j in range(steps)
        ]
        tokens_load = pltpu.make_async_copy(tokens_any, tokens_ref, sems.at[2 * steps])
        tokens_load.start()
        for load in loads:
            load.start()
        tokens_load.wait()
        values = tokens_ref[...].astype(f32)
        normed = normalize(values, gain_ref[...])
        token_mean = jnp.mean(values.reshape(images, per_image, width), axis=1)
        for load in out_loads:
            load.start()
        total, before = 0.0, None
        for j in range(steps):
            taken = slice(j * tile, (j + 1) * tile)
            loads[j].wait()
            pre_act = jnp.dot(normed, in_ref[j], preferred_element_type=f32) + bias_ref[:, taken]
            if j > 0:
                out_loads[j - 1].wait()
                total += contract_last(before, out_w_ref[j - 1])
            before = jnp.mean(
                gelu_tanh(pre_act).reshape(images, per_image, tile), axis=1
            ).astype(bf16)
            pooled_ref[:, taken] = before
        out_loads[-1].wait()
        total += contract_last(before, out_w_ref[steps - 1])
        total += jnp.where(first_ref[0] == 0, token_mean + out_b_ref[...], 0.0)
        folded = fold_rows(total, lanes).astype(bf16)
        payload_ref[...] = jnp.broadcast_to(folded[None], payload_ref.shape)

    whole = pl.BlockSpec(memory_space=pltpu.VMEM)
    payload = (copies, images * folds, lanes)
    return pl.pallas_call(
        kernel,
        in_specs=[pl.BlockSpec(memory_space=pltpu.SMEM)] + [whole] * 3 + [in_hbm] * 3,
        out_specs=[whole, whole],
        out_shape=[
            jax.ShapeDtypeStruct((images, hidden), bf16),
            pltpu.HBM(payload, bf16),
        ],
        scratch_shapes=[
            pltpu.VMEM((rows, width), bf16),
            pltpu.VMEM((steps, width, tile), bf16),
            pltpu.VMEM((steps, width, tile), bf16),
            pltpu.SemaphoreType.DMA((2 * steps + 1,)),
        ],
        compiler_params=vmem_params(
            rows * width + width * hidden + copies * images * width
        ),
        cost_estimate=pl.CostEstimate(
            flops=2 * rows * width * hidden,
            bytes_accessed=4 * width * hidden,
            transcendentals=rows * hidden,
        ),
        name="forward",
    )(
        first, hbm(norm_gain[None]), hbm(b_in[None]), hbm(b_out[None]),
        hbm(tokens), hbm(w_in), hbm(w_out),
    )


def mate_slopes(share_index, blocks, norm_gain, w_in, b_in, share):
    rows, width = blocks[0].shape
    count = len(blocks)
    keep = rows <= 512

    def kernel(index_ref, *refs):
        token_refs = refs[:count]
        gain_ref, bias_ref, in_any_ref, slope_ref, turned_ref = refs[count : count + 5]
        held_ref, in_ref, sems = refs[count + 5 :]
        first_unit = pl.multiple_of(index_ref[0] * share, share)
        weight = pltpu.make_async_copy(
            in_any_ref.at[:, pl.ds(first_unit, share)], in_ref, sems.at[count]
        )
        loads = [
            pltpu.make_async_copy(token_refs[k], held_ref.at[k], sems.at[k]) for k in range(count)
        ]
        loads[0].start()
        weight.start()
        for load in loads[1:]:
            load.start()
        for k in range(count):
            taken = slice(k * rows, (k + 1) * rows)
            loads[k].wait()
            normed = normalize(held_ref[k].astype(f32), gain_ref[...])
            if k == 0:
                weight.wait()
            pre_act = jnp.dot(normed, in_ref[...], preferred_element_type=f32) + bias_ref[...]
            slope_ref[taken] = gelu_slope(pre_act).astype(bf16)
            turned_ref[:, taken] = normed.T

    return pl.pallas_call(
        kernel,
        grid_spec=pltpu.PrefetchScalarGridSpec(
            num_scalar_prefetch=1,
            grid=(1,),
            in_specs=[in_any] * count
            + [
                pl.BlockSpec((1, width), lambda j, s: (0, 0)),
                pl.BlockSpec((1, share), lambda j, s: (0, s[0])),
                in_hbm,
            ],
            out_specs=[
                pl.BlockSpec((count * rows, share), lambda j, s: (0, 0)),
                pl.BlockSpec((width, count * rows), lambda j, s: (0, 0)),
            ],
            scratch_shapes=[
                pltpu.VMEM((count, rows, width), bf16),
                pltpu.VMEM((width, share), bf16),
                pltpu.SemaphoreType.DMA((count + 1,)),
            ],
        ),
        out_shape=[
            near_shape((count * rows, share), bf16, keep),
            near_shape((width, count * rows), bf16, keep),
        ],
        compiler_params=vmem_params(count * rows * (width + share)),
        cost_estimate=pl.CostEstimate(
            flops=2 * rows * count * width * share,
            bytes_accessed=4 * rows * count * width,
            transcendentals=rows * count * share,
        ),
        name="mate_slopes",
    )(
        share_index,
        *[hbm(block) for block in blocks],
        hbm(norm_gain[None]),
        hbm(b_in[None]),
        hbm(w_in),
    )


def target_gram(arrived, images):
    senders, folded, fold = arrived.shape
    folds = senders * folded // images
    keep = images <= 64

    def kernel(arrived_ref, gram_ref, wide_ref):
        wide_ref[...] = arrived_ref[...].astype(f32).reshape(images, folds, fold)
        rows = jnp.concatenate([wide_ref[:, k, :].astype(bf16) for k in range(folds)], axis=1)
        gram_ref[...] = contract_last(rows, rows)

    return pl.pallas_call(
        kernel,
        out_shape=jax.ShapeDtypeStruct((images, images), f32),
        scratch_shapes=[pltpu.VMEM((images, folds, fold), f32)],
        compiler_params=vmem_params(images * folds * fold),
        cost_estimate=pl.CostEstimate(
            flops=2 * images * images * folds * fold,
            bytes_accessed=2 * images * folds * fold,
            transcendentals=0,
        ),
        name="target_gram",
    )(near(arrived, keep))


def unit_gram(parts):
    images = parts[0].shape[0]

    def kernel(*refs):
        gram_ref = refs[-1]
        gram = sum((ref[...] for ref in refs[1:-1]), refs[0][...])
        row = lax.broadcasted_iota(jnp.int32, gram.shape, 0)
        column = lax.broadcasted_iota(jnp.int32, gram.shape, 1)
        diagonal = jnp.where(row == column, gram, 0.0)
        down = lax.rsqrt(jnp.sum(diagonal, axis=1, keepdims=True) + 1e-06)
        across = lax.rsqrt(jnp.sum(diagonal, axis=0, keepdims=True) + 1e-06)
        gram_ref[...] = gram * down * across

    return pl.pallas_call(
        kernel,
        out_shape=jax.ShapeDtypeStruct((images, images), f32),
        compiler_params=vmem_params(4 * images * images),
        cost_estimate=pl.CostEstimate(
            flops=8 * images * images, bytes_accessed=8 * images * images, transcendentals=0
        ),
        name="unit_gram",
    )(*parts)


def backward(
    index, arrived, gram, final_gain, pooled, w_out, slopes, turns, sends, mates, dp_size, per_image
):
    senders, folded, _ = arrived.shape
    width = w_out.shape[0]
    images = gram.shape[0]
    own_images, hidden = pooled.shape
    fsdp_size = senders // dp_size
    folds = width // lanes
    share = hidden // mates
    parts = len(turns)
    part_rows = [turned.shape[1] for turned in turns]
    mate_rows = sum(part_rows)
    out_rows = width // dp_size
    piece = min(share, 256)
    pieces = share // piece
    extra = own_images * hidden // piece
    groups = dp_size // mates
    group_rows = mates * out_rows
    shapes = [
        (len(send) * group_rows + (extra if i < groups else 0), piece)
        for i, send in enumerate(sends)
    ]
    keep = images <= 64

    def kernel(index_ref, arrived_ref, gram_ref, gain_ref, pooled_ref, out_w_any, *refs):
        slope_refs, turned_refs, refs = refs[:parts], refs[parts : 2 * parts], refs[2 * parts :]
        loss_ref, dembed_ref, refs = refs[0], refs[1], refs[2:]
        part_refs, refs = refs[: len(sends)], refs[len(sends) :]
        wide_ref, hidden_ref, out_w_ref, sems = refs[:4]
        payload_refs = refs[4:]
        first_unit = pl.multiple_of(lax.rem(index_ref[0], mates) * share, share)
        load = pltpu.make_async_copy(
            out_w_any.at[:, pl.ds(first_unit, share)], out_w_ref, sems.at[0]
        )
        load.start()
        embeds = arrived_ref[...].astype(f32).reshape(dp_size, fsdp_size, folded, lanes)
        wide_ref[...] = jnp.sum(embeds, axis=1).reshape(images, folds, lanes)
        embedding = jnp.concatenate([wide_ref[:, k, :] for k in range(folds)], axis=1)
        gain = gain_ref[...]
        centered = embedding - jnp.mean(embedding, axis=-1, keepdims=True)
        inv_std = lax.rsqrt(jnp.mean(centered * centered, axis=-1, keepdims=True) + 1e-05)
        normed = centered * inv_std
        scaled = normed * gain
        square = jnp.sum(scaled * scaled, axis=-1, keepdims=True) + 1e-06
        inv_norm = lax.rsqrt(square)
        unit = scaled * inv_norm
        student = unit.astype(bf16)
        resid = contract_last(student, student) - gram_ref[...]
        loss_ref[0, 0] = jnp.sum(resid * resid) / images
        dstudent = (loss_scale * 4.0 / images) * jnp.dot(
            resid.astype(bf16), student, preferred_element_type=f32
        )
        dunit = (dstudent - unit * jnp.sum(unit * dstudent, axis=-1, keepdims=True)) * inv_norm
        gain_grad = dunit * gain
        dembed = inv_std * (
            gain_grad
            - jnp.mean(gain_grad, axis=-1, keepdims=True)
            - normed * jnp.mean(gain_grad * normed, axis=-1, keepdims=True)
        )
        dembed_b = dembed.astype(bf16)
        dembed_ref[...] = dembed_b
        shape = (mates * own_images, images)
        row = lax.broadcasted_iota(jnp.int32, shape, 0)
        column = lax.broadcasted_iota(jnp.int32, shape, 1)
        owner = (row // own_images) ^ index_ref[0]
        pick = (owner * own_images + row % own_images == column).astype(f32).astype(bf16)
        mate_dembed = jnp.dot(pick, dembed_b, preferred_element_type=f32).astype(bf16)
        load.wait()
        dpooled = jnp.dot(mate_dembed, out_w_ref[...], preferred_element_type=f32) / per_image
        k = 0
        for part in range(parts):
            for j in range(part_rows[part] // per_image):
                rows = slice(k * per_image, (k + 1) * per_image)
                taken = slice(j * per_image, (j + 1) * per_image)
                hidden_ref[rows] = (
                    dpooled[k : k + 1] * slope_refs[part][taken].astype(f32)
                ).astype(bf16)
                k += 1
        folded_pooled = fold_rows(pooled_ref[...].astype(f32), piece).astype(bf16)
        stores = []
        for k in list(range(1, groups))[::-1] + [0]:
            first_row = pl.multiple_of(
                ((index_ref[0] // mates) ^ k) * group_rows, group_rows
            )
            term, start = 0.0, 0
            for part in range(parts):
                rows = slice(start, start + part_rows[part])
                start += part_rows[part]
                term += jnp.dot(
                    turned_refs[part][pl.ds(first_row, group_rows)],
                    hidden_ref[rows],
                    preferred_element_type=f32,
                )
            term = term.astype(bf16)
            for i, send in enumerate(sends):
                for at, (group, j) in enumerate(send):
                    if group == k:
                        payload_refs[i][at * group_rows : (at + 1) * group_rows] = term[
                            :, j * piece : (j + 1) * piece
                        ]
        for i, send in enumerate(sends):
            if i < groups:
                payload_refs[i][len(send) * group_rows :] = folded_pooled
            stores.append(pltpu.make_async_copy(payload_refs[i], part_refs[i], sems.at[i]))
            stores[-1].start()
        for store in stores:
            store.wait()

    whole = pl.BlockSpec(memory_space=pltpu.VMEM)
    smem = pl.BlockSpec(memory_space=pltpu.SMEM)
    return pl.pallas_call(
        kernel,
        in_specs=[smem, whole, whole, whole, whole, in_hbm] + [whole] * (2 * parts),
        out_specs=[smem, whole] + [in_any] * len(sends),
        out_shape=[
            jax.ShapeDtypeStruct((1, 1), f32),
            jax.ShapeDtypeStruct((images, width), bf16),
        ]
        + [
            near_shape(shape, bf16, keep) if i in (0, groups) else pltpu.HBM(shape, bf16)
            for i, shape in enumerate(shapes)
        ],
        scratch_shapes=[
            pltpu.VMEM((images, folds, lanes), f32),
            pltpu.VMEM((mate_rows, share), bf16),
            pltpu.VMEM((width, share), bf16),
            pltpu.SemaphoreType.DMA((len(sends),)),
        ]
        + [pltpu.VMEM(shape, bf16) for shape in shapes],
        compiler_params=vmem_params(mate_rows * (width + share) // 2 + arrived.size),
        cost_estimate=pl.CostEstimate(
            flops=2 * mate_rows * width * share,
            bytes_accessed=2 * mate_rows * (width + share),
            transcendentals=0,
        ),
        name="backward",
    )(
        index, near(arrived, keep), gram, hbm(final_gain[None]), pooled, hbm(w_out),
        *[near(slope, keep) for slope in slopes], *[near(turned, keep) for turned in turns],
    )


def own_columns(index, dembed, out_rows):
    images, width = dembed.shape
    keep = images <= 64

    def kernel(index_ref, dembed_ref, columns_ref):
        row = lax.broadcasted_iota(jnp.int32, (out_rows, width), 0)
        column = lax.broadcasted_iota(jnp.int32, (out_rows, width), 1)
        pick = (row + index_ref[0] * out_rows == column).astype(f32).astype(bf16)
        columns_ref[...] = contract_last(pick, dembed_ref[...]).astype(bf16)

    return pl.pallas_call(
        kernel,
        in_specs=[
            pl.BlockSpec(memory_space=pltpu.SMEM),
            pl.BlockSpec(memory_space=pltpu.VMEM),
        ],
        out_shape=near_shape((out_rows, images), bf16, keep),
        compiler_params=vmem_params(images * width),
        cost_estimate=pl.CostEstimate(
            flops=2 * images * out_rows * width,
            bytes_accessed=2 * images * width,
            transcendentals=0,
        ),
        name="own_columns",
    )(index, dembed)


def add_pair(kept, arrived):

    def kernel(kept_ref, arrived_ref, sum_ref):
        sum_ref[...] = (kept_ref[...].astype(f32) + arrived_ref[...].astype(f32)).astype(bf16)

    return pl.pallas_call(
        kernel,
        out_shape=jax.ShapeDtypeStruct(kept.shape, bf16),
        compiler_params=vmem_params(kept.size + arrived.size),
        cost_estimate=pl.CostEstimate(
            flops=kept.size, bytes_accessed=6 * kept.size, transcendentals=0
        ),
        name="add_pair",
    )(kept, arrived)


def sum_groups(index, parts, sources, pooled_at, mates, out_rows, extra):
    piece = parts[0].shape[1]
    group_rows = mates * out_rows
    pieces = len(sources)
    block = (pieces * out_rows + len(pooled_at) * extra, piece)

    def kernel(index_ref, *refs):
        part_refs, refs = refs[: len(parts)], refs[len(parts) :]
        block_refs, total_ref = refs[:-1], refs[-1]
        for j in range(pieces):
            total = 0.0
            for at, start in sources[j]:
                total += part_refs[at][start : start + group_rows].astype(f32)
            total_ref[j * group_rows : (j + 1) * group_rows] = total.astype(bf16)
        for j in range(mates):
            mate = lax.rem(index_ref[0], mates) ^ j
            for k in range(pieces):
                start = pl.multiple_of(k * group_rows + mate * out_rows, out_rows)
                block_refs[j][k * out_rows : (k + 1) * out_rows] = total_ref[
                    pl.ds(start, out_rows)
                ]
            for k, (at, first) in enumerate(pooled_at):
                start = pieces * out_rows + k * extra
                block_refs[j][start : start + extra] = part_refs[at][first : first + extra]

    return pl.pallas_call(
        kernel,
        in_specs=[pl.BlockSpec(memory_space=pltpu.SMEM)]
        + [pl.BlockSpec(memory_space=pltpu.VMEM)] * len(parts),
        out_shape=[jax.ShapeDtypeStruct(block, bf16)] * mates,
        scratch_shapes=[pltpu.VMEM((pieces * group_rows, piece), bf16)],
        compiler_params=vmem_params(sum(part.size for part in parts)),
        cost_estimate=pl.CostEstimate(
            flops=sum(part.size for part in parts),
            bytes_accessed=4 * sum(part.size for part in parts),
            transcendentals=0,
        ),
        name="sum_groups",
    )(index, *parts)


def finish(index, blocks, columns, hidden, own_images):
    mates = len(blocks)
    rows, piece = blocks[0].shape
    out_rows, images = columns.shape
    pieces = hidden // mates // piece
    in_rows = out_rows * pieces
    folds = hidden // piece
    extra = own_images * folds
    groups = (rows - in_rows) // extra

    def kernel(index_ref, *refs):
        block_refs, (columns_ref, in_ref, out_ref, wide_ref) = refs[:mates], refs[mates:]
        for j in range(mates):
            mate = lax.rem(index_ref[0], mates) ^ j
            for k in range(pieces):
                start = pl.multiple_of((mate * pieces + k) * piece, piece)
                in_ref[:, pl.ds(start, piece)] = block_refs[j][k * out_rows : (k + 1) * out_rows]
            for k in range(groups):
                sender = ((index_ref[0] // mates) ^ k) * mates + mate
                start = in_rows + k * extra
                taken = block_refs[j][start : start + extra].astype(f32)
                wide_ref[pl.ds(sender * own_images, own_images)] = taken.reshape(
                    own_images, folds, piece
                )
        pooled = jnp.concatenate([wide_ref[:, k, :].astype(bf16) for k in range(folds)], axis=1)
        out_ref[...] = jnp.dot(columns_ref[...], pooled, preferred_element_type=f32).astype(bf16)

    return pl.pallas_call(
        kernel,
        in_specs=[pl.BlockSpec(memory_space=pltpu.SMEM)]
        + [pl.BlockSpec(memory_space=pltpu.VMEM)] * (mates + 1),
        out_shape=[jax.ShapeDtypeStruct((out_rows, hidden), bf16)] * 2,
        scratch_shapes=[pltpu.VMEM((images, folds, piece), f32)],
        compiler_params=vmem_params(2 * images * folds * piece + out_rows * hidden),
        cost_estimate=pl.CostEstimate(
            flops=2 * images * out_rows * hidden,
            bytes_accessed=2 * mates * rows * piece,
            transcendentals=0,
        ),
        name="finish",
    )(index, *blocks, columns)


def exchange(blocks, axes):
    return lax.all_to_all(blocks, axes, split_axis=0, concat_axis=0, tiled=True)


def mates_of(dp_size, hidden):
    mates = 4
    while dp_size % mates or hidden % (lanes * mates):
        mates //= 2
    return mates


def swap(value, axis, step):
    return lax.ppermute(value, axis, [(i, i ^ step) for i in range(lax.axis_size(axis))])


def after(value, other):
    return lax.optimization_barrier((value, other))[0]


def body(tokens, teacher, norm_gain, w_in, b_in, w_out, b_out, final_gain):
    dp_size = lax.axis_size("dp")
    fsdp_size = lax.axis_size("fsdp")
    images = teacher.shape[0] * dp_size
    per_image = tokens.shape[0] // teacher.shape[0]
    hidden = w_in.shape[1]
    mates = mates_of(dp_size, hidden)
    index = lax.axis_index("dp").astype(jnp.int32)[None]
    first = lax.axis_index("fsdp").astype(jnp.int32)[None]

    splits = fsdp_size if teacher.shape[1] % (fsdp_size * 8 * lanes) == 0 else 1

    blocks = {0: tokens}
    for bit in (2, 4, 1):
        if bit < mates:
            blocks[bit] = swap(tokens, "dp", bit)
    all_teacher = exchange(teacher_payload(first, teacher, dp_size, splits), "dp")
    pooled, embed_rows = forward(
        first, tokens, norm_gain, w_in, b_in, w_out, b_out, dp_size * fsdp_size, teacher.shape[0]
    )
    all_embed = exchange(embed_rows, ("dp", "fsdp"))
    gram = target_gram(after(all_teacher, [pooled] + [blocks[k] for k in (1,) if k in blocks]), images)
    for k, source, bit in ((6, 4, 2), (3, 2, 1), (5, 4, 1)):
        if k < mates:
            blocks[k] = swap(after(blocks[source], gram), "dp", bit)
    near_mates = [blocks[k] for k in range(min(mates, 6))]
    slope, turned = mate_slopes(index % mates, near_mates, norm_gain, w_in, b_in, hidden // mates)
    slopes, turns = [slope], [turned]
    if mates > 6:
        blocks[7] = swap(after(blocks[6], [slope, all_embed]), "dp", 1)
        far_mates = [blocks[6], blocks[7]]
        slope, turned = mate_slopes(
            index % mates, far_mates, norm_gain, w_in, b_in, hidden // mates
        )
        slopes, turns = slopes + [slope], turns + [turned]
    if splits == 1:
        grams = [gram]
    elif splits == 2:
        grams = [gram, after(swap(gram, "fsdp", 1), slopes[-1])]
    else:
        grams = [lax.psum(gram, "fsdp")]
    groups = dp_size // mates
    share = hidden // mates
    pieces = share // min(share, 256)
    out_rows = w_out.shape[0] // dp_size
    group_rows = mates * out_rows
    half = pieces // 2
    paired = groups == 4 and half > 0
    if paired:
        sends = [
            [(0, j) for j in range(pieces)],
            [(1, j) for j in range(pieces)],
            [(2, j) for j in range(half, pieces)],
            [(3, j) for j in range(half, pieces)],
            [(2, j) for j in range(half)],
            [(3, j) for j in range(half)],
        ]
    else:
        sends = [[(k, j) for j in range(pieces)] for k in range(groups)]
    pooled_at = [(k, len(sends[k]) * group_rows) for k in range(groups)]
    loss, dembed, *parts = backward(
        index, all_embed, unit_gram(grams), final_gain, pooled, w_out, slopes, turns, sends,
        mates, dp_size, per_image,
    )
    if paired:
        pair = add_pair(parts[groups], swap(parts[groups + 1], "dp", mates))
        parts[1] = after(parts[1], pair)
    swapped = [parts[0]] + [
        swap(parts[k], "dp", k * mates) for k in list(range(2, groups)) + [1] if k < groups
    ]
    if groups > 1:
        swapped.insert(1, swapped.pop())
    sources = [[(0, j * group_rows), (1, j * group_rows)] for j in range(pieces)]
    if paired:
        swapped.append(swap(pair, "dp", 2 * mates))
        for j in range(pieces):
            arrays, first = ((4,), 0) if j < half else ((2, 3), half)
            sources[j] += [(k, (j - first) * group_rows) for k in arrays]
    else:
        sources = [[(k, j * group_rows) for k in range(groups)] for j in range(pieces)]
    columns = own_columns(index, dembed, out_rows)
    extra = teacher.shape[0] * hidden // parts[0].shape[1]
    shares = sum_groups(index, swapped, sources, pooled_at, mates, out_rows, extra)
    shares = [shares[0]] + [swap(part, "dp", j + 1) for j, part in enumerate(shares[1:])]
    grad_in, grad_out = finish(index, shares, columns, hidden, teacher.shape[0])
    return (loss[0, 0], grad_in, grad_out)


def solution(mesh):
    return jax.shard_map(
        body,
        mesh=mesh,
        in_specs=(
            P("dp", None),
            P("dp", None),
            P(),
            P(None, "fsdp"),
            P("fsdp"),
            P(None, "fsdp"),
            P(),
            P(),
        ),
        out_specs=(P(), P("dp", "fsdp"), P("dp", "fsdp")),
        check_vma=False,
    )
```

```python
import jax
import jax.numpy as jnp
from jax import lax
from jax.experimental import pallas as pl
from jax.experimental.pallas import tpu as pltpu
from jax.sharding import PartitionSpec as P

loss_scale = 4096.0
lanes = 128
f32 = jnp.float32
bf16 = jnp.bfloat16


def gelu_tanh(values):
    inner = 0.7978845608 * (values + 0.044715 * values * values * values)
    return 0.5 * values * (1.0 + jnp.tanh(inner))


def gelu_slope(values):
    square = values * values
    tangent = jnp.tanh(0.7978845608 * (values + 0.044715 * values * square))
    return 0.5 * (1.0 + tangent) + 0.5 * values * (1.0 - tangent * tangent) * 0.7978845608 * (
        1.0 + 3.0 * 0.044715 * square
    )


def contract_last(left_side, right_side):
    return lax.dot_general(
        left_side, right_side, (((1,), (1,)), ((), ())), preferred_element_type=f32
    )


def fold_rows(values, width):
    count = values.shape[1] // width
    return jnp.concatenate(
        [
            values[i : i + 1, k * width : (k + 1) * width]
            for i in range(values.shape[0])
            for k in range(count)
        ],
        axis=0,
    )


def vmem_params(elements):
    return pltpu.CompilerParams(vmem_limit_bytes=min(56 * 2**20, 8 * elements + 8 * 2**20))


in_hbm = pl.BlockSpec(memory_space=pltpu.HBM)
in_any = pl.BlockSpec(memory_space=pl.ANY)


def hbm(value):
    return pltpu.with_memory_space_constraint(value, pltpu.HBM)


def near(value, keep):
    return pltpu.with_memory_space_constraint(value, pltpu.VMEM) if keep else value


def near_shape(shape, dtype, keep):
    return pltpu.VMEM(shape, dtype) if keep else jax.ShapeDtypeStruct(shape, dtype)


def normalize(values, gain):
    centered = values - jnp.mean(values, axis=-1, keepdims=True)
    inv_std = lax.rsqrt(jnp.mean(centered * centered, axis=-1, keepdims=True) + 1e-05)
    return (centered * inv_std * gain).astype(bf16)


def teacher_payload(first, teacher, copies, splits):
    images = teacher.shape[0]
    features = teacher.shape[1] // splits
    fold = features // 8

    def kernel(first_ref, teacher_ref, out_ref):
        start = 0
        if splits > 1:
            start = pl.multiple_of(first_ref[0] * features, features)
        folded = fold_rows(teacher_ref[:, pl.ds(start, features)].astype(f32), fold).astype(bf16)
        out_ref[...] = jnp.broadcast_to(folded[None], out_ref.shape)

    return pl.pallas_call(
        kernel,
        in_specs=[
            pl.BlockSpec(memory_space=pltpu.SMEM),
            pl.BlockSpec(memory_space=pltpu.VMEM),
        ],
        out_shape=pltpu.HBM((copies, images * 8, fold), bf16),
        compiler_params=vmem_params(copies * images * features),
        cost_estimate=pl.CostEstimate(
            flops=copies * images * features,
            bytes_accessed=2 * copies * images * features,
            transcendentals=0,
        ),
        name="teacher_payload",
    )(first, hbm(teacher))


def forward(first, tokens, norm_gain, w_in, b_in, w_out, b_out, copies, images):
    rows, width = tokens.shape
    hidden = w_in.shape[1]
    per_image = rows // images
    tile = min(512, hidden)
    steps = hidden // tile
    folds = width // lanes

    def kernel(
        first_ref, gain_ref, bias_ref, out_b_ref, tokens_any, in_any_ref, out_any_ref,
        pooled_ref, payload_ref, tokens_ref, in_ref, out_w_ref, sems,
    ):
        loads = [
            pltpu.make_async_copy(
                in_any_ref.at[:, pl.ds(j * tile, tile)], in_ref.at[j], sems.at[j]
            )
            for j in range(steps)
        ]
        loads.append(pltpu.make_async_copy(out_any_ref, out_w_ref, sems.at[steps]))
        loads.append(pltpu.make_async_copy(tokens_any, tokens_ref, sems.at[steps + 1]))
        loads[-1].start()
        for load in loads[:-1]:
            load.start()
        loads[-1].wait()
        values = tokens_ref[...].astype(f32)
        normed = normalize(values, gain_ref[...])
        token_mean = jnp.mean(values.reshape(images, per_image, width), axis=1)
        for j in range(steps):
            taken = slice(j * tile, (j + 1) * tile)
            loads[j].wait()
            pre_act = jnp.dot(normed, in_ref[j], preferred_element_type=f32) + bias_ref[:, taken]
            pooled_ref[:, taken] = jnp.mean(
                gelu_tanh(pre_act).reshape(images, per_image, tile), axis=1
            ).astype(bf16)
        loads[steps].wait()
        total = contract_last(pooled_ref[...], out_w_ref[...])
        total += jnp.where(first_ref[0] == 0, token_mean + out_b_ref[...], 0.0)
        folded = fold_rows(total, lanes).astype(bf16)
        payload_ref[...] = jnp.broadcast_to(folded[None], payload_ref.shape)

    whole = pl.BlockSpec(memory_space=pltpu.VMEM)
    payload = (copies, images * folds, lanes)
    return pl.pallas_call(
        kernel,
        in_specs=[pl.BlockSpec(memory_space=pltpu.SMEM)] + [whole] * 3 + [in_hbm] * 3,
        out_specs=[whole, whole],
        out_shape=[
            jax.ShapeDtypeStruct((images, hidden), bf16),
            pltpu.HBM(payload, bf16),
        ],
        scratch_shapes=[
            pltpu.VMEM((rows, width), bf16),
            pltpu.VMEM((steps, width, tile), bf16),
            pltpu.VMEM((width, hidden), bf16),
            pltpu.SemaphoreType.DMA((steps + 2,)),
        ],
        compiler_params=vmem_params(
            rows * width + width * hidden + copies * images * width
        ),
        cost_estimate=pl.CostEstimate(
            flops=2 * rows * width * hidden,
            bytes_accessed=4 * width * hidden,
            transcendentals=rows * hidden,
        ),
        name="forward",
    )(
        first, hbm(norm_gain[None]), hbm(b_in[None]), hbm(b_out[None]),
        hbm(tokens), hbm(w_in), hbm(w_out),
    )


def mate_slopes(share_index, blocks, norm_gain, w_in, b_in, share):
    rows, width = blocks[0].shape
    count = len(blocks)
    keep = rows <= 512

    def kernel(index_ref, *refs):
        token_refs = refs[:count]
        gain_ref, bias_ref, in_any_ref, slope_ref, turned_ref = refs[count : count + 5]
        held_ref, in_ref, sems = refs[count + 5 :]
        first_unit = pl.multiple_of(index_ref[0] * share, share)
        weight = pltpu.make_async_copy(
            in_any_ref.at[:, pl.ds(first_unit, share)], in_ref, sems.at[count]
        )
        loads = [
            pltpu.make_async_copy(token_refs[k], held_ref.at[k], sems.at[k]) for k in range(count)
        ]
        loads[0].start()
        weight.start()
        for load in loads[1:]:
            load.start()
        for k in range(count):
            taken = slice(k * rows, (k + 1) * rows)
            loads[k].wait()
            normed = normalize(held_ref[k].astype(f32), gain_ref[...])
            if k == 0:
                weight.wait()
            pre_act = jnp.dot(normed, in_ref[...], preferred_element_type=f32) + bias_ref[...]
            slope_ref[taken] = gelu_slope(pre_act).astype(bf16)
            turned_ref[:, taken] = normed.T

    return pl.pallas_call(
        kernel,
        grid_spec=pltpu.PrefetchScalarGridSpec(
            num_scalar_prefetch=1,
            grid=(1,),
            in_specs=[in_any] * count
            + [
                pl.BlockSpec((1, width), lambda j, s: (0, 0)),
                pl.BlockSpec((1, share), lambda j, s: (0, s[0])),
                in_hbm,
            ],
            out_specs=[
                pl.BlockSpec((count * rows, share), lambda j, s: (0, 0)),
                pl.BlockSpec((width, count * rows), lambda j, s: (0, 0)),
            ],
            scratch_shapes=[
                pltpu.VMEM((count, rows, width), bf16),
                pltpu.VMEM((width, share), bf16),
                pltpu.SemaphoreType.DMA((count + 1,)),
            ],
        ),
        out_shape=[
            near_shape((count * rows, share), bf16, keep),
            near_shape((width, count * rows), bf16, keep),
        ],
        compiler_params=vmem_params(count * rows * (width + share)),
        cost_estimate=pl.CostEstimate(
            flops=2 * rows * count * width * share,
            bytes_accessed=4 * rows * count * width,
            transcendentals=rows * count * share,
        ),
        name="mate_slopes",
    )(
        share_index,
        *[hbm(block) for block in blocks],
        hbm(norm_gain[None]),
        hbm(b_in[None]),
        hbm(w_in),
    )


def target_gram(arrived, images):
    senders, folded, fold = arrived.shape
    folds = senders * folded // images
    keep = images <= 64

    def kernel(arrived_ref, gram_ref, wide_ref):
        wide_ref[...] = arrived_ref[...].astype(f32).reshape(images, folds, fold)
        rows = jnp.concatenate([wide_ref[:, k, :].astype(bf16) for k in range(folds)], axis=1)
        gram_ref[...] = contract_last(rows, rows)

    return pl.pallas_call(
        kernel,
        out_shape=jax.ShapeDtypeStruct((images, images), f32),
        scratch_shapes=[pltpu.VMEM((images, folds, fold), f32)],
        compiler_params=vmem_params(images * folds * fold),
        cost_estimate=pl.CostEstimate(
            flops=2 * images * images * folds * fold,
            bytes_accessed=2 * images * folds * fold,
            transcendentals=0,
        ),
        name="target_gram",
    )(near(arrived, keep))


def unit_gram(parts):
    images = parts[0].shape[0]

    def kernel(*refs):
        gram_ref = refs[-1]
        gram = sum((ref[...] for ref in refs[1:-1]), refs[0][...])
        row = lax.broadcasted_iota(jnp.int32, gram.shape, 0)
        column = lax.broadcasted_iota(jnp.int32, gram.shape, 1)
        diagonal = jnp.where(row == column, gram, 0.0)
        down = lax.rsqrt(jnp.sum(diagonal, axis=1, keepdims=True) + 1e-06)
        across = lax.rsqrt(jnp.sum(diagonal, axis=0, keepdims=True) + 1e-06)
        gram_ref[...] = gram * down * across

    return pl.pallas_call(
        kernel,
        out_shape=jax.ShapeDtypeStruct((images, images), f32),
        compiler_params=vmem_params(4 * images * images),
        cost_estimate=pl.CostEstimate(
            flops=8 * images * images, bytes_accessed=8 * images * images, transcendentals=0
        ),
        name="unit_gram",
    )(*parts)


def backward(
    index, arrived, gram, final_gain, pooled, w_out, slopes, turns, sends, mates, dp_size, per_image
):
    senders, folded, _ = arrived.shape
    width = w_out.shape[0]
    images = gram.shape[0]
    own_images, hidden = pooled.shape
    fsdp_size = senders // dp_size
    folds = width // lanes
    share = hidden // mates
    parts = len(turns)
    part_rows = [turned.shape[1] for turned in turns]
    mate_rows = sum(part_rows)
    out_rows = width // dp_size
    piece = min(share, 256)
    pieces = share // piece
    extra = own_images * hidden // piece
    groups = dp_size // mates
    group_rows = mates * out_rows
    shapes = [
        (len(send) * group_rows + (extra if i < groups else 0), piece)
        for i, send in enumerate(sends)
    ]
    keep = images <= 64

    def kernel(index_ref, arrived_ref, gram_ref, gain_ref, pooled_ref, out_w_any, *refs):
        slope_refs, turned_refs, refs = refs[:parts], refs[parts : 2 * parts], refs[2 * parts :]
        loss_ref, dembed_ref, refs = refs[0], refs[1], refs[2:]
        part_refs, refs = refs[: len(sends)], refs[len(sends) :]
        wide_ref, hidden_ref, out_w_ref, sems = refs[:4]
        payload_refs = refs[4:]
        first_unit = pl.multiple_of(lax.rem(index_ref[0], mates) * share, share)
        load = pltpu.make_async_copy(
            out_w_any.at[:, pl.ds(first_unit, share)], out_w_ref, sems.at[0]
        )
        load.start()
        embeds = arrived_ref[...].astype(f32).reshape(dp_size, fsdp_size, folded, lanes)
        wide_ref[...] = jnp.sum(embeds, axis=1).reshape(images, folds, lanes)
        embedding = jnp.concatenate([wide_ref[:, k, :] for k in range(folds)], axis=1)
        gain = gain_ref[...]
        centered = embedding - jnp.mean(embedding, axis=-1, keepdims=True)
        inv_std = lax.rsqrt(jnp.mean(centered * centered, axis=-1, keepdims=True) + 1e-05)
        normed = centered * inv_std
        scaled = normed * gain
        square = jnp.sum(scaled * scaled, axis=-1, keepdims=True) + 1e-06
        inv_norm = lax.rsqrt(square)
        unit = scaled * inv_norm
        student = unit.astype(bf16)
        resid = contract_last(student, student) - gram_ref[...]
        loss_ref[0, 0] = jnp.sum(resid * resid) / images
        dstudent = (loss_scale * 4.0 / images) * jnp.dot(
            resid.astype(bf16), student, preferred_element_type=f32
        )
        dunit = (dstudent - unit * jnp.sum(unit * dstudent, axis=-1, keepdims=True)) * inv_norm
        gain_grad = dunit * gain
        dembed = inv_std * (
            gain_grad
            - jnp.mean(gain_grad, axis=-1, keepdims=True)
            - normed * jnp.mean(gain_grad * normed, axis=-1, keepdims=True)
        )
        dembed_b = dembed.astype(bf16)
        dembed_ref[...] = dembed_b
        shape = (mates * own_images, images)
        row = lax.broadcasted_iota(jnp.int32, shape, 0)
        column = lax.broadcasted_iota(jnp.int32, shape, 1)
        owner = (row // own_images) ^ index_ref[0]
        pick = (owner * own_images + row % own_images == column).astype(f32).astype(bf16)
        mate_dembed = jnp.dot(pick, dembed_b, preferred_element_type=f32).astype(bf16)
        load.wait()
        dpooled = jnp.dot(mate_dembed, out_w_ref[...], preferred_element_type=f32) / per_image
        k = 0
        for part in range(parts):
            for j in range(part_rows[part] // per_image):
                rows = slice(k * per_image, (k + 1) * per_image)
                taken = slice(j * per_image, (j + 1) * per_image)
                hidden_ref[rows] = (
                    dpooled[k : k + 1] * slope_refs[part][taken].astype(f32)
                ).astype(bf16)
                k += 1
        folded_pooled = fold_rows(pooled_ref[...].astype(f32), piece).astype(bf16)
        stores = []
        for k in list(range(1, groups))[::-1] + [0]:
            first_row = pl.multiple_of(
                ((index_ref[0] // mates) ^ k) * group_rows, group_rows
            )
            term, start = 0.0, 0
            for part in range(parts):
                rows = slice(start, start + part_rows[part])
                start += part_rows[part]
                term += jnp.dot(
                    turned_refs[part][pl.ds(first_row, group_rows)],
                    hidden_ref[rows],
                    preferred_element_type=f32,
                )
            term = term.astype(bf16)
            for i, send in enumerate(sends):
                for at, (group, j) in enumerate(send):
                    if group == k:
                        payload_refs[i][at * group_rows : (at + 1) * group_rows] = term[
                            :, j * piece : (j + 1) * piece
                        ]
        for i, send in enumerate(sends):
            if i < groups:
                payload_refs[i][len(send) * group_rows :] = folded_pooled
            stores.append(pltpu.make_async_copy(payload_refs[i], part_refs[i], sems.at[i]))
            stores[-1].start()
        for store in stores:
            store.wait()

    whole = pl.BlockSpec(memory_space=pltpu.VMEM)
    smem = pl.BlockSpec(memory_space=pltpu.SMEM)
    return pl.pallas_call(
        kernel,
        in_specs=[smem, whole, whole, whole, whole, in_hbm] + [whole] * (2 * parts),
        out_specs=[smem, whole] + [in_any] * len(sends),
        out_shape=[
            jax.ShapeDtypeStruct((1, 1), f32),
            jax.ShapeDtypeStruct((images, width), bf16),
        ]
        + [
            near_shape(shape, bf16, keep) if i in (0, groups) else pltpu.HBM(shape, bf16)
            for i, shape in enumerate(shapes)
        ],
        scratch_shapes=[
            pltpu.VMEM((images, folds, lanes), f32),
            pltpu.VMEM((mate_rows, share), bf16),
            pltpu.VMEM((width, share), bf16),
            pltpu.SemaphoreType.DMA((len(sends),)),
        ]
        + [pltpu.VMEM(shape, bf16) for shape in shapes],
        compiler_params=vmem_params(mate_rows * (width + share) // 2 + arrived.size),
        cost_estimate=pl.CostEstimate(
            flops=2 * mate_rows * width * share,
            bytes_accessed=2 * mate_rows * (width + share),
            transcendentals=0,
        ),
        name="backward",
    )(
        index, near(arrived, keep), gram, hbm(final_gain[None]), pooled, hbm(w_out),
        *[near(slope, keep) for slope in slopes], *[near(turned, keep) for turned in turns],
    )


def own_columns(index, dembed, out_rows):
    images, width = dembed.shape
    keep = images <= 64

    def kernel(index_ref, dembed_ref, columns_ref):
        row = lax.broadcasted_iota(jnp.int32, (out_rows, width), 0)
        column = lax.broadcasted_iota(jnp.int32, (out_rows, width), 1)
        pick = (row + index_ref[0] * out_rows == column).astype(f32).astype(bf16)
        columns_ref[...] = contract_last(pick, dembed_ref[...]).astype(bf16)

    return pl.pallas_call(
        kernel,
        in_specs=[
            pl.BlockSpec(memory_space=pltpu.SMEM),
            pl.BlockSpec(memory_space=pltpu.VMEM),
        ],
        out_shape=near_shape((out_rows, images), bf16, keep),
        compiler_params=vmem_params(images * width),
        cost_estimate=pl.CostEstimate(
            flops=2 * images * out_rows * width,
            bytes_accessed=2 * images * width,
            transcendentals=0,
        ),
        name="own_columns",
    )(index, dembed)


def add_pair(kept, arrived):

    def kernel(kept_ref, arrived_ref, sum_ref):
        sum_ref[...] = (kept_ref[...].astype(f32) + arrived_ref[...].astype(f32)).astype(bf16)

    return pl.pallas_call(
        kernel,
        out_shape=jax.ShapeDtypeStruct(kept.shape, bf16),
        compiler_params=vmem_params(kept.size + arrived.size),
        cost_estimate=pl.CostEstimate(
            flops=kept.size, bytes_accessed=6 * kept.size, transcendentals=0
        ),
        name="add_pair",
    )(kept, arrived)


def sum_groups(index, parts, sources, pooled_at, mates, out_rows, extra):
    piece = parts[0].shape[1]
    group_rows = mates * out_rows
    pieces = len(sources)
    block = (pieces * out_rows + len(pooled_at) * extra, piece)

    def kernel(index_ref, *refs):
        part_refs, refs = refs[: len(parts)], refs[len(parts) :]
        block_refs, total_ref = refs[:-1], refs[-1]
        for j in range(pieces):
            total = 0.0
            for at, start in sources[j]:
                total += part_refs[at][start : start + group_rows].astype(f32)
            total_ref[j * group_rows : (j + 1) * group_rows] = total.astype(bf16)
        for j in range(mates):
            mate = lax.rem(index_ref[0], mates) ^ j
            for k in range(pieces):
                start = pl.multiple_of(k * group_rows + mate * out_rows, out_rows)
                block_refs[j][k * out_rows : (k + 1) * out_rows] = total_ref[
                    pl.ds(start, out_rows)
                ]
            for k, (at, first) in enumerate(pooled_at):
                start = pieces * out_rows + k * extra
                block_refs[j][start : start + extra] = part_refs[at][first : first + extra]

    return pl.pallas_call(
        kernel,
        in_specs=[pl.BlockSpec(memory_space=pltpu.SMEM)]
        + [pl.BlockSpec(memory_space=pltpu.VMEM)] * len(parts),
        out_shape=[jax.ShapeDtypeStruct(block, bf16)] * mates,
        scratch_shapes=[pltpu.VMEM((pieces * group_rows, piece), bf16)],
        compiler_params=vmem_params(sum(part.size for part in parts)),
        cost_estimate=pl.CostEstimate(
            flops=sum(part.size for part in parts),
            bytes_accessed=4 * sum(part.size for part in parts),
            transcendentals=0,
        ),
        name="sum_groups",
    )(index, *parts)


def finish(index, blocks, columns, hidden, own_images):
    mates = len(blocks)
    rows, piece = blocks[0].shape
    out_rows, images = columns.shape
    pieces = hidden // mates // piece
    in_rows = out_rows * pieces
    folds = hidden // piece
    extra = own_images * folds
    groups = (rows - in_rows) // extra

    def kernel(index_ref, *refs):
        block_refs, (columns_ref, in_ref, out_ref, wide_ref) = refs[:mates], refs[mates:]
        for j in range(mates):
            mate = lax.rem(index_ref[0], mates) ^ j
            for k in range(pieces):
                start = pl.multiple_of((mate * pieces + k) * piece, piece)
                in_ref[:, pl.ds(start, piece)] = block_refs[j][k * out_rows : (k + 1) * out_rows]
            for k in range(groups):
                sender = ((index_ref[0] // mates) ^ k) * mates + mate
                start = in_rows + k * extra
                taken = block_refs[j][start : start + extra].astype(f32)
                wide_ref[pl.ds(sender * own_images, own_images)] = taken.reshape(
                    own_images, folds, piece
                )
        pooled = jnp.concatenate([wide_ref[:, k, :].astype(bf16) for k in range(folds)], axis=1)
        out_ref[...] = jnp.dot(columns_ref[...], pooled, preferred_element_type=f32).astype(bf16)

    return pl.pallas_call(
        kernel,
        in_specs=[pl.BlockSpec(memory_space=pltpu.SMEM)]
        + [pl.BlockSpec(memory_space=pltpu.VMEM)] * (mates + 1),
        out_shape=[jax.ShapeDtypeStruct((out_rows, hidden), bf16)] * 2,
        scratch_shapes=[pltpu.VMEM((images, folds, piece), f32)],
        compiler_params=vmem_params(2 * images * folds * piece + out_rows * hidden),
        cost_estimate=pl.CostEstimate(
            flops=2 * images * out_rows * hidden,
            bytes_accessed=2 * mates * rows * piece,
            transcendentals=0,
        ),
        name="finish",
    )(index, *blocks, columns)


def exchange(blocks, axes):
    return lax.all_to_all(blocks, axes, split_axis=0, concat_axis=0, tiled=True)


def mates_of(dp_size, hidden):
    mates = 4
    while dp_size % mates or hidden % (lanes * mates):
        mates //= 2
    return mates


def swap(value, axis, step):
    return lax.ppermute(value, axis, [(i, i ^ step) for i in range(lax.axis_size(axis))])


def after(value, other):
    return lax.optimization_barrier((value, other))[0]


def body(tokens, teacher, norm_gain, w_in, b_in, w_out, b_out, final_gain):
    dp_size = lax.axis_size("dp")
    fsdp_size = lax.axis_size("fsdp")
    images = teacher.shape[0] * dp_size
    per_image = tokens.shape[0] // teacher.shape[0]
    hidden = w_in.shape[1]
    mates = mates_of(dp_size, hidden)
    index = lax.axis_index("dp").astype(jnp.int32)[None]
    first = lax.axis_index("fsdp").astype(jnp.int32)[None]

    splits = fsdp_size if teacher.shape[1] % (fsdp_size * 8 * lanes) == 0 else 1

    blocks = {0: tokens}
    for bit in (2, 4, 1):
        if bit < mates:
            blocks[bit] = swap(tokens, "dp", bit)
    all_teacher = exchange(teacher_payload(first, teacher, dp_size, splits), "dp")
    pooled, embed_rows = forward(
        first, tokens, norm_gain, w_in, b_in, w_out, b_out, dp_size * fsdp_size, teacher.shape[0]
    )
    all_embed = exchange(embed_rows, ("dp", "fsdp"))
    gram = target_gram(after(all_teacher, [pooled] + [blocks[k] for k in (1,) if k in blocks]), images)
    for k, source, bit in ((6, 4, 2), (3, 2, 1), (5, 4, 1)):
        if k < mates:
            blocks[k] = swap(after(blocks[source], gram), "dp", bit)
    near_mates = [blocks[k] for k in range(min(mates, 6))]
    slope, turned = mate_slopes(index % mates, near_mates, norm_gain, w_in, b_in, hidden // mates)
    slopes, turns = [slope], [turned]
    if mates > 6:
        blocks[7] = swap(after(blocks[6], [slope, all_embed]), "dp", 1)
        far_mates = [blocks[6], blocks[7]]
        slope, turned = mate_slopes(
            index % mates, far_mates, norm_gain, w_in, b_in, hidden // mates
        )
        slopes, turns = slopes + [slope], turns + [turned]
    if splits == 1:
        grams = [gram]
    elif splits == 2:
        grams = [gram, after(swap(gram, "fsdp", 1), slopes[-1])]
    else:
        grams = [lax.psum(gram, "fsdp")]
    groups = dp_size // mates
    share = hidden // mates
    pieces = share // min(share, 256)
    out_rows = w_out.shape[0] // dp_size
    group_rows = mates * out_rows
    half = pieces // 2
    paired = groups == 4 and half > 0
    if paired:
        sends = [
            [(0, j) for j in range(pieces)],
            [(1, j) for j in range(pieces)],
            [(2, j) for j in range(half, pieces)],
            [(3, j) for j in range(half, pieces)],
            [(2, j) for j in range(half)],
            [(3, j) for j in range(half)],
        ]
    else:
        sends = [[(k, j) for j in range(pieces)] for k in range(groups)]
    pooled_at = [(k, len(sends[k]) * group_rows) for k in range(groups)]
    loss, dembed, *parts = backward(
        index, all_embed, unit_gram(grams), final_gain, pooled, w_out, slopes, turns, sends,
        mates, dp_size, per_image,
    )
    if paired:
        pair = add_pair(parts[groups], swap(parts[groups + 1], "dp", mates))
    swapped = [parts[0]] + [
        swap(parts[k], "dp", k * mates) for k in list(range(2, groups)) + [1] if k < groups
    ]
    if groups > 1:
        swapped.insert(1, swapped.pop())
    sources = [[(0, j * group_rows), (1, j * group_rows)] for j in range(pieces)]
    if paired:
        swapped.append(swap(pair, "dp", 2 * mates))
        for j in range(pieces):
            arrays, first = ((4,), 0) if j < half else ((2, 3), half)
            sources[j] += [(k, (j - first) * group_rows) for k in arrays]
    else:
        sources = [[(k, j * group_rows) for k in range(groups)] for j in range(pieces)]
    columns = own_columns(index, dembed, out_rows)
    extra = teacher.shape[0] * hidden // parts[0].shape[1]
    shares = sum_groups(index, swapped, sources, pooled_at, mates, out_rows, extra)
    shares = [shares[0]] + [swap(part, "dp", j + 1) for j, part in enumerate(shares[1:])]
    grad_in, grad_out = finish(index, shares, columns, hidden, teacher.shape[0])
    return (loss[0, 0], grad_in, grad_out)


def solution(mesh):
    return jax.shard_map(
        body,
        mesh=mesh,
        in_specs=(
            P("dp", None),
            P("dp", None),
            P(),
            P(None, "fsdp"),
            P("fsdp"),
            P(None, "fsdp"),
            P(),
            P(),
        ),
        out_specs=(P(), P("dp", "fsdp"), P("dp", "fsdp")),
        check_vma=False,
    )
```

```python
import jax
import jax.numpy as jnp
from jax import lax
from jax.experimental import pallas as pl
from jax.experimental.pallas import tpu as pltpu
from jax.sharding import PartitionSpec as P

loss_scale = 4096.0
lanes = 128
f32 = jnp.float32
bf16 = jnp.bfloat16


def gelu_tanh(values):
    inner = 0.7978845608 * (values + 0.044715 * values * values * values)
    return 0.5 * values * (1.0 + jnp.tanh(inner))


def gelu_slope(values):
    square = values * values
    tangent = jnp.tanh(0.7978845608 * (values + 0.044715 * values * square))
    return 0.5 * (1.0 + tangent) + 0.5 * values * (1.0 - tangent * tangent) * 0.7978845608 * (
        1.0 + 3.0 * 0.044715 * square
    )


def contract_last(left_side, right_side):
    return lax.dot_general(
        left_side, right_side, (((1,), (1,)), ((), ())), preferred_element_type=f32
    )


def fold_rows(values, width):
    count = values.shape[1] // width
    return jnp.concatenate(
        [
            values[i : i + 1, k * width : (k + 1) * width]
            for i in range(values.shape[0])
            for k in range(count)
        ],
        axis=0,
    )


def vmem_params(elements):
    return pltpu.CompilerParams(vmem_limit_bytes=min(56 * 2**20, 8 * elements + 8 * 2**20))


in_hbm = pl.BlockSpec(memory_space=pltpu.HBM)
in_any = pl.BlockSpec(memory_space=pl.ANY)


def hbm(value):
    return pltpu.with_memory_space_constraint(value, pltpu.HBM)


def near(value, keep):
    return pltpu.with_memory_space_constraint(value, pltpu.VMEM) if keep else value


def near_shape(shape, dtype, keep):
    return pltpu.VMEM(shape, dtype) if keep else jax.ShapeDtypeStruct(shape, dtype)


def normalize(values, gain):
    centered = values - jnp.mean(values, axis=-1, keepdims=True)
    inv_std = lax.rsqrt(jnp.mean(centered * centered, axis=-1, keepdims=True) + 1e-05)
    return (centered * inv_std * gain).astype(bf16)


def teacher_payload(first, teacher, copies, splits):
    images = teacher.shape[0]
    features = teacher.shape[1] // splits
    fold = features // 8

    def kernel(first_ref, teacher_ref, out_ref):
        start = 0
        if splits > 1:
            start = pl.multiple_of(first_ref[0] * features, features)
        folded = fold_rows(teacher_ref[:, pl.ds(start, features)].astype(f32), fold).astype(bf16)
        out_ref[...] = jnp.broadcast_to(folded[None], out_ref.shape)

    return pl.pallas_call(
        kernel,
        in_specs=[
            pl.BlockSpec(memory_space=pltpu.SMEM),
            pl.BlockSpec(memory_space=pltpu.VMEM),
        ],
        out_shape=pltpu.HBM((copies, images * 8, fold), bf16),
        compiler_params=vmem_params(copies * images * features),
        cost_estimate=pl.CostEstimate(
            flops=copies * images * features,
            bytes_accessed=2 * copies * images * features,
            transcendentals=0,
        ),
        name="teacher_payload",
    )(first, hbm(teacher))


def forward(first, tokens, norm_gain, w_in, b_in, w_out, b_out, copies, images):
    rows, width = tokens.shape
    hidden = w_in.shape[1]
    per_image = rows // images
    tile = min(512, hidden)
    steps = hidden // tile
    folds = width // lanes

    def kernel(
        first_ref, gain_ref, bias_ref, out_b_ref, tokens_any, in_any_ref, out_any_ref,
        pooled_ref, payload_ref, tokens_ref, in_ref, out_w_ref, sems,
    ):
        loads = [
            pltpu.make_async_copy(
                in_any_ref.at[:, pl.ds(j * tile, tile)], in_ref.at[j], sems.at[j]
            )
            for j in range(steps)
        ]
        loads.append(pltpu.make_async_copy(out_any_ref, out_w_ref, sems.at[steps]))
        loads.append(pltpu.make_async_copy(tokens_any, tokens_ref, sems.at[steps + 1]))
        loads[-1].start()
        for load in loads[:-1]:
            load.start()
        loads[-1].wait()
        values = tokens_ref[...].astype(f32)
        normed = normalize(values, gain_ref[...])
        token_mean = jnp.mean(values.reshape(images, per_image, width), axis=1)
        for j in range(steps):
            taken = slice(j * tile, (j + 1) * tile)
            loads[j].wait()
            pre_act = jnp.dot(normed, in_ref[j], preferred_element_type=f32) + bias_ref[:, taken]
            pooled_ref[:, taken] = jnp.mean(
                gelu_tanh(pre_act).reshape(images, per_image, tile), axis=1
            ).astype(bf16)
        loads[steps].wait()
        total = contract_last(pooled_ref[...], out_w_ref[...])
        total += jnp.where(first_ref[0] == 0, token_mean + out_b_ref[...], 0.0)
        folded = fold_rows(total, lanes).astype(bf16)
        payload_ref[...] = jnp.broadcast_to(folded[None], payload_ref.shape)

    whole = pl.BlockSpec(memory_space=pltpu.VMEM)
    payload = (copies, images * folds, lanes)
    return pl.pallas_call(
        kernel,
        in_specs=[pl.BlockSpec(memory_space=pltpu.SMEM)] + [whole] * 3 + [in_hbm] * 3,
        out_specs=[whole, whole],
        out_shape=[
            jax.ShapeDtypeStruct((images, hidden), bf16),
            pltpu.HBM(payload, bf16),
        ],
        scratch_shapes=[
            pltpu.VMEM((rows, width), bf16),
            pltpu.VMEM((steps, width, tile), bf16),
            pltpu.VMEM((width, hidden), bf16),
            pltpu.SemaphoreType.DMA((steps + 2,)),
        ],
        compiler_params=vmem_params(
            rows * width + width * hidden + copies * images * width
        ),
        cost_estimate=pl.CostEstimate(
            flops=2 * rows * width * hidden,
            bytes_accessed=4 * width * hidden,
            transcendentals=rows * hidden,
        ),
        name="forward",
    )(
        first, hbm(norm_gain[None]), hbm(b_in[None]), hbm(b_out[None]),
        hbm(tokens), hbm(w_in), hbm(w_out),
    )


def mate_slopes(share_index, blocks, norm_gain, w_in, b_in, share):
    rows, width = blocks[0].shape
    count = len(blocks)
    keep = rows <= 512

    def kernel(index_ref, *refs):
        token_refs = refs[:count]
        gain_ref, bias_ref, in_any_ref, slope_ref, turned_ref = refs[count : count + 5]
        held_ref, in_ref, sems = refs[count + 5 :]
        first_unit = pl.multiple_of(index_ref[0] * share, share)
        weight = pltpu.make_async_copy(
            in_any_ref.at[:, pl.ds(first_unit, share)], in_ref, sems.at[count]
        )
        loads = [
            pltpu.make_async_copy(token_refs[k], held_ref.at[k], sems.at[k]) for k in range(count)
        ]
        loads[0].start()
        weight.start()
        for load in loads[1:]:
            load.start()
        for k in range(count):
            taken = slice(k * rows, (k + 1) * rows)
            loads[k].wait()
            normed = normalize(held_ref[k].astype(f32), gain_ref[...])
            if k == 0:
                weight.wait()
            pre_act = jnp.dot(normed, in_ref[...], preferred_element_type=f32) + bias_ref[...]
            slope_ref[taken] = gelu_slope(pre_act).astype(bf16)
            turned_ref[:, taken] = normed.T

    return pl.pallas_call(
        kernel,
        grid_spec=pltpu.PrefetchScalarGridSpec(
            num_scalar_prefetch=1,
            grid=(1,),
            in_specs=[in_any] * count
            + [
                pl.BlockSpec((1, width), lambda j, s: (0, 0)),
                pl.BlockSpec((1, share), lambda j, s: (0, s[0])),
                in_hbm,
            ],
            out_specs=[
                pl.BlockSpec((count * rows, share), lambda j, s: (0, 0)),
                pl.BlockSpec((width, count * rows), lambda j, s: (0, 0)),
            ],
            scratch_shapes=[
                pltpu.VMEM((count, rows, width), bf16),
                pltpu.VMEM((width, share), bf16),
                pltpu.SemaphoreType.DMA((count + 1,)),
            ],
        ),
        out_shape=[
            near_shape((count * rows, share), bf16, keep),
            near_shape((width, count * rows), bf16, keep),
        ],
        compiler_params=vmem_params(count * rows * (width + share)),
        cost_estimate=pl.CostEstimate(
            flops=2 * rows * count * width * share,
            bytes_accessed=4 * rows * count * width,
            transcendentals=rows * count * share,
        ),
        name="mate_slopes",
    )(
        share_index,
        *[hbm(block) for block in blocks],
        hbm(norm_gain[None]),
        hbm(b_in[None]),
        hbm(w_in),
    )


def target_gram(arrived, images):
    senders, folded, fold = arrived.shape
    folds = senders * folded // images
    keep = images <= 64

    def kernel(arrived_ref, gram_ref, wide_ref):
        wide_ref[...] = arrived_ref[...].astype(f32).reshape(images, folds, fold)
        rows = jnp.concatenate([wide_ref[:, k, :].astype(bf16) for k in range(folds)], axis=1)
        gram_ref[...] = contract_last(rows, rows)

    return pl.pallas_call(
        kernel,
        out_shape=jax.ShapeDtypeStruct((images, images), f32),
        scratch_shapes=[pltpu.VMEM((images, folds, fold), f32)],
        compiler_params=vmem_params(images * folds * fold),
        cost_estimate=pl.CostEstimate(
            flops=2 * images * images * folds * fold,
            bytes_accessed=2 * images * folds * fold,
            transcendentals=0,
        ),
        name="target_gram",
    )(near(arrived, keep))


def unit_gram(parts):
    images = parts[0].shape[0]

    def kernel(*refs):
        gram_ref = refs[-1]
        gram = sum((ref[...] for ref in refs[1:-1]), refs[0][...])
        row = lax.broadcasted_iota(jnp.int32, gram.shape, 0)
        column = lax.broadcasted_iota(jnp.int32, gram.shape, 1)
        diagonal = jnp.where(row == column, gram, 0.0)
        down = lax.rsqrt(jnp.sum(diagonal, axis=1, keepdims=True) + 1e-06)
        across = lax.rsqrt(jnp.sum(diagonal, axis=0, keepdims=True) + 1e-06)
        gram_ref[...] = gram * down * across

    return pl.pallas_call(
        kernel,
        out_shape=jax.ShapeDtypeStruct((images, images), f32),
        compiler_params=vmem_params(4 * images * images),
        cost_estimate=pl.CostEstimate(
            flops=8 * images * images, bytes_accessed=8 * images * images, transcendentals=0
        ),
        name="unit_gram",
    )(*parts)


def backward(
    index, arrived, gram, final_gain, pooled, w_out, slopes, turns, sends, mates, dp_size, per_image
):
    senders, folded, _ = arrived.shape
    width = w_out.shape[0]
    images = gram.shape[0]
    own_images, hidden = pooled.shape
    fsdp_size = senders // dp_size
    folds = width // lanes
    share = hidden // mates
    parts = len(turns)
    part_rows = [turned.shape[1] for turned in turns]
    mate_rows = sum(part_rows)
    out_rows = width // dp_size
    piece = min(share, 256)
    pieces = share // piece
    extra = own_images * hidden // piece
    groups = dp_size // mates
    group_rows = mates * out_rows
    shapes = [
        (len(send) * group_rows + (extra if i < groups else 0), piece)
        for i, send in enumerate(sends)
    ]
    keep = images <= 64

    def kernel(index_ref, arrived_ref, gram_ref, gain_ref, pooled_ref, out_w_any, *refs):
        slope_refs, turned_refs, refs = refs[:parts], refs[parts : 2 * parts], refs[2 * parts :]
        loss_ref, dembed_ref, refs = refs[0], refs[1], refs[2:]
        part_refs, refs = refs[: len(sends)], refs[len(sends) :]
        wide_ref, hidden_ref, out_w_ref, sems = refs[:4]
        payload_refs = refs[4:]
        first_unit = pl.multiple_of(lax.rem(index_ref[0], mates) * share, share)
        load = pltpu.make_async_copy(
            out_w_any.at[:, pl.ds(first_unit, share)], out_w_ref, sems.at[0]
        )
        load.start()
        embeds = arrived_ref[...].astype(f32).reshape(dp_size, fsdp_size, folded, lanes)
        wide_ref[...] = jnp.sum(embeds, axis=1).reshape(images, folds, lanes)
        embedding = jnp.concatenate([wide_ref[:, k, :] for k in range(folds)], axis=1)
        gain = gain_ref[...]
        centered = embedding - jnp.mean(embedding, axis=-1, keepdims=True)
        inv_std = lax.rsqrt(jnp.mean(centered * centered, axis=-1, keepdims=True) + 1e-05)
        normed = centered * inv_std
        scaled = normed * gain
        square = jnp.sum(scaled * scaled, axis=-1, keepdims=True) + 1e-06
        inv_norm = lax.rsqrt(square)
        unit = scaled * inv_norm
        student = unit.astype(bf16)
        resid = contract_last(student, student) - gram_ref[...]
        loss_ref[0, 0] = jnp.sum(resid * resid) / images
        dstudent = (loss_scale * 4.0 / images) * jnp.dot(
            resid.astype(bf16), student, preferred_element_type=f32
        )
        dunit = (dstudent - unit * jnp.sum(unit * dstudent, axis=-1, keepdims=True)) * inv_norm
        gain_grad = dunit * gain
        dembed = inv_std * (
            gain_grad
            - jnp.mean(gain_grad, axis=-1, keepdims=True)
            - normed * jnp.mean(gain_grad * normed, axis=-1, keepdims=True)
        )
        dembed_b = dembed.astype(bf16)
        dembed_ref[...] = dembed_b
        shape = (mates * own_images, images)
        row = lax.broadcasted_iota(jnp.int32, shape, 0)
        column = lax.broadcasted_iota(jnp.int32, shape, 1)
        owner = (row // own_images) ^ index_ref[0]
        pick = (owner * own_images + row % own_images == column).astype(f32).astype(bf16)
        mate_dembed = jnp.dot(pick, dembed_b, preferred_element_type=f32).astype(bf16)
        load.wait()
        dpooled = jnp.dot(mate_dembed, out_w_ref[...], preferred_element_type=f32) / per_image
        k = 0
        for part in range(parts):
            for j in range(part_rows[part] // per_image):
                rows = slice(k * per_image, (k + 1) * per_image)
                taken = slice(j * per_image, (j + 1) * per_image)
                hidden_ref[rows] = (
                    dpooled[k : k + 1] * slope_refs[part][taken].astype(f32)
                ).astype(bf16)
                k += 1
        folded_pooled = fold_rows(pooled_ref[...].astype(f32), piece).astype(bf16)
        stores = []
        for k in list(range(1, groups))[::-1] + [0]:
            first_row = pl.multiple_of(
                ((index_ref[0] // mates) ^ k) * group_rows, group_rows
            )
            term, start = 0.0, 0
            for part in range(parts):
                rows = slice(start, start + part_rows[part])
                start += part_rows[part]
                term += jnp.dot(
                    turned_refs[part][pl.ds(first_row, group_rows)],
                    hidden_ref[rows],
                    preferred_element_type=f32,
                )
            term = term.astype(bf16)
            for i, send in enumerate(sends):
                for at, (group, j) in enumerate(send):
                    if group == k:
                        payload_refs[i][at * group_rows : (at + 1) * group_rows] = term[
                            :, j * piece : (j + 1) * piece
                        ]
        for i, send in enumerate(sends):
            if i < groups:
                payload_refs[i][len(send) * group_rows :] = folded_pooled
            stores.append(pltpu.make_async_copy(payload_refs[i], part_refs[i], sems.at[i]))
            stores[-1].start()
        for store in stores:
            store.wait()

    whole = pl.BlockSpec(memory_space=pltpu.VMEM)
    smem = pl.BlockSpec(memory_space=pltpu.SMEM)
    return pl.pallas_call(
        kernel,
        in_specs=[smem, whole, whole, whole, whole, in_hbm] + [whole] * (2 * parts),
        out_specs=[smem, whole] + [in_any] * len(sends),
        out_shape=[
            jax.ShapeDtypeStruct((1, 1), f32),
            jax.ShapeDtypeStruct((images, width), bf16),
        ]
        + [
            near_shape(shape, bf16, keep) if i in (0, groups) else pltpu.HBM(shape, bf16)
            for i, shape in enumerate(shapes)
        ],
        scratch_shapes=[
            pltpu.VMEM((images, folds, lanes), f32),
            pltpu.VMEM((mate_rows, share), bf16),
            pltpu.VMEM((width, share), bf16),
            pltpu.SemaphoreType.DMA((len(sends),)),
        ]
        + [pltpu.VMEM(shape, bf16) for shape in shapes],
        compiler_params=vmem_params(mate_rows * (width + share) // 2 + arrived.size),
        cost_estimate=pl.CostEstimate(
            flops=2 * mate_rows * width * share,
            bytes_accessed=2 * mate_rows * (width + share),
            transcendentals=0,
        ),
        name="backward",
    )(
        index, near(arrived, keep), gram, hbm(final_gain[None]), pooled, hbm(w_out),
        *[near(slope, keep) for slope in slopes], *[near(turned, keep) for turned in turns],
    )


def own_columns(index, dembed, out_rows):
    images, width = dembed.shape
    keep = images <= 64

    def kernel(index_ref, dembed_ref, columns_ref):
        row = lax.broadcasted_iota(jnp.int32, (out_rows, width), 0)
        column = lax.broadcasted_iota(jnp.int32, (out_rows, width), 1)
        pick = (row + index_ref[0] * out_rows == column).astype(f32).astype(bf16)
        columns_ref[...] = contract_last(pick, dembed_ref[...]).astype(bf16)

    return pl.pallas_call(
        kernel,
        in_specs=[
            pl.BlockSpec(memory_space=pltpu.SMEM),
            pl.BlockSpec(memory_space=pltpu.VMEM),
        ],
        out_shape=near_shape((out_rows, images), bf16, keep),
        compiler_params=vmem_params(images * width),
        cost_estimate=pl.CostEstimate(
            flops=2 * images * out_rows * width,
            bytes_accessed=2 * images * width,
            transcendentals=0,
        ),
        name="own_columns",
    )(index, dembed)


def add_pair(kept, arrived):

    def kernel(kept_ref, arrived_ref, sum_ref):
        sum_ref[...] = (kept_ref[...].astype(f32) + arrived_ref[...].astype(f32)).astype(bf16)

    return pl.pallas_call(
        kernel,
        out_shape=jax.ShapeDtypeStruct(kept.shape, bf16),
        compiler_params=vmem_params(kept.size + arrived.size),
        cost_estimate=pl.CostEstimate(
            flops=kept.size, bytes_accessed=6 * kept.size, transcendentals=0
        ),
        name="add_pair",
    )(kept, arrived)


def sum_groups(index, parts, sources, pooled_at, mates, out_rows, extra):
    piece = parts[0].shape[1]
    group_rows = mates * out_rows
    pieces = len(sources)
    block = (pieces * out_rows + len(pooled_at) * extra, piece)

    def kernel(index_ref, *refs):
        part_refs, refs = refs[: len(parts)], refs[len(parts) :]
        block_refs, total_ref = refs[:-1], refs[-1]
        for j in range(pieces):
            total = 0.0
            for at, start in sources[j]:
                total += part_refs[at][start : start + group_rows].astype(f32)
            total_ref[j * group_rows : (j + 1) * group_rows] = total.astype(bf16)
        for j in range(mates):
            mate = lax.rem(index_ref[0], mates) ^ j
            for k in range(pieces):
                start = pl.multiple_of(k * group_rows + mate * out_rows, out_rows)
                block_refs[j][k * out_rows : (k + 1) * out_rows] = total_ref[
                    pl.ds(start, out_rows)
                ]
            for k, (at, first) in enumerate(pooled_at):
                start = pieces * out_rows + k * extra
                block_refs[j][start : start + extra] = part_refs[at][first : first + extra]

    return pl.pallas_call(
        kernel,
        in_specs=[pl.BlockSpec(memory_space=pltpu.SMEM)]
        + [pl.BlockSpec(memory_space=pltpu.VMEM)] * len(parts),
        out_shape=[jax.ShapeDtypeStruct(block, bf16)] * mates,
        scratch_shapes=[pltpu.VMEM((pieces * group_rows, piece), bf16)],
        compiler_params=vmem_params(sum(part.size for part in parts)),
        cost_estimate=pl.CostEstimate(
            flops=sum(part.size for part in parts),
            bytes_accessed=4 * sum(part.size for part in parts),
            transcendentals=0,
        ),
        name="sum_groups",
    )(index, *parts)


def finish(index, blocks, columns, hidden, own_images):
    mates = len(blocks)
    rows, piece = blocks[0].shape
    out_rows, images = columns.shape
    pieces = hidden // mates // piece
    in_rows = out_rows * pieces
    folds = hidden // piece
    extra = own_images * folds
    groups = (rows - in_rows) // extra

    def kernel(index_ref, *refs):
        block_refs, (columns_ref, in_ref, out_ref, wide_ref) = refs[:mates], refs[mates:]
        for j in range(mates):
            mate = lax.rem(index_ref[0], mates) ^ j
            for k in range(pieces):
                start = pl.multiple_of((mate * pieces + k) * piece, piece)
                in_ref[:, pl.ds(start, piece)] = block_refs[j][k * out_rows : (k + 1) * out_rows]
            for k in range(groups):
                sender = ((index_ref[0] // mates) ^ k) * mates + mate
                start = in_rows + k * extra
                taken = block_refs[j][start : start + extra].astype(f32)
                wide_ref[pl.ds(sender * own_images, own_images)] = taken.reshape(
                    own_images, folds, piece
                )
        pooled = jnp.concatenate([wide_ref[:, k, :].astype(bf16) for k in range(folds)], axis=1)
        out_ref[...] = jnp.dot(columns_ref[...], pooled, preferred_element_type=f32).astype(bf16)

    return pl.pallas_call(
        kernel,
        in_specs=[pl.BlockSpec(memory_space=pltpu.SMEM)]
        + [pl.BlockSpec(memory_space=pltpu.VMEM)] * (mates + 1),
        out_shape=[jax.ShapeDtypeStruct((out_rows, hidden), bf16)] * 2,
        scratch_shapes=[pltpu.VMEM((images, folds, piece), f32)],
        compiler_params=vmem_params(2 * images * folds * piece + out_rows * hidden),
        cost_estimate=pl.CostEstimate(
            flops=2 * images * out_rows * hidden,
            bytes_accessed=2 * mates * rows * piece,
            transcendentals=0,
        ),
        name="finish",
    )(index, *blocks, columns)


def exchange(blocks, axes):
    return lax.all_to_all(blocks, axes, split_axis=0, concat_axis=0, tiled=True)


def mates_of(dp_size, hidden):
    mates = 4
    while dp_size % mates or hidden % (lanes * mates):
        mates //= 2
    return mates


def swap(value, axis, step):
    return lax.ppermute(value, axis, [(i, i ^ step) for i in range(lax.axis_size(axis))])


def after(value, other):
    return lax.optimization_barrier((value, other))[0]


def body(tokens, teacher, norm_gain, w_in, b_in, w_out, b_out, final_gain):
    dp_size = lax.axis_size("dp")
    fsdp_size = lax.axis_size("fsdp")
    images = teacher.shape[0] * dp_size
    per_image = tokens.shape[0] // teacher.shape[0]
    hidden = w_in.shape[1]
    mates = mates_of(dp_size, hidden)
    index = lax.axis_index("dp").astype(jnp.int32)[None]
    first = lax.axis_index("fsdp").astype(jnp.int32)[None]

    splits = fsdp_size if teacher.shape[1] % (fsdp_size * 8 * lanes) == 0 else 1

    blocks = {0: tokens}
    for bit in (2, 4, 1):
        if bit < mates:
            blocks[bit] = swap(tokens, "dp", bit)
    all_teacher = exchange(teacher_payload(first, teacher, dp_size, splits), "dp")
    pooled, embed_rows = forward(
        first, tokens, norm_gain, w_in, b_in, w_out, b_out, dp_size * fsdp_size, teacher.shape[0]
    )
    all_embed = exchange(embed_rows, ("dp", "fsdp"))
    gram = target_gram(after(all_teacher, [pooled] + [blocks[k] for k in (1,) if k in blocks]), images)
    for k, source, bit in ((6, 4, 2), (3, 2, 1), (5, 4, 1)):
        if k < mates:
            blocks[k] = swap(after(blocks[source], gram), "dp", bit)
    near_mates = [blocks[k] for k in range(min(mates, 6))]
    slope, turned = mate_slopes(index % mates, near_mates, norm_gain, w_in, b_in, hidden // mates)
    slopes, turns = [slope], [turned]
    if mates > 6:
        blocks[7] = swap(after(blocks[6], [slope, all_embed]), "dp", 1)
        far_mates = [blocks[6], blocks[7]]
        slope, turned = mate_slopes(
            index % mates, far_mates, norm_gain, w_in, b_in, hidden // mates
        )
        slopes, turns = slopes + [slope], turns + [turned]
    if splits == 1:
        grams = [gram]
    elif splits == 2:
        grams = [gram, after(swap(gram, "fsdp", 1), slopes[-1])]
    else:
        grams = [lax.psum(gram, "fsdp")]
    groups = dp_size // mates
    share = hidden // mates
    pieces = share // min(share, 256)
    out_rows = w_out.shape[0] // dp_size
    group_rows = mates * out_rows
    half = pieces // 2
    paired = groups == 4 and half > 0
    if paired:
        sends = [
            [(0, j) for j in range(pieces)],
            [(1, j) for j in range(half)],
            [(2, j) for j in range(half, pieces)],
            [(3, j) for j in range(half, pieces)],
            [(2, j) for j in range(half)],
            [(3, j) for j in range(half)],
            [(1, j) for j in range(half, pieces)],
        ]
    else:
        sends = [[(k, j) for j in range(pieces)] for k in range(groups)]
    pooled_at = [(k, len(sends[k]) * group_rows) for k in range(groups)]
    loss, dembed, *parts = backward(
        index, all_embed, unit_gram(grams), final_gain, pooled, w_out, slopes, turns, sends,
        mates, dp_size, per_image,
    )
    if paired:
        pair = add_pair(parts[groups], swap(parts[groups + 1], "dp", mates))
    swapped = [parts[0]] + [
        swap(parts[k], "dp", k * mates) for k in list(range(2, groups)) + [1] if k < groups
    ]
    if groups > 1:
        swapped.insert(1, swapped.pop())
    if paired:
        swapped.append(swap(pair, "dp", 2 * mates))
        swapped.append(swap(parts[groups + 2], "dp", mates))
        sources = []
        for j in range(pieces):
            arrays, first = ((1, 4), 0) if j < half else ((5, 2, 3), half)
            sources.append(
                [(0, j * group_rows)] + [(k, (j - first) * group_rows) for k in arrays]
            )
    else:
        sources = [[(k, j * group_rows) for k in range(groups)] for j in range(pieces)]
    columns = own_columns(index, dembed, out_rows)
    extra = teacher.shape[0] * hidden // parts[0].shape[1]
    shares = sum_groups(index, swapped, sources, pooled_at, mates, out_rows, extra)
    shares = [shares[0]] + [swap(part, "dp", j + 1) for j, part in enumerate(shares[1:])]
    grad_in, grad_out = finish(index, shares, columns, hidden, teacher.shape[0])
    return (loss[0, 0], grad_in, grad_out)


def solution(mesh):
    return jax.shard_map(
        body,
        mesh=mesh,
        in_specs=(
            P("dp", None),
            P("dp", None),
            P(),
            P(None, "fsdp"),
            P("fsdp"),
            P(None, "fsdp"),
            P(),
            P(),
        ),
        out_specs=(P(), P("dp", "fsdp"), P("dp", "fsdp")),
        check_vma=False,
    )
```

```python
import jax
import jax.numpy as jnp
from jax import lax
from jax.experimental import pallas as pl
from jax.experimental.pallas import tpu as pltpu
from jax.sharding import PartitionSpec as P

loss_scale = 4096.0
lanes = 128
f32 = jnp.float32
bf16 = jnp.bfloat16


def gelu_tanh(values):
    inner = 0.7978845608 * (values + 0.044715 * values * values * values)
    return 0.5 * values * (1.0 + jnp.tanh(inner))


def gelu_slope(values):
    square = values * values
    tangent = jnp.tanh(0.7978845608 * (values + 0.044715 * values * square))
    return 0.5 * (1.0 + tangent) + 0.5 * values * (1.0 - tangent * tangent) * 0.7978845608 * (
        1.0 + 3.0 * 0.044715 * square
    )


def contract_last(left_side, right_side):
    return lax.dot_general(
        left_side, right_side, (((1,), (1,)), ((), ())), preferred_element_type=f32
    )


def fold_rows(values, width):
    count = values.shape[1] // width
    return jnp.concatenate(
        [
            values[i : i + 1, k * width : (k + 1) * width]
            for i in range(values.shape[0])
            for k in range(count)
        ],
        axis=0,
    )


def vmem_params(elements):
    return pltpu.CompilerParams(vmem_limit_bytes=min(56 * 2**20, 8 * elements + 8 * 2**20))


in_hbm = pl.BlockSpec(memory_space=pltpu.HBM)
in_any = pl.BlockSpec(memory_space=pl.ANY)


def hbm(value):
    return pltpu.with_memory_space_constraint(value, pltpu.HBM)


def near(value, keep):
    return pltpu.with_memory_space_constraint(value, pltpu.VMEM) if keep else value


def near_shape(shape, dtype, keep):
    return pltpu.VMEM(shape, dtype) if keep else jax.ShapeDtypeStruct(shape, dtype)


def normalize(values, gain):
    centered = values - jnp.mean(values, axis=-1, keepdims=True)
    inv_std = lax.rsqrt(jnp.mean(centered * centered, axis=-1, keepdims=True) + 1e-05)
    return (centered * inv_std * gain).astype(bf16)


def teacher_payload(first, teacher, copies, splits):
    images = teacher.shape[0]
    features = teacher.shape[1] // splits
    fold = features // 8

    def kernel(first_ref, teacher_ref, out_ref):
        start = 0
        if splits > 1:
            start = pl.multiple_of(first_ref[0] * features, features)
        folded = fold_rows(teacher_ref[:, pl.ds(start, features)].astype(f32), fold).astype(bf16)
        out_ref[...] = jnp.broadcast_to(folded[None], out_ref.shape)

    return pl.pallas_call(
        kernel,
        in_specs=[
            pl.BlockSpec(memory_space=pltpu.SMEM),
            pl.BlockSpec(memory_space=pltpu.VMEM),
        ],
        out_shape=pltpu.HBM((copies, images * 8, fold), bf16),
        compiler_params=vmem_params(copies * images * features),
        cost_estimate=pl.CostEstimate(
            flops=copies * images * features,
            bytes_accessed=2 * copies * images * features,
            transcendentals=0,
        ),
        name="teacher_payload",
    )(first, hbm(teacher))


def forward(first, tokens, norm_gain, w_in, b_in, w_out, b_out, copies, images):
    rows, width = tokens.shape
    hidden = w_in.shape[1]
    per_image = rows // images
    tile = min(512, hidden)
    steps = hidden // tile
    folds = width // lanes

    def kernel(
        first_ref, gain_ref, bias_ref, out_b_ref, tokens_any, in_any_ref, out_any_ref,
        pooled_ref, payload_ref, tokens_ref, in_ref, out_w_ref, sems,
    ):
        loads = [
            pltpu.make_async_copy(
                in_any_ref.at[:, pl.ds(j * tile, tile)], in_ref.at[j], sems.at[j]
            )
            for j in range(steps)
        ]
        loads.append(pltpu.make_async_copy(out_any_ref, out_w_ref, sems.at[steps]))
        loads.append(pltpu.make_async_copy(tokens_any, tokens_ref, sems.at[steps + 1]))
        loads[-1].start()
        for load in loads[:-1]:
            load.start()
        loads[-1].wait()
        values = tokens_ref[...].astype(f32)
        normed = normalize(values, gain_ref[...])
        token_mean = jnp.mean(values.reshape(images, per_image, width), axis=1)
        for j in range(steps):
            taken = slice(j * tile, (j + 1) * tile)
            loads[j].wait()
            pre_act = jnp.dot(normed, in_ref[j], preferred_element_type=f32) + bias_ref[:, taken]
            pooled_ref[:, taken] = jnp.mean(
                gelu_tanh(pre_act).reshape(images, per_image, tile), axis=1
            ).astype(bf16)
        loads[steps].wait()
        total = contract_last(pooled_ref[...], out_w_ref[...])
        total += jnp.where(first_ref[0] == 0, token_mean + out_b_ref[...], 0.0)
        folded = fold_rows(total, lanes).astype(bf16)
        payload_ref[...] = jnp.broadcast_to(folded[None], payload_ref.shape)

    whole = pl.BlockSpec(memory_space=pltpu.VMEM)
    payload = (copies, images * folds, lanes)
    return pl.pallas_call(
        kernel,
        in_specs=[pl.BlockSpec(memory_space=pltpu.SMEM)] + [whole] * 3 + [in_hbm] * 3,
        out_specs=[whole, whole],
        out_shape=[
            jax.ShapeDtypeStruct((images, hidden), bf16),
            pltpu.HBM(payload, bf16),
        ],
        scratch_shapes=[
            pltpu.VMEM((rows, width), bf16),
            pltpu.VMEM((steps, width, tile), bf16),
            pltpu.VMEM((width, hidden), bf16),
            pltpu.SemaphoreType.DMA((steps + 2,)),
        ],
        compiler_params=vmem_params(
            rows * width + width * hidden + copies * images * width
        ),
        cost_estimate=pl.CostEstimate(
            flops=2 * rows * width * hidden,
            bytes_accessed=4 * width * hidden,
            transcendentals=rows * hidden,
        ),
        name="forward",
    )(
        first, hbm(norm_gain[None]), hbm(b_in[None]), hbm(b_out[None]),
        hbm(tokens), hbm(w_in), hbm(w_out),
    )


def mate_slopes(share_index, blocks, norm_gain, w_in, b_in, share):
    rows, width = blocks[0].shape
    count = len(blocks)
    keep = rows <= 512

    def kernel(index_ref, *refs):
        token_refs = refs[:count]
        gain_ref, bias_ref, in_any_ref, slope_ref, turned_ref = refs[count : count + 5]
        held_ref, in_ref, sems = refs[count + 5 :]
        first_unit = pl.multiple_of(index_ref[0] * share, share)
        weight = pltpu.make_async_copy(
            in_any_ref.at[:, pl.ds(first_unit, share)], in_ref, sems.at[count]
        )
        loads = [
            pltpu.make_async_copy(token_refs[k], held_ref.at[k], sems.at[k]) for k in range(count)
        ]
        loads[0].start()
        weight.start()
        for load in loads[1:]:
            load.start()
        for k in range(count):
            taken = slice(k * rows, (k + 1) * rows)
            loads[k].wait()
            normed = normalize(held_ref[k].astype(f32), gain_ref[...])
            if k == 0:
                weight.wait()
            pre_act = jnp.dot(normed, in_ref[...], preferred_element_type=f32) + bias_ref[...]
            slope_ref[taken] = gelu_slope(pre_act).astype(bf16)
            turned_ref[:, taken] = normed.T

    return pl.pallas_call(
        kernel,
        grid_spec=pltpu.PrefetchScalarGridSpec(
            num_scalar_prefetch=1,
            grid=(1,),
            in_specs=[in_any] * count
            + [
                pl.BlockSpec((1, width), lambda j, s: (0, 0)),
                pl.BlockSpec((1, share), lambda j, s: (0, s[0])),
                in_hbm,
            ],
            out_specs=[
                pl.BlockSpec((count * rows, share), lambda j, s: (0, 0)),
                pl.BlockSpec((width, count * rows), lambda j, s: (0, 0)),
            ],
            scratch_shapes=[
                pltpu.VMEM((count, rows, width), bf16),
                pltpu.VMEM((width, share), bf16),
                pltpu.SemaphoreType.DMA((count + 1,)),
            ],
        ),
        out_shape=[
            near_shape((count * rows, share), bf16, keep),
            near_shape((width, count * rows), bf16, keep),
        ],
        compiler_params=vmem_params(count * rows * (width + share)),
        cost_estimate=pl.CostEstimate(
            flops=2 * rows * count * width * share,
            bytes_accessed=4 * rows * count * width,
            transcendentals=rows * count * share,
        ),
        name="mate_slopes",
    )(
        share_index,
        *[hbm(block) for block in blocks],
        hbm(norm_gain[None]),
        hbm(b_in[None]),
        hbm(w_in),
    )


def target_gram(arrived, images):
    senders, folded, fold = arrived.shape
    folds = senders * folded // images
    keep = images <= 64

    def kernel(arrived_ref, gram_ref, wide_ref):
        wide_ref[...] = arrived_ref[...].astype(f32).reshape(images, folds, fold)
        rows = jnp.concatenate([wide_ref[:, k, :].astype(bf16) for k in range(folds)], axis=1)
        gram_ref[...] = contract_last(rows, rows)

    return pl.pallas_call(
        kernel,
        out_shape=jax.ShapeDtypeStruct((images, images), f32),
        scratch_shapes=[pltpu.VMEM((images, folds, fold), f32)],
        compiler_params=vmem_params(images * folds * fold),
        cost_estimate=pl.CostEstimate(
            flops=2 * images * images * folds * fold,
            bytes_accessed=2 * images * folds * fold,
            transcendentals=0,
        ),
        name="target_gram",
    )(near(arrived, keep))


def unit_gram(parts):
    images = parts[0].shape[0]

    def kernel(*refs):
        gram_ref = refs[-1]
        gram = sum((ref[...] for ref in refs[1:-1]), refs[0][...])
        row = lax.broadcasted_iota(jnp.int32, gram.shape, 0)
        column = lax.broadcasted_iota(jnp.int32, gram.shape, 1)
        diagonal = jnp.where(row == column, gram, 0.0)
        down = lax.rsqrt(jnp.sum(diagonal, axis=1, keepdims=True) + 1e-06)
        across = lax.rsqrt(jnp.sum(diagonal, axis=0, keepdims=True) + 1e-06)
        gram_ref[...] = gram * down * across

    return pl.pallas_call(
        kernel,
        out_shape=jax.ShapeDtypeStruct((images, images), f32),
        compiler_params=vmem_params(4 * images * images),
        cost_estimate=pl.CostEstimate(
            flops=8 * images * images, bytes_accessed=8 * images * images, transcendentals=0
        ),
        name="unit_gram",
    )(*parts)


def backward(
    index, arrived, gram, final_gain, pooled, w_out, slopes, turns, sends, mates, dp_size, per_image
):
    senders, folded, _ = arrived.shape
    width = w_out.shape[0]
    images = gram.shape[0]
    own_images, hidden = pooled.shape
    fsdp_size = senders // dp_size
    folds = width // lanes
    share = hidden // mates
    parts = len(turns)
    part_rows = [turned.shape[1] for turned in turns]
    mate_rows = sum(part_rows)
    out_rows = width // dp_size
    piece = min(share, 256)
    pieces = share // piece
    extra = own_images * hidden // piece
    groups = dp_size // mates
    group_rows = mates * out_rows
    shapes = [
        (len(send) * group_rows + (extra if i < groups else 0), piece)
        for i, send in enumerate(sends)
    ]
    keep = images <= 64

    def kernel(index_ref, arrived_ref, gram_ref, gain_ref, pooled_ref, out_w_any, *refs):
        slope_refs, turned_refs, refs = refs[:parts], refs[parts : 2 * parts], refs[2 * parts :]
        loss_ref, dembed_ref, refs = refs[0], refs[1], refs[2:]
        part_refs, refs = refs[: len(sends)], refs[len(sends) :]
        wide_ref, hidden_ref, out_w_ref, sems = refs[:4]
        payload_refs = refs[4:]
        first_unit = pl.multiple_of(lax.rem(index_ref[0], mates) * share, share)
        load = pltpu.make_async_copy(
            out_w_any.at[:, pl.ds(first_unit, share)], out_w_ref, sems.at[0]
        )
        load.start()
        embeds = arrived_ref[...].astype(f32).reshape(dp_size, fsdp_size, folded, lanes)
        wide_ref[...] = jnp.sum(embeds, axis=1).reshape(images, folds, lanes)
        embedding = jnp.concatenate([wide_ref[:, k, :] for k in range(folds)], axis=1)
        gain = gain_ref[...]
        centered = embedding - jnp.mean(embedding, axis=-1, keepdims=True)
        inv_std = lax.rsqrt(jnp.mean(centered * centered, axis=-1, keepdims=True) + 1e-05)
        normed = centered * inv_std
        scaled = normed * gain
        square = jnp.sum(scaled * scaled, axis=-1, keepdims=True) + 1e-06
        inv_norm = lax.rsqrt(square)
        unit = scaled * inv_norm
        student = unit.astype(bf16)
        resid = contract_last(student, student) - gram_ref[...]
        loss_ref[0, 0] = jnp.sum(resid * resid) / images
        dstudent = (loss_scale * 4.0 / images) * jnp.dot(
            resid.astype(bf16), student, preferred_element_type=f32
        )
        dunit = (dstudent - unit * jnp.sum(unit * dstudent, axis=-1, keepdims=True)) * inv_norm
        gain_grad = dunit * gain
        dembed = inv_std * (
            gain_grad
            - jnp.mean(gain_grad, axis=-1, keepdims=True)
            - normed * jnp.mean(gain_grad * normed, axis=-1, keepdims=True)
        )
        dembed_b = dembed.astype(bf16)
        dembed_ref[...] = dembed_b
        shape = (mates * own_images, images)
        row = lax.broadcasted_iota(jnp.int32, shape, 0)
        column = lax.broadcasted_iota(jnp.int32, shape, 1)
        owner = (row // own_images) ^ index_ref[0]
        pick = (owner * own_images + row % own_images == column).astype(f32).astype(bf16)
        mate_dembed = jnp.dot(pick, dembed_b, preferred_element_type=f32).astype(bf16)
        load.wait()
        dpooled = jnp.dot(mate_dembed, out_w_ref[...], preferred_element_type=f32) / per_image
        k = 0
        for part in range(parts):
            for j in range(part_rows[part] // per_image):
                rows = slice(k * per_image, (k + 1) * per_image)
                taken = slice(j * per_image, (j + 1) * per_image)
                hidden_ref[rows] = (
                    dpooled[k : k + 1] * slope_refs[part][taken].astype(f32)
                ).astype(bf16)
                k += 1
        folded_pooled = fold_rows(pooled_ref[...].astype(f32), piece).astype(bf16)
        stores = []
        for k in list(range(1, groups))[::-1] + [0]:
            first_row = pl.multiple_of(
                ((index_ref[0] // mates) ^ k) * group_rows, group_rows
            )
            term, start = 0.0, 0
            for part in range(parts):
                rows = slice(start, start + part_rows[part])
                start += part_rows[part]
                term += jnp.dot(
                    turned_refs[part][pl.ds(first_row, group_rows)],
                    hidden_ref[rows],
                    preferred_element_type=f32,
                )
            term = term.astype(bf16)
            for i, send in enumerate(sends):
                for at, (group, j) in enumerate(send):
                    if group == k:
                        payload_refs[i][at * group_rows : (at + 1) * group_rows] = term[
                            :, j * piece : (j + 1) * piece
                        ]
        for i, send in enumerate(sends):
            if i < groups:
                payload_refs[i][len(send) * group_rows :] = folded_pooled
            stores.append(pltpu.make_async_copy(payload_refs[i], part_refs[i], sems.at[i]))
            stores[-1].start()
        for store in stores:
            store.wait()

    whole = pl.BlockSpec(memory_space=pltpu.VMEM)
    smem = pl.BlockSpec(memory_space=pltpu.SMEM)
    return pl.pallas_call(
        kernel,
        in_specs=[smem, whole, whole, whole, whole, in_hbm] + [whole] * (2 * parts),
        out_specs=[smem, whole] + [in_any] * len(sends),
        out_shape=[
            jax.ShapeDtypeStruct((1, 1), f32),
            jax.ShapeDtypeStruct((images, width), bf16),
        ]
        + [
            near_shape(shape, bf16, keep) if i in (0, groups) else pltpu.HBM(shape, bf16)
            for i, shape in enumerate(shapes)
        ],
        scratch_shapes=[
            pltpu.VMEM((images, folds, lanes), f32),
            pltpu.VMEM((mate_rows, share), bf16),
            pltpu.VMEM((width, share), bf16),
            pltpu.SemaphoreType.DMA((len(sends),)),
        ]
        + [pltpu.VMEM(shape, bf16) for shape in shapes],
        compiler_params=vmem_params(mate_rows * (width + share) // 2 + arrived.size),
        cost_estimate=pl.CostEstimate(
            flops=2 * mate_rows * width * share,
            bytes_accessed=2 * mate_rows * (width + share),
            transcendentals=0,
        ),
        name="backward",
    )(
        index, near(arrived, keep), gram, hbm(final_gain[None]), pooled, hbm(w_out),
        *[near(slope, keep) for slope in slopes], *[near(turned, keep) for turned in turns],
    )


def own_columns(index, dembed, out_rows):
    images, width = dembed.shape
    keep = images <= 64

    def kernel(index_ref, dembed_ref, columns_ref):
        row = lax.broadcasted_iota(jnp.int32, (out_rows, width), 0)
        column = lax.broadcasted_iota(jnp.int32, (out_rows, width), 1)
        pick = (row + index_ref[0] * out_rows == column).astype(f32).astype(bf16)
        columns_ref[...] = contract_last(pick, dembed_ref[...]).astype(bf16)

    return pl.pallas_call(
        kernel,
        in_specs=[
            pl.BlockSpec(memory_space=pltpu.SMEM),
            pl.BlockSpec(memory_space=pltpu.VMEM),
        ],
        out_shape=near_shape((out_rows, images), bf16, keep),
        compiler_params=vmem_params(images * width),
        cost_estimate=pl.CostEstimate(
            flops=2 * images * out_rows * width,
            bytes_accessed=2 * images * width,
            transcendentals=0,
        ),
        name="own_columns",
    )(index, dembed)


def add_pair(kept, arrived):

    def kernel(kept_ref, arrived_ref, sum_ref):
        sum_ref[...] = (kept_ref[...].astype(f32) + arrived_ref[...].astype(f32)).astype(bf16)

    return pl.pallas_call(
        kernel,
        out_shape=jax.ShapeDtypeStruct(kept.shape, bf16),
        compiler_params=vmem_params(kept.size + arrived.size),
        cost_estimate=pl.CostEstimate(
            flops=kept.size, bytes_accessed=6 * kept.size, transcendentals=0
        ),
        name="add_pair",
    )(kept, arrived)


def sum_groups(index, parts, sources, pooled_at, mates, out_rows, extra):
    piece = parts[0].shape[1]
    group_rows = mates * out_rows
    pieces = len(sources)
    block = (pieces * out_rows + len(pooled_at) * extra, piece)

    def kernel(index_ref, *refs):
        part_refs, refs = refs[: len(parts)], refs[len(parts) :]
        block_refs, total_ref = refs[:-1], refs[-1]
        for j in range(pieces):
            total = 0.0
            for at, start in sources[j]:
                total += part_refs[at][start : start + group_rows].astype(f32)
            total_ref[j * group_rows : (j + 1) * group_rows] = total.astype(bf16)
        for j in range(mates):
            mate = lax.rem(index_ref[0], mates) ^ j
            for k in range(pieces):
                start = pl.multiple_of(k * group_rows + mate * out_rows, out_rows)
                block_refs[j][k * out_rows : (k + 1) * out_rows] = total_ref[
                    pl.ds(start, out_rows)
                ]
            for k, (at, first) in enumerate(pooled_at):
                start = pieces * out_rows + k * extra
                block_refs[j][start : start + extra] = part_refs[at][first : first + extra]

    return pl.pallas_call(
        kernel,
        in_specs=[pl.BlockSpec(memory_space=pltpu.SMEM)]
        + [pl.BlockSpec(memory_space=pltpu.VMEM)] * len(parts),
        out_shape=[jax.ShapeDtypeStruct(block, bf16)] * mates,
        scratch_shapes=[pltpu.VMEM((pieces * group_rows, piece), bf16)],
        compiler_params=vmem_params(sum(part.size for part in parts)),
        cost_estimate=pl.CostEstimate(
            flops=sum(part.size for part in parts),
            bytes_accessed=4 * sum(part.size for part in parts),
            transcendentals=0,
        ),
        name="sum_groups",
    )(index, *parts)


def finish(index, blocks, columns, hidden, own_images):
    mates = len(blocks)
    rows, piece = blocks[0].shape
    out_rows, images = columns.shape
    pieces = hidden // mates // piece
    in_rows = out_rows * pieces
    folds = hidden // piece
    extra = own_images * folds
    groups = (rows - in_rows) // extra

    def kernel(index_ref, *refs):
        block_refs, (columns_ref, in_ref, out_ref, wide_ref) = refs[:mates], refs[mates:]
        for j in range(mates):
            mate = lax.rem(index_ref[0], mates) ^ j
            for k in range(pieces):
                start = pl.multiple_of((mate * pieces + k) * piece, piece)
                in_ref[:, pl.ds(start, piece)] = block_refs[j][k * out_rows : (k + 1) * out_rows]
            for k in range(groups):
                sender = ((index_ref[0] // mates) ^ k) * mates + mate
                start = in_rows + k * extra
                taken = block_refs[j][start : start + extra].astype(f32)
                wide_ref[pl.ds(sender * own_images, own_images)] = taken.reshape(
                    own_images, folds, piece
                )
        pooled = jnp.concatenate([wide_ref[:, k, :].astype(bf16) for k in range(folds)], axis=1)
        out_ref[...] = jnp.dot(columns_ref[...], pooled, preferred_element_type=f32).astype(bf16)

    return pl.pallas_call(
        kernel,
        in_specs=[pl.BlockSpec(memory_space=pltpu.SMEM)]
        + [pl.BlockSpec(memory_space=pltpu.VMEM)] * (mates + 1),
        out_shape=[jax.ShapeDtypeStruct((out_rows, hidden), bf16)] * 2,
        scratch_shapes=[pltpu.VMEM((images, folds, piece), f32)],
        compiler_params=vmem_params(2 * images * folds * piece + out_rows * hidden),
        cost_estimate=pl.CostEstimate(
            flops=2 * images * out_rows * hidden,
            bytes_accessed=2 * mates * rows * piece,
            transcendentals=0,
        ),
        name="finish",
    )(index, *blocks, columns)


def exchange(blocks, axes):
    return lax.all_to_all(blocks, axes, split_axis=0, concat_axis=0, tiled=True)


def mates_of(dp_size, hidden):
    mates = 4
    while dp_size % mates or hidden % (lanes * mates):
        mates //= 2
    return mates


def swap(value, axis, step):
    return lax.ppermute(value, axis, [(i, i ^ step) for i in range(lax.axis_size(axis))])


def after(value, other):
    return lax.optimization_barrier((value, other))[0]


def body(tokens, teacher, norm_gain, w_in, b_in, w_out, b_out, final_gain):
    dp_size = lax.axis_size("dp")
    fsdp_size = lax.axis_size("fsdp")
    images = teacher.shape[0] * dp_size
    per_image = tokens.shape[0] // teacher.shape[0]
    hidden = w_in.shape[1]
    mates = mates_of(dp_size, hidden)
    index = lax.axis_index("dp").astype(jnp.int32)[None]
    first = lax.axis_index("fsdp").astype(jnp.int32)[None]

    splits = fsdp_size if teacher.shape[1] % (fsdp_size * 8 * lanes) == 0 else 1

    blocks = {0: tokens}
    for bit in (2, 4, 1):
        if bit < mates:
            blocks[bit] = swap(tokens, "dp", bit)
    all_teacher = exchange(teacher_payload(first, teacher, dp_size, splits), "dp")
    pooled, embed_rows = forward(
        first, tokens, norm_gain, w_in, b_in, w_out, b_out, dp_size * fsdp_size, teacher.shape[0]
    )
    all_embed = exchange(embed_rows, ("dp", "fsdp"))
    gram = target_gram(after(all_teacher, [pooled] + [blocks[k] for k in (1,) if k in blocks]), images)
    for k, source, bit in ((6, 4, 2), (3, 2, 1), (5, 4, 1)):
        if k < mates:
            blocks[k] = swap(after(blocks[source], gram), "dp", bit)
    near_mates = [blocks[k] for k in range(min(mates, 6))]
    slope, turned = mate_slopes(index % mates, near_mates, norm_gain, w_in, b_in, hidden // mates)
    slopes, turns = [slope], [turned]
    if mates > 6:
        blocks[7] = swap(after(blocks[6], [slope, all_embed]), "dp", 1)
        far_mates = [blocks[6], blocks[7]]
        slope, turned = mate_slopes(
            index % mates, far_mates, norm_gain, w_in, b_in, hidden // mates
        )
        slopes, turns = slopes + [slope], turns + [turned]
    if splits == 1:
        grams = [gram]
    elif splits == 2:
        grams = [gram, after(swap(gram, "fsdp", 1), slopes[-1])]
    else:
        grams = [lax.psum(gram, "fsdp")]
    groups = dp_size // mates
    share = hidden // mates
    pieces = share // min(share, 256)
    out_rows = w_out.shape[0] // dp_size
    group_rows = mates * out_rows
    half = pieces // 2
    paired = groups == 4 and half > 0
    if paired:
        sends = [
            [(0, j) for j in range(pieces)],
            [(1, j) for j in range(half)],
            [(2, j) for j in range(half, pieces)],
            [(3, j) for j in range(half, pieces)],
            [(2, j) for j in range(half)],
            [(3, j) for j in range(half)],
            [(1, j) for j in range(half, pieces)],
        ]
    else:
        sends = [[(k, j) for j in range(pieces)] for k in range(groups)]
    pooled_at = [(k, len(sends[k]) * group_rows) for k in range(groups)]
    loss, dembed, *parts = backward(
        index, all_embed, unit_gram(grams), final_gain, pooled, w_out, slopes, turns, sends,
        mates, dp_size, per_image,
    )
    if paired:
        pair = add_pair(parts[groups], swap(parts[groups + 1], "dp", mates))
    swapped = [parts[0]] + [
        swap(parts[k], "dp", k * mates) for k in list(range(2, groups)) + [1] if k < groups
    ]
    if groups > 1:
        swapped.insert(1, swapped.pop())
    if paired:
        swapped.append(swap(pair, "dp", 2 * mates))
        swapped.append(swap(after(parts[groups + 2], swapped[1]), "dp", mates))
        sources = []
        for j in range(pieces):
            arrays, first = ((1, 4), 0) if j < half else ((5, 2, 3), half)
            sources.append(
                [(0, j * group_rows)] + [(k, (j - first) * group_rows) for k in arrays]
            )
    else:
        sources = [[(k, j * group_rows) for k in range(groups)] for j in range(pieces)]
    columns = own_columns(index, dembed, out_rows)
    extra = teacher.shape[0] * hidden // parts[0].shape[1]
    shares = sum_groups(index, swapped, sources, pooled_at, mates, out_rows, extra)
    shares = [shares[0]] + [swap(part, "dp", j + 1) for j, part in enumerate(shares[1:])]
    grad_in, grad_out = finish(index, shares, columns, hidden, teacher.shape[0])
    return (loss[0, 0], grad_in, grad_out)


def solution(mesh):
    return jax.shard_map(
        body,
        mesh=mesh,
        in_specs=(
            P("dp", None),
            P("dp", None),
            P(),
            P(None, "fsdp"),
            P("fsdp"),
            P(None, "fsdp"),
            P(),
            P(),
        ),
        out_specs=(P(), P("dp", "fsdp"), P("dp", "fsdp")),
        check_vma=False,
    )
```

```python
import jax
import jax.numpy as jnp
from jax import lax
from jax.experimental import pallas as pl
from jax.experimental.pallas import tpu as pltpu
from jax.sharding import PartitionSpec as P

loss_scale = 4096.0
lanes = 128
f32 = jnp.float32
bf16 = jnp.bfloat16


def gelu_tanh(values):
    inner = 0.7978845608 * (values + 0.044715 * values * values * values)
    return 0.5 * values * (1.0 + jnp.tanh(inner))


def gelu_slope(values):
    square = values * values
    tangent = jnp.tanh(0.7978845608 * (values + 0.044715 * values * square))
    return 0.5 * (1.0 + tangent) + 0.5 * values * (1.0 - tangent * tangent) * 0.7978845608 * (
        1.0 + 3.0 * 0.044715 * square
    )


def contract_last(left_side, right_side):
    return lax.dot_general(
        left_side, right_side, (((1,), (1,)), ((), ())), preferred_element_type=f32
    )


def fold_rows(values, width):
    count = values.shape[1] // width
    return jnp.concatenate(
        [
            values[i : i + 1, k * width : (k + 1) * width]
            for i in range(values.shape[0])
            for k in range(count)
        ],
        axis=0,
    )


def vmem_params(elements):
    return pltpu.CompilerParams(vmem_limit_bytes=min(56 * 2**20, 8 * elements + 8 * 2**20))


in_hbm = pl.BlockSpec(memory_space=pltpu.HBM)
in_any = pl.BlockSpec(memory_space=pl.ANY)


def hbm(value):
    return pltpu.with_memory_space_constraint(value, pltpu.HBM)


def near(value, keep):
    return pltpu.with_memory_space_constraint(value, pltpu.VMEM) if keep else value


def near_shape(shape, dtype, keep):
    return pltpu.VMEM(shape, dtype) if keep else jax.ShapeDtypeStruct(shape, dtype)


def normalize(values, gain):
    centered = values - jnp.mean(values, axis=-1, keepdims=True)
    inv_std = lax.rsqrt(jnp.mean(centered * centered, axis=-1, keepdims=True) + 1e-05)
    return (centered * inv_std * gain).astype(bf16)


def teacher_payload(first, teacher, copies, splits):
    images = teacher.shape[0]
    features = teacher.shape[1] // splits
    fold = features // 8

    def kernel(first_ref, teacher_ref, out_ref):
        start = 0
        if splits > 1:
            start = pl.multiple_of(first_ref[0] * features, features)
        folded = fold_rows(teacher_ref[:, pl.ds(start, features)].astype(f32), fold).astype(bf16)
        out_ref[...] = jnp.broadcast_to(folded[None], out_ref.shape)

    return pl.pallas_call(
        kernel,
        in_specs=[
            pl.BlockSpec(memory_space=pltpu.SMEM),
            pl.BlockSpec(memory_space=pltpu.VMEM),
        ],
        out_shape=pltpu.HBM((copies, images * 8, fold), bf16),
        compiler_params=vmem_params(copies * images * features),
        cost_estimate=pl.CostEstimate(
            flops=copies * images * features,
            bytes_accessed=2 * copies * images * features,
            transcendentals=0,
        ),
        name="teacher_payload",
    )(first, hbm(teacher))


def forward(first, tokens, norm_gain, w_in, b_in, w_out, b_out, copies, images):
    rows, width = tokens.shape
    hidden = w_in.shape[1]
    per_image = rows // images
    tile = min(512, hidden)
    steps = hidden // tile
    folds = width // lanes

    def kernel(
        first_ref, gain_ref, bias_ref, out_b_ref, tokens_any, in_any_ref, out_any_ref,
        pooled_ref, payload_ref, tokens_ref, in_ref, out_w_ref, sems,
    ):
        loads = [
            pltpu.make_async_copy(
                in_any_ref.at[:, pl.ds(j * tile, tile)], in_ref.at[j], sems.at[j]
            )
            for j in range(steps)
        ]
        loads.append(pltpu.make_async_copy(out_any_ref, out_w_ref, sems.at[steps]))
        loads.append(pltpu.make_async_copy(tokens_any, tokens_ref, sems.at[steps + 1]))
        loads[-1].start()
        for load in loads[:steps]:
            load.start()
        loads[-1].wait()
        loads[steps].start()
        values = tokens_ref[...].astype(f32)
        normed = normalize(values, gain_ref[...])
        token_mean = jnp.mean(values.reshape(images, per_image, width), axis=1)
        for j in range(steps):
            taken = slice(j * tile, (j + 1) * tile)
            loads[j].wait()
            pre_act = jnp.dot(normed, in_ref[j], preferred_element_type=f32) + bias_ref[:, taken]
            pooled_ref[:, taken] = jnp.mean(
                gelu_tanh(pre_act).reshape(images, per_image, tile), axis=1
            ).astype(bf16)
        loads[steps].wait()
        total = contract_last(pooled_ref[...], out_w_ref[...])
        total += jnp.where(first_ref[0] == 0, token_mean + out_b_ref[...], 0.0)
        folded = fold_rows(total, lanes).astype(bf16)
        payload_ref[...] = jnp.broadcast_to(folded[None], payload_ref.shape)

    whole = pl.BlockSpec(memory_space=pltpu.VMEM)
    payload = (copies, images * folds, lanes)
    return pl.pallas_call(
        kernel,
        in_specs=[pl.BlockSpec(memory_space=pltpu.SMEM)] + [whole] * 3 + [in_hbm] * 3,
        out_specs=[whole, whole],
        out_shape=[
            jax.ShapeDtypeStruct((images, hidden), bf16),
            pltpu.HBM(payload, bf16),
        ],
        scratch_shapes=[
            pltpu.VMEM((rows, width), bf16),
            pltpu.VMEM((steps, width, tile), bf16),
            pltpu.VMEM((width, hidden), bf16),
            pltpu.SemaphoreType.DMA((steps + 2,)),
        ],
        compiler_params=vmem_params(
            rows * width + width * hidden + copies * images * width
        ),
        cost_estimate=pl.CostEstimate(
            flops=2 * rows * width * hidden,
            bytes_accessed=4 * width * hidden,
            transcendentals=rows * hidden,
        ),
        name="forward",
    )(
        first, hbm(norm_gain[None]), hbm(b_in[None]), hbm(b_out[None]),
        hbm(tokens), hbm(w_in), hbm(w_out),
    )


def mate_slopes(share_index, blocks, norm_gain, w_in, b_in, share):
    rows, width = blocks[0].shape
    count = len(blocks)
    keep = rows <= 512

    def kernel(index_ref, *refs):
        token_refs = refs[:count]
        gain_ref, bias_ref, in_any_ref, slope_ref, turned_ref = refs[count : count + 5]
        held_ref, in_ref, sems = refs[count + 5 :]
        first_unit = pl.multiple_of(index_ref[0] * share, share)
        weight = pltpu.make_async_copy(
            in_any_ref.at[:, pl.ds(first_unit, share)], in_ref, sems.at[count]
        )
        loads = [
            pltpu.make_async_copy(token_refs[k], held_ref.at[k], sems.at[k]) for k in range(count)
        ]
        loads[0].start()
        weight.start()
        for load in loads[1:]:
            load.start()
        for k in range(count):
            taken = slice(k * rows, (k + 1) * rows)
            loads[k].wait()
            normed = normalize(held_ref[k].astype(f32), gain_ref[...])
            if k == 0:
                weight.wait()
            pre_act = jnp.dot(normed, in_ref[...], preferred_element_type=f32) + bias_ref[...]
            slope_ref[taken] = gelu_slope(pre_act).astype(bf16)
            turned_ref[:, taken] = normed.T

    return pl.pallas_call(
        kernel,
        grid_spec=pltpu.PrefetchScalarGridSpec(
            num_scalar_prefetch=1,
            grid=(1,),
            in_specs=[in_any] * count
            + [
                pl.BlockSpec((1, width), lambda j, s: (0, 0)),
                pl.BlockSpec((1, share), lambda j, s: (0, s[0])),
                in_hbm,
            ],
            out_specs=[
                pl.BlockSpec((count * rows, share), lambda j, s: (0, 0)),
                pl.BlockSpec((width, count * rows), lambda j, s: (0, 0)),
            ],
            scratch_shapes=[
                pltpu.VMEM((count, rows, width), bf16),
                pltpu.VMEM((width, share), bf16),
                pltpu.SemaphoreType.DMA((count + 1,)),
            ],
        ),
        out_shape=[
            near_shape((count * rows, share), bf16, keep),
            near_shape((width, count * rows), bf16, keep),
        ],
        compiler_params=vmem_params(count * rows * (width + share)),
        cost_estimate=pl.CostEstimate(
            flops=2 * rows * count * width * share,
            bytes_accessed=4 * rows * count * width,
            transcendentals=rows * count * share,
        ),
        name="mate_slopes",
    )(
        share_index,
        *[hbm(block) for block in blocks],
        hbm(norm_gain[None]),
        hbm(b_in[None]),
        hbm(w_in),
    )


def target_gram(arrived, images):
    senders, folded, fold = arrived.shape
    folds = senders * folded // images
    keep = images <= 64

    def kernel(arrived_ref, gram_ref, wide_ref):
        wide_ref[...] = arrived_ref[...].astype(f32).reshape(images, folds, fold)
        rows = jnp.concatenate([wide_ref[:, k, :].astype(bf16) for k in range(folds)], axis=1)
        gram_ref[...] = contract_last(rows, rows)

    return pl.pallas_call(
        kernel,
        out_shape=jax.ShapeDtypeStruct((images, images), f32),
        scratch_shapes=[pltpu.VMEM((images, folds, fold), f32)],
        compiler_params=vmem_params(images * folds * fold),
        cost_estimate=pl.CostEstimate(
            flops=2 * images * images * folds * fold,
            bytes_accessed=2 * images * folds * fold,
            transcendentals=0,
        ),
        name="target_gram",
    )(near(arrived, keep))


def unit_gram(parts):
    images = parts[0].shape[0]

    def kernel(*refs):
        gram_ref = refs[-1]
        gram = sum((ref[...] for ref in refs[1:-1]), refs[0][...])
        row = lax.broadcasted_iota(jnp.int32, gram.shape, 0)
        column = lax.broadcasted_iota(jnp.int32, gram.shape, 1)
        diagonal = jnp.where(row == column, gram, 0.0)
        down = lax.rsqrt(jnp.sum(diagonal, axis=1, keepdims=True) + 1e-06)
        across = lax.rsqrt(jnp.sum(diagonal, axis=0, keepdims=True) + 1e-06)
        gram_ref[...] = gram * down * across

    return pl.pallas_call(
        kernel,
        out_shape=jax.ShapeDtypeStruct((images, images), f32),
        compiler_params=vmem_params(4 * images * images),
        cost_estimate=pl.CostEstimate(
            flops=8 * images * images, bytes_accessed=8 * images * images, transcendentals=0
        ),
        name="unit_gram",
    )(*parts)


def backward(
    index, arrived, gram, final_gain, pooled, w_out, slopes, turns, sends, mates, dp_size, per_image
):
    senders, folded, _ = arrived.shape
    width = w_out.shape[0]
    images = gram.shape[0]
    own_images, hidden = pooled.shape
    fsdp_size = senders // dp_size
    folds = width // lanes
    share = hidden // mates
    parts = len(turns)
    part_rows = [turned.shape[1] for turned in turns]
    mate_rows = sum(part_rows)
    out_rows = width // dp_size
    piece = min(share, 256)
    pieces = share // piece
    extra = own_images * hidden // piece
    groups = dp_size // mates
    group_rows = mates * out_rows
    shapes = [
        (len(send) * group_rows + (extra if i < groups else 0), piece)
        for i, send in enumerate(sends)
    ]
    keep = images <= 64

    def kernel(index_ref, arrived_ref, gram_ref, gain_ref, pooled_ref, out_w_any, *refs):
        slope_refs, turned_refs, refs = refs[:parts], refs[parts : 2 * parts], refs[2 * parts :]
        loss_ref, dembed_ref, refs = refs[0], refs[1], refs[2:]
        part_refs, refs = refs[: len(sends)], refs[len(sends) :]
        wide_ref, hidden_ref, out_w_ref, sems = refs[:4]
        payload_refs = refs[4:]
        first_unit = pl.multiple_of(lax.rem(index_ref[0], mates) * share, share)
        load = pltpu.make_async_copy(
            out_w_any.at[:, pl.ds(first_unit, share)], out_w_ref, sems.at[0]
        )
        load.start()
        embeds = arrived_ref[...].astype(f32).reshape(dp_size, fsdp_size, folded, lanes)
        wide_ref[...] = jnp.sum(embeds, axis=1).reshape(images, folds, lanes)
        embedding = jnp.concatenate([wide_ref[:, k, :] for k in range(folds)], axis=1)
        gain = gain_ref[...]
        centered = embedding - jnp.mean(embedding, axis=-1, keepdims=True)
        inv_std = lax.rsqrt(jnp.mean(centered * centered, axis=-1, keepdims=True) + 1e-05)
        normed = centered * inv_std
        scaled = normed * gain
        square = jnp.sum(scaled * scaled, axis=-1, keepdims=True) + 1e-06
        inv_norm = lax.rsqrt(square)
        unit = scaled * inv_norm
        student = unit.astype(bf16)
        resid = contract_last(student, student) - gram_ref[...]
        loss_ref[0, 0] = jnp.sum(resid * resid) / images
        dstudent = (loss_scale * 4.0 / images) * jnp.dot(
            resid.astype(bf16), student, preferred_element_type=f32
        )
        dunit = (dstudent - unit * jnp.sum(unit * dstudent, axis=-1, keepdims=True)) * inv_norm
        gain_grad = dunit * gain
        dembed = inv_std * (
            gain_grad
            - jnp.mean(gain_grad, axis=-1, keepdims=True)
            - normed * jnp.mean(gain_grad * normed, axis=-1, keepdims=True)
        )
        dembed_b = dembed.astype(bf16)
        dembed_ref[...] = dembed_b
        shape = (mates * own_images, images)
        row = lax.broadcasted_iota(jnp.int32, shape, 0)
        column = lax.broadcasted_iota(jnp.int32, shape, 1)
        owner = (row // own_images) ^ index_ref[0]
        pick = (owner * own_images + row % own_images == column).astype(f32).astype(bf16)
        mate_dembed = jnp.dot(pick, dembed_b, preferred_element_type=f32).astype(bf16)
        load.wait()
        dpooled = jnp.dot(mate_dembed, out_w_ref[...], preferred_element_type=f32) / per_image
        k = 0
        for part in range(parts):
            for j in range(part_rows[part] // per_image):
                rows = slice(k * per_image, (k + 1) * per_image)
                taken = slice(j * per_image, (j + 1) * per_image)
                hidden_ref[rows] = (
                    dpooled[k : k + 1] * slope_refs[part][taken].astype(f32)
                ).astype(bf16)
                k += 1
        folded_pooled = fold_rows(pooled_ref[...].astype(f32), piece).astype(bf16)
        stores = []
        for k in list(range(1, groups))[::-1] + [0]:
            first_row = pl.multiple_of(
                ((index_ref[0] // mates) ^ k) * group_rows, group_rows
            )
            term, start = 0.0, 0
            for part in range(parts):
                rows = slice(start, start + part_rows[part])
                start += part_rows[part]
                term += jnp.dot(
                    turned_refs[part][pl.ds(first_row, group_rows)],
                    hidden_ref[rows],
                    preferred_element_type=f32,
                )
            term = term.astype(bf16)
            for i, send in enumerate(sends):
                for at, (group, j) in enumerate(send):
                    if group == k:
                        payload_refs[i][at * group_rows : (at + 1) * group_rows] = term[
                            :, j * piece : (j + 1) * piece
                        ]
        for i, send in enumerate(sends):
            if i < groups:
                payload_refs[i][len(send) * group_rows :] = folded_pooled
            stores.append(pltpu.make_async_copy(payload_refs[i], part_refs[i], sems.at[i]))
            stores[-1].start()
        for store in stores:
            store.wait()

    whole = pl.BlockSpec(memory_space=pltpu.VMEM)
    smem = pl.BlockSpec(memory_space=pltpu.SMEM)
    return pl.pallas_call(
        kernel,
        in_specs=[smem, whole, whole, whole, whole, in_hbm] + [whole] * (2 * parts),
        out_specs=[smem, whole] + [in_any] * len(sends),
        out_shape=[
            jax.ShapeDtypeStruct((1, 1), f32),
            jax.ShapeDtypeStruct((images, width), bf16),
        ]
        + [
            near_shape(shape, bf16, keep) if i in (0, groups) else pltpu.HBM(shape, bf16)
            for i, shape in enumerate(shapes)
        ],
        scratch_shapes=[
            pltpu.VMEM((images, folds, lanes), f32),
            pltpu.VMEM((mate_rows, share), bf16),
            pltpu.VMEM((width, share), bf16),
            pltpu.SemaphoreType.DMA((len(sends),)),
        ]
        + [pltpu.VMEM(shape, bf16) for shape in shapes],
        compiler_params=vmem_params(mate_rows * (width + share) // 2 + arrived.size),
        cost_estimate=pl.CostEstimate(
            flops=2 * mate_rows * width * share,
            bytes_accessed=2 * mate_rows * (width + share),
            transcendentals=0,
        ),
        name="backward",
    )(
        index, near(arrived, keep), gram, hbm(final_gain[None]), pooled, hbm(w_out),
        *[near(slope, keep) for slope in slopes], *[near(turned, keep) for turned in turns],
    )


def own_columns(index, dembed, out_rows):
    images, width = dembed.shape
    keep = images <= 64

    def kernel(index_ref, dembed_ref, columns_ref):
        row = lax.broadcasted_iota(jnp.int32, (out_rows, width), 0)
        column = lax.broadcasted_iota(jnp.int32, (out_rows, width), 1)
        pick = (row + index_ref[0] * out_rows == column).astype(f32).astype(bf16)
        columns_ref[...] = contract_last(pick, dembed_ref[...]).astype(bf16)

    return pl.pallas_call(
        kernel,
        in_specs=[
            pl.BlockSpec(memory_space=pltpu.SMEM),
            pl.BlockSpec(memory_space=pltpu.VMEM),
        ],
        out_shape=near_shape((out_rows, images), bf16, keep),
        compiler_params=vmem_params(images * width),
        cost_estimate=pl.CostEstimate(
            flops=2 * images * out_rows * width,
            bytes_accessed=2 * images * width,
            transcendentals=0,
        ),
        name="own_columns",
    )(index, dembed)


def add_pair(kept, arrived):

    def kernel(kept_ref, arrived_ref, sum_ref):
        sum_ref[...] = (kept_ref[...].astype(f32) + arrived_ref[...].astype(f32)).astype(bf16)

    return pl.pallas_call(
        kernel,
        out_shape=jax.ShapeDtypeStruct(kept.shape, bf16),
        compiler_params=vmem_params(kept.size + arrived.size),
        cost_estimate=pl.CostEstimate(
            flops=kept.size, bytes_accessed=6 * kept.size, transcendentals=0
        ),
        name="add_pair",
    )(kept, arrived)


def sum_groups(index, parts, sources, pooled_at, mates, out_rows, extra):
    piece = parts[0].shape[1]
    group_rows = mates * out_rows
    pieces = len(sources)
    block = (pieces * out_rows + len(pooled_at) * extra, piece)

    def kernel(index_ref, *refs):
        part_refs, refs = refs[: len(parts)], refs[len(parts) :]
        block_refs, total_ref = refs[:-1], refs[-1]
        for j in range(pieces):
            total = 0.0
            for at, start in sources[j]:
                total += part_refs[at][start : start + group_rows].astype(f32)
            total_ref[j * group_rows : (j + 1) * group_rows] = total.astype(bf16)
        for j in range(mates):
            mate = lax.rem(index_ref[0], mates) ^ j
            for k in range(pieces):
                start = pl.multiple_of(k * group_rows + mate * out_rows, out_rows)
                block_refs[j][k * out_rows : (k + 1) * out_rows] = total_ref[
                    pl.ds(start, out_rows)
                ]
            for k, (at, first) in enumerate(pooled_at):
                start = pieces * out_rows + k * extra
                block_refs[j][start : start + extra] = part_refs[at][first : first + extra]

    return pl.pallas_call(
        kernel,
        in_specs=[pl.BlockSpec(memory_space=pltpu.SMEM)]
        + [pl.BlockSpec(memory_space=pltpu.VMEM)] * len(parts),
        out_shape=[jax.ShapeDtypeStruct(block, bf16)] * mates,
        scratch_shapes=[pltpu.VMEM((pieces * group_rows, piece), bf16)],
        compiler_params=vmem_params(sum(part.size for part in parts)),
        cost_estimate=pl.CostEstimate(
            flops=sum(part.size for part in parts),
            bytes_accessed=4 * sum(part.size for part in parts),
            transcendentals=0,
        ),
        name="sum_groups",
    )(index, *parts)


def finish(index, blocks, columns, hidden, own_images):
    mates = len(blocks)
    rows, piece = blocks[0].shape
    out_rows, images = columns.shape
    pieces = hidden // mates // piece
    in_rows = out_rows * pieces
    folds = hidden // piece
    extra = own_images * folds
    groups = (rows - in_rows) // extra

    def kernel(index_ref, *refs):
        block_refs, (columns_ref, in_ref, out_ref, wide_ref) = refs[:mates], refs[mates:]
        for j in range(mates):
            mate = lax.rem(index_ref[0], mates) ^ j
            for k in range(pieces):
                start = pl.multiple_of((mate * pieces + k) * piece, piece)
                in_ref[:, pl.ds(start, piece)] = block_refs[j][k * out_rows : (k + 1) * out_rows]
            for k in range(groups):
                sender = ((index_ref[0] // mates) ^ k) * mates + mate
                start = in_rows + k * extra
                taken = block_refs[j][start : start + extra].astype(f32)
                wide_ref[pl.ds(sender * own_images, own_images)] = taken.reshape(
                    own_images, folds, piece
                )
        pooled = jnp.concatenate([wide_ref[:, k, :].astype(bf16) for k in range(folds)], axis=1)
        out_ref[...] = jnp.dot(columns_ref[...], pooled, preferred_element_type=f32).astype(bf16)

    return pl.pallas_call(
        kernel,
        in_specs=[pl.BlockSpec(memory_space=pltpu.SMEM)]
        + [pl.BlockSpec(memory_space=pltpu.VMEM)] * (mates + 1),
        out_shape=[jax.ShapeDtypeStruct((out_rows, hidden), bf16)] * 2,
        scratch_shapes=[pltpu.VMEM((images, folds, piece), f32)],
        compiler_params=vmem_params(2 * images * folds * piece + out_rows * hidden),
        cost_estimate=pl.CostEstimate(
            flops=2 * images * out_rows * hidden,
            bytes_accessed=2 * mates * rows * piece,
            transcendentals=0,
        ),
        name="finish",
    )(index, *blocks, columns)


def exchange(blocks, axes):
    return lax.all_to_all(blocks, axes, split_axis=0, concat_axis=0, tiled=True)


def mates_of(dp_size, hidden):
    mates = 4
    while dp_size % mates or hidden % (lanes * mates):
        mates //= 2
    return mates


def swap(value, axis, step):
    return lax.ppermute(value, axis, [(i, i ^ step) for i in range(lax.axis_size(axis))])


def after(value, other):
    return lax.optimization_barrier((value, other))[0]


def body(tokens, teacher, norm_gain, w_in, b_in, w_out, b_out, final_gain):
    dp_size = lax.axis_size("dp")
    fsdp_size = lax.axis_size("fsdp")
    images = teacher.shape[0] * dp_size
    per_image = tokens.shape[0] // teacher.shape[0]
    hidden = w_in.shape[1]
    mates = mates_of(dp_size, hidden)
    index = lax.axis_index("dp").astype(jnp.int32)[None]
    first = lax.axis_index("fsdp").astype(jnp.int32)[None]

    splits = fsdp_size if teacher.shape[1] % (fsdp_size * 8 * lanes) == 0 else 1

    blocks = {0: tokens}
    for bit in (2, 4, 1):
        if bit < mates:
            blocks[bit] = swap(tokens, "dp", bit)
    all_teacher = exchange(teacher_payload(first, teacher, dp_size, splits), "dp")
    pooled, embed_rows = forward(
        first, tokens, norm_gain, w_in, b_in, w_out, b_out, dp_size * fsdp_size, teacher.shape[0]
    )
    all_embed = exchange(embed_rows, ("dp", "fsdp"))
    gram = target_gram(after(all_teacher, [pooled] + [blocks[k] for k in (1,) if k in blocks]), images)
    for k, source, bit in ((6, 4, 2), (3, 2, 1), (5, 4, 1)):
        if k < mates:
            blocks[k] = swap(after(blocks[source], gram), "dp", bit)
    near_mates = [blocks[k] for k in range(min(mates, 6))]
    slope, turned = mate_slopes(index % mates, near_mates, norm_gain, w_in, b_in, hidden // mates)
    slopes, turns = [slope], [turned]
    if mates > 6:
        blocks[7] = swap(after(blocks[6], [slope, all_embed]), "dp", 1)
        far_mates = [blocks[6], blocks[7]]
        slope, turned = mate_slopes(
            index % mates, far_mates, norm_gain, w_in, b_in, hidden // mates
        )
        slopes, turns = slopes + [slope], turns + [turned]
    if splits == 1:
        grams = [gram]
    elif splits == 2:
        grams = [gram, after(swap(gram, "fsdp", 1), slopes[-1])]
    else:
        grams = [lax.psum(gram, "fsdp")]
    groups = dp_size // mates
    share = hidden // mates
    pieces = share // min(share, 256)
    out_rows = w_out.shape[0] // dp_size
    group_rows = mates * out_rows
    half = pieces // 2
    paired = groups == 4 and half > 0
    if paired:
        sends = [
            [(0, j) for j in range(pieces)],
            [(1, j) for j in range(half)],
            [(2, j) for j in range(half, pieces)],
            [(3, j) for j in range(half, pieces)],
            [(2, j) for j in range(half)],
            [(3, j) for j in range(half)],
            [(1, j) for j in range(half, pieces)],
        ]
    else:
        sends = [[(k, j) for j in range(pieces)] for k in range(groups)]
    pooled_at = [(k, len(sends[k]) * group_rows) for k in range(groups)]
    loss, dembed, *parts = backward(
        index, all_embed, unit_gram(grams), final_gain, pooled, w_out, slopes, turns, sends,
        mates, dp_size, per_image,
    )
    if paired:
        pair = add_pair(parts[groups], swap(parts[groups + 1], "dp", mates))
    swapped = [parts[0]] + [
        swap(parts[k], "dp", k * mates) for k in list(range(2, groups)) + [1] if k < groups
    ]
    if groups > 1:
        swapped.insert(1, swapped.pop())
    if paired:
        swapped.append(swap(pair, "dp", 2 * mates))
        swapped.append(swap(after(parts[groups + 2], swapped[1]), "dp", mates))
        sources = []
        for j in range(pieces):
            arrays, first = ((1, 4), 0) if j < half else ((5, 2, 3), half)
            sources.append(
                [(0, j * group_rows)] + [(k, (j - first) * group_rows) for k in arrays]
            )
    else:
        sources = [[(k, j * group_rows) for k in range(groups)] for j in range(pieces)]
    columns = own_columns(index, dembed, out_rows)
    extra = teacher.shape[0] * hidden // parts[0].shape[1]
    shares = sum_groups(index, swapped, sources, pooled_at, mates, out_rows, extra)
    shares = [shares[0]] + [swap(part, "dp", j + 1) for j, part in enumerate(shares[1:])]
    grad_in, grad_out = finish(index, shares, columns, hidden, teacher.shape[0])
    return (loss[0, 0], grad_in, grad_out)


def solution(mesh):
    return jax.shard_map(
        body,
        mesh=mesh,
        in_specs=(
            P("dp", None),
            P("dp", None),
            P(),
            P(None, "fsdp"),
            P("fsdp"),
            P(None, "fsdp"),
            P(),
            P(),
        ),
        out_specs=(P(), P("dp", "fsdp"), P("dp", "fsdp")),
        check_vma=False,
    )
```
